32 devices in a mesh: dp: 4 (over y, core), seq: 8 (over z, x).
Axes of the slice: x: 2, y: 2, z: 4, core: 2. Of those that a mesh axis runs over, the one named last changes fastest.
Arguments:
- hidden: bfloat16 [4, 2048, 2048], P('dp', 'seq'), may hold values from -6 to 6
- targets: int32 [4, 2048], P('dp'), may hold values from 0 to 26623
- lengths: int32 [4, 8], P('dp'), may hold values from 1 to 1024, 2048 in all within a row
- labels: int32 [4, 8], P('dp'), may hold values 0 or 1
- ref_logps: float32 [4, 8], P('dp'), may hold values from -26 to -1
- ln1_gain: bfloat16 [2048], replicated, may hold values from 0.5 to 1.5
- ln1_bias: bfloat16 [2048], replicated, may hold values from -1.796875 to 1.796875
- ln2_gain: bfloat16 [2048], replicated, may hold values from 0.5 to 1.5
- ln2_bias: bfloat16 [2048], replicated, may hold values from -1.796875 to 1.796875
- qkv_weight: bfloat16 [2048, 16, 384], P(None, 'seq'), may hold values from -0.125 to 0.125
- qv_bias: bfloat16 [16, 256], P('seq'), may hold values from -1.796875 to 1.796875
- out_weight: bfloat16 [16, 128, 2048], P('seq'), may hold values from -0.5 to 0.5
- up_weight: bfloat16 [2048, 8192], P(None, 'seq'), may hold values from -0.125 to 0.125
- up_bias: bfloat16 [8192], P('seq'), may hold values from -1.796875 to 1.796875
- down_weight: bfloat16 [8192, 2048], P('seq'), may hold values from -0.0625 to 0.0625
- branch_bias: bfloat16 [2048], replicated, may hold values from -1.796875 to 1.796875
- lnf_gain: bfloat16 [2048], replicated, may hold values from 0.5 to 1.5
- lnf_bias: bfloat16 [2048], replicated, may hold values from -1.796875 to 1.796875
- head_weight: bfloat16 [2048, 26624], P(None, 'seq'), may hold values from -0.25 to 0.25
Outputs:
- losses: float32 [4, 8], P('dp')
- output: bfloat16 [4, 2048, 2048], P('dp', 'seq')
- grad_hidden: float32 [4, 2048, 2048], P('dp', 'seq')
- grad_ln1_gain: float32 [2048], replicated
- grad_ln1_bias: float32 [2048], replicated
- grad_ln2_gain: float32 [2048], replicated
- grad_ln2_bias: float32 [2048], replicated
- grad_qkv_weight: float32 [2048, 16, 384], P(None, 'seq')
- grad_qv_bias: float32 [16, 256], P('seq')
- grad_out_weight: float32 [16, 128, 2048], P('seq')
- grad_up_weight: float32 [2048, 8192], P(None, 'seq')
- grad_up_bias: float32 [8192], P('seq')
- grad_down_weight: float32 [8192, 2048], P('seq')
- grad_branch_bias: float32 [2048], replicated
- grad_lnf_gain: float32 [2048], replicated
- grad_lnf_bias: float32 [2048], replicated
- grad_head_weight: float32 [2048, 26624], P(None, 'seq')
The draws below stay inside these ranges and needn't reach their ends.
Inputs may be any that keep to these rules, and one draw needn't show every extreme that they name: Each block's lengths sum to 2048; the longest example of every block has exactly 1024 rows. `labels`: 1 marks a desirable example, 0 an undesirable one.
All inputs are finite; a program needn't handle non-finite values. No bound on the sum of `labels` on one device may be relied on, other than what follows from the above.
Results may differ from the reference program's by a relative error of at most 0.018.
Values may be sent and summed in bfloat16 or wider, within the bound.
A program may use at most 256 MiB of HBM per device.

```python
import math
import jax
import jax.numpy as jnp
import numpy as np
from jax import lax

D = 2048
HEADS = 16
HEAD_DIM = 128
ROT = 32
FF = 8192
VOCAB = 26624
BLOCK = 2048
EXB = 8
ATT_BLK = 512
BLOCKS = 4


def draw_ref_logps(key, part):
    key = jax.random.fold_in(key, 7)
    rise = jnp.arange(BLOCKS, dtype=jnp.float32)[:, None] / max(BLOCKS - 1, 1)
    spread_part = jax.random.uniform(key, (BLOCKS, EXB), jnp.float32, -1.5, 1.5)
    values = -4.0 - 12.0 * rise + spread_part
    return values.astype(jnp.float32)


def plant(entries, own_key, least, largest):
    spot = [jax.random.randint(jax.random.fold_in(own_key, axis), (), 0, length) for axis, length in enumerate(entries.shape)]
    main_axis = entries.shape.index(max(entries.shape))
    next_to = spot[:main_axis] + [(spot[main_axis] + 1) % entries.shape[main_axis]] + spot[main_axis + 1:]
    return entries.at[tuple(spot)].set(least).at[tuple(next_to)].set(largest)


def level_of(key, dims, shards, low, largest):
    def one(dim, parts):
        steps = jax.random.uniform(jax.random.fold_in(jax.random.fold_in(key, 6), dim), (parts,), jnp.float32, low / len(shards), largest / len(shards))
        return jnp.repeat(jnp.exp(steps), dims[dim] // parts).reshape((-1,) + (1,) * (len(dims) - dim - 1))

    loudness = one(*shards[0])
    for cut in shards[1:]:
        loudness = loudness * one(*cut)
    return loudness


def rank_bounds(amount, skew):
    loads = [(1 << 20) // math.isqrt(rank ** skew) + 1 for rank in range(1, amount + 1)]
    deviation = 1 + sum(loads) // (1 << 30)
    return np.cumsum(np.array([max(1, weight // deviation) for weight in loads]))


def ranked(own_key, extent, amount, lean):
    grid = rank_bounds(amount, lean)
    lot = jax.random.randint(jax.random.fold_in(own_key, 1), extent, 0, int(grid[amount - 1]))
    rank = jnp.searchsorted(jnp.asarray(grid, jnp.int32), lot, side="right")
    return jax.random.permutation(jax.random.fold_in(own_key, 2), amount)[rank].astype(jnp.int32)


def profile(amount, total, reach, skew):
    weights = [(1 << 20) // math.isqrt(rank ** skew) + 1 for rank in range(2, amount + 1)]
    surplus, counts = total - reach - (amount - 1), [1] * (amount - 1)
    while surplus > 0:
        free = [i for i in range(amount - 1) if counts[i] < reach]
        whole, left = sum([weights[i] for i in free]), surplus
        for i in free:
            addition = min(reach - counts[i], max(1, left * weights[i] // whole), surplus)
            counts[i] = counts[i] + addition
            surplus = surplus - addition
    return np.array([reach] + counts)


def uneven_parts(stream_key, amount, total, limit, skew):
    if amount == 2:
        one = jax.random.randint(stream_key, (), max(1, total - limit), min(limit, total - 1) + 1)
        return jnp.stack([one, total - one])
    sizes = jnp.asarray(profile(amount, total, limit, skew), jnp.int32)
    twos = (amount - 1) // 2
    giver, sink = sizes[1:1 + 2 * twos:2], sizes[2:2 + 2 * twos:2]
    margin = jnp.minimum(giver - 1, limit - sink)
    shifted = jax.random.randint(jax.random.fold_in(stream_key, 1), (twos,), 0, 1 << 20) % (margin + 1)
    sizes = sizes.at[1:1 + 2 * twos:2].set(giver - shifted).at[2:2 + 2 * twos:2].set(sink + shifted)
    return sizes[jax.random.permutation(jax.random.fold_in(stream_key, 2), amount)]


def normal_values(key, dims, deviation, most, shards=(), kind=jnp.bfloat16):
    values = jax.random.normal(key, dims, jnp.float32) * deviation
    if len(shards) > 0:
        values = level_of(key, dims, shards, -0.22, 0.18) * values
    return jnp.clip(values, min=-most, max=most).astype(kind)


def setup_inputs(seed: int = 0) -> dict:
    streams_of = jax.random.split(jax.random.key(seed), 20)
    return {
        "hidden": normal_values(streams_of[0], (BLOCKS, BLOCK, D), 1.0, 6.0, ((0, 4), (1, 8))),
        "targets": plant(ranked(streams_of[1], (BLOCKS, BLOCK), VOCAB, 2), jax.random.fold_in(streams_of[1], 3), 0, VOCAB - 1).astype(jnp.int32),
        "lengths": jax.vmap(lambda own: uneven_parts(own, EXB, BLOCK, BLOCK // 2, 1))(jax.random.split(streams_of[2], BLOCKS)).reshape((BLOCKS, EXB)).astype(jnp.int32),
        "labels": plant((jax.random.randint(streams_of[3], (BLOCKS, EXB), 0, 2) < 1).astype(jnp.int32), jax.random.fold_in(streams_of[3], 1), 0, 1),
        "ref_logps": draw_ref_logps(jax.random.fold_in(streams_of[19], 71), 0),
        "ln1_gain": jnp.clip(1.0 + 0.1 * jax.random.normal(streams_of[5], (D,), jnp.float32), 0.5, 1.5).astype(jnp.bfloat16),
        "ln1_bias": normal_values(streams_of[6], (D,), 0.3, 1.796875),
        "ln2_gain": jnp.clip(1.0 + 0.1 * jax.random.normal(streams_of[7], (D,), jnp.float32), 0.5, 1.5).astype(jnp.bfloat16),
        "ln2_bias": normal_values(streams_of[8], (D,), 0.3, 1.796875),
        "qkv_weight": normal_values(streams_of[9], (D, HEADS, 3 * HEAD_DIM), D ** -0.5, 0.125, ((1, 8),)),
        "qv_bias": normal_values(streams_of[10], (HEADS, 2 * HEAD_DIM), 0.3, 1.796875, ((0, 8),)),
        "out_weight": normal_values(streams_of[11], (HEADS, HEAD_DIM, D), HEAD_DIM ** -0.5, 0.5, ((0, 8),)),
        "up_weight": normal_values(streams_of[12], (D, FF), D ** -0.5, 0.125, ((1, 8),)),
        "up_bias": normal_values(streams_of[13], (FF,), 0.3, 1.796875, ((0, 8),)),
        "down_weight": normal_values(streams_of[14], (FF, D), FF ** -0.5, 0.0625, ((0, 8),)),
        "branch_bias": normal_values(streams_of[15], (D,), 0.3, 1.796875),
        "lnf_gain": jnp.clip(1.0 + 0.1 * jax.random.normal(streams_of[16], (D,), jnp.float32), 0.5, 1.5).astype(jnp.bfloat16),
        "lnf_bias": normal_values(streams_of[17], (D,), 0.3, 1.796875),
        "head_weight": normal_values(streams_of[18], (D, VOCAB), (D // 4) ** -0.5, 0.25, ((1, 8),)),
    }


@jax.custom_vjp
def low(v):
    return lax.optimization_barrier(v.astype(jnp.bfloat16)).astype(jnp.float32)

@jax.custom_vjp
def low_back(v):
    return v

def low_keep(v):
    return (low(v), None)

def low_pass(kept, grad):
    return (grad,)

def back_keep(v):
    return (v, None)

def back_low(kept, grad):
    return (low(grad),)
low.defvjp(low_keep, low_pass)
low_back.defvjp(back_keep, back_low)
EPSILON = 1e-05
BETA = 0.25
LOSS_SCALE = 65536.0
HIGHEST = lax.Precision.HIGHEST

def layer_norm(values, norm_gain, norm_shift):
    centered = values - lax.optimization_barrier(jnp.mean(values, axis=-1, keepdims=True))
    spread = lax.optimization_barrier(jnp.mean(centered * centered, axis=-1, keepdims=True))
    return centered * lax.rsqrt(spread + EPSILON) * norm_gain + norm_shift

def segment_rows(block_lengths):
    row_ends = jnp.cumsum(block_lengths)
    row_ids = jnp.arange(BLOCK, dtype=jnp.int32)
    passed = (row_ids[:, None] >= row_ends[None, :]).astype(jnp.int32)
    segment = lax.optimization_barrier(jnp.sum(passed, axis=1))
    position = row_ids - lax.optimization_barrier(jnp.sum(passed * block_lengths[None, :], axis=1))
    return (segment, position)

def rotate(vector, position):
    half_rot = ROT // 2
    frequency = 10000.0 ** (-2.0 * jnp.arange(half_rot, dtype=jnp.float32) / ROT)
    angles = position.astype(jnp.float32)[:, None] * frequency[None, :]
    cos_table = jnp.cos(angles)[:, None, :]
    sin_table = jnp.sin(angles)[:, None, :]
    first_half = vector[..., :half_rot]
    second_half = vector[..., half_rot:ROT]
    return jnp.concatenate([first_half * cos_table - second_half * sin_table, second_half * cos_table + first_half * sin_table, vector[..., ROT:]], axis=-1)

def attend(queries, key_rows, values, segment):
    row_ids = jnp.arange(BLOCK, dtype=jnp.int32)

    def one_block(block_index):
        first_row = block_index * ATT_BLK
        query_block = lax.dynamic_slice_in_dim(queries, first_row, ATT_BLK, 0)
        query_ids = lax.dynamic_slice_in_dim(row_ids, first_row, ATT_BLK, 0)
        query_seg = lax.dynamic_slice_in_dim(segment, first_row, ATT_BLK, 0)
        scores = low_back(HEAD_DIM ** (-0.5) * jnp.einsum('qhd,khd->hqk', query_block, key_rows, precision=HIGHEST))
        allowed = (query_seg[:, None] == segment[None, :]) & (row_ids[None, :] <= query_ids[:, None])
        scores = jnp.where(allowed[None], scores, -1e+30)
        weights = jnp.exp(scores - lax.optimization_barrier(jnp.max(scores, axis=-1, keepdims=True)))
        prob_rows = weights / lax.optimization_barrier(jnp.sum(weights, axis=-1, keepdims=True))
        return jnp.einsum('hqk,khd->qhd', low(prob_rows), values, precision=HIGHEST)
    blocks_out = lax.map(jax.checkpoint(one_block), jnp.arange(BLOCK // ATT_BLK, dtype=jnp.int32))
    return blocks_out.reshape(BLOCK, HEADS * HEAD_DIM)

def block_forward(params, inputs, block_targets, block_lengths):
    segment, position = segment_rows(block_lengths)
    first_norm = low(layer_norm(inputs, params['ln1_gain'], params['ln1_bias']))
    second_norm = low(layer_norm(inputs, params['ln2_gain'], params['ln2_bias']))
    qv_part = params['qv_bias']
    full_bias = jnp.concatenate([qv_part[:, :HEAD_DIM], jnp.zeros_like(qv_part[:, :HEAD_DIM]), qv_part[:, HEAD_DIM:]], axis=-1)
    projected = low_back(jnp.einsum('nd,dhe->nhe', first_norm, params['qkv_weight'], precision=HIGHEST) + full_bias)
    queries = low(rotate(projected[..., :HEAD_DIM], position))
    key_rows = low(rotate(projected[..., HEAD_DIM:2 * HEAD_DIM], position))
    values = low(projected[..., 2 * HEAD_DIM:])
    context = low(low_back(attend(queries, key_rows, values, segment)))
    up_pre = low_back(jnp.dot(second_norm, params['up_weight'], precision=HIGHEST) + params['up_bias'])
    activated = low(jax.nn.gelu(up_pre, approximate=False))
    branch = low_back(jnp.dot(context, params['out_weight'].reshape(HEADS * HEAD_DIM, D), precision=HIGHEST) + jnp.dot(activated, params['down_weight'], precision=HIGHEST))
    stream = inputs + branch + params['branch_bias']
    final_norm = low(layer_norm(stream, params['lnf_gain'], params['lnf_bias']))
    vocab_ids = jnp.arange(VOCAB, dtype=jnp.int32)

    def logit_block(block_index):
        first_row = block_index * ATT_BLK
        rows_in = lax.dynamic_slice_in_dim(final_norm, first_row, ATT_BLK, 0)
        row_targets = lax.dynamic_slice_in_dim(block_targets, first_row, ATT_BLK, 0)
        logits = low_back(jnp.dot(rows_in, params['head_weight'], precision=HIGHEST))
        row_top = lax.optimization_barrier(jnp.max(logits, axis=-1, keepdims=True))
        log_total = row_top[:, 0] + jnp.log(lax.optimization_barrier(jnp.sum(jnp.exp(logits - row_top), axis=-1)))
        picked = lax.optimization_barrier(jnp.sum(jnp.where(vocab_ids[None, :] == row_targets[:, None], logits, 0.0), axis=-1))
        return picked - log_total
    token_logp = lax.map(jax.checkpoint(logit_block), jnp.arange(BLOCK // ATT_BLK, dtype=jnp.int32)).reshape(BLOCK)
    member = (segment[:, None] == jnp.arange(EXB, dtype=jnp.int32)[None, :]).astype(token_logp.dtype)
    mean_logp = lax.optimization_barrier(jnp.sum(member * token_logp[:, None], axis=0)) / block_lengths.astype(token_logp.dtype)
    return (mean_logp, stream)

def reference(hidden, targets, lengths, labels, ref_logps, ln1_gain, ln1_bias, ln2_gain, ln2_bias, qkv_weight, qv_bias, out_weight, up_weight, up_bias, down_weight, branch_bias, lnf_gain, lnf_bias, head_weight):
    params = {'ln1_gain': ln1_gain.astype(jnp.float32), 'ln1_bias': ln1_bias.astype(jnp.float32), 'ln2_gain': ln2_gain.astype(jnp.float32), 'ln2_bias': ln2_bias.astype(jnp.float32), 'qkv_weight': qkv_weight.astype(jnp.float32), 'qv_bias': qv_bias.astype(jnp.float32), 'out_weight': out_weight.astype(jnp.float32), 'up_weight': up_weight.astype(jnp.float32), 'up_bias': up_bias.astype(jnp.float32), 'down_weight': down_weight.astype(jnp.float32), 'branch_bias': branch_bias.astype(jnp.float32), 'lnf_gain': lnf_gain.astype(jnp.float32), 'lnf_bias': lnf_bias.astype(jnp.float32), 'head_weight': head_weight.astype(jnp.float32)}
    inputs = hidden.astype(jnp.float32)

    def forward(weights_in, rows_in):

        def step(carry, item):
            mean_logp, stream = block_forward(weights_in, item[0], item[1], item[2])
            return (carry, (mean_logp, stream))
        carry_out, outputs = lax.scan(jax.checkpoint(step), jnp.zeros((), jnp.float32), (rows_in, targets, lengths))
        return outputs
    (mean_logp, stream), pullback = jax.vjp(forward, params, inputs)
    log_ratio = mean_logp - ref_logps
    center = jnp.mean(log_ratio)
    label_sign = (2 * labels - 1).astype(log_ratio.dtype)

    def kto_loss(ratio_in):
        return 1.0 - jax.nn.sigmoid(BETA * label_sign * (ratio_in - center))
    losses, loss_pull = jax.vjp(kto_loss, log_ratio)
    grad_ratio, = loss_pull(jnp.full_like(losses, LOSS_SCALE))
    grads, grad_inputs = pullback((grad_ratio, jnp.zeros_like(stream)))
    return (losses, stream.astype(jnp.bfloat16), grad_inputs, grads['ln1_gain'], grads['ln1_bias'], grads['ln2_gain'], grads['ln2_bias'], grads['qkv_weight'], grads['qv_bias'], grads['out_weight'], grads['up_weight'], grads['up_bias'], grads['down_weight'], grads['branch_bias'], grads['lnf_gain'], grads['lnf_bias'], grads['head_weight'])
```

```python
import jax
import jax.numpy as jnp
from jax import lax
from jax.experimental import pallas as pl
from jax.experimental.pallas import tpu as pltpu
from jax.sharding import PartitionSpec as P

D = 2048
HEAD_DIM = 128
ROT = 32
BLOCK = 2048
EXB = 8
ATT_BLK = 512


EPSILON = 1e-05
BETA = 0.25
LOSS_SCALE = 65536.0


MESH = pl.DeviceIdType.MESH


class Grid2:
    def __init__(self, sizes):
        self.n = sizes
        place = lax.axis_index("seq")
        self.me = (place // sizes[1], lax.rem(place, sizes[1]))

    def index(self, slow, fast):
        return slow * self.n[1] + fast

    def device(self, axis, spot):
        here = list(self.me)
        here[axis] = spot
        return {"seq": self.index(*here)}

    def nearest(self, axis, rank):
        n, m = self.n[axis], self.me[axis]
        if rank == 0:
            return m
        if n == 2:
            return 1 - m
        after = n - 1 - m
        both = jnp.minimum(m, after)
        dist = (rank + 1) // 2
        near = m - dist if rank % 2 else m + dist
        far = jnp.where(m < after, m + (rank - both), m - (rank - both))
        return jnp.where(rank <= 2 * both, near, far)

    def neighbours(self):
        found = []
        for axis in (0, 1):
            m, n = self.me[axis], self.n[axis]
            if n == 2:
                found.append((None, self.device(axis, 1 - m)))
            elif n > 2:
                found.append((m > 0, self.device(axis, m - 1)))
                found.append((m < n - 1, self.device(axis, m + 1)))
        return found

    def barrier(self):
        sem = pltpu.get_barrier_semaphore()
        amount = jnp.int32(0)
        for there, device in self.neighbours():
            def tell(device=device):
                pl.semaphore_signal(sem, inc=1, device_id=device, device_id_type=MESH)
            if there is None:
                tell()
                amount = amount + 1
            else:
                pl.when(there)(tell)
                amount = amount + there.astype(jnp.int32)
        pl.semaphore_wait(sem, amount)


class Sender:
    def __init__(self, send_sems):
        self.sems = send_sems
        self.used = 0
        self.open = []

    def send(self, src, dst, recv_sem, device, when=None):
        copy = pltpu.make_async_remote_copy(
            src_ref=src, dst_ref=dst, send_sem=self.sems.at[self.used], recv_sem=recv_sem,
            device_id=device, device_id_type=MESH)
        self.used += 1
        if when is None:
            copy.start()
        else:
            pl.when(when)(copy.start)
        self.open.append((when, copy))

    def finish(self):
        for when, copy in self.open:
            if when is None:
                copy.wait_send()
            else:
                pl.when(when)(copy.wait_send)
        self.open = []


def gather_sends(sizes, halves):
    return halves * 2 * (sizes[0] * sizes[1] * 2 + 8)


def gather_rounds(grid, sender, piece, recv_sems, halves, cut, ready):
    n, me = grid.n, grid.me

    def arrived(slow, fast, half, kind):
        ref = piece(grid.index(slow, fast), half, kind)
        sem = recv_sems.at[kind, half, grid.index(slow, fast)]
        pltpu.make_async_copy(ref, ref, sem).wait()

    def push(slow, fast, half, kind, axis, spot, when):
        ref = piece(grid.index(slow, fast), half, kind)
        sem = recv_sems.at[kind, half, grid.index(slow, fast)]
        sender.send(ref, ref, sem, grid.device(axis, spot), when)

    def spread(slow, fast, half, kind, axis):
        m, size = me[axis], n[axis]
        if size == 2:
            push(slow, fast, half, kind, axis, 1 - m, None)
        elif size > 2:
            push(slow, fast, half, kind, axis, m + 1, m < size - 1)
            push(slow, fast, half, kind, axis, m - 1, m > 0)

    def onward(slow, fast, half, kind, axis):
        m, size = me[axis], n[axis]
        if size <= 2:
            return
        source = (slow, fast)[axis]
        below = source < m
        when = (below & (m < size - 1)) | (jnp.logical_not(below) & (m > 0))
        push(slow, fast, half, kind, axis, jnp.where(below, m + 1, m - 1), when)

    todo = []

    def work(count=1):
        for _ in range(count):
            if todo:
                ready(*todo.pop(0))

    def settle(k):
        slow = grid.nearest(0, k)
        for half in range(halves):
            for l in range(n[1]):
                fast = grid.nearest(1, l)
                if k > 0:
                    arrived(slow, fast, half, 1)
                    onward(slow, fast, half, 1, 0)
                else:
                    spread(slow, fast, half, 1, 0)

    def complete(k):
        slow = grid.nearest(0, k)
        if k > 0:
            todo.append((slow, me[1], k * n[1]))
        for l in range(1, n[1]):
            fast = grid.nearest(1, l)
            if cut[0]:
                for half in range(halves):
                    arrived(slow, fast, half, 0)
                    onward(slow, fast, half, 0, 1)
            todo.append((slow, fast, k * n[1] + l))

    for half in range(halves):
        for kind in (1, 0):
            if cut[kind]:
                spread(me[0], me[1], half, kind, kind)
        if cut[0]:
            spread(me[0], me[1], half, 0, 1)
    todo.append((me[0], me[1], 0))
    work()
    if cut[1]:
        for half in range(halves):
            for l in range(1, n[1]):
                fast = grid.nearest(1, l)
                arrived(me[0], fast, half, 1)
                onward(me[0], fast, half, 1, 1)
    for k in range(1, n[0]):
        slow = grid.nearest(0, k)
        for half in range(halves):
            if cut[0]:
                arrived(slow, me[1], half, 0)
                onward(slow, me[1], half, 0, 0)
                spread(slow, me[1], half, 0, 1)
            if half < halves - 1:
                work()
        if cut[1]:
            settle(k - 1)
        complete(k - 1)
        work()
    if cut[1]:
        settle(n[0] - 1)
    work(len(todo))
    complete(n[0] - 1)
    work(len(todo))


def scatter_slots(n):
    return 1 if n == 2 else n + 1


class Scatter:
    def __init__(self, grid, sender, part, bufs, sems, halves, cut):
        self.grid, self.sender, self.part = grid, sender, part
        self.bufs, self.sems, self.halves, self.cut = bufs, sems, halves, cut

    def slot(self, axis, target, from_below):
        if self.grid.n[axis] == 2:
            return 0
        return target + jnp.where(from_below, 1, 0)

    def take(self, kind, stage, axis, other, target, from_below, half, when, slot_index):
        buf, sem = self.bufs[kind][stage], self.sems[kind][stage]
        slot = self.slot(axis, target, from_below)

        def add():
            ref = buf.at[other, slot, half]
            pltpu.make_async_copy(ref, ref, sem.at[other, slot, half]).wait()
            mine = self.part(slot_index, half, kind)
            mine[...] = (mine[...].astype(jnp.float32) + ref[...].astype(jnp.float32)).astype(mine.dtype)

        if when is None:
            add()
        else:
            pl.when(when)(add)

    def toward(self, kind, stage, axis, other, target, half, slow, fast):
        grid = self.grid
        m, n = grid.me[axis], grid.n[axis]
        up = target > m
        index = grid.index(slow, fast)
        if n > 2:
            incoming = (up & (m > 0)) | (jnp.logical_not(up) & (m < n - 1))
            self.take(kind, stage, axis, other, target, up, half, incoming, index)
        buf, sem = self.bufs[kind][stage], self.sems[kind][stage]
        slot = self.slot(axis, target, up)
        spot = 1 - m if n == 2 else jnp.where(up, m + 1, m - 1)
        self.sender.send(
            self.part(index, half, kind), buf.at[other, slot, half], sem.at[other, slot, half],
            grid.device(axis, spot))

    def last(self, kind, stage, axis, other, half, slow, fast):
        grid = self.grid
        m, n = grid.me[axis], grid.n[axis]
        index = grid.index(slow, fast)
        if n == 2:
            self.take(kind, stage, axis, other, m, m > 0, half, None, index)
        elif n > 2:
            self.take(kind, stage, axis, other, m, jnp.bool_(True), half, m > 0, index)
            self.take(kind, stage, axis, other, m, jnp.bool_(False), half, m < n - 1, index)

    def run(self, produce):
        grid, n, me = self.grid, self.grid.n, self.grid.me
        for k in reversed(range(n[0])):
            slow = grid.nearest(0, k)
            for l in reversed(range(n[1])):
                fast = grid.nearest(1, l)
                produce(slow, fast)
                for half in range(self.halves):
                    if self.cut[0] and l > 0:
                        self.toward(0, 0, 1, slow, fast, half, slow, fast)
                    if self.cut[1] and k > 0:
                        self.toward(1, 0, 0, fast, slow, half, slow, fast)
        if self.cut[1]:
            for half in range(self.halves):
                for l in reversed(range(n[1])):
                    fast = grid.nearest(1, l)
                    self.last(1, 0, 0, fast, half, me[0], fast)
                    if l > 0:
                        self.toward(1, 1, 1, 0, fast, half, me[0], fast)
        if self.cut[0]:
            for k in reversed(range(1, n[0])):
                slow = grid.nearest(0, k)
                for half in range(self.halves):
                    self.last(0, 0, 1, slow, half, slow, me[1])
                    self.toward(0, 1, 0, 0, slow, half, slow, me[1])
            for half in range(self.halves):
                self.last(0, 0, 1, me[0], half, me[0], me[1])
        for half in range(self.halves):
            if self.cut[1]:
                self.last(1, 1, 1, 0, half, me[0], me[1])
            if self.cut[0]:
                self.last(0, 1, 0, 0, half, me[0], me[1])


def scatter_scratch(sizes, halves, rows, cols, cut):
    bufs, sems = [], []
    for kind, stages in ((0, (1, 0)), (1, (0, 1))):
        for stage, axis in enumerate(stages):
            lead = (sizes[1 - axis] if stage == 0 else 1, scatter_slots(sizes[axis]), halves)
            width = max(cut[kind], 128)
            bufs.append(pltpu.VMEM(lead + (rows // halves, width), jnp.bfloat16))
            sems.append(pltpu.SemaphoreType.DMA(lead))
    return bufs, sems


def scatter_sends(sizes, halves):
    return halves * 2 * (sizes[0] * sizes[1] + sizes[0] + sizes[1])


def lines_of(seq):
    fast = 2 if seq <= 8 else 4
    return (seq // fast, fast)

VMEM_LIMIT = 60 * 2**20


def gather_cut(sizes):
    if sizes[0] == 4 and sizes[1] == 2:
        return (1664, 384)
    return (D // 2, D // 2)


def columns_of(cut, kind):
    return pl.ds(0, cut[0]) if kind == 0 else pl.ds(cut[0], cut[1])


def gather_rows(rows_own, sizes, collective):
    rows = rows_own.shape[0]
    shards = sizes[0] * sizes[1]
    cut, halves = gather_cut(sizes), 2

    def kernel(own_ref, out_ref, full, send_sems, recv_sems, local_sems):
        grid = Grid2(sizes)
        grid.barrier()
        full[grid.index(*grid.me)] = own_ref[...]
        sender = Sender(send_sems)
        step = rows // halves

        def piece(slot, half, kind):
            return full.at[slot, pl.ds(half * step, step), columns_of(cut, kind)]

        copies = []

        def ready(slow, fast, order):
            slot = grid.index(slow, fast)
            copy = pltpu.make_async_copy(full.at[slot], out_ref.at[slot], local_sems.at[order])
            copy.start()
            copies.append(copy)

        gather_rounds(grid, sender, piece, recv_sems, halves, cut, ready)
        for copy in copies:
            copy.wait()
        sender.finish()

    gathered = pl.pallas_call(
        kernel,
        out_shape=jax.ShapeDtypeStruct((shards, rows, D), jnp.bfloat16),
        in_specs=[pl.BlockSpec(memory_space=pltpu.VMEM)],
        out_specs=pl.BlockSpec(memory_space=pl.ANY),
        scratch_shapes=[
            pltpu.VMEM((shards, rows, D), jnp.bfloat16),
            pltpu.SemaphoreType.DMA((gather_sends(sizes, halves),)),
            pltpu.SemaphoreType.DMA((2, halves, shards)),
            pltpu.SemaphoreType.DMA((shards,)),
        ],
        compiler_params=pltpu.CompilerParams(
            collective_id=collective, has_side_effects=True, vmem_limit_bytes=VMEM_LIMIT
        ),
    )(rows_own)
    return gathered.reshape(shards * rows, D)


def scatter_rows(partial, sizes, collective):
    shards = sizes[0] * sizes[1]
    rows = partial.shape[0] // shards
    cut, halves = gather_cut(sizes), 2
    bufs, sems = scatter_scratch(sizes, halves, rows, D, cut)

    def kernel(in_ref, out_ref, part_ref, in_sem, b0, b1, b2, b3, s0, s1, s2, s3, send_sems):
        grid = Grid2(sizes)
        copy = pltpu.make_async_copy(in_ref, part_ref, in_sem)
        copy.start()
        grid.barrier()
        copy.wait()
        sender = Sender(send_sems)
        step = rows // halves

        def part(slot, half, kind):
            return part_ref.at[slot, pl.ds(half * step, step), columns_of(cut, kind)]

        scatter = Scatter(
            grid, sender, part, ((b0, b1), (b2, b3)), ((s0, s1), (s2, s3)), halves, cut
        )
        scatter.run(lambda slow, fast: None)
        sender.finish()
        out_ref[...] = part_ref[grid.index(*grid.me)].astype(jnp.float32)

    return pl.pallas_call(
        kernel,
        out_shape=jax.ShapeDtypeStruct((rows, D), jnp.float32),
        in_specs=[pl.BlockSpec(memory_space=pl.ANY)],
        out_specs=pl.BlockSpec(memory_space=pltpu.VMEM),
        scratch_shapes=[pltpu.VMEM((shards, rows, D), jnp.bfloat16), pltpu.SemaphoreType.DMA]
        + bufs
        + sems
        + [pltpu.SemaphoreType.DMA((scatter_sends(sizes, halves),))],
        compiler_params=pltpu.CompilerParams(
            collective_id=collective, has_side_effects=True, vmem_limit_bytes=VMEM_LIMIT
        ),
    )(partial.reshape(shards, rows, D))


def joined(value, axis, join):
    gathered = lax.all_gather(jnp.stack(value), axis)
    pieces = tuple(gathered[:, i] for i in range(len(value)))
    head = tuple(part[0] for part in pieces)
    tail = tuple(part[1:] for part in pieces)
    so_far, _ = lax.scan(lambda so_far, piece: (join(so_far, piece), None), head, tail)
    return so_far


def norm_parts(values, norm_gain, norm_shift):
    centered = values - jnp.mean(values, axis=-1, keepdims=True)
    inverse = lax.rsqrt(jnp.mean(centered * centered, axis=-1, keepdims=True) + EPSILON)
    normed = centered * inverse
    return (normed * norm_gain + norm_shift, normed, inverse)


def norm_back(grad_rows, normed, inverse, norm_gain):
    scaled = grad_rows * norm_gain
    inner_part = (
        scaled
        - jnp.mean(scaled, axis=-1, keepdims=True)
        - normed * jnp.mean(scaled * normed, axis=-1, keepdims=True)
    )
    return (inner_part * inverse, jnp.sum(grad_rows * normed, axis=0), jnp.sum(grad_rows, axis=0))


def exact_gelu(vector):
    return jax.nn.gelu(vector, approximate=False)


def segment_rows(block_lengths):
    row_ends = jnp.cumsum(block_lengths)
    row_ids = jnp.arange(BLOCK, dtype=jnp.int32)
    passed = (row_ids[:, None] >= row_ends[None, :]).astype(jnp.int32)
    segment = jnp.sum(passed, axis=1)
    position = row_ids - jnp.sum(passed * block_lengths[None, :], axis=1)
    return (segment, position)


def rotary_tables(position):
    half_rot = ROT // 2
    frequency = 10000.0 ** (-2.0 * jnp.arange(half_rot, dtype=jnp.float32) / ROT)
    angles = position.astype(jnp.float32)[:, None] * frequency[None, :]
    return (jnp.cos(angles)[:, None, :], jnp.sin(angles)[:, None, :])


def rotate(vector, cos_table, sin_table, direction):
    half_rot = ROT // 2
    first_half = vector[..., :half_rot]
    second_half = vector[..., half_rot:ROT]
    return jnp.concatenate(
        [
            first_half * cos_table - direction * second_half * sin_table,
            second_half * cos_table + direction * first_half * sin_table,
            vector[..., ROT:],
        ],
        axis=-1,
    )


def block_scores(query_block, key_rows, segment, first_row):
    row_ids = jnp.arange(BLOCK, dtype=jnp.int32)
    raw_scores = jnp.einsum(
        "qhd,khd->hqk", query_block, key_rows, preferred_element_type=jnp.float32
    ) * HEAD_DIM ** (-0.5)
    query_ids = lax.dynamic_slice_in_dim(row_ids, first_row, ATT_BLK, 0)
    query_seg = lax.dynamic_slice_in_dim(segment, first_row, ATT_BLK, 0)
    allowed = (query_seg[:, None] == segment[None, :]) & (row_ids[None, :] <= query_ids[:, None])
    return jnp.where(allowed[None], raw_scores, -1e30)


def attention_forward(queries, key_rows, values, segment):

    def one_block(block_index):
        first_row = block_index * ATT_BLK
        query_block = lax.dynamic_slice_in_dim(queries, first_row, ATT_BLK, 0)
        scores = block_scores(query_block, key_rows, segment, first_row)
        row_top = jnp.max(scores, axis=-1, keepdims=True)
        weights = jnp.exp(scores - row_top)
        summed = jnp.sum(weights, axis=-1, keepdims=True)
        prob_rows = (weights / summed).astype(jnp.bfloat16)
        context = jnp.einsum("hqk,khd->qhd", prob_rows, values, preferred_element_type=jnp.float32)
        return (context, (row_top + jnp.log(summed))[..., 0])

    contexts, row_lse = lax.map(one_block, jnp.arange(BLOCK // ATT_BLK, dtype=jnp.int32))
    return (contexts.reshape(BLOCK, queries.shape[1], HEAD_DIM), row_lse)


def attention_backward(queries, key_rows, values, segment, row_lse, grad_context):

    def one_block(carry, block_index):
        grad_keys, grad_values = carry
        first_row = block_index * ATT_BLK
        query_block = lax.dynamic_slice_in_dim(queries, first_row, ATT_BLK, 0)
        grad_block = lax.dynamic_slice_in_dim(grad_context, first_row, ATT_BLK, 0)
        scores = block_scores(query_block, key_rows, segment, first_row)
        block_lse = lax.dynamic_index_in_dim(row_lse, block_index, 0, keepdims=False)
        prob_rows = jnp.exp(scores - block_lse[:, :, None])
        grad_probs = jnp.einsum(
            "qhd,khd->hqk", grad_block, values, preferred_element_type=jnp.float32
        )
        inner_sum = jnp.sum(prob_rows * grad_probs, axis=-1, keepdims=True)
        grad_scores = (prob_rows * (grad_probs - inner_sum)).astype(jnp.bfloat16)
        grad_query = jnp.einsum(
            "hqk,khd->qhd", grad_scores, key_rows, preferred_element_type=jnp.float32
        ) * HEAD_DIM ** (-0.5)
        grad_keys = grad_keys + jnp.einsum(
            "hqk,qhd->khd", grad_scores, query_block, preferred_element_type=jnp.float32
        ) * HEAD_DIM ** (-0.5)
        grad_values = grad_values + jnp.einsum(
            "hqk,qhd->khd",
            prob_rows.astype(jnp.bfloat16),
            grad_block,
            preferred_element_type=jnp.float32,
        )
        return ((grad_keys, grad_values), grad_query)

    empty = jnp.zeros(key_rows.shape, jnp.float32)
    (grad_keys, grad_values), grad_queries = lax.scan(
        one_block, (empty, empty), jnp.arange(BLOCK // ATT_BLK, dtype=jnp.int32)
    )
    return (grad_queries.reshape(key_rows.shape), grad_keys, grad_values)


def merge_stats(left_stats, right_stats):
    left_top, left_sum, left_pick = left_stats
    right_top, right_sum, right_pick = right_stats
    joint_top = jnp.maximum(left_top, right_top)
    joint_sum = left_sum * jnp.exp(left_top - joint_top) + right_sum * jnp.exp(
        right_top - joint_top
    )
    return (joint_top, joint_sum, left_pick + right_pick)


def per_device(
    hidden,
    targets,
    lengths,
    labels,
    ref_logps,
    ln1_gain,
    ln1_bias,
    ln2_gain,
    ln2_bias,
    qkv_weight,
    qv_bias,
    out_weight,
    up_weight,
    up_bias,
    down_weight,
    branch_bias,
    lnf_gain,
    lnf_bias,
    head_weight,
):
    num_blocks = hidden.shape[0]
    sizes = lines_of(lax.axis_size("seq"))
    shard_rows = hidden.shape[1]
    local_heads = qkv_weight.shape[1]
    local_vocab = head_weight.shape[1]
    row_blocks = BLOCK // ATT_BLK
    gain_one = ln1_gain.astype(jnp.float32)
    shift_one = ln1_bias.astype(jnp.float32)
    gain_two = ln2_gain.astype(jnp.float32)
    shift_two = ln2_bias.astype(jnp.float32)
    gain_final = lnf_gain.astype(jnp.float32)
    shift_final = lnf_bias.astype(jnp.float32)
    branch_float = branch_bias.astype(jnp.float32)
    up_float = up_bias.astype(jnp.float32)
    qv_float = qv_bias.astype(jnp.float32)
    full_bias = jnp.concatenate(
        [qv_float[:, :HEAD_DIM], jnp.zeros_like(qv_float[:, :HEAD_DIM]), qv_float[:, HEAD_DIM:]],
        axis=-1,
    )
    qkv_flat = qkv_weight.reshape(D, local_heads * 3 * HEAD_DIM)
    out_flat = out_weight.reshape(local_heads * HEAD_DIM, D)
    vocab_ids = lax.axis_index("seq") * local_vocab + jnp.arange(local_vocab, dtype=jnp.int32)
    block_num = 0
    own_rows = hidden[block_num].astype(jnp.float32)
    segment, position = segment_rows(lengths[block_num])
    gathered = gather_rows(hidden[block_num], sizes, 0).astype(jnp.float32)
    first_norm, normed_one, inverse_one = norm_parts(gathered, gain_one, shift_one)
    second_norm, normed_two, inverse_two = norm_parts(gathered, gain_two, shift_two)
    first_full = first_norm.astype(jnp.bfloat16)
    second_full = second_norm.astype(jnp.bfloat16)
    projected = (
        jnp.dot(first_full, qkv_flat, preferred_element_type=jnp.float32).reshape(
            BLOCK, local_heads, 3 * HEAD_DIM
        )
        + full_bias
    )
    cos_table, sin_table = rotary_tables(position)
    queries = rotate(projected[..., :HEAD_DIM], cos_table, sin_table, 1.0).astype(jnp.bfloat16)
    key_rows = rotate(projected[..., HEAD_DIM : 2 * HEAD_DIM], cos_table, sin_table, 1.0).astype(
        jnp.bfloat16
    )
    values = projected[..., 2 * HEAD_DIM :].astype(jnp.bfloat16)
    context, row_lse = attention_forward(queries, key_rows, values, segment)
    context = context.reshape(BLOCK, local_heads * HEAD_DIM).astype(jnp.bfloat16)
    up_pre = jnp.dot(second_full, up_weight, preferred_element_type=jnp.float32) + up_float
    activated = exact_gelu(up_pre).astype(jnp.bfloat16)

    def branch_term(first_row, row_count, context=context, activated=activated):
        return jnp.dot(context, out_flat, preferred_element_type=jnp.float32) + jnp.dot(
            activated, down_weight, preferred_element_type=jnp.float32
        )

    stream = (
        own_rows
        + scatter_rows(
            branch_term(jnp.int32(0), BLOCK).astype(jnp.bfloat16), sizes, 1
        )
        + branch_float
    )
    final_norm, normed_final, inverse_final = norm_parts(stream, gain_final, shift_final)
    final_full = gather_rows(final_norm.astype(jnp.bfloat16), sizes, 2)
    block_targets = targets[block_num]

    def logit_stats(row_block, final_full=final_full, block_targets=block_targets):
        first_row = row_block * ATT_BLK
        rows_in = lax.dynamic_slice_in_dim(final_full, first_row, ATT_BLK, 0)
        row_targets = lax.dynamic_slice_in_dim(block_targets, first_row, ATT_BLK, 0)
        logits = jnp.dot(rows_in, head_weight, preferred_element_type=jnp.float32)
        row_top = jnp.max(logits, axis=-1)
        summed = jnp.sum(jnp.exp(logits - row_top[:, None]), axis=-1)
        picked = jnp.sum(
            jnp.where(vocab_ids[None, :] == row_targets[:, None], logits, 0.0), axis=-1
        )
        return (row_top, summed, picked)

    row_tops, row_sums, row_picks = lax.map(logit_stats, jnp.arange(row_blocks, dtype=jnp.int32))
    top_all, sum_all, pick_all = joined(
        (row_tops.reshape(BLOCK), row_sums.reshape(BLOCK), row_picks.reshape(BLOCK)),
        "seq",
        merge_stats,
    )
    log_total = top_all + jnp.log(sum_all)
    token_logp = pick_all - log_total
    member = (segment[:, None] == jnp.arange(EXB, dtype=jnp.int32)[None, :]).astype(jnp.float32)
    mean_rows = [
        jnp.sum(member * token_logp[:, None], axis=0) / lengths[block_num].astype(jnp.float32)
    ]
    saved = [
        {
            "own_rows": own_rows,
            "segment": segment,
            "cos_table": cos_table,
            "sin_table": sin_table,
            "normed_one": normed_one,
            "inverse_one": inverse_one,
            "normed_two": normed_two,
            "inverse_two": inverse_two,
            "first_full": first_full,
            "second_full": second_full,
            "queries": queries,
            "key_rows": key_rows,
            "values": values,
            "row_lse": row_lse,
            "context": context,
            "up_pre": up_pre,
            "activated": activated,
            "stream": stream,
            "normed_final": normed_final,
            "inverse_final": inverse_final,
            "final_full": final_full,
            "log_total": log_total,
            "member": member,
        }
    ]
    log_ratio = jnp.stack(mean_rows) - ref_logps
    total_ratio = lax.psum(jnp.sum(log_ratio), "dp")
    center = total_ratio / (num_blocks * lax.axis_size("dp") * EXB)
    label_sign = (2 * labels - 1).astype(jnp.float32)
    squashed = jax.nn.sigmoid(BETA * label_sign * (log_ratio - center))
    losses = 1.0 - squashed
    grad_ratio = -LOSS_SCALE * BETA * label_sign * squashed * (1.0 - squashed)
    block_num = 0
    kept = saved[block_num]
    example_grad = grad_ratio[block_num] / lengths[block_num].astype(jnp.float32)
    token_grad = jnp.sum(kept["member"] * example_grad[None, :], axis=1)
    block_targets = targets[block_num]

    def logit_grads(row_block, kept=kept, token_grad=token_grad, block_targets=block_targets):
        first_row = row_block * ATT_BLK
        rows_in = lax.dynamic_slice_in_dim(kept["final_full"], first_row, ATT_BLK, 0)
        row_targets = lax.dynamic_slice_in_dim(block_targets, first_row, ATT_BLK, 0)
        row_total = lax.dynamic_slice_in_dim(kept["log_total"], first_row, ATT_BLK, 0)
        row_scale = lax.dynamic_slice_in_dim(token_grad, first_row, ATT_BLK, 0)
        logits = jnp.dot(rows_in, head_weight, preferred_element_type=jnp.float32)
        prob_rows = jnp.exp(logits - row_total[:, None])
        onehot = (vocab_ids[None, :] == row_targets[:, None]).astype(jnp.float32)
        return (row_scale[:, None] * (onehot - prob_rows)).astype(jnp.bfloat16)

    grad_logits = lax.map(logit_grads, jnp.arange(row_blocks, dtype=jnp.int32)).reshape(
        BLOCK, local_vocab
    )
    head_grad = jnp.einsum(
        "nd,nv->dv", kept["final_full"], grad_logits, preferred_element_type=jnp.float32
    )

    def final_term(first_row, row_count, grad_logits=grad_logits):
        return jnp.einsum("nv,dv->nd", grad_logits, head_weight, preferred_element_type=jnp.float32)

    grad_final = scatter_rows(final_term(jnp.int32(0), BLOCK).astype(jnp.bfloat16), sizes, 3)
    grad_stream, part_gain, part_shift = norm_back(
        grad_final, kept["normed_final"], kept["inverse_final"], gain_final
    )
    branch_grad = jnp.sum(grad_stream, axis=0)
    grad_full = gather_rows(grad_stream.astype(jnp.bfloat16), sizes, 4)
    out_grad = jnp.einsum(
        "nc,nd->cd", kept["context"], grad_full, preferred_element_type=jnp.float32
    )
    down_grad = jnp.einsum(
        "nf,nd->fd", kept["activated"], grad_full, preferred_element_type=jnp.float32
    )
    grad_context = (
        jnp.einsum("nd,cd->nc", grad_full, out_flat, preferred_element_type=jnp.float32)
        .astype(jnp.bfloat16)
        .reshape(BLOCK, local_heads, HEAD_DIM)
    )
    grad_active = jnp.einsum(
        "nd,fd->nf", grad_full, down_weight, preferred_element_type=jnp.float32
    )
    gelu_pull = jax.vjp(exact_gelu, kept["up_pre"])[1]
    grad_up = gelu_pull(grad_active)[0].astype(jnp.bfloat16)
    up_grad = jnp.einsum(
        "nd,nf->df", kept["second_full"], grad_up, preferred_element_type=jnp.float32
    )
    up_bias_grad = jnp.sum(grad_up, axis=0, dtype=jnp.float32)
    grad_query, grad_keys, grad_values = attention_backward(
        kept["queries"],
        kept["key_rows"],
        kept["values"],
        kept["segment"],
        kept["row_lse"],
        grad_context,
    )
    grad_qkv = jnp.concatenate(
        [
            rotate(grad_query, kept["cos_table"], kept["sin_table"], -1.0),
            rotate(grad_keys, kept["cos_table"], kept["sin_table"], -1.0),
            grad_values,
        ],
        axis=-1,
    ).astype(jnp.bfloat16)
    qkv_sums = jnp.sum(grad_qkv, axis=0, dtype=jnp.float32)
    qv_grad = jnp.concatenate([qkv_sums[:, :HEAD_DIM], qkv_sums[:, 2 * HEAD_DIM :]], axis=-1)
    qkv_grad = jnp.einsum(
        "nd,nhe->dhe", kept["first_full"], grad_qkv, preferred_element_type=jnp.float32
    )
    grad_first = jnp.einsum("nhe,dhe->nd", grad_qkv, qkv_weight, preferred_element_type=jnp.float32)
    grad_second = jnp.einsum("nf,df->nd", grad_up, up_weight, preferred_element_type=jnp.float32)
    part_one, gain_part_one, shift_part_one = norm_back(
        grad_first, kept["normed_one"], kept["inverse_one"], gain_one
    )
    part_two, gain_part_two, shift_part_two = norm_back(
        grad_second, kept["normed_two"], kept["inverse_two"], gain_two
    )
    grad_input = grad_stream + scatter_rows(
        (part_one + part_two).astype(jnp.bfloat16), sizes, 5
    )
    outputs = [kept["stream"].astype(jnp.bfloat16)]
    input_grads = [grad_input]
    small_sums = lax.psum(
        (
            gain_part_one,
            shift_part_one,
            gain_part_two,
            shift_part_two,
            part_gain,
            part_shift,
            branch_grad,
        ),
        ("dp", "seq"),
    )
    large_sums = (
        lax.psum(qkv_grad.astype(jnp.bfloat16), "dp").astype(jnp.float32),
        lax.psum(qv_grad.astype(jnp.bfloat16), "dp").astype(jnp.float32),
        lax.psum(out_grad.astype(jnp.bfloat16), "dp").astype(jnp.float32),
        lax.psum(up_grad.astype(jnp.bfloat16), "dp").astype(jnp.float32),
        lax.psum(up_bias_grad.astype(jnp.bfloat16), "dp").astype(jnp.float32),
        lax.psum(down_grad.astype(jnp.bfloat16), "dp").astype(jnp.float32),
        lax.psum(head_grad.astype(jnp.bfloat16), "dp").astype(jnp.float32),
    )
    return (
        losses,
        jnp.stack(outputs),
        jnp.stack(input_grads),
        small_sums[0],
        small_sums[1],
        small_sums[2],
        small_sums[3],
        large_sums[0],
        large_sums[1],
        large_sums[2].reshape(out_weight.shape),
        large_sums[3],
        large_sums[4],
        large_sums[5],
        small_sums[6],
        small_sums[4],
        small_sums[5],
        large_sums[6],
    )


def solution(mesh):
    return jax.shard_map(
        per_device,
        mesh=mesh,
        in_specs=(
            P("dp", "seq", None),
            P("dp", None),
            P("dp", None),
            P("dp", None),
            P("dp", None),
            P(),
            P(),
            P(),
            P(),
            P(None, "seq", None),
            P("seq", None),
            P("seq", None, None),
            P(None, "seq"),
            P("seq"),
            P("seq", None),
            P(),
            P(),
            P(),
            P(None, "seq"),
        ),
        out_specs=(
            P("dp", None),
            P("dp", "seq", None),
            P("dp", "seq", None),
            P(),
            P(),
            P(),
            P(),
            P(None, "seq", None),
            P("seq", None),
            P("seq", None, None),
            P(None, "seq"),
            P("seq"),
            P("seq", None),
            P(),
            P(),
            P(),
            P(None, "seq"),
        ),
        check_vma=False,
    )
```

```python
import jax
import jax.numpy as jnp
from jax import lax
from jax.experimental import pallas as pl
from jax.experimental.pallas import tpu as pltpu
from jax.sharding import PartitionSpec as P

D = 2048
HEAD_DIM = 128
ROT = 32
BLOCK = 2048
EXB = 8
EPSILON = 1e-05
BETA = 0.25
LOSS_SCALE = 65536.0
HALVES = 2
VMEM_LIMIT = 62 * 2**20

MESH = pl.DeviceIdType.MESH


class Grid2:
    def __init__(self, sizes):
        self.n = sizes
        place = lax.axis_index("seq")
        self.me = (place // sizes[1], lax.rem(place, sizes[1]))

    def index(self, slow, fast):
        return slow * self.n[1] + fast

    def device(self, axis, spot):
        here = list(self.me)
        here[axis] = spot
        return {"seq": self.index(*here)}

    def nearest(self, axis, rank):
        n, m = self.n[axis], self.me[axis]
        if rank == 0:
            return m
        if n == 2:
            return 1 - m
        after = n - 1 - m
        both = jnp.minimum(m, after)
        dist = (rank + 1) // 2
        near = m - dist if rank % 2 else m + dist
        far = jnp.where(m < after, m + (rank - both), m - (rank - both))
        return jnp.where(rank <= 2 * both, near, far)

    def neighbours(self):
        found = []
        for axis in (0, 1):
            m, n = self.me[axis], self.n[axis]
            if n == 2:
                found.append((None, self.device(axis, 1 - m)))
            elif n > 2:
                found.append((m > 0, self.device(axis, m - 1)))
                found.append((m < n - 1, self.device(axis, m + 1)))
        return found

    def barrier(self):
        sem = pltpu.get_barrier_semaphore()
        amount = jnp.int32(0)
        for there, device in self.neighbours():
            def tell(device=device):
                pl.semaphore_signal(sem, inc=1, device_id=device, device_id_type=MESH)
            if there is None:
                tell()
                amount = amount + 1
            else:
                pl.when(there)(tell)
                amount = amount + there.astype(jnp.int32)
        pl.semaphore_wait(sem, amount)


class Sender:
    def __init__(self, send_sems):
        self.sems = send_sems
        self.used = 0
        self.open = []

    def send(self, src, dst, recv_sem, device, when=None):
        copy = pltpu.make_async_remote_copy(
            src_ref=src, dst_ref=dst, send_sem=self.sems.at[self.used], recv_sem=recv_sem,
            device_id=device, device_id_type=MESH)
        self.used += 1
        if when is None:
            copy.start()
        else:
            pl.when(when)(copy.start)
        self.open.append((when, copy))

    def finish(self):
        for when, copy in self.open:
            if when is None:
                copy.wait_send()
            else:
                pl.when(when)(copy.wait_send)
        self.open = []


def gather_sends(sizes, halves):
    return halves * 2 * (sizes[0] * sizes[1] * 2 + 8)


def gather_rounds(grid, sender, piece, recv_sems, halves, cut, ready):
    n, me = grid.n, grid.me

    def arrived(slow, fast, half, kind):
        ref = piece(grid.index(slow, fast), half, kind)
        sem = recv_sems.at[kind, half, grid.index(slow, fast)]
        pltpu.make_async_copy(ref, ref, sem).wait()

    def push(slow, fast, half, kind, axis, spot, when):
        ref = piece(grid.index(slow, fast), half, kind)
        sem = recv_sems.at[kind, half, grid.index(slow, fast)]
        sender.send(ref, ref, sem, grid.device(axis, spot), when)

    def spread(slow, fast, half, kind, axis):
        m, size = me[axis], n[axis]
        if size == 2:
            push(slow, fast, half, kind, axis, 1 - m, None)
        elif size > 2:
            push(slow, fast, half, kind, axis, m + 1, m < size - 1)
            push(slow, fast, half, kind, axis, m - 1, m > 0)

    def onward(slow, fast, half, kind, axis):
        m, size = me[axis], n[axis]
        if size <= 2:
            return
        source = (slow, fast)[axis]
        below = source < m
        when = (below & (m < size - 1)) | (jnp.logical_not(below) & (m > 0))
        push(slow, fast, half, kind, axis, jnp.where(below, m + 1, m - 1), when)

    todo = []

    def work(count=1):
        for _ in range(count):
            if todo:
                ready(*todo.pop(0))

    def settle(k):
        slow = grid.nearest(0, k)
        for half in range(halves):
            for l in range(n[1]):
                fast = grid.nearest(1, l)
                if k > 0:
                    arrived(slow, fast, half, 1)
                    onward(slow, fast, half, 1, 0)
                else:
                    spread(slow, fast, half, 1, 0)

    def complete(k):
        slow = grid.nearest(0, k)
        if k > 0:
            todo.append((slow, me[1], k * n[1]))
        for l in range(1, n[1]):
            fast = grid.nearest(1, l)
            if cut[0]:
                for half in range(halves):
                    arrived(slow, fast, half, 0)
                    onward(slow, fast, half, 0, 1)
            todo.append((slow, fast, k * n[1] + l))

    for half in range(halves):
        for kind in (1, 0):
            if cut[kind]:
                spread(me[0], me[1], half, kind, kind)
        if cut[0]:
            spread(me[0], me[1], half, 0, 1)
    todo.append((me[0], me[1], 0))
    work()
    if cut[1]:
        for half in range(halves):
            for l in range(1, n[1]):
                fast = grid.nearest(1, l)
                arrived(me[0], fast, half, 1)
                onward(me[0], fast, half, 1, 1)
    for k in range(1, n[0]):
        slow = grid.nearest(0, k)
        for half in range(halves):
            if cut[0]:
                arrived(slow, me[1], half, 0)
                onward(slow, me[1], half, 0, 0)
                spread(slow, me[1], half, 0, 1)
            if half < halves - 1:
                work()
        if cut[1]:
            settle(k - 1)
        complete(k - 1)
        work()
    if cut[1]:
        settle(n[0] - 1)
    work(len(todo))
    complete(n[0] - 1)
    work(len(todo))


def scatter_slots(n):
    return 1 if n == 2 else n + 1


class Scatter:
    def __init__(self, grid, sender, part, bufs, sems, halves, cut):
        self.grid, self.sender, self.part = grid, sender, part
        self.bufs, self.sems, self.halves, self.cut = bufs, sems, halves, cut

    def slot(self, axis, target, from_below):
        if self.grid.n[axis] == 2:
            return 0
        return target + jnp.where(from_below, 1, 0)

    def take(self, kind, stage, axis, other, target, from_below, half, when, slot_index):
        buf, sem = self.bufs[kind][stage], self.sems[kind][stage]
        slot = self.slot(axis, target, from_below)

        def add():
            ref = buf.at[other, slot, half]
            pltpu.make_async_copy(ref, ref, sem.at[other, slot, half]).wait()
            mine = self.part(slot_index, half, kind)
            mine[...] = (mine[...].astype(jnp.float32) + ref[...].astype(jnp.float32)).astype(mine.dtype)

        if when is None:
            add()
        else:
            pl.when(when)(add)

    def toward(self, kind, stage, axis, other, target, half, slow, fast):
        grid = self.grid
        m, n = grid.me[axis], grid.n[axis]
        up = target > m
        index = grid.index(slow, fast)
        if n > 2:
            incoming = (up & (m > 0)) | (jnp.logical_not(up) & (m < n - 1))
            self.take(kind, stage, axis, other, target, up, half, incoming, index)
        buf, sem = self.bufs[kind][stage], self.sems[kind][stage]
        slot = self.slot(axis, target, up)
        spot = 1 - m if n == 2 else jnp.where(up, m + 1, m - 1)
        self.sender.send(
            self.part(index, half, kind), buf.at[other, slot, half], sem.at[other, slot, half],
            grid.device(axis, spot))

    def last(self, kind, stage, axis, other, half, slow, fast):
        grid = self.grid
        m, n = grid.me[axis], grid.n[axis]
        index = grid.index(slow, fast)
        if n == 2:
            self.take(kind, stage, axis, other, m, m > 0, half, None, index)
        elif n > 2:
            self.take(kind, stage, axis, other, m, jnp.bool_(True), half, m > 0, index)
            self.take(kind, stage, axis, other, m, jnp.bool_(False), half, m < n - 1, index)

    def run(self, produce):
        grid, n, me = self.grid, self.grid.n, self.grid.me
        for k in reversed(range(n[0])):
            slow = grid.nearest(0, k)
            for l in reversed(range(n[1])):
                fast = grid.nearest(1, l)
                produce(slow, fast)
                for half in range(self.halves):
                    if self.cut[0] and l > 0:
                        self.toward(0, 0, 1, slow, fast, half, slow, fast)
                    if self.cut[1] and k > 0:
                        self.toward(1, 0, 0, fast, slow, half, slow, fast)
        if self.cut[1]:
            for half in range(self.halves):
                for l in reversed(range(n[1])):
                    fast = grid.nearest(1, l)
                    self.last(1, 0, 0, fast, half, me[0], fast)
                    if l > 0:
                        self.toward(1, 1, 1, 0, fast, half, me[0], fast)
        if self.cut[0]:
            for k in reversed(range(1, n[0])):
                slow = grid.nearest(0, k)
                for half in range(self.halves):
                    self.last(0, 0, 1, slow, half, slow, me[1])
                    self.toward(0, 1, 0, 0, slow, half, slow, me[1])
            for half in range(self.halves):
                self.last(0, 0, 1, me[0], half, me[0], me[1])
        for half in range(self.halves):
            if self.cut[1]:
                self.last(1, 1, 1, 0, half, me[0], me[1])
            if self.cut[0]:
                self.last(0, 1, 0, 0, half, me[0], me[1])


def scatter_scratch(sizes, halves, rows, cols, cut):
    bufs, sems = [], []
    for kind, stages in ((0, (1, 0)), (1, (0, 1))):
        for stage, axis in enumerate(stages):
            lead = (sizes[1 - axis] if stage == 0 else 1, scatter_slots(sizes[axis]), halves)
            width = max(cut[kind], 128)
            bufs.append(pltpu.VMEM(lead + (rows // halves, width), jnp.bfloat16))
            sems.append(pltpu.SemaphoreType.DMA(lead))
    return bufs, sems


def scatter_sends(sizes, halves):
    return halves * 2 * (sizes[0] * sizes[1] + sizes[0] + sizes[1])


def lines_of(seq):
    fast = 2 if seq <= 8 else 4
    return (seq // fast, fast)


ATT_TILE = 256
SCALE = HEAD_DIM ** (-0.5)


def dot_nt(left, right):
    return lax.dot_general(left, right, (((1,), (1,)), ((), ())), preferred_element_type=jnp.float32)


def dot_tn(left, right):
    return lax.dot_general(left, right, (((0,), (0,)), ((), ())), preferred_element_type=jnp.float32)


def rotary_planes(position):
    half_rot = ROT // 2
    frequency = 10000.0 ** (-2.0 * jnp.arange(half_rot, dtype=jnp.float32) / ROT)
    angles = position.astype(jnp.float32)[:, None] * frequency[None, :]
    cos, sin = jnp.cos(angles), jnp.sin(angles)
    rows = position.shape[0]
    rest = jnp.zeros((rows, HEAD_DIM - ROT), jnp.float32)
    none = jnp.zeros_like(sin)
    return (
        jnp.concatenate([cos, cos, rest + 1.0], axis=1),
        jnp.concatenate([none, sin, rest], axis=1),
        jnp.concatenate([-sin, none, rest], axis=1),
    )


def turn(vector, cos, from_below, from_above):
    half_rot = ROT // 2
    return (
        vector * cos
        + pltpu.roll(vector, half_rot, 1) * from_below
        + pltpu.roll(vector, HEAD_DIM - half_rot, 1) * from_above
    )


def tile_mask(start_col, query_tile, key_tile):
    shape = (ATT_TILE, ATT_TILE)
    query_ids = query_tile * ATT_TILE + lax.broadcasted_iota(jnp.int32, shape, 0)
    key_ids = key_tile * ATT_TILE + lax.broadcasted_iota(jnp.int32, shape, 1)
    return (key_ids >= start_col) & (key_ids <= query_ids)


def attention_forward(qkv, start_col, first_tile, heads):
    tiles = BLOCK // ATT_TILE

    def kernel(first_ref, q_ref, k_ref, v_ref, start_ref, ctx_ref, lse_ref):
        tile = pl.program_id(1)
        queries = q_ref[...]
        start = start_ref[...]

        def step(key_tile, carry):
            top, total, acc = carry
            rows = pl.ds(pl.multiple_of(key_tile * ATT_TILE, ATT_TILE), ATT_TILE)
            scores = dot_nt(queries, k_ref[rows, :]) * SCALE
            scores = jnp.where(tile_mask(start, tile, key_tile), scores, -1e30)
            new_top = jnp.maximum(top, jnp.max(scores, axis=1, keepdims=True))
            shrink = jnp.exp(top - new_top)
            weights = jnp.exp(scores - new_top)
            total = total * shrink + jnp.sum(weights, axis=1, keepdims=True)
            acc = acc * shrink + jnp.dot(
                weights.astype(jnp.bfloat16), v_ref[rows, :], preferred_element_type=jnp.float32
            )
            return (new_top, total, acc)

        begin = (
            jnp.full((ATT_TILE, 1), -1e30, jnp.float32),
            jnp.zeros((ATT_TILE, 1), jnp.float32),
            jnp.zeros((ATT_TILE, HEAD_DIM), jnp.float32),
        )
        begin = step(tile, begin)
        top, total, acc = lax.fori_loop(first_ref[tile], tile, step, begin)
        ctx_ref[...] = (acc / total).astype(jnp.bfloat16)
        lse_ref[...] = top + jnp.log(total)

    return pl.pallas_call(
        kernel,
        grid_spec=pltpu.PrefetchScalarGridSpec(
            num_scalar_prefetch=1,
            grid=(heads, tiles),
            in_specs=[
                pl.BlockSpec((ATT_TILE, HEAD_DIM), lambda h, i, first: (i, 3 * h)),
                pl.BlockSpec((BLOCK, HEAD_DIM), lambda h, i, first: (0, 3 * h + 1)),
                pl.BlockSpec((BLOCK, HEAD_DIM), lambda h, i, first: (0, 3 * h + 2)),
                pl.BlockSpec((ATT_TILE, 1), lambda h, i, first: (i, 0)),
            ],
            out_specs=[
                pl.BlockSpec((ATT_TILE, HEAD_DIM), lambda h, i, first: (i, h)),
                pl.BlockSpec((pl.squeezed, ATT_TILE, 1), lambda h, i, first: (h, i, 0)),
            ],
        ),
        out_shape=[
            jax.ShapeDtypeStruct((BLOCK, heads * HEAD_DIM), jnp.bfloat16),
            jax.ShapeDtypeStruct((heads, BLOCK, 1), jnp.float32),
        ],
        compiler_params=pltpu.CompilerParams(vmem_limit_bytes=VMEM_LIMIT),
    )(first_tile, qkv, qkv, qkv, start_col)


def attention_backward(qkv, start_col, first_tile, heads, ctx, lse, grad_ctx, planes):
    tiles = BLOCK // ATT_TILE

    def kernel(
        first_ref, q_ref, k_ref, v_ref, start_ref, ctx_ref, lse_ref, do_ref, cos_ref, below_ref,
        above_ref, out_ref, sums_ref, dk_ref, dv_ref,
    ):
        tile = pl.program_id(1)

        @pl.when(tile == 0)
        def _():
            dk_ref[...] = jnp.zeros_like(dk_ref)
            dv_ref[...] = jnp.zeros_like(dv_ref)

        queries = q_ref[...]
        start = start_ref[...]
        grads = do_ref[...]
        lse_rows = lse_ref[...]
        inner = jnp.sum(
            grads.astype(jnp.float32) * ctx_ref[...].astype(jnp.float32), axis=1, keepdims=True
        )

        def step(key_tile, dq):
            rows = pl.ds(pl.multiple_of(key_tile * ATT_TILE, ATT_TILE), ATT_TILE)
            keys = k_ref[rows, :]
            scores = dot_nt(queries, keys) * SCALE
            probs = jnp.where(
                tile_mask(start, tile, key_tile), jnp.exp(scores - lse_rows), 0.0
            )
            grad_probs = dot_nt(grads, v_ref[rows, :])
            grad_scores = (probs * (grad_probs - inner)).astype(jnp.bfloat16)
            dv_ref[rows, :] += dot_tn(probs.astype(jnp.bfloat16), grads)
            dk_ref[rows, :] += dot_tn(grad_scores, queries)
            return dq + jnp.dot(grad_scores, keys, preferred_element_type=jnp.float32)

        dq = lax.fori_loop(
            first_ref[tile], tile + 1, step, jnp.zeros((ATT_TILE, HEAD_DIM), jnp.float32)
        )
        here = pl.ds(pl.multiple_of(tile * ATT_TILE, ATT_TILE), ATT_TILE)
        out_ref[here, :HEAD_DIM] = turn(
            dq * SCALE, cos_ref[here, :], -below_ref[here, :], -above_ref[here, :]
        ).astype(jnp.bfloat16)

        @pl.when(tile == tiles - 1)
        def _():
            def finish(index, sums):
                rows = pl.ds(pl.multiple_of(index * ATT_TILE, ATT_TILE), ATT_TILE)
                out_ref[rows, HEAD_DIM : 2 * HEAD_DIM] = turn(
                    dk_ref[rows, :] * SCALE, cos_ref[rows, :], -below_ref[rows, :], -above_ref[rows, :]
                ).astype(jnp.bfloat16)
                out_ref[rows, 2 * HEAD_DIM :] = dv_ref[rows, :].astype(jnp.bfloat16)
                return sums + jnp.sum(out_ref[rows, :].astype(jnp.float32), axis=0, keepdims=True)

            sums_ref[...] = lax.fori_loop(
                0, tiles, finish, jnp.zeros((1, 3 * HEAD_DIM), jnp.float32)
            )

    whole = pl.BlockSpec((BLOCK, HEAD_DIM), lambda h, i, first: (0, 0))
    return pl.pallas_call(
        kernel,
        grid_spec=pltpu.PrefetchScalarGridSpec(
            num_scalar_prefetch=1,
            grid=(heads, tiles),
            in_specs=[
                pl.BlockSpec((ATT_TILE, HEAD_DIM), lambda h, i, first: (i, 3 * h)),
                pl.BlockSpec((BLOCK, HEAD_DIM), lambda h, i, first: (0, 3 * h + 1)),
                pl.BlockSpec((BLOCK, HEAD_DIM), lambda h, i, first: (0, 3 * h + 2)),
                pl.BlockSpec((ATT_TILE, 1), lambda h, i, first: (i, 0)),
                pl.BlockSpec((ATT_TILE, HEAD_DIM), lambda h, i, first: (i, h)),
                pl.BlockSpec((pl.squeezed, ATT_TILE, 1), lambda h, i, first: (h, i, 0)),
                pl.BlockSpec((ATT_TILE, HEAD_DIM), lambda h, i, first: (i, h)),
                whole,
                whole,
                whole,
            ],
            out_specs=[
                pl.BlockSpec((BLOCK, 3 * HEAD_DIM), lambda h, i, first: (0, h)),
                pl.BlockSpec((pl.squeezed, 1, 3 * HEAD_DIM), lambda h, i, first: (h, 0, 0)),
            ],
            scratch_shapes=[
                pltpu.VMEM((BLOCK, HEAD_DIM), jnp.float32),
                pltpu.VMEM((BLOCK, HEAD_DIM), jnp.float32),
            ],
        ),
        out_shape=[
            jax.ShapeDtypeStruct((BLOCK, heads * 3 * HEAD_DIM), jnp.bfloat16),
            jax.ShapeDtypeStruct((heads, 1, 3 * HEAD_DIM), jnp.float32),
        ],
        compiler_params=pltpu.CompilerParams(vmem_limit_bytes=VMEM_LIMIT),
    )(first_tile, qkv, qkv, qkv, start_col, ctx, lse, grad_ctx, *planes)


def gather_cut(sizes):
    if sizes[0] == 4 and sizes[1] == 2:
        return (1664, 384)
    return (D // 2, D // 2)


def columns_of(cut, kind):
    return pl.ds(0, cut[0]) if kind == 0 else pl.ds(cut[0], cut[1])


def tile_of(width):
    return 256 if width % 256 == 0 else 128


def span(index, size):
    return pl.ds(pl.multiple_of(index * size, size), size)


ANY = pl.BlockSpec(memory_space=pl.ANY)
VMEM = pl.BlockSpec(memory_space=pltpu.VMEM)


def row_kernel(kernel, collective, out_shape, in_specs, out_specs, scratch, cost):
    return pl.pallas_call(
        kernel,
        out_shape=out_shape,
        in_specs=in_specs,
        out_specs=out_specs,
        scratch_shapes=scratch,
        cost_estimate=pl.CostEstimate(flops=cost, bytes_accessed=2**25, transcendentals=0),
        compiler_params=pltpu.CompilerParams(
            collective_id=collective, has_side_effects=True, vmem_limit_bytes=VMEM_LIMIT
        ),
    )


def gather_scratch(sizes, rows):
    shards = sizes[0] * sizes[1]
    return [
        pltpu.VMEM((shards, rows, D), jnp.bfloat16),
        pltpu.SemaphoreType.DMA((gather_sends(sizes, HALVES),)),
        pltpu.SemaphoreType.DMA((2, HALVES, shards)),
    ]


def run_gather(grid, sizes, rows, full, send_sems, recv_sems, ready):
    cut = gather_cut(sizes)
    step = rows // HALVES
    sender = Sender(send_sems)

    def piece(slot, half, kind):
        return full.at[slot, pl.ds(half * step, step), columns_of(cut, kind)]

    gather_rounds(grid, sender, piece, recv_sems, HALVES, cut, ready)
    sender.finish()


def sum_scratch(sizes, rows):
    shards = sizes[0] * sizes[1]
    bufs, sems = scatter_scratch(sizes, HALVES, rows, D, gather_cut(sizes))
    return (
        [pltpu.VMEM((shards, rows, D), jnp.bfloat16)]
        + bufs
        + sems
        + [pltpu.SemaphoreType.DMA((scatter_sends(sizes, HALVES),))]
    )


def run_scatter(grid, sizes, rows, scratch, produce):
    cut = gather_cut(sizes)
    step = rows // HALVES
    parts, b0, b1, b2, b3, s0, s1, s2, s3, send_sems = scratch
    sender = Sender(send_sems)

    def part(slot, half, kind):
        return parts.at[slot, pl.ds(half * step, step), columns_of(cut, kind)]

    scatter = Scatter(
        grid, sender, part, ((b0, b1), (b2, b3)), ((s0, s1), (s2, s3)), HALVES, cut
    )
    scatter.run(produce)
    sender.finish()


def production_order(grid):
    return [
        grid.index(grid.nearest(0, k), grid.nearest(1, l))
        for k in reversed(range(grid.n[0]))
        for l in reversed(range(grid.n[1]))
    ]


ROW_TILE = 32


def tile_stats(values):
    centered = values - jnp.mean(values, axis=1, keepdims=True)
    inverse = lax.rsqrt(jnp.mean(centered * centered, axis=1, keepdims=True) + EPSILON)
    return centered, inverse


def open_rows(own, sizes, collective, norms, qkv_flat, qkv_bias, up_weight, up_bias, planes):
    rows = own.shape[0]
    shards = sizes[0] * sizes[1]
    width, hidden = qkv_flat.shape[1], up_weight.shape[1]
    heads = width // (3 * HEAD_DIM)

    def kernel(
        own_ref, norms_ref, qkvw_any, qkvb_ref, upw_any, upb_ref, cos_ref, below_ref, above_ref,
        hid_any, one_any, two_any, qkv_any, act_any, slope_any,
        full, send_sems, recv_sems, qkvw, upw, load_sems, one, two, qkv, act, slope, out_sems, row_sems,
    ):
        grid = Grid2(sizes)
        loads = [
            pltpu.make_async_copy(qkvw_any, qkvw, load_sems.at[0]),
            pltpu.make_async_copy(upw_any, upw, load_sems.at[1]),
        ]
        for copy in loads:
            copy.start()
        full[grid.index(*grid.me)] = own_ref[...]
        grid.barrier()
        open_copies = []

        def outs(place, slot):
            pairs = ((one, one_any), (two, two_any), (qkv, qkv_any), (act, act_any), (slope, slope_any))
            return [
                pltpu.make_async_copy(here.at[slot], there.at[place], out_sems.at[slot, i])
                for i, (here, there) in enumerate(pairs)
            ]

        def ready(slow, fast, order):
            place = grid.index(slow, fast)
            slot = order % 2
            if order == 0:
                for copy in loads:
                    copy.wait()
            if order >= 2:
                for copy in open_copies.pop(0):
                    copy.wait()

            def norm_tile(index, _):
                here = span(index, ROW_TILE)
                centered, inverse = tile_stats(full[place, here].astype(jnp.float32))
                normed = centered * inverse
                one[slot, here] = (normed * norms_ref[0:1] + norms_ref[1:2]).astype(jnp.bfloat16)
                two[slot, here] = (normed * norms_ref[2:3] + norms_ref[3:4]).astype(jnp.bfloat16)
                return _

            lax.fori_loop(0, rows // ROW_TILE, norm_tile, 0)
            places = pl.ds(pl.multiple_of(place * rows, rows), rows)
            cos, below, above = cos_ref[places, :], below_ref[places, :], above_ref[places, :]
            for head in range(heads):
                first = head * 3 * HEAD_DIM
                found = jnp.dot(
                    one[slot], qkvw[:, first : first + 3 * HEAD_DIM], preferred_element_type=jnp.float32
                ) + qkvb_ref[:, first : first + 3 * HEAD_DIM]
                qkv[slot, :, first : first + HEAD_DIM] = turn(
                    found[:, :HEAD_DIM], cos, below, above
                ).astype(jnp.bfloat16)
                qkv[slot, :, first + HEAD_DIM : first + 2 * HEAD_DIM] = turn(
                    found[:, HEAD_DIM : 2 * HEAD_DIM], cos, below, above
                ).astype(jnp.bfloat16)
                qkv[slot, :, first + 2 * HEAD_DIM : first + 3 * HEAD_DIM] = found[
                    :, 2 * HEAD_DIM :
                ].astype(jnp.bfloat16)
            tile = tile_of(hidden)

            def up_tile(index, _):
                here = span(index, tile)
                pre = jnp.dot(two[slot], upw[:, here], preferred_element_type=jnp.float32) + upb_ref[:, here]
                share = 0.5 * (1.0 + lax.erf(pre * 0.7071067811865476))
                act[slot, :, here] = (pre * share).astype(jnp.bfloat16)
                slope[slot, :, here] = (
                    share + pre * (jnp.exp(-0.5 * pre * pre) * 0.3989422804014327)
                ).astype(jnp.bfloat16)
                return _

            lax.fori_loop(0, hidden // tile, up_tile, 0)
            copies = outs(place, slot)
            for copy in copies:
                copy.start()
            open_copies.append(copies)
            raw = pltpu.make_async_copy(full.at[place], hid_any.at[place], row_sems.at[order])
            raw.start()
            raw_copies.append(raw)

        raw_copies = []
        run_gather(grid, sizes, rows, full, send_sems, recv_sems, ready)
        for copies in open_copies:
            for copy in copies:
                copy.wait()
        for copy in raw_copies:
            copy.wait()

    def out(columns):
        return jax.ShapeDtypeStruct((shards, rows, columns), jnp.bfloat16)

    def staged(columns):
        return pltpu.VMEM((2, rows, columns), jnp.bfloat16)

    return row_kernel(
        kernel, collective,
        [out(D), out(D), out(D), out(width), out(hidden), out(hidden)],
        [VMEM, VMEM, ANY, VMEM, ANY, VMEM, VMEM, VMEM, VMEM],
        [ANY] * 6,
        gather_scratch(sizes, rows)
        + [
            pltpu.VMEM(qkv_flat.shape, jnp.bfloat16),
            pltpu.VMEM(up_weight.shape, jnp.bfloat16),
            pltpu.SemaphoreType.DMA((2,)),
            staged(D), staged(D), staged(width), staged(hidden), staged(hidden),
            pltpu.SemaphoreType.DMA((2, 5)),
            pltpu.SemaphoreType.DMA((shards,)),
        ],
        2 * BLOCK * D * (width + hidden),
    )(own, norms, qkv_flat, qkv_bias, up_weight, up_bias, *planes)


def branch_rows(own, ctx, act, out_flat, down_weight, norms, sizes, collective):
    rows = own.shape[0]
    shards = sizes[0] * sizes[1]
    inner, hidden = out_flat.shape[0], down_weight.shape[0]

    def kernel(
        own_ref, ctx_any, act_any, outw_any, downw_any, norms_ref, out_ref, final_ref, normed_ref, inverse_ref,
        ctx, act, outw, downw, load_sems, *scratch,
    ):
        grid = Grid2(sizes)
        parts = scratch[0]
        weights = [
            pltpu.make_async_copy(outw_any, outw, load_sems.at[0, 0]),
            pltpu.make_async_copy(downw_any, downw, load_sems.at[0, 1]),
        ]
        order = production_order(grid)
        loads = [
            [
                pltpu.make_async_copy(ctx_any.at[place], ctx.at[place], load_sems.at[1 + i, 0]),
                pltpu.make_async_copy(act_any.at[place], act.at[place], load_sems.at[1 + i, 1]),
            ]
            for i, place in enumerate(order)
        ]
        for copy in loads[0] + weights:
            copy.start()
        for copies in loads[1:]:
            for copy in copies:
                copy.start()
        grid.barrier()
        for copy in weights:
            copy.wait()

        def produce(slow, fast):
            place = grid.index(slow, fast)
            for copy in loads.pop(0):
                copy.wait()

            def columns(index, _):
                here = span(index, 512)
                parts[place, :, here] = (
                    jnp.dot(ctx[place], outw[:, here], preferred_element_type=jnp.float32)
                    + jnp.dot(act[place], downw[:, here], preferred_element_type=jnp.float32)
                ).astype(jnp.bfloat16)
                return _

            lax.fori_loop(0, D // 512, columns, 0)

        run_scatter(grid, sizes, rows, scratch, produce)
        mine = grid.index(*grid.me)

        def norm_tile(index, _):
            here = span(index, ROW_TILE)
            stream = own_ref[here].astype(jnp.float32) + parts[mine, here].astype(jnp.float32) + norms_ref[2:3]
            out_ref[here] = stream.astype(jnp.bfloat16)
            centered, inverse = tile_stats(stream)
            normed = centered * inverse
            final_ref[here] = (normed * norms_ref[0:1] + norms_ref[1:2]).astype(jnp.bfloat16)
            normed_ref[here] = normed
            inverse_ref[here] = inverse
            return _

        lax.fori_loop(0, rows // ROW_TILE, norm_tile, 0)

    return row_kernel(
        kernel, collective,
        [
            jax.ShapeDtypeStruct((rows, D), jnp.bfloat16),
            jax.ShapeDtypeStruct((rows, D), jnp.bfloat16),
            jax.ShapeDtypeStruct((rows, D), jnp.float32),
            jax.ShapeDtypeStruct((rows, 1), jnp.float32),
        ],
        [VMEM, ANY, ANY, ANY, ANY, VMEM],
        [VMEM] * 4,
        [
            pltpu.VMEM(ctx.shape, jnp.bfloat16),
            pltpu.VMEM(act.shape, jnp.bfloat16),
            pltpu.VMEM(out_flat.shape, jnp.bfloat16),
            pltpu.VMEM(down_weight.shape, jnp.bfloat16),
            pltpu.SemaphoreType.DMA((1 + shards, 2)),
        ]
        + sum_scratch(sizes, rows),
        2 * BLOCK * D * (inner + hidden),
    )(own, ctx, act, out_flat, down_weight, norms)


def logit_rows(final, head_weight, targets_col, sizes, collective):
    rows = final.shape[0]
    shards = sizes[0] * sizes[1]
    vocab = head_weight.shape[1]
    tile = tile_of(vocab)
    tiles = vocab // tile

    def kernel(
        own_ref, headw_any, target_ref, final_any, weights_any, stats_ref,
        full, send_sems, recv_sems, headw, load_sem, logits, weights, out_sems, row_sems,
    ):
        grid = Grid2(sizes)
        load = pltpu.make_async_copy(headw_any, headw, load_sem)
        load.start()
        full[grid.index(*grid.me)] = own_ref[...]
        grid.barrier()
        base = lax.axis_index("seq") * vocab
        open_copies, raw_copies = [], []

        def ready(slow, fast, order):
            place = grid.index(slow, fast)
            slot = order % 2
            if order == 0:
                load.wait()
            if order >= 2:
                open_copies.pop(0).wait()
            places = pl.ds(pl.multiple_of(place * rows, rows), rows)
            target = target_ref[places, :] - base

            def fold(values, join):
                while values.shape[1] > 128:
                    half = values.shape[1] // 2
                    values = join(values[:, :half], values[:, half:])
                return values

            def logit_tile(index, carry):
                top, pick = carry
                here = span(index, tile)
                found = jnp.dot(full[place], headw[:, here], preferred_element_type=jnp.float32)
                logits[:, here] = found
                ids = index * tile + lax.broadcasted_iota(jnp.int32, (rows, tile), 1)
                top = jnp.maximum(top, fold(found, jnp.maximum))
                pick = pick + fold(jnp.where(ids == target, found, 0.0), jnp.add)
                return (top, pick)

            top, pick = lax.fori_loop(
                0, tiles, logit_tile,
                (jnp.full((rows, 128), -jnp.inf, jnp.float32), jnp.zeros((rows, 128), jnp.float32)),
            )
            top = jnp.max(top, axis=1, keepdims=True)
            pick = jnp.sum(pick, axis=1, keepdims=True)

            def weight_tile(index, total):
                here = span(index, tile)
                found = jnp.exp(logits[:, here] - top)
                weights[slot, :, here] = found.astype(jnp.bfloat16)
                return total + fold(found, jnp.add)

            total = lax.fori_loop(0, tiles, weight_tile, jnp.zeros((rows, 128), jnp.float32))
            total = jnp.sum(total, axis=1, keepdims=True)
            lane = lax.broadcasted_iota(jnp.int32, (rows, 128), 1)
            stats_ref[places, :] = jnp.where(lane == 0, top, jnp.where(lane == 1, total, pick))
            copy = pltpu.make_async_copy(weights.at[slot], weights_any.at[place], out_sems.at[slot])
            copy.start()
            open_copies.append(copy)
            raw = pltpu.make_async_copy(full.at[place], final_any.at[place], row_sems.at[order])
            raw.start()
            raw_copies.append(raw)

        run_gather(grid, sizes, rows, full, send_sems, recv_sems, ready)
        for copy in open_copies + raw_copies:
            copy.wait()

    return row_kernel(
        kernel, collective,
        [
            jax.ShapeDtypeStruct((shards, rows, D), jnp.bfloat16),
            jax.ShapeDtypeStruct((shards, rows, vocab), jnp.bfloat16),
            jax.ShapeDtypeStruct((shards * rows, 128), jnp.float32),
        ],
        [VMEM, ANY, VMEM],
        [ANY, ANY, VMEM],
        gather_scratch(sizes, rows)
        + [
            pltpu.VMEM(head_weight.shape, jnp.bfloat16),
            pltpu.SemaphoreType.DMA,
            pltpu.VMEM((rows, vocab), jnp.float32),
            pltpu.VMEM((2, rows, vocab), jnp.bfloat16),
            pltpu.SemaphoreType.DMA((2,)),
            pltpu.SemaphoreType.DMA((shards,)),
        ],
        2 * BLOCK * D * vocab,
    )(final, head_weight, targets_col)


def final_grad_rows(grad_logits, head_weight, normed, inverse, gain, sizes, collective):
    shards, rows, vocab = grad_logits.shape

    def kernel(
        grads_any, headw_any, normed_ref, inverse_ref, gain_ref, stream_ref, down_ref, sums_ref,
        headw, grads, load_sems, *scratch,
    ):
        grid = Grid2(sizes)
        parts = scratch[0]
        order = production_order(grid)
        loads = [
            pltpu.make_async_copy(grads_any.at[place], grads.at[i % 2], load_sems.at[1 + i])
            for i, place in enumerate(order)
        ]
        weights = pltpu.make_async_copy(headw_any, headw, load_sems.at[0])
        loads[0].start()
        weights.start()
        grid.barrier()
        weights.wait()
        count = [0]

        def produce(slow, fast):
            place = grid.index(slow, fast)
            i = count[0]
            count[0] += 1
            if i + 1 < shards:
                loads[i + 1].start()
            loads[i].wait()

            def columns(index, _):
                here = span(index, 256)
                parts[place, :, here] = dot_nt(grads[i % 2], headw[here, :]).astype(jnp.bfloat16)
                return _

            lax.fori_loop(0, D // 256, columns, 0)

        run_scatter(grid, sizes, rows, scratch, produce)
        mine = grid.index(*grid.me)
        sums_ref[...] = jnp.zeros_like(sums_ref)

        def norm_tile(index, _):
            here = span(index, ROW_TILE)
            grad = parts[mine, here].astype(jnp.float32)
            norm = normed_ref[here]
            scaled = grad * gain_ref[...]
            stream = inverse_ref[here] * (
                scaled
                - jnp.mean(scaled, axis=1, keepdims=True)
                - norm * jnp.mean(scaled * norm, axis=1, keepdims=True)
            )
            stream_ref[here] = stream
            down_ref[here] = stream.astype(jnp.bfloat16)
            sums_ref[0:1] += jnp.sum(grad * norm, axis=0, keepdims=True)
            sums_ref[1:2] += jnp.sum(grad, axis=0, keepdims=True)
            sums_ref[2:3] += jnp.sum(stream, axis=0, keepdims=True)
            return _

        lax.fori_loop(0, rows // ROW_TILE, norm_tile, 0)

    return row_kernel(
        kernel, collective,
        [
            jax.ShapeDtypeStruct((rows, D), jnp.float32),
            jax.ShapeDtypeStruct((rows, D), jnp.bfloat16),
            jax.ShapeDtypeStruct((8, D), jnp.float32),
        ],
        [ANY, ANY, VMEM, VMEM, VMEM],
        [VMEM] * 3,
        [
            pltpu.VMEM(head_weight.shape, jnp.bfloat16),
            pltpu.VMEM((2, rows, vocab), jnp.bfloat16),
            pltpu.SemaphoreType.DMA((1 + shards,)),
        ]
        + sum_scratch(sizes, rows),
        2 * BLOCK * D * vocab,
    )(grad_logits, head_weight, normed, inverse, gain)


def branch_grad_rows(own, out_flat, down_weight, slope, sizes, collective):
    rows = own.shape[0]
    shards = sizes[0] * sizes[1]
    inner, hidden = out_flat.shape[0], down_weight.shape[0]

    def kernel(
        own_ref, outw_any, downw_any, slope_any, rows_any, ctx_any, up_any, sums_ref,
        full, send_sems, recv_sems, outw, downw, load_sems, slope, slope_sems, ctx, up, out_sems, row_sems,
    ):
        grid = Grid2(sizes)
        loads = [
            pltpu.make_async_copy(outw_any, outw, load_sems.at[0]),
            pltpu.make_async_copy(downw_any, downw, load_sems.at[1]),
        ]
        for copy in loads:
            copy.start()
        slopes = pltpu.make_async_copy(slope_any, slope, slope_sems)
        slopes.start()
        full[grid.index(*grid.me)] = own_ref[...]
        sums_ref[...] = jnp.zeros_like(sums_ref)
        grid.barrier()
        open_copies, raw_copies = [], []

        def ready(slow, fast, order):
            place = grid.index(slow, fast)
            slot = order % 2
            if order == 0:
                for copy in loads + [slopes]:
                    copy.wait()
            if order >= 2:
                for copy in open_copies.pop(0):
                    copy.wait()
            ctx[slot] = dot_nt(full[place], outw[...]).astype(jnp.bfloat16)
            tile = tile_of(hidden)

            def up_tile(index, _):
                here = span(index, tile)
                found = dot_nt(full[place], downw[here, :]) * slope[place, :, here].astype(jnp.float32)
                rounded = found.astype(jnp.bfloat16)
                up[slot, :, here] = rounded
                sums_ref[0:1, here] += jnp.sum(rounded.astype(jnp.float32), axis=0, keepdims=True)
                return _

            lax.fori_loop(0, hidden // tile, up_tile, 0)
            copies = [
                pltpu.make_async_copy(ctx.at[slot], ctx_any.at[place], out_sems.at[slot, 0]),
                pltpu.make_async_copy(up.at[slot], up_any.at[place], out_sems.at[slot, 1]),
            ]
            for copy in copies:
                copy.start()
            open_copies.append(copies)
            raw = pltpu.make_async_copy(full.at[place], rows_any.at[place], row_sems.at[order])
            raw.start()
            raw_copies.append(raw)

        run_gather(grid, sizes, rows, full, send_sems, recv_sems, ready)
        for copies in open_copies:
            for copy in copies:
                copy.wait()
        for copy in raw_copies:
            copy.wait()

    def out(columns):
        return jax.ShapeDtypeStruct((shards, rows, columns), jnp.bfloat16)

    return row_kernel(
        kernel, collective,
        [out(D), out(inner), out(hidden), jax.ShapeDtypeStruct((8, hidden), jnp.float32)],
        [VMEM, ANY, ANY, ANY],
        [ANY, ANY, ANY, VMEM],
        gather_scratch(sizes, rows)
        + [
            pltpu.VMEM(out_flat.shape, jnp.bfloat16),
            pltpu.VMEM(down_weight.shape, jnp.bfloat16),
            pltpu.SemaphoreType.DMA((2,)),
            pltpu.VMEM((shards, rows, hidden), jnp.bfloat16),
            pltpu.SemaphoreType.DMA,
            pltpu.VMEM((2, rows, inner), jnp.bfloat16),
            pltpu.VMEM((2, rows, hidden), jnp.bfloat16),
            pltpu.SemaphoreType.DMA((2, 2)),
            pltpu.SemaphoreType.DMA((shards,)),
        ],
        2 * BLOCK * D * (inner + hidden),
    )(own, out_flat, down_weight, slope)


def input_grad_rows(
    own, grad_stream, hid, grad_qkv, grad_up, qkv_flat, up_weight, gains, sizes, collective
):
    shards, rows, width = grad_qkv.shape
    hidden = grad_up.shape[2]

    def kernel(
        own_ref, stream_ref, hid_any, qkv_any, up_any, qkvw_any, upw_any, gains_ref, out_ref, sums_ref,
        qkvw, upw, weight_sems, hid, qkv, up, load_sems, stats, *scratch,
    ):
        grid = Grid2(sizes)
        parts = scratch[0]
        order = production_order(grid)

        def loads(i):
            place = order[i]
            return [
                pltpu.make_async_copy(hid_any.at[place], hid.at[i % 2], load_sems.at[i, 0]),
                pltpu.make_async_copy(qkv_any.at[place], qkv.at[i % 2], load_sems.at[i, 1]),
                pltpu.make_async_copy(up_any.at[place], up.at[i % 2], load_sems.at[i, 2]),
            ]

        copies = [loads(i) for i in range(shards)]
        weights = [
            pltpu.make_async_copy(qkvw_any, qkvw, weight_sems.at[0]),
            pltpu.make_async_copy(upw_any, upw, weight_sems.at[1]),
        ]
        for copy in copies[0] + weights:
            copy.start()
        sums_ref[...] = jnp.zeros_like(sums_ref)
        grid.barrier()
        for copy in weights:
            copy.wait()
        count = [0]

        def produce(slow, fast):
            place = grid.index(slow, fast)
            i = count[0]
            count[0] += 1
            if i + 1 < shards:
                for copy in copies[i + 1]:
                    copy.start()
            for copy in copies[i]:
                copy.wait()
            slot = i % 2

            def stats_tile(index, _):
                here = span(index, ROW_TILE)
                values = hid[slot, here].astype(jnp.float32)
                mean = jnp.mean(values, axis=1, keepdims=True)
                centered = values - mean
                stats[0, here] = mean
                stats[1, here] = lax.rsqrt(jnp.mean(centered * centered, axis=1, keepdims=True) + EPSILON)
                return _

            lax.fori_loop(0, rows // ROW_TILE, stats_tile, 0)

            def columns(index, _):
                here = span(index, 256)
                one = dot_nt(qkv[slot], qkvw[here, :])
                two = dot_nt(up[slot], upw[here, :])
                normed = (hid[slot, :, here].astype(jnp.float32) - stats[0]) * stats[1]
                parts[place, :, here] = (one * gains_ref[0:1, here] + two * gains_ref[1:2, here]).astype(
                    jnp.bfloat16
                )
                sums_ref[0:1, here] += jnp.sum(one * normed, axis=0, keepdims=True)
                sums_ref[1:2, here] += jnp.sum(one, axis=0, keepdims=True)
                sums_ref[2:3, here] += jnp.sum(two * normed, axis=0, keepdims=True)
                sums_ref[3:4, here] += jnp.sum(two, axis=0, keepdims=True)
                return _

            lax.fori_loop(0, D // 256, columns, 0)

        run_scatter(grid, sizes, rows, scratch, produce)
        mine = grid.index(*grid.me)

        def norm_tile(index, _):
            here = span(index, ROW_TILE)
            grad = parts[mine, here].astype(jnp.float32)
            centered, inverse = tile_stats(own_ref[here].astype(jnp.float32))
            normed = centered * inverse
            out_ref[here] = stream_ref[here] + inverse * (
                grad
                - jnp.mean(grad, axis=1, keepdims=True)
                - normed * jnp.mean(grad * normed, axis=1, keepdims=True)
            )
            return _

        lax.fori_loop(0, rows // ROW_TILE, norm_tile, 0)

    return row_kernel(
        kernel, collective,
        [jax.ShapeDtypeStruct((rows, D), jnp.float32), jax.ShapeDtypeStruct((8, D), jnp.float32)],
        [VMEM, VMEM, ANY, ANY, ANY, ANY, ANY, VMEM],
        [VMEM, VMEM],
        [
            pltpu.VMEM(qkv_flat.shape, jnp.bfloat16),
            pltpu.VMEM(up_weight.shape, jnp.bfloat16),
            pltpu.SemaphoreType.DMA((2,)),
            pltpu.VMEM((2, rows, D), jnp.bfloat16),
            pltpu.VMEM((2, rows, width), jnp.bfloat16),
            pltpu.VMEM((2, rows, hidden), jnp.bfloat16),
            pltpu.SemaphoreType.DMA((shards, 3)),
            pltpu.VMEM((2, rows, 1), jnp.float32),
        ]
        + sum_scratch(sizes, rows),
        2 * BLOCK * D * (width + hidden),
    )(own, grad_stream, hid, grad_qkv, grad_up, qkv_flat, up_weight, gains)


def segment_rows(block_lengths):
    row_ends = jnp.cumsum(block_lengths)
    row_ids = jnp.arange(BLOCK, dtype=jnp.int32)
    passed = (row_ids[:, None] >= row_ends[None, :]).astype(jnp.int32)
    segment = jnp.sum(passed, axis=1)
    position = row_ids - jnp.sum(passed * block_lengths[None, :], axis=1)
    return (segment, position)


def merge_stats(left_stats, right_stats):
    left_top, left_sum, left_pick = left_stats
    right_top, right_sum, right_pick = right_stats
    joint_top = jnp.maximum(left_top, right_top)
    joint_sum = left_sum * jnp.exp(left_top - joint_top) + right_sum * jnp.exp(
        right_top - joint_top
    )
    return (joint_top, joint_sum, left_pick + right_pick)


def row_of(vector):
    return vector.astype(jnp.float32)[None, :]


def rounded_sum(values):
    return lax.psum(values.astype(jnp.bfloat16), "dp")


def after(values, earlier):
    flat, tree = jax.tree.flatten(values)

    def kernel(*refs):
        del refs

    held = pl.pallas_call(
        kernel,
        out_shape=[jax.ShapeDtypeStruct(v.shape, v.dtype) for v in flat],
        in_specs=[ANY] * (len(flat) + 1),
        out_specs=[ANY] * len(flat),
        input_output_aliases={i: i for i in range(len(flat))},
    )(*flat, earlier)
    return jax.tree.unflatten(tree, held)


def per_device(
    hidden, targets, lengths, labels, ref_logps, ln1_gain, ln1_bias, ln2_gain, ln2_bias, qkv_weight, qv_bias,
    out_weight, up_weight, up_bias, down_weight, branch_bias, lnf_gain, lnf_bias, head_weight,
):
    sizes = lines_of(lax.axis_size("seq"))
    own = hidden[0]
    local_heads = qkv_weight.shape[1]
    local_vocab = head_weight.shape[1]
    local_hidden = up_weight.shape[1]
    width = local_heads * 3 * HEAD_DIM
    inner = local_heads * HEAD_DIM
    qv_float = qv_bias.astype(jnp.float32)
    full_bias = jnp.concatenate(
        [qv_float[:, :HEAD_DIM], jnp.zeros_like(qv_float[:, :HEAD_DIM]), qv_float[:, HEAD_DIM:]], axis=-1
    ).reshape(1, width)
    qkv_flat = qkv_weight.reshape(D, width)
    out_flat = out_weight.reshape(inner, D)
    block_lengths = lengths[0]
    segment, position = segment_rows(block_lengths)
    start = jnp.arange(BLOCK, dtype=jnp.int32) - position
    start_col = start[:, None]
    first_tile = start[::ATT_TILE] // ATT_TILE
    planes = rotary_planes(position)

    norms = jnp.concatenate([row_of(v) for v in (ln1_gain, ln1_bias, ln2_gain, ln2_bias)], axis=0)
    hid, first_full, second_full, qkv, act, slope = open_rows(
        own, sizes, 0, norms, qkv_flat, full_bias, up_weight, row_of(up_bias), planes
    )
    flat_qkv = qkv.reshape(BLOCK, width)
    ctx, lse = attention_forward(flat_qkv, start_col, first_tile, local_heads)
    shards, rows = hid.shape[0], hid.shape[1]
    end_norms = jnp.concatenate([row_of(v) for v in (lnf_gain, lnf_bias, branch_bias)], axis=0)
    output, final, normed, inverse = branch_rows(
        own, ctx.reshape(shards, rows, inner), act, out_flat, down_weight, end_norms, sizes, 1
    )
    final_full, weights, stats = logit_rows(final, head_weight, targets[0][:, None], sizes, 2)

    local_top = stats[:, 0]
    gathered = lax.all_gather(stats[:, :3].T, "seq")
    merged = tuple(gathered[0, i] for i in range(3))
    for other in range(1, gathered.shape[0]):
        merged = merge_stats(merged, tuple(gathered[other, i] for i in range(3)))
    log_total = merged[0] + jnp.log(merged[1])
    token_logp = merged[2] - log_total
    member = (jnp.arange(EXB, dtype=jnp.int32)[:, None] == segment[None, :]).astype(jnp.float32)
    float_lengths = block_lengths.astype(jnp.float32)
    mean_logp = jnp.sum(member * token_logp[None, :], axis=1) / float_lengths
    log_ratio = mean_logp - ref_logps[0]
    center = lax.psum(jnp.sum(log_ratio), "dp") / (lax.axis_size("dp") * EXB)
    label_sign = (2 * labels[0] - 1).astype(jnp.float32)
    squashed = jax.nn.sigmoid(BETA * label_sign * (log_ratio - center))
    losses = 1.0 - squashed
    grad_ratio = -LOSS_SCALE * BETA * label_sign * squashed * (1.0 - squashed)
    token_grad = jnp.sum(member * (grad_ratio / float_lengths)[:, None], axis=0)

    vocab_ids = lax.axis_index("seq") * local_vocab + jnp.arange(local_vocab, dtype=jnp.int32)
    onehot = (vocab_ids[None, :] == targets[0][:, None]).astype(jnp.float32)
    share = jnp.exp(local_top - log_total)
    grad_logits = (
        token_grad[:, None] * (onehot - weights.reshape(BLOCK, local_vocab).astype(jnp.float32) * share[:, None])
    ).astype(jnp.bfloat16)
    head_sum = rounded_sum(dot_tn(final_full.reshape(BLOCK, D), grad_logits))

    grad_stream, grad_own, end_sums = final_grad_rows(
        grad_logits.reshape(shards, rows, local_vocab), head_weight, normed, inverse, row_of(lnf_gain), sizes, 3
    )
    grad_full, grad_ctx, grad_up, up_sums = branch_grad_rows(
        grad_own, out_flat, down_weight, slope, sizes, 4
    )
    grad_rows = grad_full.reshape(BLOCK, D)
    out_grad = dot_tn(ctx, grad_rows).astype(jnp.bfloat16)
    down_grad = dot_tn(act.reshape(BLOCK, local_hidden), grad_rows).astype(jnp.bfloat16)
    up_grad = dot_tn(second_full.reshape(BLOCK, D), grad_up.reshape(BLOCK, local_hidden)).astype(jnp.bfloat16)
    middle = lax.psum(after((out_grad, down_grad, up_grad, up_sums[0].astype(jnp.bfloat16)), head_sum[:8, :128]), "dp")
    grad_qkv, qkv_sums = attention_backward(
        flat_qkv, start_col, first_tile, local_heads, ctx, lse, grad_ctx.reshape(BLOCK, inner), planes
    )
    qkv_grad = dot_tn(first_full.reshape(BLOCK, D), grad_qkv).astype(jnp.bfloat16)
    qkv_sums = qkv_sums[:, 0]
    qv_grad = jnp.concatenate([qkv_sums[:, :HEAD_DIM], qkv_sums[:, 2 * HEAD_DIM :]], axis=-1)
    last = lax.psum(after((qkv_grad, qv_grad.astype(jnp.bfloat16)), jnp.concatenate([v[:8, :128] for v in middle[:3]] + [jnp.broadcast_to(middle[3][None, :128], (8, 128))])), "dp")
    gains = jnp.concatenate([row_of(ln1_gain), row_of(ln2_gain)], axis=0)
    grad_input, start_sums = input_grad_rows(
        own, grad_stream, hid, grad_qkv.reshape(shards, rows, width), grad_up, qkv_flat, up_weight, gains,
        sizes, 5,
    )
    small = lax.psum(jnp.concatenate([start_sums[:4], end_sums[:3]], axis=0), ("dp", "seq"))
    wide = lambda values: values.astype(jnp.float32)
    return (
        losses[None],
        output[None],
        grad_input[None],
        small[0],
        small[1],
        small[2],
        small[3],
        wide(last[0]).reshape(qkv_weight.shape),
        wide(last[1]),
        wide(middle[0]).reshape(out_weight.shape),
        wide(middle[2]),
        wide(middle[3]),
        wide(middle[1]),
        small[6],
        small[4],
        small[5],
        wide(head_sum),
    )


def solution(mesh):
    return jax.shard_map(
        per_device,
        mesh=mesh,
        in_specs=(
            P("dp", "seq", None),
            P("dp", None),
            P("dp", None),
            P("dp", None),
            P("dp", None),
            P(),
            P(),
            P(),
            P(),
            P(None, "seq", None),
            P("seq", None),
            P("seq", None, None),
            P(None, "seq"),
            P("seq"),
            P("seq", None),
            P(),
            P(),
            P(),
            P(None, "seq"),
        ),
        out_specs=(
            P("dp", None),
            P("dp", "seq", None),
            P("dp", "seq", None),
            P(),
            P(),
            P(),
            P(),
            P(None, "seq", None),
            P("seq", None),
            P("seq", None, None),
            P(None, "seq"),
            P("seq"),
            P("seq", None),
            P(),
            P(),
            P(),
            P(None, "seq"),
        ),
        check_vma=False,
    )
```

```python
import jax
import jax.numpy as jnp
from jax import lax
from jax.experimental import pallas as pl
from jax.experimental.pallas import tpu as pltpu
from jax.sharding import PartitionSpec as P

D = 2048
HEAD_DIM = 128
ROT = 32
BLOCK = 2048
EXB = 8
EPSILON = 1e-05
BETA = 0.25
LOSS_SCALE = 65536.0
HALVES = 2
VMEM_LIMIT = 62 * 2**20

MESH = pl.DeviceIdType.MESH


class Grid2:
    def __init__(self, sizes):
        self.n = sizes
        place = lax.axis_index("seq")
        self.me = (place // sizes[1], lax.rem(place, sizes[1]))

    def index(self, slow, fast):
        return slow * self.n[1] + fast

    def device(self, axis, spot):
        here = list(self.me)
        here[axis] = spot
        return {"seq": self.index(*here)}

    def nearest(self, axis, rank):
        n, m = self.n[axis], self.me[axis]
        if rank == 0:
            return m
        if n == 2:
            return 1 - m
        after = n - 1 - m
        both = jnp.minimum(m, after)
        dist = (rank + 1) // 2
        near = m - dist if rank % 2 else m + dist
        far = jnp.where(m < after, m + (rank - both), m - (rank - both))
        return jnp.where(rank <= 2 * both, near, far)

    def neighbours(self):
        found = []
        for axis in (0, 1):
            m, n = self.me[axis], self.n[axis]
            if n == 2:
                found.append((None, self.device(axis, 1 - m)))
            elif n > 2:
                found.append((m > 0, self.device(axis, m - 1)))
                found.append((m < n - 1, self.device(axis, m + 1)))
        return found

    def barrier(self):
        sem = pltpu.get_barrier_semaphore()
        amount = jnp.int32(0)
        for there, device in self.neighbours():
            def tell(device=device):
                pl.semaphore_signal(sem, inc=1, device_id=device, device_id_type=MESH)
            if there is None:
                tell()
                amount = amount + 1
            else:
                pl.when(there)(tell)
                amount = amount + there.astype(jnp.int32)
        pl.semaphore_wait(sem, amount)


class Sender:
    def __init__(self, send_sems):
        self.sems = send_sems
        self.used = 0
        self.open = []

    def send(self, src, dst, recv_sem, device, when=None):
        copy = pltpu.make_async_remote_copy(
            src_ref=src, dst_ref=dst, send_sem=self.sems.at[self.used], recv_sem=recv_sem,
            device_id=device, device_id_type=MESH)
        self.used += 1
        if when is None:
            copy.start()
        else:
            pl.when(when)(copy.start)
        self.open.append((when, copy))

    def finish(self):
        for when, copy in self.open:
            if when is None:
                copy.wait_send()
            else:
                pl.when(when)(copy.wait_send)
        self.open = []


def gather_sends(sizes, halves):
    return halves * 2 * (sizes[0] * sizes[1] * 2 + 8)


def gather_rounds(grid, sender, piece, recv_sems, halves, cut, ready):
    n, me = grid.n, grid.me

    def arrived(slow, fast, half, kind):
        ref = piece(grid.index(slow, fast), half, kind)
        sem = recv_sems.at[kind, half, grid.index(slow, fast)]
        pltpu.make_async_copy(ref, ref, sem).wait()

    def push(slow, fast, half, kind, axis, spot, when):
        ref = piece(grid.index(slow, fast), half, kind)
        sem = recv_sems.at[kind, half, grid.index(slow, fast)]
        sender.send(ref, ref, sem, grid.device(axis, spot), when)

    def spread(slow, fast, half, kind, axis):
        m, size = me[axis], n[axis]
        if size == 2:
            push(slow, fast, half, kind, axis, 1 - m, None)
        elif size > 2:
            push(slow, fast, half, kind, axis, m + 1, m < size - 1)
            push(slow, fast, half, kind, axis, m - 1, m > 0)

    def onward(slow, fast, half, kind, axis):
        m, size = me[axis], n[axis]
        if size <= 2:
            return
        source = (slow, fast)[axis]
        below = source < m
        when = (below & (m < size - 1)) | (jnp.logical_not(below) & (m > 0))
        push(slow, fast, half, kind, axis, jnp.where(below, m + 1, m - 1), when)

    todo = []

    def work(count=1):
        for _ in range(count):
            if todo:
                ready(*todo.pop(0))

    def settle(k):
        slow = grid.nearest(0, k)
        for half in range(halves):
            for l in range(n[1]):
                fast = grid.nearest(1, l)
                if k > 0:
                    arrived(slow, fast, half, 1)
                    onward(slow, fast, half, 1, 0)
                else:
                    spread(slow, fast, half, 1, 0)

    def complete(k):
        slow = grid.nearest(0, k)
        if k > 0:
            todo.append((slow, me[1], k * n[1]))
        for l in range(1, n[1]):
            fast = grid.nearest(1, l)
            if cut[0]:
                for half in range(halves):
                    arrived(slow, fast, half, 0)
                    onward(slow, fast, half, 0, 1)
            todo.append((slow, fast, k * n[1] + l))

    for half in range(halves):
        for kind in (1, 0):
            if cut[kind]:
                spread(me[0], me[1], half, kind, kind)
        if cut[0]:
            spread(me[0], me[1], half, 0, 1)
    todo.append((me[0], me[1], 0))
    work()
    if cut[1]:
        for half in range(halves):
            for l in range(1, n[1]):
                fast = grid.nearest(1, l)
                arrived(me[0], fast, half, 1)
                onward(me[0], fast, half, 1, 1)
    for k in range(1, n[0]):
        slow = grid.nearest(0, k)
        for half in range(halves):
            if cut[0]:
                arrived(slow, me[1], half, 0)
                onward(slow, me[1], half, 0, 0)
                spread(slow, me[1], half, 0, 1)
            if half < halves - 1:
                work()
        if cut[1]:
            settle(k - 1)
        complete(k - 1)
        work()
    if cut[1]:
        settle(n[0] - 1)
    work(len(todo))
    complete(n[0] - 1)
    work(len(todo))


def scatter_slots(n):
    return 1 if n == 2 else n + 1


class Scatter:
    def __init__(self, grid, sender, part, bufs, sems, halves, cut):
        self.grid, self.sender, self.part = grid, sender, part
        self.bufs, self.sems, self.halves, self.cut = bufs, sems, halves, cut

    def slot(self, axis, target, from_below):
        if self.grid.n[axis] == 2:
            return 0
        return target + jnp.where(from_below, 1, 0)

    def take(self, kind, stage, axis, other, target, from_below, half, when, slot_index):
        buf, sem = self.bufs[kind][stage], self.sems[kind][stage]
        slot = self.slot(axis, target, from_below)

        def add():
            ref = buf.at[other, slot, half]
            pltpu.make_async_copy(ref, ref, sem.at[other, slot, half]).wait()
            mine = self.part(slot_index, half, kind)
            mine[...] = (mine[...].astype(jnp.float32) + ref[...].astype(jnp.float32)).astype(mine.dtype)

        if when is None:
            add()
        else:
            pl.when(when)(add)

    def toward(self, kind, stage, axis, other, target, half, slow, fast):
        grid = self.grid
        m, n = grid.me[axis], grid.n[axis]
        up = target > m
        index = grid.index(slow, fast)
        if n > 2:
            incoming = (up & (m > 0)) | (jnp.logical_not(up) & (m < n - 1))
            self.take(kind, stage, axis, other, target, up, half, incoming, index)
        buf, sem = self.bufs[kind][stage], self.sems[kind][stage]
        slot = self.slot(axis, target, up)
        spot = 1 - m if n == 2 else jnp.where(up, m + 1, m - 1)
        self.sender.send(
            self.part(index, half, kind), buf.at[other, slot, half], sem.at[other, slot, half],
            grid.device(axis, spot))

    def last(self, kind, stage, axis, other, half, slow, fast):
        grid = self.grid
        m, n = grid.me[axis], grid.n[axis]
        index = grid.index(slow, fast)
        if n == 2:
            self.take(kind, stage, axis, other, m, m > 0, half, None, index)
        elif n > 2:
            self.take(kind, stage, axis, other, m, jnp.bool_(True), half, m > 0, index)
            self.take(kind, stage, axis, other, m, jnp.bool_(False), half, m < n - 1, index)

    def run(self, produce, made=lambda: None, between=lambda: None):
        grid, n, me = self.grid, self.grid.n, self.grid.me

        def chain(k):
            slow = grid.nearest(0, k)
            for half in range(self.halves):
                self.last(0, 0, 1, slow, half, slow, me[1])
                self.toward(0, 1, 0, 0, slow, half, slow, me[1])

        for k in reversed(range(n[0])):
            slow = grid.nearest(0, k)
            for l in reversed(range(n[1])):
                fast = grid.nearest(1, l)
                produce(slow, fast)
                for half in range(self.halves):
                    if self.cut[0] and l > 0:
                        self.toward(0, 0, 1, slow, fast, half, slow, fast)
                    if self.cut[1] and k > 0:
                        self.toward(1, 0, 0, fast, slow, half, slow, fast)
            if k == 0:
                made()
            if self.cut[0] and k < n[0] - 1:
                chain(k + 1)
        between()
        if self.cut[1]:
            for half in range(self.halves):
                for l in reversed(range(n[1])):
                    fast = grid.nearest(1, l)
                    self.last(1, 0, 0, fast, half, me[0], fast)
                    if l > 0:
                        self.toward(1, 1, 1, 0, fast, half, me[0], fast)
        if self.cut[0]:
            for half in range(self.halves):
                self.last(0, 0, 1, me[0], half, me[0], me[1])
        for half in range(self.halves):
            if self.cut[1]:
                self.last(1, 1, 1, 0, half, me[0], me[1])
            if self.cut[0]:
                self.last(0, 1, 0, 0, half, me[0], me[1])


def scatter_scratch(sizes, halves, rows, cols, cut):
    bufs, sems = [], []
    for kind, stages in ((0, (1, 0)), (1, (0, 1))):
        for stage, axis in enumerate(stages):
            lead = (sizes[1 - axis] if stage == 0 else 1, scatter_slots(sizes[axis]), halves)
            width = max(cut[kind], 128)
            bufs.append(pltpu.VMEM(lead + (rows // halves, width), jnp.bfloat16))
            sems.append(pltpu.SemaphoreType.DMA(lead))
    return bufs, sems


def scatter_sends(sizes, halves):
    return halves * 2 * (sizes[0] * sizes[1] + sizes[0] + sizes[1])


def lines_of(seq):
    fast = 2 if seq <= 8 else 4
    return (seq // fast, fast)


ATT_TILE = 256
SCALE = HEAD_DIM ** (-0.5)


def dot_nt(left, right):
    return lax.dot_general(left, right, (((1,), (1,)), ((), ())), preferred_element_type=jnp.float32)


def dot_tn(left, right):
    return lax.dot_general(left, right, (((0,), (0,)), ((), ())), preferred_element_type=jnp.float32)


def rotary_planes(position):
    half_rot = ROT // 2
    frequency = 10000.0 ** (-2.0 * jnp.arange(half_rot, dtype=jnp.float32) / ROT)
    angles = position.astype(jnp.float32)[:, None] * frequency[None, :]
    cos, sin = jnp.cos(angles), jnp.sin(angles)
    rows = position.shape[0]
    rest = jnp.zeros((rows, HEAD_DIM - ROT), jnp.float32)
    none = jnp.zeros_like(sin)
    return (
        jnp.concatenate([cos, cos, rest + 1.0], axis=1),
        jnp.concatenate([none, sin, rest], axis=1),
        jnp.concatenate([-sin, none, rest], axis=1),
    )


def turn(vector, cos, from_below, from_above):
    half_rot = ROT // 2
    return (
        vector * cos
        + pltpu.roll(vector, half_rot, 1) * from_below
        + pltpu.roll(vector, HEAD_DIM - half_rot, 1) * from_above
    )


def tile_mask(start_col, query_tile, key_tile):
    shape = (ATT_TILE, ATT_TILE)
    query_ids = query_tile * ATT_TILE + lax.broadcasted_iota(jnp.int32, shape, 0)
    key_ids = key_tile * ATT_TILE + lax.broadcasted_iota(jnp.int32, shape, 1)
    return (key_ids >= start_col) & (key_ids <= query_ids)


def attention_forward(qkv, start_col, first_tile, heads):
    tiles = BLOCK // ATT_TILE

    def kernel(first_ref, q_ref, k_ref, v_ref, start_ref, ctx_ref, lse_ref):
        tile = pl.program_id(1)
        queries = q_ref[...]
        start = start_ref[...]

        def step(key_tile, carry):
            top, total, acc = carry
            rows = pl.ds(pl.multiple_of(key_tile * ATT_TILE, ATT_TILE), ATT_TILE)
            scores = dot_nt(queries, k_ref[rows, :]) * SCALE
            scores = jnp.where(tile_mask(start, tile, key_tile), scores, -1e30)
            new_top = jnp.maximum(top, jnp.max(scores, axis=1, keepdims=True))
            shrink = jnp.exp(top - new_top)
            weights = jnp.exp(scores - new_top)
            total = total * shrink + jnp.sum(weights, axis=1, keepdims=True)
            acc = acc * shrink + jnp.dot(
                weights.astype(jnp.bfloat16), v_ref[rows, :], preferred_element_type=jnp.float32
            )
            return (new_top, total, acc)

        begin = (
            jnp.full((ATT_TILE, 1), -1e30, jnp.float32),
            jnp.zeros((ATT_TILE, 1), jnp.float32),
            jnp.zeros((ATT_TILE, HEAD_DIM), jnp.float32),
        )
        begin = step(tile, begin)
        top, total, acc = lax.fori_loop(first_ref[tile], tile, step, begin)
        ctx_ref[...] = (acc / total).astype(jnp.bfloat16)
        lse_ref[...] = top + jnp.log(total)

    return pl.pallas_call(
        kernel,
        grid_spec=pltpu.PrefetchScalarGridSpec(
            num_scalar_prefetch=1,
            grid=(heads, tiles),
            in_specs=[
                pl.BlockSpec((ATT_TILE, HEAD_DIM), lambda h, i, first: (i, 3 * h)),
                pl.BlockSpec((BLOCK, HEAD_DIM), lambda h, i, first: (0, 3 * h + 1)),
                pl.BlockSpec((BLOCK, HEAD_DIM), lambda h, i, first: (0, 3 * h + 2)),
                pl.BlockSpec((ATT_TILE, 1), lambda h, i, first: (i, 0)),
            ],
            out_specs=[
                pl.BlockSpec((ATT_TILE, HEAD_DIM), lambda h, i, first: (i, h)),
                pl.BlockSpec((pl.squeezed, ATT_TILE, 1), lambda h, i, first: (h, i, 0)),
            ],
        ),
        out_shape=[
            jax.ShapeDtypeStruct((BLOCK, heads * HEAD_DIM), jnp.bfloat16),
            jax.ShapeDtypeStruct((heads, BLOCK, 1), jnp.float32),
        ],
        compiler_params=pltpu.CompilerParams(vmem_limit_bytes=VMEM_LIMIT),
    )(first_tile, qkv, qkv, qkv, start_col)


def attention_backward(qkv, start_col, first_tile, heads, ctx, lse, grad_ctx, planes, before):
    tiles = BLOCK // ATT_TILE

    def kernel(
        first_ref, q_ref, k_ref, v_ref, start_ref, ctx_ref, lse_ref, do_ref, cos_ref, below_ref,
        above_ref, *rest,
    ):
        out_ref, sums_ref, dk_ref, dv_ref = rest[len(before) :]
        tile = pl.program_id(1)

        @pl.when(tile == 0)
        def _():
            dk_ref[...] = jnp.zeros_like(dk_ref)
            dv_ref[...] = jnp.zeros_like(dv_ref)

        queries = q_ref[...]
        start = start_ref[...]
        grads = do_ref[...]
        lse_rows = lse_ref[...]
        inner = jnp.sum(
            grads.astype(jnp.float32) * ctx_ref[...].astype(jnp.float32), axis=1, keepdims=True
        )

        def step(key_tile, dq):
            rows = pl.ds(pl.multiple_of(key_tile * ATT_TILE, ATT_TILE), ATT_TILE)
            keys = k_ref[rows, :]
            scores = dot_nt(queries, keys) * SCALE
            probs = jnp.where(
                tile_mask(start, tile, key_tile), jnp.exp(scores - lse_rows), 0.0
            )
            grad_probs = dot_nt(grads, v_ref[rows, :])
            grad_scores = (probs * (grad_probs - inner)).astype(jnp.bfloat16)
            dv_ref[rows, :] += dot_tn(probs.astype(jnp.bfloat16), grads)
            dk_ref[rows, :] += dot_tn(grad_scores, queries)
            return dq + jnp.dot(grad_scores, keys, preferred_element_type=jnp.float32)

        dq = lax.fori_loop(
            first_ref[tile], tile + 1, step, jnp.zeros((ATT_TILE, HEAD_DIM), jnp.float32)
        )
        here = pl.ds(pl.multiple_of(tile * ATT_TILE, ATT_TILE), ATT_TILE)
        out_ref[here, :HEAD_DIM] = turn(
            dq * SCALE, cos_ref[here, :], -below_ref[here, :], -above_ref[here, :]
        ).astype(jnp.bfloat16)

        @pl.when(tile == tiles - 1)
        def _():
            def finish(index, sums):
                rows = pl.ds(pl.multiple_of(index * ATT_TILE, ATT_TILE), ATT_TILE)
                out_ref[rows, HEAD_DIM : 2 * HEAD_DIM] = turn(
                    dk_ref[rows, :] * SCALE, cos_ref[rows, :], -below_ref[rows, :], -above_ref[rows, :]
                ).astype(jnp.bfloat16)
                out_ref[rows, 2 * HEAD_DIM :] = dv_ref[rows, :].astype(jnp.bfloat16)
                return sums + jnp.sum(out_ref[rows, :].astype(jnp.float32), axis=0, keepdims=True)

            sums_ref[...] = lax.fori_loop(
                0, tiles, finish, jnp.zeros((1, 3 * HEAD_DIM), jnp.float32)
            )

    whole = pl.BlockSpec((BLOCK, HEAD_DIM), lambda h, i, first: (0, 0))
    return pl.pallas_call(
        kernel,
        grid_spec=pltpu.PrefetchScalarGridSpec(
            num_scalar_prefetch=1,
            grid=(heads, tiles),
            in_specs=[
                pl.BlockSpec((ATT_TILE, HEAD_DIM), lambda h, i, first: (i, 3 * h)),
                pl.BlockSpec((BLOCK, HEAD_DIM), lambda h, i, first: (0, 3 * h + 1)),
                pl.BlockSpec((BLOCK, HEAD_DIM), lambda h, i, first: (0, 3 * h + 2)),
                pl.BlockSpec((ATT_TILE, 1), lambda h, i, first: (i, 0)),
                pl.BlockSpec((ATT_TILE, HEAD_DIM), lambda h, i, first: (i, h)),
                pl.BlockSpec((pl.squeezed, ATT_TILE, 1), lambda h, i, first: (h, i, 0)),
                pl.BlockSpec((ATT_TILE, HEAD_DIM), lambda h, i, first: (i, h)),
                whole,
                whole,
                whole,
            ]
            + [pl.BlockSpec(memory_space=pl.ANY)] * len(before),
            out_specs=[
                pl.BlockSpec((BLOCK, 3 * HEAD_DIM), lambda h, i, first: (0, h)),
                pl.BlockSpec((pl.squeezed, 1, 3 * HEAD_DIM), lambda h, i, first: (h, 0, 0)),
            ],
            scratch_shapes=[
                pltpu.VMEM((BLOCK, HEAD_DIM), jnp.float32),
                pltpu.VMEM((BLOCK, HEAD_DIM), jnp.float32),
            ],
        ),
        out_shape=[
            jax.ShapeDtypeStruct((BLOCK, heads * 3 * HEAD_DIM), jnp.bfloat16),
            jax.ShapeDtypeStruct((heads, 1, 3 * HEAD_DIM), jnp.float32),
        ],
        compiler_params=pltpu.CompilerParams(vmem_limit_bytes=VMEM_LIMIT),
    )(first_tile, qkv, qkv, qkv, start_col, ctx, lse, grad_ctx, *planes, *before)


def gather_cut(sizes):
    if sizes[0] == 4 and sizes[1] == 2:
        return (1664, 384)
    return (D // 2, D // 2)


def columns_of(cut, kind):
    return pl.ds(0, cut[0]) if kind == 0 else pl.ds(cut[0], cut[1])


def tile_of(width):
    return 256 if width % 256 == 0 else 128


def span(index, size):
    return pl.ds(pl.multiple_of(index * size, size), size)


ANY = pl.BlockSpec(memory_space=pl.ANY)
VMEM = pl.BlockSpec(memory_space=pltpu.VMEM)


def row_kernel(kernel, collective, out_shape, in_specs, out_specs, scratch, cost, before=()):
    def body(*refs):
        kernel(*refs[len(before):])

    def call(*args):
        return pl.pallas_call(
            body,
            out_shape=out_shape,
            in_specs=[ANY] * len(before) + in_specs,
            out_specs=out_specs,
            scratch_shapes=scratch,
            cost_estimate=pl.CostEstimate(flops=cost, bytes_accessed=2**28, transcendentals=0),
            compiler_params=pltpu.CompilerParams(
                collective_id=collective, has_side_effects=True, vmem_limit_bytes=VMEM_LIMIT
            ),
        )(*before, *args)

    return call


def gather_scratch(sizes, rows):
    shards = sizes[0] * sizes[1]
    return [
        pltpu.VMEM((shards, rows, D), jnp.bfloat16),
        pltpu.SemaphoreType.DMA((gather_sends(sizes, HALVES),)),
        pltpu.SemaphoreType.DMA((2, HALVES, shards)),
    ]


def run_gather(grid, sizes, rows, full, send_sems, recv_sems, ready):
    cut = gather_cut(sizes)
    step = rows // HALVES
    sender = Sender(send_sems)

    def piece(slot, half, kind):
        return full.at[slot, pl.ds(half * step, step), columns_of(cut, kind)]

    gather_rounds(grid, sender, piece, recv_sems, HALVES, cut, ready)
    sender.finish()


def sum_scratch(sizes, rows):
    shards = sizes[0] * sizes[1]
    bufs, sems = scatter_scratch(sizes, HALVES, rows, D, gather_cut(sizes))
    return (
        [pltpu.VMEM((shards, rows, D), jnp.bfloat16)]
        + bufs
        + sems
        + [pltpu.SemaphoreType.DMA((scatter_sends(sizes, HALVES),))]
    )


def run_scatter(grid, sizes, rows, scratch, produce, *hooks):
    cut = gather_cut(sizes)
    step = rows // HALVES
    parts, b0, b1, b2, b3, s0, s1, s2, s3, send_sems = scratch
    sender = Sender(send_sems)

    def part(slot, half, kind):
        return parts.at[slot, pl.ds(half * step, step), columns_of(cut, kind)]

    scatter = Scatter(
        grid, sender, part, ((b0, b1), (b2, b3)), ((s0, s1), (s2, s3)), HALVES, cut
    )
    scatter.run(produce, *hooks)
    sender.finish()


def production_order(grid):
    return [
        grid.index(grid.nearest(0, k), grid.nearest(1, l))
        for k in reversed(range(grid.n[0]))
        for l in reversed(range(grid.n[1]))
    ]


ROW_TILE = 32


def tile_stats(values):
    centered = values - jnp.mean(values, axis=1, keepdims=True)
    inverse = lax.rsqrt(jnp.mean(centered * centered, axis=1, keepdims=True) + EPSILON)
    return centered, inverse


def open_rows(own, sizes, collective, norms, qkv_flat, qkv_bias, up_weight, up_bias, planes):
    rows = own.shape[0]
    shards = sizes[0] * sizes[1]
    width, hidden = qkv_flat.shape[1], up_weight.shape[1]
    heads = width // (3 * HEAD_DIM)

    def kernel(
        own_ref, norms_ref, qkvw_any, qkvb_ref, upw_any, upb_ref, cos_ref, below_ref, above_ref,
        hid_any, one_any, two_any, qkv_any, act_any, slope_any,
        full, send_sems, recv_sems, qkvw, upw, load_sems, one, two, qkv, act, slope, out_sems, row_sems,
    ):
        grid = Grid2(sizes)
        loads = [
            pltpu.make_async_copy(qkvw_any, qkvw, load_sems.at[0]),
            pltpu.make_async_copy(upw_any, upw, load_sems.at[1]),
        ]
        for copy in loads:
            copy.start()
        full[grid.index(*grid.me)] = own_ref[...]
        grid.barrier()
        open_copies = []

        def outs(place, slot):
            pairs = ((one, one_any), (two, two_any), (qkv, qkv_any), (act, act_any), (slope, slope_any))
            return [
                pltpu.make_async_copy(here.at[slot], there.at[place], out_sems.at[slot, i])
                for i, (here, there) in enumerate(pairs)
            ]

        def ready(slow, fast, order):
            place = grid.index(slow, fast)
            slot = order % 2
            if order == 0:
                for copy in loads:
                    copy.wait()
            if order >= 2:
                for copy in open_copies.pop(0):
                    copy.wait()

            def norm_tile(index, _):
                here = span(index, ROW_TILE)
                centered, inverse = tile_stats(full[place, here].astype(jnp.float32))
                normed = centered * inverse
                one[slot, here] = (normed * norms_ref[0:1] + norms_ref[1:2]).astype(jnp.bfloat16)
                two[slot, here] = (normed * norms_ref[2:3] + norms_ref[3:4]).astype(jnp.bfloat16)
                return _

            lax.fori_loop(0, rows // ROW_TILE, norm_tile, 0)
            places = pl.ds(pl.multiple_of(place * rows, rows), rows)
            cos, below, above = cos_ref[places, :], below_ref[places, :], above_ref[places, :]
            for head in range(heads):
                first = head * 3 * HEAD_DIM
                found = jnp.dot(
                    one[slot], qkvw[:, first : first + 3 * HEAD_DIM], preferred_element_type=jnp.float32
                ) + qkvb_ref[:, first : first + 3 * HEAD_DIM]
                qkv[slot, :, first : first + HEAD_DIM] = turn(
                    found[:, :HEAD_DIM], cos, below, above
                ).astype(jnp.bfloat16)
                qkv[slot, :, first + HEAD_DIM : first + 2 * HEAD_DIM] = turn(
                    found[:, HEAD_DIM : 2 * HEAD_DIM], cos, below, above
                ).astype(jnp.bfloat16)
                qkv[slot, :, first + 2 * HEAD_DIM : first + 3 * HEAD_DIM] = found[
                    :, 2 * HEAD_DIM :
                ].astype(jnp.bfloat16)
            tile = tile_of(hidden)

            def up_tile(index, _):
                here = span(index, tile)
                pre = jnp.dot(two[slot], upw[:, here], preferred_element_type=jnp.float32) + upb_ref[:, here]
                share = 0.5 * (1.0 + lax.erf(pre * 0.7071067811865476))
                act[slot, :, here] = (pre * share).astype(jnp.bfloat16)
                slope[slot, :, here] = (
                    share + pre * (jnp.exp(-0.5 * pre * pre) * 0.3989422804014327)
                ).astype(jnp.bfloat16)
                return _

            lax.fori_loop(0, hidden // tile, up_tile, 0)
            copies = outs(place, slot)
            for copy in copies:
                copy.start()
            open_copies.append(copies)
            raw = pltpu.make_async_copy(full.at[place], hid_any.at[place], row_sems.at[order])
            raw.start()
            raw_copies.append(raw)

        raw_copies = []
        run_gather(grid, sizes, rows, full, send_sems, recv_sems, ready)
        for copies in open_copies:
            for copy in copies:
                copy.wait()
        for copy in raw_copies:
            copy.wait()

    def out(columns):
        return jax.ShapeDtypeStruct((shards, rows, columns), jnp.bfloat16)

    def staged(columns):
        return pltpu.VMEM((2, rows, columns), jnp.bfloat16)

    return row_kernel(
        kernel, collective,
        [out(D), out(D), out(D), out(width), out(hidden), out(hidden)],
        [VMEM, VMEM, ANY, VMEM, ANY, VMEM, VMEM, VMEM, VMEM],
        [ANY] * 6,
        gather_scratch(sizes, rows)
        + [
            pltpu.VMEM(qkv_flat.shape, jnp.bfloat16),
            pltpu.VMEM(up_weight.shape, jnp.bfloat16),
            pltpu.SemaphoreType.DMA((2,)),
            staged(D), staged(D), staged(width), staged(hidden), staged(hidden),
            pltpu.SemaphoreType.DMA((2, 5)),
            pltpu.SemaphoreType.DMA((shards,)),
        ],
        2 * BLOCK * D * (width + hidden),
    )(own, norms, qkv_flat, qkv_bias, up_weight, up_bias, *planes)


def branch_rows(own, ctx, act, out_flat, down_weight, norms, sizes, collective):
    rows = own.shape[0]
    shards = sizes[0] * sizes[1]
    inner, hidden = out_flat.shape[0], down_weight.shape[0]

    def kernel(
        own_ref, ctx_any, act_any, outw_any, downw_any, norms_ref, out_ref, final_ref, normed_ref, inverse_ref,
        ctx, act, outw, downw, load_sems, *scratch,
    ):
        grid = Grid2(sizes)
        parts = scratch[0]
        weights = [
            pltpu.make_async_copy(outw_any, outw, load_sems.at[0, 0]),
            pltpu.make_async_copy(downw_any, downw, load_sems.at[0, 1]),
        ]
        order = production_order(grid)
        loads = [
            [
                pltpu.make_async_copy(ctx_any.at[place], ctx.at[place], load_sems.at[1 + i, 0]),
                pltpu.make_async_copy(act_any.at[place], act.at[place], load_sems.at[1 + i, 1]),
            ]
            for i, place in enumerate(order)
        ]
        for copy in loads[0] + weights:
            copy.start()
        for copies in loads[1:]:
            for copy in copies:
                copy.start()
        grid.barrier()
        for copy in weights:
            copy.wait()

        def produce(slow, fast):
            place = grid.index(slow, fast)
            for copy in loads.pop(0):
                copy.wait()

            def columns(index, _):
                here = span(index, 512)
                parts[place, :, here] = (
                    jnp.dot(ctx[place], outw[:, here], preferred_element_type=jnp.float32)
                    + jnp.dot(act[place], downw[:, here], preferred_element_type=jnp.float32)
                ).astype(jnp.bfloat16)
                return _

            lax.fori_loop(0, D // 512, columns, 0)

        run_scatter(grid, sizes, rows, scratch, produce)
        mine = grid.index(*grid.me)

        def norm_tile(index, _):
            here = span(index, ROW_TILE)
            stream = own_ref[here].astype(jnp.float32) + parts[mine, here].astype(jnp.float32) + norms_ref[2:3]
            out_ref[here] = stream.astype(jnp.bfloat16)
            centered, inverse = tile_stats(stream)
            normed = centered * inverse
            final_ref[here] = (normed * norms_ref[0:1] + norms_ref[1:2]).astype(jnp.bfloat16)
            normed_ref[here] = normed
            inverse_ref[here] = inverse
            return _

        lax.fori_loop(0, rows // ROW_TILE, norm_tile, 0)

    return row_kernel(
        kernel, collective,
        [
            jax.ShapeDtypeStruct((rows, D), jnp.bfloat16),
            jax.ShapeDtypeStruct((rows, D), jnp.bfloat16),
            jax.ShapeDtypeStruct((rows, D), jnp.float32),
            jax.ShapeDtypeStruct((rows, 1), jnp.float32),
        ],
        [VMEM, ANY, ANY, ANY, ANY, VMEM],
        [VMEM] * 4,
        [
            pltpu.VMEM(ctx.shape, jnp.bfloat16),
            pltpu.VMEM(act.shape, jnp.bfloat16),
            pltpu.VMEM(out_flat.shape, jnp.bfloat16),
            pltpu.VMEM(down_weight.shape, jnp.bfloat16),
            pltpu.SemaphoreType.DMA((1 + shards, 2)),
        ]
        + sum_scratch(sizes, rows),
        2 * BLOCK * D * (inner + hidden),
    )(own, ctx, act, out_flat, down_weight, norms)


def logit_rows(final, head_weight, targets_col, sizes, collective):
    rows = final.shape[0]
    shards = sizes[0] * sizes[1]
    vocab = head_weight.shape[1]
    tile = tile_of(vocab)
    tiles = vocab // tile

    def kernel(
        own_ref, headw_any, target_ref, final_any, weights_any, stats_ref,
        full, send_sems, recv_sems, headw, load_sem, logits, weights, out_sems, row_sems,
    ):
        grid = Grid2(sizes)
        load = pltpu.make_async_copy(headw_any, headw, load_sem)
        load.start()
        full[grid.index(*grid.me)] = own_ref[...]
        grid.barrier()
        base = lax.axis_index("seq") * vocab
        open_copies, raw_copies = [], []

        def ready(slow, fast, order):
            place = grid.index(slow, fast)
            slot = order % 2
            if order == 0:
                load.wait()
            if order >= 2:
                open_copies.pop(0).wait()
            places = pl.ds(pl.multiple_of(place * rows, rows), rows)
            target = target_ref[places, :] - base

            def fold(values, join):
                while values.shape[1] > 128:
                    half = values.shape[1] // 2
                    values = join(values[:, :half], values[:, half:])
                return values

            def logit_tile(index, carry):
                top, pick = carry
                here = span(index, tile)
                found = jnp.dot(full[place], headw[:, here], preferred_element_type=jnp.float32)
                logits[:, here] = found
                ids = index * tile + lax.broadcasted_iota(jnp.int32, (rows, tile), 1)
                top = jnp.maximum(top, fold(found, jnp.maximum))
                pick = pick + fold(jnp.where(ids == target, found, 0.0), jnp.add)
                return (top, pick)

            top, pick = lax.fori_loop(
                0, tiles, logit_tile,
                (jnp.full((rows, 128), -jnp.inf, jnp.float32), jnp.zeros((rows, 128), jnp.float32)),
            )
            top = jnp.max(top, axis=1, keepdims=True)
            pick = jnp.sum(pick, axis=1, keepdims=True)

            def weight_tile(index, total):
                here = span(index, tile)
                found = jnp.exp(logits[:, here] - top)
                weights[slot, :, here] = found.astype(jnp.bfloat16)
                return total + fold(found, jnp.add)

            total = lax.fori_loop(0, tiles, weight_tile, jnp.zeros((rows, 128), jnp.float32))
            total = jnp.sum(total, axis=1, keepdims=True)
            lane = lax.broadcasted_iota(jnp.int32, (rows, 128), 1)
            stats_ref[places, :] = jnp.where(lane == 0, top, jnp.where(lane == 1, total, pick))
            copy = pltpu.make_async_copy(weights.at[slot], weights_any.at[place], out_sems.at[slot])
            copy.start()
            open_copies.append(copy)
            raw = pltpu.make_async_copy(full.at[place], final_any.at[place], row_sems.at[order])
            raw.start()
            raw_copies.append(raw)

        run_gather(grid, sizes, rows, full, send_sems, recv_sems, ready)
        for copy in open_copies + raw_copies:
            copy.wait()

    return row_kernel(
        kernel, collective,
        [
            jax.ShapeDtypeStruct((shards, rows, D), jnp.bfloat16),
            jax.ShapeDtypeStruct((shards, rows, vocab), jnp.bfloat16),
            jax.ShapeDtypeStruct((shards * rows, 128), jnp.float32),
        ],
        [VMEM, ANY, VMEM],
        [ANY, ANY, VMEM],
        gather_scratch(sizes, rows)
        + [
            pltpu.VMEM(head_weight.shape, jnp.bfloat16),
            pltpu.SemaphoreType.DMA,
            pltpu.VMEM((rows, vocab), jnp.float32),
            pltpu.VMEM((2, rows, vocab), jnp.bfloat16),
            pltpu.SemaphoreType.DMA((2,)),
            pltpu.SemaphoreType.DMA((shards,)),
        ],
        2 * BLOCK * D * vocab,
    )(final, head_weight, targets_col)


def final_grad_rows(grad_logits, head_weight, normed, inverse, gain, sizes, collective, before):
    shards, rows, vocab = grad_logits.shape

    def kernel(
        grads_any, headw_any, normed_ref, inverse_ref, gain_ref, stream_ref, down_ref, sums_ref,
        headw, grads, load_sems, *scratch,
    ):
        grid = Grid2(sizes)
        parts = scratch[0]
        order = production_order(grid)
        loads = [
            pltpu.make_async_copy(grads_any.at[place], grads.at[i % 2], load_sems.at[1 + i])
            for i, place in enumerate(order)
        ]
        weights = pltpu.make_async_copy(headw_any, headw, load_sems.at[0])
        loads[0].start()
        weights.start()
        grid.barrier()
        weights.wait()
        count = [0]

        def produce(slow, fast):
            place = grid.index(slow, fast)
            i = count[0]
            count[0] += 1
            if i + 1 < shards:
                loads[i + 1].start()
            loads[i].wait()

            def columns(index, _):
                here = span(index, 256)
                parts[place, :, here] = dot_nt(grads[i % 2], headw[here, :]).astype(jnp.bfloat16)
                return _

            lax.fori_loop(0, D // 256, columns, 0)

        run_scatter(grid, sizes, rows, scratch, produce)
        mine = grid.index(*grid.me)
        sums_ref[...] = jnp.zeros_like(sums_ref)

        def norm_tile(index, _):
            here = span(index, ROW_TILE)
            grad = parts[mine, here].astype(jnp.float32)
            norm = normed_ref[here]
            scaled = grad * gain_ref[...]
            stream = inverse_ref[here] * (
                scaled
                - jnp.mean(scaled, axis=1, keepdims=True)
                - norm * jnp.mean(scaled * norm, axis=1, keepdims=True)
            )
            stream_ref[here] = stream
            down_ref[here] = stream.astype(jnp.bfloat16)
            sums_ref[0:1] += jnp.sum(grad * norm, axis=0, keepdims=True)
            sums_ref[1:2] += jnp.sum(grad, axis=0, keepdims=True)
            sums_ref[2:3] += jnp.sum(stream, axis=0, keepdims=True)
            return _

        lax.fori_loop(0, rows // ROW_TILE, norm_tile, 0)

    return row_kernel(
        kernel, collective,
        [
            jax.ShapeDtypeStruct((rows, D), jnp.float32),
            jax.ShapeDtypeStruct((rows, D), jnp.bfloat16),
            jax.ShapeDtypeStruct((8, D), jnp.float32),
        ],
        [ANY, ANY, VMEM, VMEM, VMEM],
        [VMEM] * 3,
        [
            pltpu.VMEM(head_weight.shape, jnp.bfloat16),
            pltpu.VMEM((2, rows, vocab), jnp.bfloat16),
            pltpu.SemaphoreType.DMA((1 + shards,)),
        ]
        + sum_scratch(sizes, rows),
        2 * BLOCK * D * vocab,
        before,
    )(grad_logits, head_weight, normed, inverse, gain)


def branch_grad_rows(own, out_flat, down_weight, slope, sizes, collective):
    rows = own.shape[0]
    shards = sizes[0] * sizes[1]
    inner, hidden = out_flat.shape[0], down_weight.shape[0]

    def kernel(
        own_ref, outw_any, downw_any, slope_any, rows_any, ctx_any, up_any, sums_ref,
        full, send_sems, recv_sems, outw, downw, load_sems, slope, slope_sems, ctx, up, out_sems, row_sems,
    ):
        grid = Grid2(sizes)
        loads = [
            pltpu.make_async_copy(outw_any, outw, load_sems.at[0]),
            pltpu.make_async_copy(downw_any, downw, load_sems.at[1]),
        ]
        for copy in loads:
            copy.start()
        slopes = pltpu.make_async_copy(slope_any, slope, slope_sems)
        slopes.start()
        full[grid.index(*grid.me)] = own_ref[...]
        sums_ref[...] = jnp.zeros_like(sums_ref)
        grid.barrier()
        open_copies, raw_copies = [], []

        def ready(slow, fast, order):
            place = grid.index(slow, fast)
            slot = order % 2
            if order == 0:
                for copy in loads + [slopes]:
                    copy.wait()
            if order >= 2:
                for copy in open_copies.pop(0):
                    copy.wait()
            ctx[slot] = dot_nt(full[place], outw[...]).astype(jnp.bfloat16)
            tile = tile_of(hidden)

            def up_tile(index, _):
                here = span(index, tile)
                found = dot_nt(full[place], downw[here, :]) * slope[place, :, here].astype(jnp.float32)
                rounded = found.astype(jnp.bfloat16)
                up[slot, :, here] = rounded
                sums_ref[0:1, here] += jnp.sum(rounded.astype(jnp.float32), axis=0, keepdims=True)
                return _

            lax.fori_loop(0, hidden // tile, up_tile, 0)
            copies = [
                pltpu.make_async_copy(ctx.at[slot], ctx_any.at[place], out_sems.at[slot, 0]),
                pltpu.make_async_copy(up.at[slot], up_any.at[place], out_sems.at[slot, 1]),
            ]
            for copy in copies:
                copy.start()
            open_copies.append(copies)
            raw = pltpu.make_async_copy(full.at[place], rows_any.at[place], row_sems.at[order])
            raw.start()
            raw_copies.append(raw)

        run_gather(grid, sizes, rows, full, send_sems, recv_sems, ready)
        for copies in open_copies:
            for copy in copies:
                copy.wait()
        for copy in raw_copies:
            copy.wait()

    def out(columns):
        return jax.ShapeDtypeStruct((shards, rows, columns), jnp.bfloat16)

    return row_kernel(
        kernel, collective,
        [out(D), out(inner), out(hidden), jax.ShapeDtypeStruct((8, hidden), jnp.float32)],
        [VMEM, ANY, ANY, ANY],
        [ANY, ANY, ANY, VMEM],
        gather_scratch(sizes, rows)
        + [
            pltpu.VMEM(out_flat.shape, jnp.bfloat16),
            pltpu.VMEM(down_weight.shape, jnp.bfloat16),
            pltpu.SemaphoreType.DMA((2,)),
            pltpu.VMEM((shards, rows, hidden), jnp.bfloat16),
            pltpu.SemaphoreType.DMA,
            pltpu.VMEM((2, rows, inner), jnp.bfloat16),
            pltpu.VMEM((2, rows, hidden), jnp.bfloat16),
            pltpu.SemaphoreType.DMA((2, 2)),
            pltpu.SemaphoreType.DMA((shards,)),
        ],
        2 * BLOCK * D * (inner + hidden),
    )(own, out_flat, down_weight, slope)


class SmallSum:
    def __init__(self, shards, replicas, sums, bias, total, bias_total, scratch):
        self.shards, self.replicas = shards, replicas
        self.sums, self.bias, self.total, self.bias_total = sums, bias, total, bias_total
        (
            self.came, self.block, self.blocks, self.biases, self.spread_send, self.spread_recv, self.cross_send,
            self.cross_recv, self.back_send, self.back_recv,
        ) = scratch
        self.seq, self.dp = lax.axis_index("seq"), lax.axis_index("dp")
        self.width = D // shards

    @staticmethod
    def scratch(shards, replicas):
        width = D // shards
        dma = pltpu.SemaphoreType.DMA
        return [
            pltpu.VMEM((shards, 8, width), jnp.float32),
            pltpu.VMEM((8, width), jnp.float32),
            pltpu.VMEM((replicas, 8, width), jnp.float32),
            pltpu.VMEM((replicas, 8, D), jnp.float32),
            dma((shards,)), dma((shards,)), dma((2, replicas)), dma((2, replicas)), dma((shards,)), dma((shards,)),
        ]

    def others(self, axis):
        count, here = (self.shards, self.seq) if axis == "seq" else (self.replicas, self.dp)
        return [(step, lax.rem(here + step, count)) for step in range(1, count)]

    def barrier(self):
        sem = pltpu.get_barrier_semaphore()
        amount = 0
        for axis in ("seq", "dp"):
            for _, place in self.others(axis):
                pl.semaphore_signal(sem, inc=1, device_id={axis: place}, device_id_type=MESH)
                amount += 1
        pl.semaphore_wait(sem, amount)

    def copy(self, axis, place, src, dst, send, recv):
        return pltpu.make_async_remote_copy(
            src_ref=src, dst_ref=dst, send_sem=send, recv_sem=recv, device_id={axis: place}, device_id_type=MESH
        )

    def columns(self, place):
        return pl.ds(pl.multiple_of(place * self.width, self.width), self.width)

    def spread(self):
        self.first = [
            self.copy(
                "seq", place, self.sums.at[:, self.columns(place)], self.came.at[step], self.spread_send.at[step],
                self.spread_recv.at[step],
            )
            for step, place in self.others("seq")
        ]
        self.second = [
            self.copy(
                "dp", place, self.bias, self.biases.at[self.dp], self.cross_send.at[1, step],
                self.cross_recv.at[1, step],
            )
            for step, place in self.others("dp")
        ]
        for copy in self.first + self.second:
            copy.start()

    def cross(self):
        total = self.sums[:, self.columns(self.seq)]
        for (step, _), copy in zip(self.others("seq"), self.first):
            copy.wait_recv()
            total = total + self.came[step]
        self.block[...] = total
        self.blocks[self.dp] = total
        self.third = [
            self.copy(
                "dp", place, self.block, self.blocks.at[self.dp], self.cross_send.at[0, step],
                self.cross_recv.at[0, step],
            )
            for step, place in self.others("dp")
        ]
        for copy in self.third:
            copy.start()

    def collect(self):
        for copy in self.third + self.second:
            copy.wait_recv()
        self.biases[self.dp] = self.bias[...]
        total, bias = self.blocks[0], self.biases[0]
        for place in range(1, self.replicas):
            total, bias = total + self.blocks[place], bias + self.biases[place]
        self.bias_total[...] = bias
        here = self.columns(self.seq)
        self.total[:, here] = total
        self.fourth = [
            self.copy(
                "seq", place, self.total.at[:, here], self.total.at[:, here], self.back_send.at[step],
                self.back_recv.at[step],
            )
            for step, place in self.others("seq")
        ]
        for copy in self.fourth:
            copy.start()

    def finish(self):
        for (step, _), copy in zip(self.others("seq"), self.fourth):
            source = lax.rem(self.seq + self.shards - step, self.shards)
            there = self.total.at[:, self.columns(source)]
            self.copy("seq", source, there, there, self.back_send.at[step], self.back_recv.at[step]).wait_recv()
        for copy in self.first + self.second + self.third + self.fourth:
            copy.wait_send()


def input_grad_rows(
    own, grad_stream, hid, grad_qkv, grad_up, qkv_flat, up_weight, gains, end_sums, biases, sizes, replicas,
    collective, before,
):
    shards, rows, width = grad_qkv.shape
    hidden = grad_up.shape[2]

    def kernel(
        own_ref, stream_ref, hid_any, qkv_any, up_any, qkvw_any, upw_any, gains_ref, end_ref,
        bias_ref, out_ref, total_ref, bias_total_ref,
        qkvw, upw, weight_sems, hid, qkv, up, load_sems, stats, sums_ref, *scratch,
    ):
        grid = Grid2(sizes)
        small = SmallSum(shards, replicas, sums_ref, bias_ref, total_ref, bias_total_ref, scratch[:10])
        scratch = scratch[10:]
        parts = scratch[0]
        order = production_order(grid)

        def loads(i):
            place = order[i]
            return [
                pltpu.make_async_copy(hid_any.at[place], hid.at[i % 2], load_sems.at[i, 0]),
                pltpu.make_async_copy(qkv_any.at[place], qkv.at[i % 2], load_sems.at[i, 1]),
                pltpu.make_async_copy(up_any.at[place], up.at[i % 2], load_sems.at[i, 2]),
            ]

        copies = [loads(i) for i in range(shards)]
        weights = [
            pltpu.make_async_copy(qkvw_any, qkvw, weight_sems.at[0]),
            pltpu.make_async_copy(upw_any, upw, weight_sems.at[1]),
        ]
        for copy in copies[0] + weights:
            copy.start()
        sums_ref[...] = jnp.zeros_like(sums_ref)
        small.barrier()
        for copy in weights:
            copy.wait()
        count = [0]

        def produce(slow, fast):
            place = grid.index(slow, fast)
            i = count[0]
            count[0] += 1
            if i + 1 < shards:
                for copy in copies[i + 1]:
                    copy.start()
            for copy in copies[i]:
                copy.wait()
            slot = i % 2

            def stats_tile(index, _):
                here = span(index, ROW_TILE)
                values = hid[slot, here].astype(jnp.float32)
                mean = jnp.mean(values, axis=1, keepdims=True)
                centered = values - mean
                stats[0, here] = mean
                stats[1, here] = lax.rsqrt(jnp.mean(centered * centered, axis=1, keepdims=True) + EPSILON)
                return _

            lax.fori_loop(0, rows // ROW_TILE, stats_tile, 0)

            def columns(index, _):
                here = span(index, 256)
                one = dot_nt(qkv[slot], qkvw[here, :])
                two = dot_nt(up[slot], upw[here, :])
                normed = (hid[slot, :, here].astype(jnp.float32) - stats[0]) * stats[1]
                parts[place, :, here] = (one * gains_ref[0:1, here] + two * gains_ref[1:2, here]).astype(
                    jnp.bfloat16
                )
                sums_ref[0:1, here] += jnp.sum(one * normed, axis=0, keepdims=True)
                sums_ref[1:2, here] += jnp.sum(one, axis=0, keepdims=True)
                sums_ref[2:3, here] += jnp.sum(two * normed, axis=0, keepdims=True)
                sums_ref[3:4, here] += jnp.sum(two, axis=0, keepdims=True)
                return _

            lax.fori_loop(0, D // 256, columns, 0)

        def made():
            sums_ref[4:8] = end_ref[0:4]
            small.spread()

        run_scatter(grid, sizes, rows, scratch, produce, made, small.cross)
        small.collect()
        mine = grid.index(*grid.me)

        def norm_tile(index, _):
            here = span(index, ROW_TILE)
            grad = parts[mine, here].astype(jnp.float32)
            centered, inverse = tile_stats(own_ref[here].astype(jnp.float32))
            normed = centered * inverse
            out_ref[here] = stream_ref[here] + inverse * (
                grad
                - jnp.mean(grad, axis=1, keepdims=True)
                - normed * jnp.mean(grad * normed, axis=1, keepdims=True)
            )
            return _

        lax.fori_loop(0, rows // ROW_TILE, norm_tile, 0)
        small.finish()

    return row_kernel(
        kernel, collective,
        [jax.ShapeDtypeStruct((rows, D), jnp.float32), jax.ShapeDtypeStruct((8, D), jnp.float32), jax.ShapeDtypeStruct((8, D), jnp.float32)],
        [VMEM, VMEM, ANY, ANY, ANY, ANY, ANY, VMEM, VMEM, VMEM],
        [VMEM, VMEM, VMEM],
        [
            pltpu.VMEM(qkv_flat.shape, jnp.bfloat16),
            pltpu.VMEM(up_weight.shape, jnp.bfloat16),
            pltpu.SemaphoreType.DMA((2,)),
            pltpu.VMEM((2, rows, D), jnp.bfloat16),
            pltpu.VMEM((2, rows, width), jnp.bfloat16),
            pltpu.VMEM((2, rows, hidden), jnp.bfloat16),
            pltpu.SemaphoreType.DMA((shards, 3)),
            pltpu.VMEM((2, rows, 1), jnp.float32),
            pltpu.VMEM((8, D), jnp.float32),
        ]
        + SmallSum.scratch(shards, replicas)
        + sum_scratch(sizes, rows),
        2 * BLOCK * D * (width + hidden),
        before,
    )(own, grad_stream, hid, grad_qkv, grad_up, qkv_flat, up_weight, gains, end_sums, biases)


def segment_rows(block_lengths):
    row_ends = jnp.cumsum(block_lengths)
    row_ids = jnp.arange(BLOCK, dtype=jnp.int32)
    passed = (row_ids[:, None] >= row_ends[None, :]).astype(jnp.int32)
    segment = jnp.sum(passed, axis=1)
    position = row_ids - jnp.sum(passed * block_lengths[None, :], axis=1)
    return (segment, position)


def merge_stats(left_stats, right_stats):
    left_top, left_sum, left_pick = left_stats
    right_top, right_sum, right_pick = right_stats
    joint_top = jnp.maximum(left_top, right_top)
    joint_sum = left_sum * jnp.exp(left_top - joint_top) + right_sum * jnp.exp(
        right_top - joint_top
    )
    return (joint_top, joint_sum, left_pick + right_pick)


def row_of(vector):
    return vector.astype(jnp.float32)[None, :]


PAIR = [(0, 1), (1, 0), (2, 3), (3, 2)]
CROSS = [(0, 2), (2, 0), (1, 3), (3, 1)]


def held(values):
    return lax.optimization_barrier(values)


def half_of(values, which):
    half = values.shape[1] // 2
    return lax.dynamic_slice_in_dim(values, which * half, half, 1)


class PairSum:
    def __init__(self, product):
        self.plain = lax.axis_size("dp") != 4
        if self.plain:
            self.sum = jnp.stack([product(0), product(1)]).astype(jnp.bfloat16)
            return
        self.core = lax.rem(lax.axis_index("dp"), 2)
        away = product(1 - self.core).astype(jnp.bfloat16)
        came = lax.ppermute(away, "dp", PAIR)
        mine = held(product(self.core))
        self.sum = (mine + came.astype(jnp.float32)).astype(jnp.bfloat16)

    def cross(self):
        self.other = lax.psum(self.sum, "dp") if self.plain else lax.ppermute(self.sum, "dp", CROSS)
        return self

    def join(self):
        if self.plain:
            self.total = self.other
        else:
            self.total = (self.sum.astype(jnp.float32) + self.other.astype(jnp.float32)).astype(jnp.bfloat16)
        return self

    def settle(self):
        if self.plain:
            first, second = self.total[0], self.total[1]
        else:
            back = lax.ppermute(self.total, "dp", PAIR)
            first = jnp.where(self.core == 0, self.total, back)
            second = jnp.where(self.core == 0, back, self.total)
        return first.astype(jnp.float32), second.astype(jnp.float32)


def after(values, earlier):
    def kernel(*refs):
        del refs

    return pl.pallas_call(
        kernel,
        out_shape=[jax.ShapeDtypeStruct(v.shape, v.dtype) for v in values],
        in_specs=[ANY] * (len(values) + 1),
        out_specs=[ANY] * len(values),
        input_output_aliases={i: i for i in range(len(values))},
    )(*values, earlier)


def per_device(
    hidden, targets, lengths, labels, ref_logps, ln1_gain, ln1_bias, ln2_gain, ln2_bias, qkv_weight, qv_bias,
    out_weight, up_weight, up_bias, down_weight, branch_bias, lnf_gain, lnf_bias, head_weight,
):
    sizes = lines_of(lax.axis_size("seq"))
    own = hidden[0]
    local_heads = qkv_weight.shape[1]
    local_vocab = head_weight.shape[1]
    local_hidden = up_weight.shape[1]
    width = local_heads * 3 * HEAD_DIM
    inner = local_heads * HEAD_DIM
    qv_float = qv_bias.astype(jnp.float32)
    full_bias = jnp.concatenate(
        [qv_float[:, :HEAD_DIM], jnp.zeros_like(qv_float[:, :HEAD_DIM]), qv_float[:, HEAD_DIM:]], axis=-1
    ).reshape(1, width)
    qkv_flat = qkv_weight.reshape(D, width)
    out_flat = out_weight.reshape(inner, D)
    block_lengths = lengths[0]
    segment, position = segment_rows(block_lengths)
    start = jnp.arange(BLOCK, dtype=jnp.int32) - position
    start_col = start[:, None]
    first_tile = start[::ATT_TILE] // ATT_TILE
    planes = rotary_planes(position)

    norms = jnp.concatenate([row_of(v) for v in (ln1_gain, ln1_bias, ln2_gain, ln2_bias)], axis=0)
    hid, first_full, second_full, qkv, act, slope = open_rows(
        own, sizes, 0, norms, qkv_flat, full_bias, up_weight, row_of(up_bias), planes
    )
    flat_qkv = qkv.reshape(BLOCK, width)
    ctx, lse = attention_forward(flat_qkv, start_col, first_tile, local_heads)
    shards, rows = hid.shape[0], hid.shape[1]
    end_norms = jnp.concatenate([row_of(v) for v in (lnf_gain, lnf_bias, branch_bias)], axis=0)
    output, final, normed, inverse = branch_rows(
        own, ctx.reshape(shards, rows, inner), act, out_flat, down_weight, end_norms, sizes, 1
    )
    final_full, weights, stats = logit_rows(final, head_weight, targets[0][:, None], sizes, 2)

    local_top = stats[:, 0]
    gathered = lax.all_gather(stats[:, :3].T, "seq")
    merged = tuple(gathered[0, i] for i in range(3))
    for other in range(1, gathered.shape[0]):
        merged = merge_stats(merged, tuple(gathered[other, i] for i in range(3)))
    log_total = merged[0] + jnp.log(merged[1])
    token_logp = merged[2] - log_total
    member = (jnp.arange(EXB, dtype=jnp.int32)[:, None] == segment[None, :]).astype(jnp.float32)
    float_lengths = block_lengths.astype(jnp.float32)
    mean_logp = jnp.sum(member * token_logp[None, :], axis=1) / float_lengths
    log_ratio = mean_logp - ref_logps[0]
    center = lax.psum(jnp.sum(log_ratio), "dp") / (lax.axis_size("dp") * EXB)
    label_sign = (2 * labels[0] - 1).astype(jnp.float32)
    squashed = jax.nn.sigmoid(BETA * label_sign * (log_ratio - center))
    losses = 1.0 - squashed
    grad_ratio = -LOSS_SCALE * BETA * label_sign * squashed * (1.0 - squashed)
    token_grad = jnp.sum(member * (grad_ratio / float_lengths)[:, None], axis=0)

    vocab_ids = lax.axis_index("seq") * local_vocab + jnp.arange(local_vocab, dtype=jnp.int32)
    onehot = (vocab_ids[None, :] == targets[0][:, None]).astype(jnp.float32)
    share = jnp.exp(local_top - log_total)
    grad_logits = (
        token_grad[:, None] * (onehot - weights.reshape(BLOCK, local_vocab).astype(jnp.float32) * share[:, None])
    ).astype(jnp.bfloat16)
    final_rows = final_full.reshape(BLOCK, D)
    head_sum = PairSum(lambda which: dot_tn(half_of(final_rows, which), grad_logits)).cross()

    grad_stream, grad_own, end_sums = final_grad_rows(
        grad_logits.reshape(shards, rows, local_vocab), head_weight, normed, inverse, row_of(lnf_gain), sizes, 3,
        (head_sum.sum,),
    )
    grad_full, grad_ctx, grad_up, up_sums = branch_grad_rows(
        grad_own, out_flat, down_weight, slope, sizes, 4
    )
    grad_rows = grad_full.reshape(BLOCK, D)
    act_rows = act.reshape(BLOCK, local_hidden)
    second_rows = second_full.reshape(BLOCK, D)
    up_rows = grad_up.reshape(BLOCK, local_hidden)
    sums = [
        PairSum(lambda which: dot_tn(ctx, half_of(grad_rows, which))),
        PairSum(lambda which: dot_tn(act_rows, half_of(grad_rows, which))),
        PairSum(lambda which: dot_tn(half_of(second_rows, which), up_rows)),
    ]
    for one in sums:
        one.cross()
    made = [one.sum for one in sums]
    grad_qkv, qkv_sums = attention_backward(
        flat_qkv, start_col, first_tile, local_heads, ctx, lse, grad_ctx.reshape(BLOCK, inner), planes,
        made,
    )
    first_rows = first_full.reshape(BLOCK, D)
    sums.append(PairSum(lambda which: dot_tn(half_of(first_rows, which), grad_qkv)))
    sums[-1].cross()
    qkv_sums = qkv_sums[:, 0]
    qv_grad = jnp.concatenate([qkv_sums[:, :HEAD_DIM], qkv_sums[:, 2 * HEAD_DIM :]], axis=-1)
    split = local_heads * 2 * HEAD_DIM
    biases = jnp.concatenate([qv_grad.reshape(-1), up_sums[0]])
    biases = jnp.pad(biases[None, :], ((0, 7), (0, D - biases.shape[0])))
    gains = jnp.concatenate([row_of(ln1_gain), row_of(ln2_gain)], axis=0)
    grad_input, small, biases = input_grad_rows(
        own, grad_stream, hid, grad_qkv.reshape(shards, rows, width), grad_up, qkv_flat, up_weight, gains,
        end_sums, biases, sizes, lax.axis_size("dp"), 5, (sums[-1].sum, head_sum.join().total),
    )
    for one, other in zip(sums, after([one.other for one in sums], small)):
        one.other = other
        one.join()
    out_grad, down_grad, up_grad, qkv_grad = [one.settle() for one in sums]
    head_grad = head_sum.settle()
    return (
        losses[None],
        output[None],
        grad_input[None],
        small[0],
        small[1],
        small[2],
        small[3],
        jnp.concatenate(qkv_grad, axis=0).reshape(qkv_weight.shape),
        biases[0, :split].reshape(local_heads, 2 * HEAD_DIM),
        jnp.concatenate(out_grad, axis=1).reshape(out_weight.shape),
        jnp.concatenate(up_grad, axis=0),
        biases[0, split : split + local_hidden],
        jnp.concatenate(down_grad, axis=1),
        small[6],
        small[4],
        small[5],
        jnp.concatenate(head_grad, axis=0),
    )


def solution(mesh):
    return jax.shard_map(
        per_device,
        mesh=mesh,
        in_specs=(
            P("dp", "seq", None),
            P("dp", None),
            P("dp", None),
            P("dp", None),
            P("dp", None),
            P(),
            P(),
            P(),
            P(),
            P(None, "seq", None),
            P("seq", None),
            P("seq", None, None),
            P(None, "seq"),
            P("seq"),
            P("seq", None),
            P(),
            P(),
            P(),
            P(None, "seq"),
        ),
        out_specs=(
            P("dp", None),
            P("dp", "seq", None),
            P("dp", "seq", None),
            P(),
            P(),
            P(),
            P(),
            P(None, "seq", None),
            P("seq", None),
            P("seq", None, None),
            P(None, "seq"),
            P("seq"),
            P("seq", None),
            P(),
            P(),
            P(),
            P(None, "seq"),
        ),
        check_vma=False,
    )
```

```python
import jax
import jax.numpy as jnp
from jax import lax
from jax.experimental import pallas as pl
from jax.experimental.pallas import tpu as pltpu
from jax.sharding import PartitionSpec as P

D = 2048
HEAD_DIM = 128
ROT = 32
BLOCK = 2048
EXB = 8
EPSILON = 1e-05
BETA = 0.25
LOSS_SCALE = 65536.0
HALVES = 2
VMEM_LIMIT = 62 * 2**20

MESH = pl.DeviceIdType.MESH


class Grid2:
    def __init__(self, sizes):
        self.n = sizes
        place = lax.axis_index("seq")
        self.me = (place // sizes[1], lax.rem(place, sizes[1]))

    def index(self, slow, fast):
        return slow * self.n[1] + fast

    def device(self, axis, spot):
        here = list(self.me)
        here[axis] = spot
        return {"seq": self.index(*here)}

    def nearest(self, axis, rank):
        n, m = self.n[axis], self.me[axis]
        if rank == 0:
            return m
        if n == 2:
            return 1 - m
        after = n - 1 - m
        both = jnp.minimum(m, after)
        dist = (rank + 1) // 2
        near = m - dist if rank % 2 else m + dist
        far = jnp.where(m < after, m + (rank - both), m - (rank - both))
        return jnp.where(rank <= 2 * both, near, far)

    def neighbours(self):
        found = []
        for axis in (0, 1):
            m, n = self.me[axis], self.n[axis]
            if n == 2:
                found.append((None, self.device(axis, 1 - m)))
            elif n > 2:
                found.append((m > 0, self.device(axis, m - 1)))
                found.append((m < n - 1, self.device(axis, m + 1)))
        return found

    def barrier(self):
        sem = pltpu.get_barrier_semaphore()
        amount = jnp.int32(0)
        for there, device in self.neighbours():
            def tell(device=device):
                pl.semaphore_signal(sem, inc=1, device_id=device, device_id_type=MESH)
            if there is None:
                tell()
                amount = amount + 1
            else:
                pl.when(there)(tell)
                amount = amount + there.astype(jnp.int32)
        pl.semaphore_wait(sem, amount)


class Sender:
    def __init__(self, send_sems):
        self.sems = send_sems
        self.used = 0
        self.open = []

    def send(self, src, dst, recv_sem, device, when=None):
        copy = pltpu.make_async_remote_copy(
            src_ref=src, dst_ref=dst, send_sem=self.sems.at[self.used], recv_sem=recv_sem,
            device_id=device, device_id_type=MESH)
        self.used += 1
        if when is None:
            copy.start()
        else:
            pl.when(when)(copy.start)
        self.open.append((when, copy))

    def finish(self):
        for when, copy in self.open:
            if when is None:
                copy.wait_send()
            else:
                pl.when(when)(copy.wait_send)
        self.open = []


def gather_sends(sizes, halves):
    return halves * 2 * (sizes[0] * sizes[1] * 2 + 8)


def gather_rounds(grid, sender, piece, recv_sems, halves, cut, ready):
    n, me = grid.n, grid.me

    def arrived(slow, fast, half, kind):
        ref = piece(grid.index(slow, fast), half, kind)
        sem = recv_sems.at[kind, half, grid.index(slow, fast)]
        pltpu.make_async_copy(ref, ref, sem).wait()

    def push(slow, fast, half, kind, axis, spot, when):
        ref = piece(grid.index(slow, fast), half, kind)
        sem = recv_sems.at[kind, half, grid.index(slow, fast)]
        sender.send(ref, ref, sem, grid.device(axis, spot), when)

    def spread(slow, fast, half, kind, axis):
        m, size = me[axis], n[axis]
        if size == 2:
            push(slow, fast, half, kind, axis, 1 - m, None)
        elif size > 2:
            push(slow, fast, half, kind, axis, m + 1, m < size - 1)
            push(slow, fast, half, kind, axis, m - 1, m > 0)

    def onward(slow, fast, half, kind, axis):
        m, size = me[axis], n[axis]
        if size <= 2:
            return
        source = (slow, fast)[axis]
        below = source < m
        when = (below & (m < size - 1)) | (jnp.logical_not(below) & (m > 0))
        push(slow, fast, half, kind, axis, jnp.where(below, m + 1, m - 1), when)

    todo = []

    def work(count=1):
        for _ in range(count):
            if todo:
                ready(*todo.pop(0))

    def settle(k):
        slow = grid.nearest(0, k)
        for half in range(halves):
            for l in range(n[1]):
                fast = grid.nearest(1, l)
                if k > 0:
                    arrived(slow, fast, half, 1)
                    onward(slow, fast, half, 1, 0)
                else:
                    spread(slow, fast, half, 1, 0)

    def complete(k):
        slow = grid.nearest(0, k)
        for l in range(1, n[1]):
            fast = grid.nearest(1, l)
            if cut[0]:
                for half in range(halves):
                    arrived(slow, fast, half, 0)
                    onward(slow, fast, half, 0, 1)
            todo.append((slow, fast, k * n[1] + l))

    for half in range(halves):
        for kind in (1, 0):
            if cut[kind]:
                spread(me[0], me[1], half, kind, kind)
        if cut[0]:
            spread(me[0], me[1], half, 0, 1)
    todo.append((me[0], me[1], 0))
    work()
    if cut[1]:
        for half in range(halves):
            for l in range(1, n[1]):
                fast = grid.nearest(1, l)
                arrived(me[0], fast, half, 1)
                onward(me[0], fast, half, 1, 1)
    if cut[1]:
        settle(0)
    for k in range(1, n[0]):
        slow = grid.nearest(0, k)
        if cut[0]:
            for half in range(halves):
                arrived(slow, me[1], half, 0)
                onward(slow, me[1], half, 0, 0)
                spread(slow, me[1], half, 0, 1)
        complete(k - 1)
        work(len(todo))
        if cut[1]:
            settle(k)
        todo.append((slow, me[1], k * n[1]))
        work()
    complete(n[0] - 1)
    work(len(todo))


def scatter_slots(n):
    return 1 if n == 2 else n + 1


def scatter_plan(n):
    plan = []
    far = n[0] - 1
    for k in range(far, -2, -1):
        near = [("make", k + 1, 0)] if k + 1 <= far else []
        back = [("chain", k + 2, 0)] if k + 2 <= far else []
        if k >= 0:
            plan += [("make", k, l) for l in range(n[1] - 1, 0, -1)] + back + near
        else:
            plan += near + back
    return plan


class Scatter:
    def __init__(self, grid, sender, part, bufs, sems, halves, cut):
        self.grid, self.sender, self.part = grid, sender, part
        self.bufs, self.sems, self.halves, self.cut = bufs, sems, halves, cut

    def slot(self, axis, target, from_below):
        if self.grid.n[axis] == 2:
            return 0
        return target + jnp.where(from_below, 1, 0)

    def take(self, kind, stage, axis, other, target, from_below, half, when, slot_index):
        buf, sem = self.bufs[kind][stage], self.sems[kind][stage]
        slot = self.slot(axis, target, from_below)

        def add():
            ref = buf.at[other, slot, half]
            pltpu.make_async_copy(ref, ref, sem.at[other, slot, half]).wait()
            mine = self.part(slot_index, half, kind)
            mine[...] = (mine[...].astype(jnp.float32) + ref[...].astype(jnp.float32)).astype(mine.dtype)

        if when is None:
            add()
        else:
            pl.when(when)(add)

    def toward(self, kind, stage, axis, other, target, half, slow, fast):
        grid = self.grid
        m, n = grid.me[axis], grid.n[axis]
        up = target > m
        index = grid.index(slow, fast)
        if n > 2:
            incoming = (up & (m > 0)) | (jnp.logical_not(up) & (m < n - 1))
            self.take(kind, stage, axis, other, target, up, half, incoming, index)
        buf, sem = self.bufs[kind][stage], self.sems[kind][stage]
        slot = self.slot(axis, target, up)
        spot = 1 - m if n == 2 else jnp.where(up, m + 1, m - 1)
        self.sender.send(
            self.part(index, half, kind), buf.at[other, slot, half], sem.at[other, slot, half],
            grid.device(axis, spot))

    def last(self, kind, stage, axis, other, half, slow, fast):
        grid = self.grid
        m, n = grid.me[axis], grid.n[axis]
        index = grid.index(slow, fast)
        if n == 2:
            self.take(kind, stage, axis, other, m, m > 0, half, None, index)
        elif n > 2:
            self.take(kind, stage, axis, other, m, jnp.bool_(True), half, m > 0, index)
            self.take(kind, stage, axis, other, m, jnp.bool_(False), half, m < n - 1, index)

    def run(self, produce, made=lambda: None, between=lambda: None):
        grid, n, me = self.grid, self.grid.n, self.grid.me

        def chain(k):
            slow = grid.nearest(0, k)
            for half in range(self.halves):
                self.last(0, 0, 1, slow, half, slow, me[1])
                self.toward(0, 1, 0, 0, slow, half, slow, me[1])

        def make(k, l):
            slow, fast = grid.nearest(0, k), grid.nearest(1, l)
            produce(slow, fast)
            for half in range(self.halves):
                if self.cut[0] and l > 0:
                    self.toward(0, 0, 1, slow, fast, half, slow, fast)
                if self.cut[1] and k > 0:
                    self.toward(1, 0, 0, fast, slow, half, slow, fast)

        for action, k, l in scatter_plan(n):
            if action == "make":
                make(k, l)
            elif self.cut[0]:
                chain(k)
        made()
        between()
        if self.cut[1]:
            for half in range(self.halves):
                for l in reversed(range(n[1])):
                    fast = grid.nearest(1, l)
                    self.last(1, 0, 0, fast, half, me[0], fast)
                    if l > 0:
                        self.toward(1, 1, 1, 0, fast, half, me[0], fast)
        if self.cut[0]:
            for half in range(self.halves):
                self.last(0, 0, 1, me[0], half, me[0], me[1])
        for half in range(self.halves):
            if self.cut[1]:
                self.last(1, 1, 1, 0, half, me[0], me[1])
            if self.cut[0]:
                self.last(0, 1, 0, 0, half, me[0], me[1])


def scatter_scratch(sizes, halves, rows, cols, cut):
    bufs, sems = [], []
    for kind, stages in ((0, (1, 0)), (1, (0, 1))):
        for stage, axis in enumerate(stages):
            lead = (sizes[1 - axis] if stage == 0 else 1, scatter_slots(sizes[axis]), halves)
            width = max(cut[kind], 128)
            bufs.append(pltpu.VMEM(lead + (rows // halves, width), jnp.bfloat16))
            sems.append(pltpu.SemaphoreType.DMA(lead))
    return bufs, sems


def scatter_sends(sizes, halves):
    return halves * 2 * (sizes[0] * sizes[1] + sizes[0] + sizes[1])


def lines_of(seq):
    fast = 2 if seq <= 8 else 4
    return (seq // fast, fast)


ATT_TILE = 256
SCALE = HEAD_DIM ** (-0.5)


def dot_nt(left, right):
    return lax.dot_general(left, right, (((1,), (1,)), ((), ())), preferred_element_type=jnp.float32)


def dot_tn(left, right):
    return lax.dot_general(left, right, (((0,), (0,)), ((), ())), preferred_element_type=jnp.float32)


def rotary_planes(position):
    half_rot = ROT // 2
    frequency = 10000.0 ** (-2.0 * jnp.arange(half_rot, dtype=jnp.float32) / ROT)
    angles = position.astype(jnp.float32)[:, None] * frequency[None, :]
    cos, sin = jnp.cos(angles), jnp.sin(angles)
    rows = position.shape[0]
    rest = jnp.zeros((rows, HEAD_DIM - ROT), jnp.float32)
    none = jnp.zeros_like(sin)
    return (
        jnp.concatenate([cos, cos, rest + 1.0], axis=1),
        jnp.concatenate([none, sin, rest], axis=1),
        jnp.concatenate([-sin, none, rest], axis=1),
    )


def turn(vector, cos, from_below, from_above):
    half_rot = ROT // 2
    return (
        vector * cos
        + pltpu.roll(vector, half_rot, 1) * from_below
        + pltpu.roll(vector, HEAD_DIM - half_rot, 1) * from_above
    )


def tile_mask(start_col, query_tile, key_tile):
    shape = (ATT_TILE, ATT_TILE)
    query_ids = query_tile * ATT_TILE + lax.broadcasted_iota(jnp.int32, shape, 0)
    key_ids = key_tile * ATT_TILE + lax.broadcasted_iota(jnp.int32, shape, 1)
    return (key_ids >= start_col) & (key_ids <= query_ids)


def attention_forward(qkv, start_col, first_tile, heads):
    tiles = BLOCK // ATT_TILE

    def kernel(first_ref, q_ref, k_ref, v_ref, start_ref, ctx_ref, lse_ref):
        tile = pl.program_id(1)
        queries = q_ref[...]
        start = start_ref[...]

        def step(key_tile, carry):
            top, total, acc = carry
            rows = pl.ds(pl.multiple_of(key_tile * ATT_TILE, ATT_TILE), ATT_TILE)
            scores = dot_nt(queries, k_ref[rows, :]) * SCALE
            scores = jnp.where(tile_mask(start, tile, key_tile), scores, -1e30)
            new_top = jnp.maximum(top, jnp.max(scores, axis=1, keepdims=True))
            shrink = jnp.exp(top - new_top)
            weights = jnp.exp(scores - new_top)
            total = total * shrink + jnp.sum(weights, axis=1, keepdims=True)
            acc = acc * shrink + jnp.dot(
                weights.astype(jnp.bfloat16), v_ref[rows, :], preferred_element_type=jnp.float32
            )
            return (new_top, total, acc)

        begin = (
            jnp.full((ATT_TILE, 1), -1e30, jnp.float32),
            jnp.zeros((ATT_TILE, 1), jnp.float32),
            jnp.zeros((ATT_TILE, HEAD_DIM), jnp.float32),
        )
        begin = step(tile, begin)
        top, total, acc = lax.fori_loop(first_ref[tile], tile, step, begin)
        ctx_ref[...] = (acc / total).astype(jnp.bfloat16)
        lse_ref[...] = top + jnp.log(total)

    return pl.pallas_call(
        kernel,
        grid_spec=pltpu.PrefetchScalarGridSpec(
            num_scalar_prefetch=1,
            grid=(heads, tiles),
            in_specs=[
                pl.BlockSpec((ATT_TILE, HEAD_DIM), lambda h, i, first: (i, 3 * h)),
                pl.BlockSpec((BLOCK, HEAD_DIM), lambda h, i, first: (0, 3 * h + 1)),
                pl.BlockSpec((BLOCK, HEAD_DIM), lambda h, i, first: (0, 3 * h + 2)),
                pl.BlockSpec((ATT_TILE, 1), lambda h, i, first: (i, 0)),
            ],
            out_specs=[
                pl.BlockSpec((ATT_TILE, HEAD_DIM), lambda h, i, first: (i, h)),
                pl.BlockSpec((pl.squeezed, ATT_TILE, 1), lambda h, i, first: (h, i, 0)),
            ],
        ),
        out_shape=[
            jax.ShapeDtypeStruct((BLOCK, heads * HEAD_DIM), jnp.bfloat16),
            jax.ShapeDtypeStruct((heads, BLOCK, 1), jnp.float32),
        ],
        compiler_params=pltpu.CompilerParams(vmem_limit_bytes=VMEM_LIMIT),
    )(first_tile, qkv, qkv, qkv, start_col)


def attention_backward(qkv, start_col, first_tile, heads, ctx, lse, grad_ctx, planes, before):
    tiles = BLOCK // ATT_TILE

    def kernel(
        first_ref, q_ref, k_ref, v_ref, start_ref, ctx_ref, lse_ref, do_ref, cos_ref, below_ref,
        above_ref, *rest,
    ):
        out_ref, sums_ref, dk_ref, dv_ref = rest[len(before) :]
        tile = pl.program_id(1)

        @pl.when(tile == 0)
        def _():
            dk_ref[...] = jnp.zeros_like(dk_ref)
            dv_ref[...] = jnp.zeros_like(dv_ref)

        queries = q_ref[...]
        start = start_ref[...]
        grads = do_ref[...]
        lse_rows = lse_ref[...]
        inner = jnp.sum(
            grads.astype(jnp.float32) * ctx_ref[...].astype(jnp.float32), axis=1, keepdims=True
        )

        def step(key_tile, dq):
            rows = pl.ds(pl.multiple_of(key_tile * ATT_TILE, ATT_TILE), ATT_TILE)
            keys = k_ref[rows, :]
            scores = dot_nt(queries, keys) * SCALE
            probs = jnp.where(
                tile_mask(start, tile, key_tile), jnp.exp(scores - lse_rows), 0.0
            )
            grad_probs = dot_nt(grads, v_ref[rows, :])
            grad_scores = (probs * (grad_probs - inner)).astype(jnp.bfloat16)
            dv_ref[rows, :] += dot_tn(probs.astype(jnp.bfloat16), grads)
            dk_ref[rows, :] += dot_tn(grad_scores, queries)
            return dq + jnp.dot(grad_scores, keys, preferred_element_type=jnp.float32)

        dq = lax.fori_loop(
            first_ref[tile], tile + 1, step, jnp.zeros((ATT_TILE, HEAD_DIM), jnp.float32)
        )
        here = pl.ds(pl.multiple_of(tile * ATT_TILE, ATT_TILE), ATT_TILE)
        out_ref[here, :HEAD_DIM] = turn(
            dq * SCALE, cos_ref[here, :], -below_ref[here, :], -above_ref[here, :]
        ).astype(jnp.bfloat16)

        @pl.when(tile == tiles - 1)
        def _():
            def finish(index, sums):
                rows = pl.ds(pl.multiple_of(index * ATT_TILE, ATT_TILE), ATT_TILE)
                out_ref[rows, HEAD_DIM : 2 * HEAD_DIM] = turn(
                    dk_ref[rows, :] * SCALE, cos_ref[rows, :], -below_ref[rows, :], -above_ref[rows, :]
                ).astype(jnp.bfloat16)
                out_ref[rows, 2 * HEAD_DIM :] = dv_ref[rows, :].astype(jnp.bfloat16)
                return sums + jnp.sum(out_ref[rows, :].astype(jnp.float32), axis=0, keepdims=True)

            sums_ref[...] = lax.fori_loop(
                0, tiles, finish, jnp.zeros((1, 3 * HEAD_DIM), jnp.float32)
            )

    whole = pl.BlockSpec((BLOCK, HEAD_DIM), lambda h, i, first: (0, 0))
    return pl.pallas_call(
        kernel,
        grid_spec=pltpu.PrefetchScalarGridSpec(
            num_scalar_prefetch=1,
            grid=(heads, tiles),
            in_specs=[
                pl.BlockSpec((ATT_TILE, HEAD_DIM), lambda h, i, first: (i, 3 * h)),
                pl.BlockSpec((BLOCK, HEAD_DIM), lambda h, i, first: (0, 3 * h + 1)),
                pl.BlockSpec((BLOCK, HEAD_DIM), lambda h, i, first: (0, 3 * h + 2)),
                pl.BlockSpec((ATT_TILE, 1), lambda h, i, first: (i, 0)),
                pl.BlockSpec((ATT_TILE, HEAD_DIM), lambda h, i, first: (i, h)),
                pl.BlockSpec((pl.squeezed, ATT_TILE, 1), lambda h, i, first: (h, i, 0)),
                pl.BlockSpec((ATT_TILE, HEAD_DIM), lambda h, i, first: (i, h)),
                whole,
                whole,
                whole,
            ]
            + [pl.BlockSpec(memory_space=pl.ANY)] * len(before),
            out_specs=[
                pl.BlockSpec((BLOCK, 3 * HEAD_DIM), lambda h, i, first: (0, h)),
                pl.BlockSpec((pl.squeezed, 1, 3 * HEAD_DIM), lambda h, i, first: (h, 0, 0)),
            ],
            scratch_shapes=[
                pltpu.VMEM((BLOCK, HEAD_DIM), jnp.float32),
                pltpu.VMEM((BLOCK, HEAD_DIM), jnp.float32),
            ],
        ),
        out_shape=[
            jax.ShapeDtypeStruct((BLOCK, heads * 3 * HEAD_DIM), jnp.bfloat16),
            jax.ShapeDtypeStruct((heads, 1, 3 * HEAD_DIM), jnp.float32),
        ],
        compiler_params=pltpu.CompilerParams(vmem_limit_bytes=VMEM_LIMIT),
    )(first_tile, qkv, qkv, qkv, start_col, ctx, lse, grad_ctx, *planes, *before)


def gather_cut(sizes):
    return (1792, 256) if sizes == (4, 2) else (D // 2, D // 2)


def scatter_cut(sizes):
    return (1664, 384) if sizes == (4, 2) else (D // 2, D // 2)


def columns_of(cut, kind):
    return pl.ds(0, cut[0]) if kind == 0 else pl.ds(cut[0], cut[1])


def tile_of(width):
    return 256 if width % 256 == 0 else 128


def span(index, size):
    return pl.ds(pl.multiple_of(index * size, size), size)


ANY = pl.BlockSpec(memory_space=pl.ANY)
VMEM = pl.BlockSpec(memory_space=pltpu.VMEM)


def row_kernel(kernel, collective, out_shape, in_specs, out_specs, scratch, cost, before=()):
    def body(*refs):
        kernel(*refs[len(before):])

    def call(*args):
        return pl.pallas_call(
            body,
            out_shape=out_shape,
            in_specs=[ANY] * len(before) + in_specs,
            out_specs=out_specs,
            scratch_shapes=scratch,
            cost_estimate=pl.CostEstimate(flops=cost, bytes_accessed=2**28, transcendentals=0),
            compiler_params=pltpu.CompilerParams(
                collective_id=collective, has_side_effects=True, vmem_limit_bytes=VMEM_LIMIT
            ),
        )(*before, *args)

    return call


def gather_scratch(sizes, rows):
    shards = sizes[0] * sizes[1]
    return [
        pltpu.VMEM((shards, rows, D), jnp.bfloat16),
        pltpu.SemaphoreType.DMA((gather_sends(sizes, HALVES),)),
        pltpu.SemaphoreType.DMA((2, HALVES, shards)),
    ]


def run_gather(grid, sizes, rows, full, send_sems, recv_sems, ready):
    cut = gather_cut(sizes)
    step = rows // HALVES
    sender = Sender(send_sems)

    def piece(slot, half, kind):
        return full.at[slot, pl.ds(half * step, step), columns_of(cut, kind)]

    gather_rounds(grid, sender, piece, recv_sems, HALVES, cut, ready)
    sender.finish()


def sum_scratch(sizes, rows):
    shards = sizes[0] * sizes[1]
    bufs, sems = scatter_scratch(sizes, HALVES, rows, D, scatter_cut(sizes))
    return (
        [pltpu.VMEM((shards, rows, D), jnp.bfloat16)]
        + bufs
        + sems
        + [pltpu.SemaphoreType.DMA((scatter_sends(sizes, HALVES),))]
    )


def run_scatter(grid, sizes, rows, scratch, produce, *hooks):
    cut = scatter_cut(sizes)
    step = rows // HALVES
    parts, b0, b1, b2, b3, s0, s1, s2, s3, send_sems = scratch
    sender = Sender(send_sems)

    def part(slot, half, kind):
        return parts.at[slot, pl.ds(half * step, step), columns_of(cut, kind)]

    scatter = Scatter(
        grid, sender, part, ((b0, b1), (b2, b3)), ((s0, s1), (s2, s3)), HALVES, cut
    )
    scatter.run(produce, *hooks)
    sender.finish()


def production_order(grid):
    return [
        grid.index(grid.nearest(0, k), grid.nearest(1, l))
        for action, k, l in scatter_plan(grid.n)
        if action == "make"
    ]


ROW_TILE = 64


def tile_stats(values):
    centered = values - jnp.mean(values, axis=1, keepdims=True)
    inverse = lax.rsqrt(jnp.mean(centered * centered, axis=1, keepdims=True) + EPSILON)
    return centered, inverse


def open_rows(own, sizes, collective, norms, qkv_flat, qkv_bias, up_weight, up_bias, planes):
    rows = own.shape[0]
    shards = sizes[0] * sizes[1]
    width, hidden = qkv_flat.shape[1], up_weight.shape[1]
    heads = width // (3 * HEAD_DIM)

    def kernel(
        own_ref, norms_ref, qkvw_any, qkvb_ref, upw_any, upb_ref, cos_ref, below_ref, above_ref,
        plain_any, one_any, two_any, qkv_any, act_any, slope_any,
        full, send_sems, recv_sems, qkvw, upw, load_sems, plain, one, two, qkv, act, slope, out_sems,
    ):
        grid = Grid2(sizes)
        loads = [
            pltpu.make_async_copy(qkvw_any, qkvw, load_sems.at[0]),
            pltpu.make_async_copy(upw_any, upw, load_sems.at[1]),
        ]
        for copy in loads:
            copy.start()
        full[grid.index(*grid.me)] = own_ref[...]
        grid.barrier()
        open_copies = []

        def outs(place, slot):
            pairs = ((plain, plain_any), (one, one_any), (two, two_any), (qkv, qkv_any), (act, act_any), (slope, slope_any))
            return [
                pltpu.make_async_copy(here.at[slot], there.at[place], out_sems.at[slot, i])
                for i, (here, there) in enumerate(pairs)
            ]

        def ready(slow, fast, order):
            place = grid.index(slow, fast)
            slot = order % 2
            if order == 0:
                for copy in loads:
                    copy.wait()
            if order >= 2:
                for copy in open_copies.pop(0):
                    copy.wait()

            def norm_tile(index, _):
                here = span(index, ROW_TILE)
                centered, inverse = tile_stats(full[place, here].astype(jnp.float32))
                normed = centered * inverse
                plain[slot, here] = normed.astype(jnp.bfloat16)
                one[slot, here] = (normed * norms_ref[0:1] + norms_ref[1:2]).astype(jnp.bfloat16)
                two[slot, here] = (normed * norms_ref[2:3] + norms_ref[3:4]).astype(jnp.bfloat16)
                return _

            lax.fori_loop(0, rows // ROW_TILE, norm_tile, 0)
            places = pl.ds(pl.multiple_of(place * rows, rows), rows)
            cos, below, above = cos_ref[places, :], below_ref[places, :], above_ref[places, :]
            for head in range(heads):
                first = head * 3 * HEAD_DIM
                found = jnp.dot(
                    one[slot], qkvw[:, first : first + 3 * HEAD_DIM], preferred_element_type=jnp.float32
                ) + qkvb_ref[:, first : first + 3 * HEAD_DIM]
                qkv[slot, :, first : first + HEAD_DIM] = turn(
                    found[:, :HEAD_DIM], cos, below, above
                ).astype(jnp.bfloat16)
                qkv[slot, :, first + HEAD_DIM : first + 2 * HEAD_DIM] = turn(
                    found[:, HEAD_DIM : 2 * HEAD_DIM], cos, below, above
                ).astype(jnp.bfloat16)
                qkv[slot, :, first + 2 * HEAD_DIM : first + 3 * HEAD_DIM] = found[
                    :, 2 * HEAD_DIM :
                ].astype(jnp.bfloat16)
            tile = tile_of(hidden)

            def up_tile(index, _):
                here = span(index, tile)
                pre = jnp.dot(two[slot], upw[:, here], preferred_element_type=jnp.float32) + upb_ref[:, here]
                share = 0.5 * (1.0 + lax.erf(pre * 0.7071067811865476))
                act[slot, :, here] = (pre * share).astype(jnp.bfloat16)
                slope[slot, :, here] = (
                    share + pre * (jnp.exp(-0.5 * pre * pre) * 0.3989422804014327)
                ).astype(jnp.bfloat16)
                return _

            lax.fori_loop(0, hidden // tile, up_tile, 0)
            copies = outs(place, slot)
            for copy in copies:
                copy.start()
            open_copies.append(copies)

        run_gather(grid, sizes, rows, full, send_sems, recv_sems, ready)
        for copies in open_copies:
            for copy in copies:
                copy.wait()

    def out(columns):
        return jax.ShapeDtypeStruct((shards, rows, columns), jnp.bfloat16)

    def staged(columns):
        return pltpu.VMEM((2, rows, columns), jnp.bfloat16)

    return row_kernel(
        kernel, collective,
        [out(D), out(D), out(D), out(width), out(hidden), out(hidden)],
        [VMEM, VMEM, ANY, VMEM, ANY, VMEM, VMEM, VMEM, VMEM],
        [ANY] * 6,
        gather_scratch(sizes, rows)
        + [
            pltpu.VMEM(qkv_flat.shape, jnp.bfloat16),
            pltpu.VMEM(up_weight.shape, jnp.bfloat16),
            pltpu.SemaphoreType.DMA((2,)),
            staged(D), staged(D), staged(D), staged(width), staged(hidden), staged(hidden),
            pltpu.SemaphoreType.DMA((2, 6)),
        ],
        2 * BLOCK * D * (width + hidden),
    )(own, norms, qkv_flat, qkv_bias, up_weight, up_bias, *planes)


def branch_rows(own, ctx, act, out_flat, down_weight, norms, sizes, collective):
    rows = own.shape[0]
    shards = sizes[0] * sizes[1]
    inner, hidden = out_flat.shape[0], down_weight.shape[0]

    def kernel(
        own_ref, ctx_any, act_any, outw_any, downw_any, norms_ref, out_ref, final_ref, normed_ref, inverse_ref,
        ctx, act, outw, downw, load_sems, *scratch,
    ):
        grid = Grid2(sizes)
        parts = scratch[0]
        weights = [
            pltpu.make_async_copy(outw_any, outw, load_sems.at[0, 0]),
            pltpu.make_async_copy(downw_any, downw, load_sems.at[0, 1]),
        ]
        order = production_order(grid)
        loads = [
            [
                pltpu.make_async_copy(ctx_any.at[place], ctx.at[place], load_sems.at[1 + i, 0]),
                pltpu.make_async_copy(act_any.at[place], act.at[place], load_sems.at[1 + i, 1]),
            ]
            for i, place in enumerate(order)
        ]
        for copy in loads[0] + weights:
            copy.start()
        for copies in loads[1:]:
            for copy in copies:
                copy.start()
        grid.barrier()
        for copy in weights:
            copy.wait()

        def produce(slow, fast):
            place = grid.index(slow, fast)
            for copy in loads.pop(0):
                copy.wait()

            def columns(index, _):
                here = span(index, 512)
                parts[place, :, here] = (
                    jnp.dot(ctx[place], outw[:, here], preferred_element_type=jnp.float32)
                    + jnp.dot(act[place], downw[:, here], preferred_element_type=jnp.float32)
                ).astype(jnp.bfloat16)
                return _

            lax.fori_loop(0, D // 512, columns, 0)

        run_scatter(grid, sizes, rows, scratch, produce)
        mine = grid.index(*grid.me)

        def norm_tile(index, _):
            here = span(index, ROW_TILE)
            stream = own_ref[here].astype(jnp.float32) + parts[mine, here].astype(jnp.float32) + norms_ref[2:3]
            out_ref[here] = stream.astype(jnp.bfloat16)
            centered, inverse = tile_stats(stream)
            normed = centered * inverse
            final_ref[here] = (normed * norms_ref[0:1] + norms_ref[1:2]).astype(jnp.bfloat16)
            normed_ref[here] = normed
            inverse_ref[here] = inverse
            return _

        lax.fori_loop(0, rows // ROW_TILE, norm_tile, 0)

    return row_kernel(
        kernel, collective,
        [
            jax.ShapeDtypeStruct((rows, D), jnp.bfloat16),
            jax.ShapeDtypeStruct((rows, D), jnp.bfloat16),
            jax.ShapeDtypeStruct((rows, D), jnp.float32),
            jax.ShapeDtypeStruct((rows, 1), jnp.float32),
        ],
        [VMEM, ANY, ANY, ANY, ANY, VMEM],
        [VMEM] * 4,
        [
            pltpu.VMEM(ctx.shape, jnp.bfloat16),
            pltpu.VMEM(act.shape, jnp.bfloat16),
            pltpu.VMEM(out_flat.shape, jnp.bfloat16),
            pltpu.VMEM(down_weight.shape, jnp.bfloat16),
            pltpu.SemaphoreType.DMA((1 + shards, 2)),
        ]
        + sum_scratch(sizes, rows),
        2 * BLOCK * D * (inner + hidden),
    )(own, ctx, act, out_flat, down_weight, norms)


def logit_rows(final, head_weight, targets_col, sizes, collective):
    rows = final.shape[0]
    shards = sizes[0] * sizes[1]
    vocab = head_weight.shape[1]
    tile = tile_of(vocab)
    tiles = vocab // tile

    def kernel(
        own_ref, headw_any, target_ref, final_any, weights_any, stats_ref,
        full, send_sems, recv_sems, headw, load_sem, logits, weights, out_sems, row_sems,
    ):
        grid = Grid2(sizes)
        load = pltpu.make_async_copy(headw_any, headw, load_sem)
        load.start()
        full[grid.index(*grid.me)] = own_ref[...]
        grid.barrier()
        base = lax.axis_index("seq") * vocab
        open_copies, raw_copies = [], []

        def ready(slow, fast, order):
            place = grid.index(slow, fast)
            slot = order % 2
            if order == 0:
                load.wait()
            if order >= 2:
                open_copies.pop(0).wait()
            places = pl.ds(pl.multiple_of(place * rows, rows), rows)
            target = target_ref[places, :] - base

            def fold(values, join):
                while values.shape[1] > 128:
                    half = values.shape[1] // 2
                    values = join(values[:, :half], values[:, half:])
                return values

            def logit_tile(index, carry):
                top, pick = carry
                here = span(index, tile)
                found = jnp.dot(full[place], headw[:, here], preferred_element_type=jnp.float32)
                logits[:, here] = found
                ids = index * tile + lax.broadcasted_iota(jnp.int32, (rows, tile), 1)
                top = jnp.maximum(top, fold(found, jnp.maximum))
                pick = pick + fold(jnp.where(ids == target, found, 0.0), jnp.add)
                return (top, pick)

            top, pick = lax.fori_loop(
                0, tiles, logit_tile,
                (jnp.full((rows, 128), -jnp.inf, jnp.float32), jnp.zeros((rows, 128), jnp.float32)),
            )
            top = jnp.max(top, axis=1, keepdims=True)
            pick = jnp.sum(pick, axis=1, keepdims=True)

            def weight_tile(index, total):
                here = span(index, tile)
                found = jnp.exp(logits[:, here] - top)
                weights[slot, :, here] = found.astype(jnp.bfloat16)
                return total + fold(found, jnp.add)

            total = lax.fori_loop(0, tiles, weight_tile, jnp.zeros((rows, 128), jnp.float32))
            total = jnp.sum(total, axis=1, keepdims=True)
            lane = lax.broadcasted_iota(jnp.int32, (rows, 128), 1)
            found = jnp.where(lane == 0, top, jnp.where(lane == 1, total, pick))
            stats_ref[:, places] = found.T[0:8]
            copy = pltpu.make_async_copy(weights.at[slot], weights_any.at[place], out_sems.at[slot])
            copy.start()
            open_copies.append(copy)
            raw = pltpu.make_async_copy(full.at[place], final_any.at[place], row_sems.at[order])
            raw.start()
            raw_copies.append(raw)

        run_gather(grid, sizes, rows, full, send_sems, recv_sems, ready)
        for copy in open_copies + raw_copies:
            copy.wait()

    return row_kernel(
        kernel, collective,
        [
            jax.ShapeDtypeStruct((shards, rows, D), jnp.bfloat16),
            jax.ShapeDtypeStruct((shards, rows, vocab), jnp.bfloat16),
            jax.ShapeDtypeStruct((8, shards * rows), jnp.float32),
        ],
        [VMEM, ANY, VMEM],
        [ANY, ANY, VMEM],
        gather_scratch(sizes, rows)
        + [
            pltpu.VMEM(head_weight.shape, jnp.bfloat16),
            pltpu.SemaphoreType.DMA,
            pltpu.VMEM((rows, vocab), jnp.float32),
            pltpu.VMEM((2, rows, vocab), jnp.bfloat16),
            pltpu.SemaphoreType.DMA((2,)),
            pltpu.SemaphoreType.DMA((shards,)),
        ],
        2 * BLOCK * D * vocab,
    )(final, head_weight, targets_col)


def final_grad_rows(grad_logits, head_weight, normed, inverse, gain, sizes, collective, before):
    shards, rows, vocab = grad_logits.shape

    def kernel(
        grads_any, headw_any, normed_ref, inverse_ref, gain_ref, stream_ref, down_ref, sums_ref,
        headw, grads, load_sems, *scratch,
    ):
        grid = Grid2(sizes)
        parts = scratch[0]
        order = production_order(grid)
        loads = [
            pltpu.make_async_copy(grads_any.at[place], grads.at[i % 2], load_sems.at[1 + i])
            for i, place in enumerate(order)
        ]
        weights = pltpu.make_async_copy(headw_any, headw, load_sems.at[0])
        loads[0].start()
        weights.start()
        grid.barrier()
        weights.wait()
        count = [0]

        def produce(slow, fast):
            place = grid.index(slow, fast)
            i = count[0]
            count[0] += 1
            if i + 1 < shards:
                loads[i + 1].start()
            loads[i].wait()

            def columns(index, _):
                here = span(index, 256)
                parts[place, :, here] = dot_nt(grads[i % 2], headw[here, :]).astype(jnp.bfloat16)
                return _

            lax.fori_loop(0, D // 256, columns, 0)

        run_scatter(grid, sizes, rows, scratch, produce)
        mine = grid.index(*grid.me)
        sums_ref[...] = jnp.zeros_like(sums_ref)

        def norm_tile(index, _):
            here = span(index, ROW_TILE)
            grad = parts[mine, here].astype(jnp.float32)
            norm = normed_ref[here]
            scaled = grad * gain_ref[...]
            stream = inverse_ref[here] * (
                scaled
                - jnp.mean(scaled, axis=1, keepdims=True)
                - norm * jnp.mean(scaled * norm, axis=1, keepdims=True)
            )
            stream_ref[here] = stream
            down_ref[here] = stream.astype(jnp.bfloat16)
            sums_ref[0:1] += jnp.sum(grad * norm, axis=0, keepdims=True)
            sums_ref[1:2] += jnp.sum(grad, axis=0, keepdims=True)
            sums_ref[2:3] += jnp.sum(stream, axis=0, keepdims=True)
            return _

        lax.fori_loop(0, rows // ROW_TILE, norm_tile, 0)

    return row_kernel(
        kernel, collective,
        [
            jax.ShapeDtypeStruct((rows, D), jnp.float32),
            jax.ShapeDtypeStruct((rows, D), jnp.bfloat16),
            jax.ShapeDtypeStruct((8, D), jnp.float32),
        ],
        [ANY, ANY, VMEM, VMEM, VMEM],
        [VMEM] * 3,
        [
            pltpu.VMEM(head_weight.shape, jnp.bfloat16),
            pltpu.VMEM((2, rows, vocab), jnp.bfloat16),
            pltpu.SemaphoreType.DMA((1 + shards,)),
        ]
        + sum_scratch(sizes, rows),
        2 * BLOCK * D * vocab,
        before,
    )(grad_logits, head_weight, normed, inverse, gain)


def branch_grad_rows(own, out_flat, down_weight, slope, sizes, collective):
    rows = own.shape[0]
    shards = sizes[0] * sizes[1]
    inner, hidden = out_flat.shape[0], down_weight.shape[0]

    def kernel(
        own_ref, outw_any, downw_any, slope_any, rows_any, ctx_any, up_any, sums_ref,
        full, send_sems, recv_sems, outw, downw, load_sems, slope, slope_sems, ctx, up, out_sems, row_sems,
    ):
        grid = Grid2(sizes)
        loads = [
            pltpu.make_async_copy(outw_any, outw, load_sems.at[0]),
            pltpu.make_async_copy(downw_any, downw, load_sems.at[1]),
        ]
        for copy in loads:
            copy.start()
        slopes = pltpu.make_async_copy(slope_any, slope, slope_sems)
        slopes.start()
        full[grid.index(*grid.me)] = own_ref[...]
        sums_ref[...] = jnp.zeros_like(sums_ref)
        grid.barrier()
        open_copies, raw_copies = [], []

        def ready(slow, fast, order):
            place = grid.index(slow, fast)
            slot = order % 2
            if order == 0:
                for copy in loads + [slopes]:
                    copy.wait()
            if order >= 2:
                for copy in open_copies.pop(0):
                    copy.wait()
            ctx[slot] = dot_nt(full[place], outw[...]).astype(jnp.bfloat16)
            tile = tile_of(hidden)

            def up_tile(index, _):
                here = span(index, tile)
                found = dot_nt(full[place], downw[here, :]) * slope[place, :, here].astype(jnp.float32)
                rounded = found.astype(jnp.bfloat16)
                up[slot, :, here] = rounded
                sums_ref[0:1, here] += jnp.sum(rounded.astype(jnp.float32), axis=0, keepdims=True)
                return _

            lax.fori_loop(0, hidden // tile, up_tile, 0)
            copies = [
                pltpu.make_async_copy(ctx.at[slot], ctx_any.at[place], out_sems.at[slot, 0]),
                pltpu.make_async_copy(up.at[slot], up_any.at[place], out_sems.at[slot, 1]),
            ]
            for copy in copies:
                copy.start()
            open_copies.append(copies)
            raw = pltpu.make_async_copy(full.at[place], rows_any.at[place], row_sems.at[order])
            raw.start()
            raw_copies.append(raw)

        run_gather(grid, sizes, rows, full, send_sems, recv_sems, ready)
        for copies in open_copies:
            for copy in copies:
                copy.wait()
        for copy in raw_copies:
            copy.wait()

    def out(columns):
        return jax.ShapeDtypeStruct((shards, rows, columns), jnp.bfloat16)

    return row_kernel(
        kernel, collective,
        [out(D), out(inner), out(hidden), jax.ShapeDtypeStruct((8, hidden), jnp.float32)],
        [VMEM, ANY, ANY, ANY],
        [ANY, ANY, ANY, VMEM],
        gather_scratch(sizes, rows)
        + [
            pltpu.VMEM(out_flat.shape, jnp.bfloat16),
            pltpu.VMEM(down_weight.shape, jnp.bfloat16),
            pltpu.SemaphoreType.DMA((2,)),
            pltpu.VMEM((shards, rows, hidden), jnp.bfloat16),
            pltpu.SemaphoreType.DMA,
            pltpu.VMEM((2, rows, inner), jnp.bfloat16),
            pltpu.VMEM((2, rows, hidden), jnp.bfloat16),
            pltpu.SemaphoreType.DMA((2, 2)),
            pltpu.SemaphoreType.DMA((shards,)),
        ],
        2 * BLOCK * D * (inner + hidden),
    )(own, out_flat, down_weight, slope)


class SmallSum:
    def __init__(self, shards, replicas, sums, bias, total, bias_total, scratch):
        self.shards, self.replicas = shards, replicas
        self.sums, self.bias, self.total, self.bias_total = sums, bias, total, bias_total
        (
            self.came, self.block, self.blocks, self.biases, self.spread_send, self.spread_recv, self.cross_send,
            self.cross_recv, self.back_send, self.back_recv,
        ) = scratch
        self.seq, self.dp = lax.axis_index("seq"), lax.axis_index("dp")
        self.width = D // shards

    @staticmethod
    def scratch(shards, replicas):
        width = D // shards
        dma = pltpu.SemaphoreType.DMA
        return [
            pltpu.VMEM((shards, 8, width), jnp.float32),
            pltpu.VMEM((8, width), jnp.float32),
            pltpu.VMEM((replicas, 8, width), jnp.float32),
            pltpu.VMEM((replicas, 8, D), jnp.float32),
            dma((shards,)), dma((shards,)), dma((2, replicas)), dma((2, replicas)), dma((shards,)), dma((shards,)),
        ]

    def others(self, axis):
        count, here = (self.shards, self.seq) if axis == "seq" else (self.replicas, self.dp)
        return [(step, lax.rem(here + step, count)) for step in range(1, count)]

    def barrier(self):
        sem = pltpu.get_barrier_semaphore()
        amount = 0
        for axis in ("seq", "dp"):
            for _, place in self.others(axis):
                pl.semaphore_signal(sem, inc=1, device_id={axis: place}, device_id_type=MESH)
                amount += 1
        pl.semaphore_wait(sem, amount)

    def copy(self, axis, place, src, dst, send, recv):
        return pltpu.make_async_remote_copy(
            src_ref=src, dst_ref=dst, send_sem=send, recv_sem=recv, device_id={axis: place}, device_id_type=MESH
        )

    def columns(self, place):
        return pl.ds(pl.multiple_of(place * self.width, self.width), self.width)

    def spread(self):
        self.first = [
            self.copy(
                "seq", place, self.sums.at[:, self.columns(place)], self.came.at[step], self.spread_send.at[step],
                self.spread_recv.at[step],
            )
            for step, place in self.others("seq")
        ]
        self.second = [
            self.copy(
                "dp", place, self.bias, self.biases.at[self.dp], self.cross_send.at[1, step],
                self.cross_recv.at[1, step],
            )
            for step, place in self.others("dp")
        ]
        for copy in self.first + self.second:
            copy.start()

    def cross(self):
        total = self.sums[:, self.columns(self.seq)]
        for (step, _), copy in zip(self.others("seq"), self.first):
            copy.wait_recv()
            total = total + self.came[step]
        self.block[...] = total
        self.blocks[self.dp] = total
        self.third = [
            self.copy(
                "dp", place, self.block, self.blocks.at[self.dp], self.cross_send.at[0, step],
                self.cross_recv.at[0, step],
            )
            for step, place in self.others("dp")
        ]
        for copy in self.third:
            copy.start()

    def collect(self):
        for copy in self.third + self.second:
            copy.wait_recv()
        self.biases[self.dp] = self.bias[...]
        total, bias = self.blocks[0], self.biases[0]
        for place in range(1, self.replicas):
            total, bias = total + self.blocks[place], bias + self.biases[place]
        self.bias_total[...] = bias
        here = self.columns(self.seq)
        self.total[:, here] = total
        self.fourth = [
            self.copy(
                "seq", place, self.total.at[:, here], self.total.at[:, here], self.back_send.at[step],
                self.back_recv.at[step],
            )
            for step, place in self.others("seq")
        ]
        for copy in self.fourth:
            copy.start()

    def finish(self):
        for (step, _), copy in zip(self.others("seq"), self.fourth):
            source = lax.rem(self.seq + self.shards - step, self.shards)
            there = self.total.at[:, self.columns(source)]
            self.copy("seq", source, there, there, self.back_send.at[step], self.back_recv.at[step]).wait_recv()
        for copy in self.first + self.second + self.third + self.fourth:
            copy.wait_send()


def score_rows(stats, seg_row, examples, sizes, replicas, collective):
    shards = sizes[0] * sizes[1]
    width = BLOCK // shards

    def kernel(
        stats_ref, seg_ref, examples_ref, coef_ref, losses_ref,
        came, full, ratio, ratios, spread_send, spread_recv, back_send, back_recv, cross_send, cross_recv,
    ):
        seq, dp = lax.axis_index("seq"), lax.axis_index("dp")
        peers = {
            "seq": [(step, lax.rem(seq + step, shards)) for step in range(1, shards)],
            "dp": [(step, lax.rem(dp + step, replicas)) for step in range(1, replicas)],
        }
        barrier = pltpu.get_barrier_semaphore()
        for axis in peers:
            for _, place in peers[axis]:
                pl.semaphore_signal(barrier, inc=1, device_id={axis: place}, device_id_type=MESH)
        pl.semaphore_wait(barrier, shards + replicas - 2)

        def columns(place):
            return pl.ds(pl.multiple_of(place * width, width), width)

        def copy(axis, place, src, dst, send, recv):
            return pltpu.make_async_remote_copy(
                src_ref=src, dst_ref=dst, send_sem=send, recv_sem=recv, device_id={axis: place}, device_id_type=MESH
            )

        sent = [
            copy("seq", place, stats_ref.at[:, columns(place)], came.at[step], spread_send.at[step], spread_recv.at[step])
            for step, place in peers["seq"]
        ]
        for one in sent:
            one.start()
        mine = stats_ref[:, columns(seq)]
        top, total, pick = mine[0:1], mine[1:2], mine[2:3]
        for (step, _), one in zip(peers["seq"], sent):
            one.wait_recv()
            other = came[step]
            joint = jnp.maximum(top, other[0:1])
            total = total * jnp.exp(top - joint) + other[1:2] * jnp.exp(other[0:1] - joint)
            pick = pick + other[2:3]
            top = joint
        log_total = top + jnp.log(total)
        here = columns(seq)
        full[0:1, here] = log_total
        full[1:2, here] = pick - log_total
        back = [
            copy("seq", place, full.at[:, here], full.at[:, here], back_send.at[step], back_recv.at[step])
            for step, place in peers["seq"]
        ]
        for one in back:
            one.start()
        for step, _ in peers["seq"]:
            source = lax.rem(seq + shards - step, shards)
            there = full.at[:, columns(source)]
            copy("seq", source, there, there, back_send.at[step], back_recv.at[step]).wait_recv()
        member = lax.broadcasted_iota(jnp.int32, (EXB, BLOCK), 0) == seg_ref[...]
        counts, reference, sign = examples_ref[:, 0:1], examples_ref[:, 1:2], examples_ref[:, 2:3]
        mean = jnp.sum(jnp.where(member, full[1:2, :], 0.0), axis=1, keepdims=True) / counts
        log_ratio = mean - reference
        ratio[...] = jnp.broadcast_to(jnp.sum(log_ratio, axis=0, keepdims=True), ratio.shape)
        crossed = [
            copy("dp", place, ratio, ratios.at[dp], cross_send.at[step], cross_recv.at[step])
            for step, place in peers["dp"]
        ]
        for one in crossed:
            one.start()
        for one in crossed:
            one.wait_recv()
        ratios[dp] = ratio[...]
        whole = ratios[0]
        for place in range(1, replicas):
            whole = whole + ratios[place]
        center = whole[:, 0:1] / (replicas * EXB)
        squashed = jax.nn.sigmoid(BETA * sign * (log_ratio - center))
        losses_ref[...] = jnp.broadcast_to(1.0 - squashed, losses_ref.shape)
        grad = -LOSS_SCALE * BETA * sign * squashed * (1.0 - squashed) / counts
        token = jnp.sum(jnp.where(member, grad, 0.0), axis=0, keepdims=True)
        coef_ref[...] = jnp.zeros_like(coef_ref)
        coef_ref[0:1, :] = token
        coef_ref[1:2, :] = token * jnp.exp(stats_ref[0:1, :] - full[0:1, :])
        for one in sent + back + crossed:
            one.wait_send()

    dma = pltpu.SemaphoreType.DMA
    return pl.pallas_call(
        kernel,
        out_shape=[
            jax.ShapeDtypeStruct((8, BLOCK), jnp.float32),
            jax.ShapeDtypeStruct((EXB, 128), jnp.float32),
        ],
        in_specs=[VMEM] * 3,
        out_specs=[VMEM] * 2,
        scratch_shapes=[
            pltpu.VMEM((shards, 8, width), jnp.float32),
            pltpu.VMEM((8, BLOCK), jnp.float32),
            pltpu.VMEM((EXB, 128), jnp.float32),
            pltpu.VMEM((replicas, EXB, 128), jnp.float32),
            dma((shards,)), dma((shards,)), dma((shards,)), dma((shards,)), dma((replicas,)), dma((replicas,)),
        ],
        compiler_params=pltpu.CompilerParams(collective_id=collective, has_side_effects=True),
    )(stats, seg_row, examples)


def input_grad_rows(
    own, grad_stream, plain, grad_qkv, grad_up, qkv_flat, up_weight, gains, end_sums, biases, sizes, replicas,
    collective, before,
):
    shards, rows, width = grad_qkv.shape
    hidden = grad_up.shape[2]

    def kernel(
        own_ref, stream_ref, normed_any, qkv_any, up_any, qkvw_any, upw_any, gains_ref, end_ref,
        bias_ref, out_ref, total_ref, bias_total_ref,
        qkvw, upw, weight_sems, normed, qkv, up, load_sems, sums_ref, *scratch,
    ):
        grid = Grid2(sizes)
        small = SmallSum(shards, replicas, sums_ref, bias_ref, total_ref, bias_total_ref, scratch[:10])
        scratch = scratch[10:]
        parts = scratch[0]
        order = production_order(grid)

        def loads(i):
            place = order[i]
            return [
                pltpu.make_async_copy(normed_any.at[place], normed.at[i % 2], load_sems.at[i, 0]),
                pltpu.make_async_copy(qkv_any.at[place], qkv.at[i % 2], load_sems.at[i, 1]),
                pltpu.make_async_copy(up_any.at[place], up.at[i % 2], load_sems.at[i, 2]),
            ]

        copies = [loads(i) for i in range(shards)]
        weights = [
            pltpu.make_async_copy(qkvw_any, qkvw, weight_sems.at[0]),
            pltpu.make_async_copy(upw_any, upw, weight_sems.at[1]),
        ]
        for copy in copies[0] + weights:
            copy.start()
        sums_ref[...] = jnp.zeros_like(sums_ref)
        small.barrier()
        for copy in weights:
            copy.wait()
        count = [0]

        def produce(slow, fast):
            place = grid.index(slow, fast)
            i = count[0]
            count[0] += 1
            if i + 1 < shards:
                for copy in copies[i + 1]:
                    copy.start()
            for copy in copies[i]:
                copy.wait()
            slot = i % 2

            def columns(index, _):
                here = span(index, 256)
                one = dot_nt(qkv[slot], qkvw[here, :])
                two = dot_nt(up[slot], upw[here, :])
                norm = normed[slot, :, here].astype(jnp.float32)
                parts[place, :, here] = (one * gains_ref[0:1, here] + two * gains_ref[1:2, here]).astype(
                    jnp.bfloat16
                )
                sums_ref[0:1, here] += jnp.sum(one * norm, axis=0, keepdims=True)
                sums_ref[1:2, here] += jnp.sum(one, axis=0, keepdims=True)
                sums_ref[2:3, here] += jnp.sum(two * norm, axis=0, keepdims=True)
                sums_ref[3:4, here] += jnp.sum(two, axis=0, keepdims=True)
                return _

            lax.fori_loop(0, D // 256, columns, 0)

        def made():
            sums_ref[4:8] = end_ref[0:4]
            small.spread()

        run_scatter(grid, sizes, rows, scratch, produce, made, small.cross)
        small.collect()
        mine = grid.index(*grid.me)

        def norm_tile(index, _):
            here = span(index, ROW_TILE)
            grad = parts[mine, here].astype(jnp.float32)
            centered, inverse = tile_stats(own_ref[here].astype(jnp.float32))
            normed = centered * inverse
            out_ref[here] = stream_ref[here] + inverse * (
                grad
                - jnp.mean(grad, axis=1, keepdims=True)
                - normed * jnp.mean(grad * normed, axis=1, keepdims=True)
            )
            return _

        lax.fori_loop(0, rows // ROW_TILE, norm_tile, 0)
        small.finish()

    return row_kernel(
        kernel, collective,
        [jax.ShapeDtypeStruct((rows, D), jnp.float32), jax.ShapeDtypeStruct((8, D), jnp.float32), jax.ShapeDtypeStruct((8, D), jnp.float32)],
        [VMEM, VMEM, ANY, ANY, ANY, ANY, ANY, VMEM, VMEM, VMEM],
        [VMEM, VMEM, VMEM],
        [
            pltpu.VMEM(qkv_flat.shape, jnp.bfloat16),
            pltpu.VMEM(up_weight.shape, jnp.bfloat16),
            pltpu.SemaphoreType.DMA((2,)),
            pltpu.VMEM((2, rows, D), jnp.bfloat16),
            pltpu.VMEM((2, rows, width), jnp.bfloat16),
            pltpu.VMEM((2, rows, hidden), jnp.bfloat16),
            pltpu.SemaphoreType.DMA((shards, 3)),
            pltpu.VMEM((8, D), jnp.float32),
        ]
        + SmallSum.scratch(shards, replicas)
        + sum_scratch(sizes, rows),
        2 * BLOCK * D * (width + hidden),
        before,
    )(own, grad_stream, plain, grad_qkv, grad_up, qkv_flat, up_weight, gains, end_sums, biases)


def segment_rows(block_lengths):
    row_ends = jnp.cumsum(block_lengths)
    row_ids = jnp.arange(BLOCK, dtype=jnp.int32)
    passed = (row_ids[:, None] >= row_ends[None, :]).astype(jnp.int32)
    segment = jnp.sum(passed, axis=1)
    position = row_ids - jnp.sum(passed * block_lengths[None, :], axis=1)
    return (segment, position)


def row_of(vector):
    return vector.astype(jnp.float32)[None, :]


PAIR = [(0, 1), (1, 0), (2, 3), (3, 2)]
CROSS = [(0, 2), (2, 0), (1, 3), (3, 1)]


def held(values):
    return lax.optimization_barrier(values)


def half_of(values, which):
    half = values.shape[1] // 2
    return lax.dynamic_slice_in_dim(values, which * half, half, 1)


class PairSum:
    def __init__(self, product):
        self.plain = lax.axis_size("dp") != 4
        if self.plain:
            self.sum = jnp.stack([product(0), product(1)]).astype(jnp.bfloat16)
            return
        self.core = lax.rem(lax.axis_index("dp"), 2)
        away = product(1 - self.core).astype(jnp.bfloat16)
        came = lax.ppermute(away, "dp", PAIR)
        mine = held(product(self.core))
        self.sum = (mine + came.astype(jnp.float32)).astype(jnp.bfloat16)

    def cross(self):
        self.other = lax.psum(self.sum, "dp") if self.plain else lax.ppermute(self.sum, "dp", CROSS)
        return self

    def join(self):
        if self.plain:
            self.total = self.other
        else:
            self.total = (self.sum.astype(jnp.float32) + self.other.astype(jnp.float32)).astype(jnp.bfloat16)
        return self

    def settle(self):
        if self.plain:
            first, second = self.total[0], self.total[1]
        else:
            back = lax.ppermute(self.total, "dp", PAIR)
            first = jnp.where(self.core == 0, self.total, back)
            second = jnp.where(self.core == 0, back, self.total)
        return first.astype(jnp.float32), second.astype(jnp.float32)


def after(values, earlier):
    def kernel(*refs):
        del refs

    return pl.pallas_call(
        kernel,
        out_shape=[jax.ShapeDtypeStruct(v.shape, v.dtype) for v in values],
        in_specs=[ANY] * (len(values) + 1),
        out_specs=[ANY] * len(values),
        input_output_aliases={i: i for i in range(len(values))},
    )(*values, earlier)


def per_device(
    hidden, targets, lengths, labels, ref_logps, ln1_gain, ln1_bias, ln2_gain, ln2_bias, qkv_weight, qv_bias,
    out_weight, up_weight, up_bias, down_weight, branch_bias, lnf_gain, lnf_bias, head_weight,
):
    sizes = lines_of(lax.axis_size("seq"))
    own = hidden[0]
    local_heads = qkv_weight.shape[1]
    local_vocab = head_weight.shape[1]
    local_hidden = up_weight.shape[1]
    width = local_heads * 3 * HEAD_DIM
    inner = local_heads * HEAD_DIM
    qv_float = qv_bias.astype(jnp.float32)
    full_bias = jnp.concatenate(
        [qv_float[:, :HEAD_DIM], jnp.zeros_like(qv_float[:, :HEAD_DIM]), qv_float[:, HEAD_DIM:]], axis=-1
    ).reshape(1, width)
    qkv_flat = qkv_weight.reshape(D, width)
    out_flat = out_weight.reshape(inner, D)
    block_lengths = lengths[0]
    segment, position = segment_rows(block_lengths)
    start = jnp.arange(BLOCK, dtype=jnp.int32) - position
    start_col = start[:, None]
    first_tile = start[::ATT_TILE] // ATT_TILE
    planes = rotary_planes(position)

    norms = jnp.concatenate([row_of(v) for v in (ln1_gain, ln1_bias, ln2_gain, ln2_bias)], axis=0)
    plain, first_full, second_full, qkv, act, slope = open_rows(
        own, sizes, 0, norms, qkv_flat, full_bias, up_weight, row_of(up_bias), planes
    )
    flat_qkv = qkv.reshape(BLOCK, width)
    ctx, lse = attention_forward(flat_qkv, start_col, first_tile, local_heads)
    shards, rows = plain.shape[0], plain.shape[1]
    end_norms = jnp.concatenate([row_of(v) for v in (lnf_gain, lnf_bias, branch_bias)], axis=0)
    output, final, normed, inverse = branch_rows(
        own, ctx.reshape(shards, rows, inner), act, out_flat, down_weight, end_norms, sizes, 1
    )
    final_full, weights, stats = logit_rows(final, head_weight, targets[0][:, None], sizes, 2)

    examples = jnp.stack(
        [block_lengths.astype(jnp.float32), ref_logps[0], (2 * labels[0] - 1).astype(jnp.float32)], axis=1
    )
    coef, losses = score_rows(
        stats, segment[None, :], jnp.pad(examples, ((0, 0), (0, 125))), sizes, lax.axis_size("dp"), 6
    )
    vocab_ids = lax.axis_index("seq") * local_vocab + jnp.arange(local_vocab, dtype=jnp.int32)
    grad_logits = (
        jnp.where(vocab_ids[None, :] == targets[0][:, None], coef[0][:, None], 0.0)
        - weights.reshape(BLOCK, local_vocab).astype(jnp.float32) * coef[1][:, None]
    ).astype(jnp.bfloat16)
    final_rows = final_full.reshape(BLOCK, D)
    head_sum = PairSum(lambda which: dot_tn(half_of(final_rows, which), grad_logits)).cross()

    grad_stream, grad_own, end_sums = final_grad_rows(
        grad_logits.reshape(shards, rows, local_vocab), head_weight, normed, inverse, row_of(lnf_gain), sizes, 3,
        (head_sum.sum,),
    )
    grad_full, grad_ctx, grad_up, up_sums = branch_grad_rows(
        grad_own, out_flat, down_weight, slope, sizes, 4
    )
    grad_rows = grad_full.reshape(BLOCK, D)
    act_rows = act.reshape(BLOCK, local_hidden)
    second_rows = second_full.reshape(BLOCK, D)
    up_rows = grad_up.reshape(BLOCK, local_hidden)
    sums = [
        PairSum(lambda which: dot_tn(ctx, half_of(grad_rows, which))),
        PairSum(lambda which: dot_tn(act_rows, half_of(grad_rows, which))),
        PairSum(lambda which: dot_tn(half_of(second_rows, which), up_rows)),
    ]
    for one in sums:
        one.cross()
    made = [one.sum for one in sums]
    grad_qkv, qkv_sums = attention_backward(
        flat_qkv, start_col, first_tile, local_heads, ctx, lse, grad_ctx.reshape(BLOCK, inner), planes,
        made,
    )
    first_rows = first_full.reshape(BLOCK, D)
    sums.append(PairSum(lambda which: dot_tn(half_of(first_rows, which), grad_qkv)))
    sums[-1].cross()
    qkv_sums = qkv_sums[:, 0]
    qv_grad = jnp.concatenate([qkv_sums[:, :HEAD_DIM], qkv_sums[:, 2 * HEAD_DIM :]], axis=-1)
    split = local_heads * 2 * HEAD_DIM
    biases = jnp.concatenate([qv_grad.reshape(-1), up_sums[0]])
    biases = jnp.pad(biases[None, :], ((0, 7), (0, D - biases.shape[0])))
    gains = jnp.concatenate([row_of(ln1_gain), row_of(ln2_gain)], axis=0)
    grad_input, small, biases = input_grad_rows(
        own, grad_stream, plain, grad_qkv.reshape(shards, rows, width), grad_up, qkv_flat, up_weight, gains,
        end_sums, biases, sizes, lax.axis_size("dp"), 5, (sums[-1].sum, head_sum.join().total),
    )
    for one, other in zip(sums, after([one.other for one in sums], small)):
        one.other = other
        one.join()
    out_grad, down_grad, up_grad, qkv_grad = [one.settle() for one in sums]
    head_grad = head_sum.settle()
    return (
        losses[:, 0][None],
        output[None],
        grad_input[None],
        small[0],
        small[1],
        small[2],
        small[3],
        jnp.concatenate(qkv_grad, axis=0).reshape(qkv_weight.shape),
        biases[0, :split].reshape(local_heads, 2 * HEAD_DIM),
        jnp.concatenate(out_grad, axis=1).reshape(out_weight.shape),
        jnp.concatenate(up_grad, axis=0),
        biases[0, split : split + local_hidden],
        jnp.concatenate(down_grad, axis=1),
        small[6],
        small[4],
        small[5],
        jnp.concatenate(head_grad, axis=0),
    )


def solution(mesh):
    return jax.shard_map(
        per_device,
        mesh=mesh,
        in_specs=(
            P("dp", "seq", None),
            P("dp", None),
            P("dp", None),
            P("dp", None),
            P("dp", None),
            P(),
            P(),
            P(),
            P(),
            P(None, "seq", None),
            P("seq", None),
            P("seq", None, None),
            P(None, "seq"),
            P("seq"),
            P("seq", None),
            P(),
            P(),
            P(),
            P(None, "seq"),
        ),
        out_specs=(
            P("dp", None),
            P("dp", "seq", None),
            P("dp", "seq", None),
            P(),
            P(),
            P(),
            P(),
            P(None, "seq", None),
            P("seq", None),
            P("seq", None, None),
            P(None, "seq"),
            P("seq"),
            P("seq", None),
            P(),
            P(),
            P(),
            P(None, "seq"),
        ),
        check_vma=False,
    )
```

```python
import jax
import jax.numpy as jnp
from jax import lax
from jax.experimental import pallas as pl
from jax.experimental.pallas import tpu as pltpu
from jax.sharding import PartitionSpec as P

D = 2048
HEAD_DIM = 128
ROT = 32
BLOCK = 2048
EXB = 8
EPSILON = 1e-05
BETA = 0.25
LOSS_SCALE = 65536.0
HALVES = 2
VMEM_LIMIT = 62 * 2**20

MESH = pl.DeviceIdType.MESH


class Grid2:
    def __init__(self, sizes):
        self.n = sizes
        place = lax.axis_index("seq")
        self.me = (place // sizes[1], lax.rem(place, sizes[1]))

    def index(self, slow, fast):
        return slow * self.n[1] + fast

    def device(self, axis, spot):
        here = list(self.me)
        here[axis] = spot
        return {"seq": self.index(*here)}

    def nearest(self, axis, rank):
        n, m = self.n[axis], self.me[axis]
        if rank == 0:
            return m
        if n == 2:
            return 1 - m
        after = n - 1 - m
        both = jnp.minimum(m, after)
        dist = (rank + 1) // 2
        near = m - dist if rank % 2 else m + dist
        far = jnp.where(m < after, m + (rank - both), m - (rank - both))
        return jnp.where(rank <= 2 * both, near, far)

    def neighbours(self):
        found = []
        for axis in (0, 1):
            m, n = self.me[axis], self.n[axis]
            if n == 2:
                found.append((None, self.device(axis, 1 - m)))
            elif n > 2:
                found.append((m > 0, self.device(axis, m - 1)))
                found.append((m < n - 1, self.device(axis, m + 1)))
        return found

    def barrier(self):
        sem = pltpu.get_barrier_semaphore()
        amount = jnp.int32(0)
        for there, device in self.neighbours():
            def tell(device=device):
                pl.semaphore_signal(sem, inc=1, device_id=device, device_id_type=MESH)
            if there is None:
                tell()
                amount = amount + 1
            else:
                pl.when(there)(tell)
                amount = amount + there.astype(jnp.int32)
        pl.semaphore_wait(sem, amount)


class Sender:
    def __init__(self, send_sems):
        self.sems = send_sems
        self.used = 0
        self.open = []

    def send(self, src, dst, recv_sem, device, when=None):
        copy = pltpu.make_async_remote_copy(
            src_ref=src, dst_ref=dst, send_sem=self.sems.at[self.used], recv_sem=recv_sem,
            device_id=device, device_id_type=MESH)
        self.used += 1
        if when is None:
            copy.start()
        else:
            pl.when(when)(copy.start)
        self.open.append((when, copy))

    def finish(self):
        for when, copy in self.open:
            if when is None:
                copy.wait_send()
            else:
                pl.when(when)(copy.wait_send)
        self.open = []


def gather_sends(sizes, halves):
    return halves * 2 * (sizes[0] * sizes[1] * 5 + 8)


def gather_rounds(grid, sender, piece, recv_sems, halves, cut, ready):
    n, me = grid.n, grid.me

    def arrived(slow, fast, half, kind, when):
        ref = piece(grid.index(slow, fast), half, kind)
        sem = recv_sems.at[kind, half, grid.index(slow, fast)]
        wait = pltpu.make_async_copy(ref, ref, sem).wait
        if when is None:
            wait()
        else:
            pl.when(when)(wait)

    def push(slow, fast, half, kind, axis, spot, *conditions):
        ref = piece(grid.index(slow, fast), half, kind)
        sem = recv_sems.at[kind, half, grid.index(slow, fast)]
        when = None
        for condition in conditions:
            if condition is not None:
                when = condition if when is None else when & condition
        sender.send(ref, ref, sem, grid.device(axis, spot), when)

    def spread(slow, fast, half, kind, axis, when):
        m, size = me[axis], n[axis]
        if size == 2:
            push(slow, fast, half, kind, axis, 1 - m, when)
        elif size > 2:
            push(slow, fast, half, kind, axis, m + 1, when, m < size - 1)
            push(slow, fast, half, kind, axis, m - 1, when, m > 0)

    def onward(slow, fast, half, kind, axis, when):
        m, size = me[axis], n[axis]
        if size <= 2:
            return
        below = (slow, fast)[axis] < m
        more = (below & (m < size - 1)) | (jnp.logical_not(below) & (m > 0))
        push(slow, fast, half, kind, axis, jnp.where(below, m + 1, m - 1), when, more)

    def sides(d):
        if d == 0:
            return [(me[0], None)]
        if n[0] == 2:
            return [(1 - me[0], None)]
        return [(me[0] - d, me[0] >= d), (me[0] + d, me[0] + d < n[0])]

    def settle(d):
        for half in range(halves):
            for slow, when in sides(d):
                for l in range(n[1]):
                    fast = grid.nearest(1, l)
                    if d > 0:
                        arrived(slow, fast, half, 1, when)
                        onward(slow, fast, half, 1, 0, when)
                    else:
                        spread(slow, fast, half, 1, 0, when)

    def complete(d):
        for l in range(1, n[1]):
            fast = grid.nearest(1, l)
            for half in range(halves):
                for slow, when in sides(d):
                    arrived(slow, fast, half, 0, when)
                    onward(slow, fast, half, 0, 1, when)

    def work(k, l):
        ready(grid.nearest(0, k), grid.nearest(1, l), k * n[1] + l)

    for half in range(halves):
        for kind in (1, 0):
            if cut[kind]:
                spread(me[0], me[1], half, kind, kind, None)
        if cut[0]:
            spread(me[0], me[1], half, 0, 1, None)
    work(0, 0)
    if cut[1]:
        for half in range(halves):
            for l in range(1, n[1]):
                fast = grid.nearest(1, l)
                arrived(me[0], fast, half, 1, None)
                onward(me[0], fast, half, 1, 1, None)
        settle(0)
    for d in range(1, n[0]):
        if cut[0]:
            for half in range(halves):
                for slow, when in sides(d):
                    arrived(slow, me[1], half, 0, when)
                    onward(slow, me[1], half, 0, 0, when)
                    spread(slow, me[1], half, 0, 1, when)
            complete(d - 1)
        for l in range(1, n[1]):
            work(d - 1, l)
        if cut[1]:
            settle(d)
        work(d, 0)
    if cut[0]:
        complete(n[0] - 1)
    for l in range(1, n[1]):
        work(n[0] - 1, l)


def scatter_slots(n):
    return 1 if n == 2 else n + 1


def scatter_plan(n):
    if n == (4, 2):
        return [
            ("make", 3, 1), ("make", 2, 1), ("make", 3, 0), ("make", 1, 1), ("first", 3), ("make", 2, 0),
            ("make", 0, 1), ("later", 3, 0), ("make", 1, 0), ("later", 3, 1), ("first", 2), ("make", 0, 0), ("made",),
            ("later", 2, 0), ("later", 2, 1), ("first", 1), ("later", 1, 0), ("later", 1, 1),
        ]
    far = n[0] - 1
    plan = [("make", k, l) for k in range(far, -1, -1) for l in range(n[1] - 1, -1, -1)] + [("made",)]
    for k in range(far, 0, -1):
        plan += [("first", k), ("later", k, 0), ("later", k, 1)]
    return plan


class Scatter:
    def __init__(self, grid, sender, part, bufs, sems, halves, cut):
        self.grid, self.sender, self.part = grid, sender, part
        self.bufs, self.sems, self.halves, self.cut = bufs, sems, halves, cut

    def slot(self, axis, target, from_below):
        if self.grid.n[axis] == 2:
            return 0
        return target + jnp.where(from_below, 1, 0)

    def take(self, kind, stage, axis, other, target, from_below, half, when, slot_index):
        buf, sem = self.bufs[kind][stage], self.sems[kind][stage]
        slot = self.slot(axis, target, from_below)

        def add():
            ref = buf.at[other, slot, half]
            pltpu.make_async_copy(ref, ref, sem.at[other, slot, half]).wait()
            mine = self.part(slot_index, half, kind)
            mine[...] = (mine[...].astype(jnp.float32) + ref[...].astype(jnp.float32)).astype(mine.dtype)

        if when is None:
            add()
        else:
            pl.when(when)(add)

    def incoming(self, axis, target):
        m, n = self.grid.me[axis], self.grid.n[axis]
        if n == 2:
            return None
        up = target > m
        return (up & (m > 0)) | (jnp.logical_not(up) & (m < n - 1))

    def toward(self, kind, stage, axis, other, target, half, slow, fast, when=None):
        grid = self.grid
        m, n = grid.me[axis], grid.n[axis]
        up = target > m
        index = grid.index(slow, fast)
        if n > 2:
            incoming = self.incoming(axis, target)
            self.take(kind, stage, axis, other, target, up, half, incoming if when is None else incoming & when, index)
        buf, sem = self.bufs[kind][stage], self.sems[kind][stage]
        slot = self.slot(axis, target, up)
        spot = 1 - m if n == 2 else jnp.where(up, m + 1, m - 1)
        self.sender.send(
            self.part(index, half, kind), buf.at[other, slot, half], sem.at[other, slot, half],
            grid.device(axis, spot), when)

    def last(self, kind, stage, axis, other, half, slow, fast):
        grid = self.grid
        m, n = grid.me[axis], grid.n[axis]
        index = grid.index(slow, fast)
        if n == 2:
            self.take(kind, stage, axis, other, m, m > 0, half, None, index)
        elif n > 2:
            self.take(kind, stage, axis, other, m, jnp.bool_(True), half, m > 0, index)
            self.take(kind, stage, axis, other, m, jnp.bool_(False), half, m < n - 1, index)

    def run(self, produce, made=lambda: None, between=lambda: None, late=lambda: None):
        grid, n, me = self.grid, self.grid.n, self.grid.me
        lagging = []

        def chain(k, half, begins):
            slow = grid.nearest(0, k)
            incoming = self.incoming(0, slow)
            if incoming is None:
                if begins:
                    self.last(0, 0, 1, slow, half, slow, me[1])
                    self.toward(0, 1, 0, 0, slow, half, slow, me[1])
                return
            when = jnp.logical_not(incoming) if begins else incoming
            pl.when(when)(lambda: self.last(0, 0, 1, slow, half, slow, me[1]))
            self.toward(0, 1, 0, 0, slow, half, slow, me[1], when)

        def catch_up():
            for step in lagging:
                self.toward(*step)
            lagging.clear()

        def make(k, l):
            slow, fast = grid.nearest(0, k), grid.nearest(1, l)
            produce(slow, fast)
            if self.cut[0] and l > 0:
                for half in range(self.halves):
                    self.toward(0, 0, 1, slow, fast, half, slow, fast)
            catch_up()
            if self.cut[1] and k > 0:
                for half in range(self.halves):
                    lagging.append((1, 0, 0, fast, slow, half, slow, fast))

        for step in scatter_plan(n):
            if step[0] == "make":
                make(*step[1:])
            elif step[0] == "made":
                catch_up()
                made()
            elif step[0] == "first" and self.cut[0]:
                for half in range(self.halves):
                    chain(step[1], half, True)
            elif self.cut[0]:
                chain(step[1], step[2], False)
        between()
        if self.cut[1]:
            for half in range(self.halves):
                for l in reversed(range(n[1])):
                    fast = grid.nearest(1, l)
                    self.last(1, 0, 0, fast, half, me[0], fast)
                    if l > 0:
                        self.toward(1, 1, 1, 0, fast, half, me[0], fast)
        late()
        if self.cut[0]:
            for half in range(self.halves):
                self.last(0, 0, 1, me[0], half, me[0], me[1])
        for half in range(self.halves):
            if self.cut[1]:
                self.last(1, 1, 1, 0, half, me[0], me[1])
            if self.cut[0]:
                self.last(0, 1, 0, 0, half, me[0], me[1])


def scatter_scratch(sizes, halves, rows, cols, cut):
    bufs, sems = [], []
    for kind, stages in ((0, (1, 0)), (1, (0, 1))):
        for stage, axis in enumerate(stages):
            lead = (sizes[1 - axis] if stage == 0 else 1, scatter_slots(sizes[axis]), halves)
            width = max(cut[kind], 128)
            bufs.append(pltpu.VMEM(lead + (rows // halves, width), jnp.bfloat16))
            sems.append(pltpu.SemaphoreType.DMA(lead))
    return bufs, sems


def scatter_sends(sizes, halves):
    return halves * 2 * (sizes[0] * sizes[1] + sizes[0] + sizes[1])


def lines_of(seq):
    fast = 2 if seq <= 8 else 4
    return (seq // fast, fast)


ATT_TILE = 256
SCALE = HEAD_DIM ** (-0.5)


def dot_nt(left, right):
    return lax.dot_general(left, right, (((1,), (1,)), ((), ())), preferred_element_type=jnp.float32)


def dot_tn(left, right):
    return lax.dot_general(left, right, (((0,), (0,)), ((), ())), preferred_element_type=jnp.float32)


def rotary_planes(position):
    half_rot = ROT // 2
    frequency = 10000.0 ** (-2.0 * jnp.arange(half_rot, dtype=jnp.float32) / ROT)
    angles = position.astype(jnp.float32)[:, None] * frequency[None, :]
    cos, sin = jnp.cos(angles), jnp.sin(angles)
    rows = position.shape[0]
    rest = jnp.zeros((rows, HEAD_DIM - ROT), jnp.float32)
    none = jnp.zeros_like(sin)
    return (
        jnp.concatenate([cos, cos, rest + 1.0], axis=1),
        jnp.concatenate([none, sin, rest], axis=1),
        jnp.concatenate([-sin, none, rest], axis=1),
    )


def turn(vector, cos, from_below, from_above):
    half_rot = ROT // 2
    return (
        vector * cos
        + pltpu.roll(vector, half_rot, 1) * from_below
        + pltpu.roll(vector, HEAD_DIM - half_rot, 1) * from_above
    )


def tile_mask(start_col, query_tile, key_tile):
    shape = (ATT_TILE, ATT_TILE)
    query_ids = query_tile * ATT_TILE + lax.broadcasted_iota(jnp.int32, shape, 0)
    key_ids = key_tile * ATT_TILE + lax.broadcasted_iota(jnp.int32, shape, 1)
    return (key_ids >= start_col) & (key_ids <= query_ids)


def attention_forward(qkv, start_col, first_tile, heads):
    tiles = BLOCK // ATT_TILE

    def kernel(first_ref, q_ref, k_ref, v_ref, start_ref, ctx_ref, lse_ref):
        tile = pl.program_id(1)
        queries = q_ref[...]
        start = start_ref[...]

        def step(key_tile, carry):
            top, total, acc = carry
            rows = pl.ds(pl.multiple_of(key_tile * ATT_TILE, ATT_TILE), ATT_TILE)
            scores = dot_nt(queries, k_ref[rows, :]) * SCALE
            scores = jnp.where(tile_mask(start, tile, key_tile), scores, -1e30)
            new_top = jnp.maximum(top, jnp.max(scores, axis=1, keepdims=True))
            shrink = jnp.exp(top - new_top)
            weights = jnp.exp(scores - new_top)
            total = total * shrink + jnp.sum(weights, axis=1, keepdims=True)
            acc = acc * shrink + jnp.dot(
                weights.astype(jnp.bfloat16), v_ref[rows, :], preferred_element_type=jnp.float32
            )
            return (new_top, total, acc)

        begin = (
            jnp.full((ATT_TILE, 1), -1e30, jnp.float32),
            jnp.zeros((ATT_TILE, 1), jnp.float32),
            jnp.zeros((ATT_TILE, HEAD_DIM), jnp.float32),
        )
        begin = step(tile, begin)
        top, total, acc = lax.fori_loop(first_ref[tile], tile, step, begin)
        ctx_ref[...] = (acc / total).astype(jnp.bfloat16)
        lse_ref[...] = top + jnp.log(total)

    return pl.pallas_call(
        kernel,
        grid_spec=pltpu.PrefetchScalarGridSpec(
            num_scalar_prefetch=1,
            grid=(heads, tiles),
            in_specs=[
                pl.BlockSpec((ATT_TILE, HEAD_DIM), lambda h, i, first: (i, 3 * h)),
                pl.BlockSpec((BLOCK, HEAD_DIM), lambda h, i, first: (0, 3 * h + 1)),
                pl.BlockSpec((BLOCK, HEAD_DIM), lambda h, i, first: (0, 3 * h + 2)),
                pl.BlockSpec((ATT_TILE, 1), lambda h, i, first: (i, 0)),
            ],
            out_specs=[
                pl.BlockSpec((ATT_TILE, HEAD_DIM), lambda h, i, first: (i, h)),
                pl.BlockSpec((pl.squeezed, ATT_TILE, 1), lambda h, i, first: (h, i, 0)),
            ],
        ),
        out_shape=[
            jax.ShapeDtypeStruct((BLOCK, heads * HEAD_DIM), jnp.bfloat16),
            jax.ShapeDtypeStruct((heads, BLOCK, 1), jnp.float32),
        ],
        compiler_params=pltpu.CompilerParams(vmem_limit_bytes=VMEM_LIMIT),
    )(first_tile, qkv, qkv, qkv, start_col)


def attention_backward(qkv, start_col, first_tile, heads, ctx, lse, grad_ctx, planes, before):
    tiles = BLOCK // ATT_TILE

    def kernel(
        first_ref, q_ref, k_ref, v_ref, start_ref, ctx_ref, lse_ref, do_ref, cos_ref, below_ref,
        above_ref, *rest,
    ):
        out_ref, sums_ref, dk_ref, dv_ref = rest[len(before) :]
        tile = pl.program_id(1)

        @pl.when(tile == 0)
        def _():
            dk_ref[...] = jnp.zeros_like(dk_ref)
            dv_ref[...] = jnp.zeros_like(dv_ref)

        queries = q_ref[...]
        start = start_ref[...]
        grads = do_ref[...]
        lse_rows = lse_ref[...]
        inner = jnp.sum(
            grads.astype(jnp.float32) * ctx_ref[...].astype(jnp.float32), axis=1, keepdims=True
        )

        def step(key_tile, dq):
            rows = pl.ds(pl.multiple_of(key_tile * ATT_TILE, ATT_TILE), ATT_TILE)
            keys = k_ref[rows, :]
            scores = dot_nt(queries, keys) * SCALE
            probs = jnp.where(
                tile_mask(start, tile, key_tile), jnp.exp(scores - lse_rows), 0.0
            )
            grad_probs = dot_nt(grads, v_ref[rows, :])
            grad_scores = (probs * (grad_probs - inner)).astype(jnp.bfloat16)
            dv_ref[rows, :] += dot_tn(probs.astype(jnp.bfloat16), grads)
            dk_ref[rows, :] += dot_tn(grad_scores, queries)
            return dq + jnp.dot(grad_scores, keys, preferred_element_type=jnp.float32)

        dq = lax.fori_loop(
            first_ref[tile], tile + 1, step, jnp.zeros((ATT_TILE, HEAD_DIM), jnp.float32)
        )
        here = pl.ds(pl.multiple_of(tile * ATT_TILE, ATT_TILE), ATT_TILE)
        out_ref[here, :HEAD_DIM] = turn(
            dq * SCALE, cos_ref[here, :], -below_ref[here, :], -above_ref[here, :]
        ).astype(jnp.bfloat16)

        @pl.when(tile == tiles - 1)
        def _():
            def finish(index, sums):
                rows = pl.ds(pl.multiple_of(index * ATT_TILE, ATT_TILE), ATT_TILE)
                out_ref[rows, HEAD_DIM : 2 * HEAD_DIM] = turn(
                    dk_ref[rows, :] * SCALE, cos_ref[rows, :], -below_ref[rows, :], -above_ref[rows, :]
                ).astype(jnp.bfloat16)
                out_ref[rows, 2 * HEAD_DIM :] = dv_ref[rows, :].astype(jnp.bfloat16)
                return sums + jnp.sum(out_ref[rows, :].astype(jnp.float32), axis=0, keepdims=True)

            sums_ref[...] = lax.fori_loop(
                0, tiles, finish, jnp.zeros((1, 3 * HEAD_DIM), jnp.float32)
            )

    whole = pl.BlockSpec((BLOCK, HEAD_DIM), lambda h, i, first: (0, 0))
    return pl.pallas_call(
        kernel,
        grid_spec=pltpu.PrefetchScalarGridSpec(
            num_scalar_prefetch=1,
            grid=(heads, tiles),
            in_specs=[
                pl.BlockSpec((ATT_TILE, HEAD_DIM), lambda h, i, first: (i, 3 * h)),
                pl.BlockSpec((BLOCK, HEAD_DIM), lambda h, i, first: (0, 3 * h + 1)),
                pl.BlockSpec((BLOCK, HEAD_DIM), lambda h, i, first: (0, 3 * h + 2)),
                pl.BlockSpec((ATT_TILE, 1), lambda h, i, first: (i, 0)),
                pl.BlockSpec((ATT_TILE, HEAD_DIM), lambda h, i, first: (i, h)),
                pl.BlockSpec((pl.squeezed, ATT_TILE, 1), lambda h, i, first: (h, i, 0)),
                pl.BlockSpec((ATT_TILE, HEAD_DIM), lambda h, i, first: (i, h)),
                whole,
                whole,
                whole,
            ]
            + [pl.BlockSpec(memory_space=pl.ANY)] * len(before),
            out_specs=[
                pl.BlockSpec((BLOCK, 3 * HEAD_DIM), lambda h, i, first: (0, h)),
                pl.BlockSpec((pl.squeezed, 1, 3 * HEAD_DIM), lambda h, i, first: (h, 0, 0)),
            ],
            scratch_shapes=[
                pltpu.VMEM((BLOCK, HEAD_DIM), jnp.float32),
                pltpu.VMEM((BLOCK, HEAD_DIM), jnp.float32),
            ],
        ),
        out_shape=[
            jax.ShapeDtypeStruct((BLOCK, heads * 3 * HEAD_DIM), jnp.bfloat16),
            jax.ShapeDtypeStruct((heads, 1, 3 * HEAD_DIM), jnp.float32),
        ],
        compiler_params=pltpu.CompilerParams(vmem_limit_bytes=VMEM_LIMIT),
    )(first_tile, qkv, qkv, qkv, start_col, ctx, lse, grad_ctx, *planes, *before)


def gather_cut(sizes):
    return (1792, 256) if sizes == (4, 2) else (D // 2, D // 2)


def scatter_cut(sizes):
    return (1664, 384) if sizes == (4, 2) else (D // 2, D // 2)


def columns_of(cut, kind):
    return pl.ds(0, cut[0]) if kind == 0 else pl.ds(cut[0], cut[1])


def tile_of(width):
    return 512 if width % 512 == 0 else 256 if width % 256 == 0 else 128


def span(index, size):
    return pl.ds(pl.multiple_of(index * size, size), size)


ANY = pl.BlockSpec(memory_space=pl.ANY)
VMEM = pl.BlockSpec(memory_space=pltpu.VMEM)


def row_kernel(kernel, collective, out_shape, in_specs, out_specs, scratch, cost, before=()):
    def body(*refs):
        kernel(*refs[len(before):])

    def call(*args):
        return pl.pallas_call(
            body,
            out_shape=out_shape,
            in_specs=[ANY] * len(before) + in_specs,
            out_specs=out_specs,
            scratch_shapes=scratch,
            cost_estimate=pl.CostEstimate(flops=cost, bytes_accessed=2**28, transcendentals=0),
            compiler_params=pltpu.CompilerParams(
                collective_id=collective, has_side_effects=True, vmem_limit_bytes=VMEM_LIMIT
            ),
        )(*before, *args)

    return call


def gather_scratch(sizes, rows):
    shards = sizes[0] * sizes[1]
    return [
        pltpu.VMEM((shards, rows, D), jnp.bfloat16),
        pltpu.SemaphoreType.DMA((gather_sends(sizes, HALVES),)),
        pltpu.SemaphoreType.DMA((2, HALVES, shards)),
    ]


def run_gather(grid, sizes, rows, full, send_sems, recv_sems, ready):
    cut = gather_cut(sizes)
    step = rows // HALVES
    sender = Sender(send_sems)

    def piece(slot, half, kind):
        return full.at[slot, pl.ds(half * step, step), columns_of(cut, kind)]

    gather_rounds(grid, sender, piece, recv_sems, HALVES, cut, ready)
    sender.finish()


def sum_scratch(sizes, rows):
    shards = sizes[0] * sizes[1]
    bufs, sems = scatter_scratch(sizes, HALVES, rows, D, scatter_cut(sizes))
    return (
        [pltpu.VMEM((shards, rows, D), jnp.bfloat16)]
        + bufs
        + sems
        + [pltpu.SemaphoreType.DMA((scatter_sends(sizes, HALVES),))]
    )


def run_scatter(grid, sizes, rows, scratch, produce, *hooks):
    cut = scatter_cut(sizes)
    step = rows // HALVES
    parts, b0, b1, b2, b3, s0, s1, s2, s3, send_sems = scratch
    sender = Sender(send_sems)

    def part(slot, half, kind):
        return parts.at[slot, pl.ds(half * step, step), columns_of(cut, kind)]

    scatter = Scatter(
        grid, sender, part, ((b0, b1), (b2, b3)), ((s0, s1), (s2, s3)), HALVES, cut
    )
    scatter.run(produce, *hooks)
    sender.finish()


def production_order(grid):
    return [
        grid.index(grid.nearest(0, k), grid.nearest(1, l))
        for action, k, l in [step for step in scatter_plan(grid.n) if step[0] == "make"]
    ]


ROW_TILE = 64


def tile_stats(values):
    centered = values - jnp.mean(values, axis=1, keepdims=True)
    inverse = lax.rsqrt(jnp.mean(centered * centered, axis=1, keepdims=True) + EPSILON)
    return centered, inverse


def open_rows(own, sizes, collective, norms, qkv_flat, qkv_bias, up_weight, up_bias, planes):
    rows = own.shape[0]
    shards = sizes[0] * sizes[1]
    width, hidden = qkv_flat.shape[1], up_weight.shape[1]
    heads = width // (3 * HEAD_DIM)

    def kernel(
        own_ref, norms_ref, qkvw_any, qkvb_ref, upw_any, upb_ref, cos_ref, below_ref, above_ref,
        plain_any, one_any, two_any, qkv_any, act_any, slope_any,
        full, send_sems, recv_sems, qkvw, upw, load_sems, plain, one, two, qkv, act, slope, out_sems,
    ):
        grid = Grid2(sizes)
        loads = [
            pltpu.make_async_copy(qkvw_any, qkvw, load_sems.at[0]),
            pltpu.make_async_copy(upw_any, upw, load_sems.at[1]),
        ]
        for copy in loads:
            copy.start()
        full[grid.index(*grid.me)] = own_ref[...]
        grid.barrier()
        open_copies = []

        def outs(place, slot):
            pairs = ((plain, plain_any), (one, one_any), (two, two_any), (qkv, qkv_any), (act, act_any), (slope, slope_any))
            return [
                pltpu.make_async_copy(here.at[slot], there.at[place], out_sems.at[slot, i])
                for i, (here, there) in enumerate(pairs)
            ]

        def ready(slow, fast, order):
            place = grid.index(slow, fast)
            slot = order % 2
            if order == 0:
                for copy in loads:
                    copy.wait()
            if order >= 2:
                for copy in open_copies.pop(0):
                    copy.wait()

            def norm_tile(index, _):
                here = span(index, ROW_TILE)
                centered, inverse = tile_stats(full[place, here].astype(jnp.float32))
                normed = centered * inverse
                plain[slot, here] = normed.astype(jnp.bfloat16)
                one[slot, here] = (normed * norms_ref[0:1] + norms_ref[1:2]).astype(jnp.bfloat16)
                two[slot, here] = (normed * norms_ref[2:3] + norms_ref[3:4]).astype(jnp.bfloat16)
                return _

            lax.fori_loop(0, rows // ROW_TILE, norm_tile, 0)
            places = pl.ds(pl.multiple_of(place * rows, rows), rows)
            cos, below, above = cos_ref[places, :], below_ref[places, :], above_ref[places, :]
            whole = jnp.dot(one[slot], qkvw[...], preferred_element_type=jnp.float32) + qkvb_ref[...]
            for head in range(heads):
                first = head * 3 * HEAD_DIM
                found = whole[:, first : first + 3 * HEAD_DIM]
                qkv[slot, :, first : first + HEAD_DIM] = turn(
                    found[:, :HEAD_DIM], cos, below, above
                ).astype(jnp.bfloat16)
                qkv[slot, :, first + HEAD_DIM : first + 2 * HEAD_DIM] = turn(
                    found[:, HEAD_DIM : 2 * HEAD_DIM], cos, below, above
                ).astype(jnp.bfloat16)
                qkv[slot, :, first + 2 * HEAD_DIM : first + 3 * HEAD_DIM] = found[
                    :, 2 * HEAD_DIM :
                ].astype(jnp.bfloat16)
            tile = tile_of(hidden)

            def up_tile(index, _):
                here = span(index, tile)
                pre = jnp.dot(two[slot], upw[:, here], preferred_element_type=jnp.float32) + upb_ref[:, here]
                share = 0.5 * (1.0 + lax.erf(pre * 0.7071067811865476))
                act[slot, :, here] = (pre * share).astype(jnp.bfloat16)
                slope[slot, :, here] = (
                    share + pre * (jnp.exp(-0.5 * pre * pre) * 0.3989422804014327)
                ).astype(jnp.bfloat16)
                return _

            lax.fori_loop(0, hidden // tile, up_tile, 0)
            copies = outs(place, slot)
            for copy in copies:
                copy.start()
            open_copies.append(copies)

        run_gather(grid, sizes, rows, full, send_sems, recv_sems, ready)
        for copies in open_copies:
            for copy in copies:
                copy.wait()

    def out(columns):
        return jax.ShapeDtypeStruct((shards, rows, columns), jnp.bfloat16)

    def staged(columns):
        return pltpu.VMEM((2, rows, columns), jnp.bfloat16)

    return row_kernel(
        kernel, collective,
        [out(D), out(D), out(D), out(width), out(hidden), out(hidden)],
        [VMEM, VMEM, ANY, VMEM, ANY, VMEM, VMEM, VMEM, VMEM],
        [ANY] * 6,
        gather_scratch(sizes, rows)
        + [
            pltpu.VMEM(qkv_flat.shape, jnp.bfloat16),
            pltpu.VMEM(up_weight.shape, jnp.bfloat16),
            pltpu.SemaphoreType.DMA((2,)),
            staged(D), staged(D), staged(D), staged(width), staged(hidden), staged(hidden),
            pltpu.SemaphoreType.DMA((2, 6)),
        ],
        2 * BLOCK * D * (width + hidden),
    )(own, norms, qkv_flat, qkv_bias, up_weight, up_bias, *planes)


def branch_rows(own, ctx, act, out_flat, down_weight, norms, sizes, collective):
    rows = own.shape[0]
    shards = sizes[0] * sizes[1]
    inner, hidden = out_flat.shape[0], down_weight.shape[0]

    def kernel(
        own_ref, ctx_any, act_any, outw_any, downw_any, norms_ref, out_ref, final_ref, normed_ref, inverse_ref,
        ctx, act, outw, downw, load_sems, *scratch,
    ):
        grid = Grid2(sizes)
        parts = scratch[0]
        weights = [
            pltpu.make_async_copy(outw_any, outw, load_sems.at[0, 0]),
            pltpu.make_async_copy(downw_any, downw, load_sems.at[0, 1]),
        ]
        order = production_order(grid)
        loads = [
            [
                pltpu.make_async_copy(ctx_any.at[place], ctx.at[place], load_sems.at[1 + i, 0]),
                pltpu.make_async_copy(act_any.at[place], act.at[place], load_sems.at[1 + i, 1]),
            ]
            for i, place in enumerate(order)
        ]
        for copy in loads[0] + weights:
            copy.start()
        for copies in loads[1:]:
            for copy in copies:
                copy.start()
        grid.barrier()
        for copy in weights:
            copy.wait()

        def produce(slow, fast):
            place = grid.index(slow, fast)
            for copy in loads.pop(0):
                copy.wait()

            def columns(index, _):
                here = span(index, 512)
                parts[place, :, here] = (
                    jnp.dot(ctx[place], outw[:, here], preferred_element_type=jnp.float32)
                    + jnp.dot(act[place], downw[:, here], preferred_element_type=jnp.float32)
                ).astype(jnp.bfloat16)
                return _

            lax.fori_loop(0, D // 512, columns, 0)

        run_scatter(grid, sizes, rows, scratch, produce)
        mine = grid.index(*grid.me)

        def norm_tile(index, _):
            here = span(index, ROW_TILE)
            stream = own_ref[here].astype(jnp.float32) + parts[mine, here].astype(jnp.float32) + norms_ref[2:3]
            out_ref[here] = stream.astype(jnp.bfloat16)
            centered, inverse = tile_stats(stream)
            normed = centered * inverse
            final_ref[here] = (normed * norms_ref[0:1] + norms_ref[1:2]).astype(jnp.bfloat16)
            normed_ref[here] = normed
            inverse_ref[here] = inverse
            return _

        lax.fori_loop(0, rows // ROW_TILE, norm_tile, 0)

    return row_kernel(
        kernel, collective,
        [
            jax.ShapeDtypeStruct((rows, D), jnp.bfloat16),
            jax.ShapeDtypeStruct((rows, D), jnp.bfloat16),
            jax.ShapeDtypeStruct((rows, D), jnp.float32),
            jax.ShapeDtypeStruct((rows, 1), jnp.float32),
        ],
        [VMEM, ANY, ANY, ANY, ANY, VMEM],
        [VMEM] * 4,
        [
            pltpu.VMEM(ctx.shape, jnp.bfloat16),
            pltpu.VMEM(act.shape, jnp.bfloat16),
            pltpu.VMEM(out_flat.shape, jnp.bfloat16),
            pltpu.VMEM(down_weight.shape, jnp.bfloat16),
            pltpu.SemaphoreType.DMA((1 + shards, 2)),
        ]
        + sum_scratch(sizes, rows),
        2 * BLOCK * D * (inner + hidden),
    )(own, ctx, act, out_flat, down_weight, norms)


def logit_rows(final, head_weight, targets_col, sizes, collective):
    rows = final.shape[0]
    shards = sizes[0] * sizes[1]
    vocab = head_weight.shape[1]

    def kernel(
        own_ref, headw_any, target_ref, final_any, weights_any, stats_ref,
        full, send_sems, recv_sems, headw, load_sem, logits, weights, out_sems, row_sems,
    ):
        grid = Grid2(sizes)
        load = pltpu.make_async_copy(headw_any, headw, load_sem)
        load.start()
        full[grid.index(*grid.me)] = own_ref[...]
        grid.barrier()
        base = lax.axis_index("seq") * vocab
        open_copies, raw_copies = [], []

        def ready(slow, fast, order):
            place = grid.index(slow, fast)
            slot = order % 2
            if order == 0:
                load.wait()
            if order >= 2:
                open_copies.pop(0).wait()
            places = pl.ds(pl.multiple_of(place * rows, rows), rows)
            target = target_ref[places, :] - base

            def fold(values, join):
                total = values[:, :128]
                for first in range(128, values.shape[1], 128):
                    total = join(total, values[:, first : first + 128])
                return total

            def logit_tile(start, size, carry):
                top, pick = carry
                here = pl.ds(start, size)
                found = jnp.dot(full[place], headw[:, here], preferred_element_type=jnp.float32)
                logits[:, here] = found
                ids = start + lax.broadcasted_iota(jnp.int32, (rows, size), 1)
                top = jnp.maximum(top, fold(found, jnp.maximum))
                pick = pick + fold(jnp.where(ids == target, found, 0.0), jnp.add)
                return (top, pick)

            def tiled(step, carry):
                count = vocab // 512
                carry = lax.fori_loop(
                    0, count, lambda i, c: step(pl.multiple_of(i * 512, 512), 512, c), carry
                )
                if vocab % 512:
                    carry = step(count * 512, vocab % 512, carry)
                return carry

            top, pick = tiled(
                logit_tile,
                (jnp.full((rows, 128), -jnp.inf, jnp.float32), jnp.zeros((rows, 128), jnp.float32)),
            )
            top = jnp.max(top, axis=1, keepdims=True)
            pick = jnp.sum(pick, axis=1, keepdims=True)

            def weight_tile(start, size, total):
                here = pl.ds(start, size)
                found = jnp.exp(logits[:, here] - top)
                weights[slot, :, here] = found.astype(jnp.bfloat16)
                return total + fold(found, jnp.add)

            total = tiled(weight_tile, jnp.zeros((rows, 128), jnp.float32))
            total = jnp.sum(total, axis=1, keepdims=True)
            lane = lax.broadcasted_iota(jnp.int32, (rows, 128), 1)
            found = jnp.where(lane == 0, top, jnp.where(lane == 1, total, pick))
            stats_ref[:, places] = found.T[0:8]
            copy = pltpu.make_async_copy(weights.at[slot], weights_any.at[place], out_sems.at[slot])
            copy.start()
            open_copies.append(copy)
            raw = pltpu.make_async_copy(full.at[place], final_any.at[place], row_sems.at[order])
            raw.start()
            raw_copies.append(raw)

        run_gather(grid, sizes, rows, full, send_sems, recv_sems, ready)
        for copy in open_copies + raw_copies:
            copy.wait()

    return row_kernel(
        kernel, collective,
        [
            jax.ShapeDtypeStruct((shards, rows, D), jnp.bfloat16),
            jax.ShapeDtypeStruct((shards, rows, vocab), jnp.bfloat16),
            jax.ShapeDtypeStruct((8, shards * rows), jnp.float32),
        ],
        [VMEM, ANY, VMEM],
        [ANY, ANY, VMEM],
        gather_scratch(sizes, rows)
        + [
            pltpu.VMEM(head_weight.shape, jnp.bfloat16),
            pltpu.SemaphoreType.DMA,
            pltpu.VMEM((rows, vocab), jnp.float32),
            pltpu.VMEM((2, rows, vocab), jnp.bfloat16),
            pltpu.SemaphoreType.DMA((2,)),
            pltpu.SemaphoreType.DMA((shards,)),
        ],
        2 * BLOCK * D * vocab,
    )(final, head_weight, targets_col)


def final_grad_rows(grad_logits, head_weight, normed, inverse, gain, sizes, collective, before):
    shards, rows, vocab = grad_logits.shape

    def kernel(
        grads_any, headw_any, normed_ref, inverse_ref, gain_ref, stream_ref, down_ref, sums_ref,
        headw, grads, load_sems, *scratch,
    ):
        grid = Grid2(sizes)
        parts = scratch[0]
        order = production_order(grid)
        loads = [
            pltpu.make_async_copy(grads_any.at[place], grads.at[i % 2], load_sems.at[i])
            for i, place in enumerate(order)
        ]
        tile = 512
        weights = [
            pltpu.make_async_copy(
                headw_any.at[pl.ds(i * tile, tile)], headw.at[pl.ds(i * tile, tile)], load_sems.at[1 + shards + i]
            )
            for i in range(D // tile)
        ]
        loads[0].start()
        for copy in weights:
            copy.start()
        grid.barrier()
        count = [0]

        def produce(slow, fast):
            place = grid.index(slow, fast)
            i = count[0]
            count[0] += 1
            if i + 1 < shards:
                loads[i + 1].start()
            loads[i].wait()

            def columns(index, _):
                here = span(index, tile)
                parts[place, :, here] = dot_nt(grads[i % 2], headw[here, :]).astype(jnp.bfloat16)
                return _

            if i == 0:
                for index, copy in enumerate(weights):
                    copy.wait()
                    columns(index, 0)
            else:
                lax.fori_loop(0, D // tile, columns, 0)

        run_scatter(grid, sizes, rows, scratch, produce)
        mine = grid.index(*grid.me)
        sums_ref[...] = jnp.zeros_like(sums_ref)

        def norm_tile(index, _):
            here = span(index, ROW_TILE)
            grad = parts[mine, here].astype(jnp.float32)
            norm = normed_ref[here]
            scaled = grad * gain_ref[...]
            stream = inverse_ref[here] * (
                scaled
                - jnp.mean(scaled, axis=1, keepdims=True)
                - norm * jnp.mean(scaled * norm, axis=1, keepdims=True)
            )
            stream_ref[here] = stream
            down_ref[here] = stream.astype(jnp.bfloat16)
            sums_ref[0:1] += jnp.sum(grad * norm, axis=0, keepdims=True)
            sums_ref[1:2] += jnp.sum(grad, axis=0, keepdims=True)
            sums_ref[2:3] += jnp.sum(stream, axis=0, keepdims=True)
            return _

        lax.fori_loop(0, rows // ROW_TILE, norm_tile, 0)

    return row_kernel(
        kernel, collective,
        [
            jax.ShapeDtypeStruct((rows, D), jnp.float32),
            jax.ShapeDtypeStruct((rows, D), jnp.bfloat16),
            jax.ShapeDtypeStruct((8, D), jnp.float32),
        ],
        [ANY, ANY, VMEM, VMEM, VMEM],
        [VMEM] * 3,
        [
            pltpu.VMEM(head_weight.shape, jnp.bfloat16),
            pltpu.VMEM((2, rows, vocab), jnp.bfloat16),
            pltpu.SemaphoreType.DMA((1 + shards + D // 512,)),
        ]
        + sum_scratch(sizes, rows),
        2 * BLOCK * D * vocab,
        before,
    )(grad_logits, head_weight, normed, inverse, gain)


def branch_grad_rows(own, out_flat, down_weight, slope, sizes, collective):
    rows = own.shape[0]
    shards = sizes[0] * sizes[1]
    inner, hidden = out_flat.shape[0], down_weight.shape[0]

    def kernel(
        own_ref, outw_any, downw_any, slope_any, rows_any, ctx_any, up_any, sums_ref,
        full, send_sems, recv_sems, outw, downw, load_sems, slope, slope_sems, ctx, up, out_sems, row_sems,
    ):
        grid = Grid2(sizes)
        loads = [
            pltpu.make_async_copy(outw_any, outw, load_sems.at[0]),
            pltpu.make_async_copy(downw_any, downw, load_sems.at[1]),
        ]
        for copy in loads:
            copy.start()
        slopes = pltpu.make_async_copy(slope_any, slope, slope_sems)
        slopes.start()
        full[grid.index(*grid.me)] = own_ref[...]
        sums_ref[...] = jnp.zeros_like(sums_ref)
        grid.barrier()
        open_copies, raw_copies = [], []

        def ready(slow, fast, order):
            place = grid.index(slow, fast)
            slot = order % 2
            if order == 0:
                for copy in loads + [slopes]:
                    copy.wait()
            if order >= 2:
                for copy in open_copies.pop(0):
                    copy.wait()
            ctx[slot] = dot_nt(full[place], outw[...]).astype(jnp.bfloat16)
            tile = tile_of(hidden)

            def up_tile(index, _):
                here = span(index, tile)
                found = dot_nt(full[place], downw[here, :]) * slope[place, :, here].astype(jnp.float32)
                rounded = found.astype(jnp.bfloat16)
                up[slot, :, here] = rounded
                sums_ref[0:1, here] += jnp.sum(rounded.astype(jnp.float32), axis=0, keepdims=True)
                return _

            lax.fori_loop(0, hidden // tile, up_tile, 0)
            copies = [
                pltpu.make_async_copy(ctx.at[slot], ctx_any.at[place], out_sems.at[slot, 0]),
                pltpu.make_async_copy(up.at[slot], up_any.at[place], out_sems.at[slot, 1]),
            ]
            for copy in copies:
                copy.start()
            open_copies.append(copies)
            raw = pltpu.make_async_copy(full.at[place], rows_any.at[place], row_sems.at[order])
            raw.start()
            raw_copies.append(raw)

        run_gather(grid, sizes, rows, full, send_sems, recv_sems, ready)
        for copies in open_copies:
            for copy in copies:
                copy.wait()
        for copy in raw_copies:
            copy.wait()

    def out(columns):
        return jax.ShapeDtypeStruct((shards, rows, columns), jnp.bfloat16)

    return row_kernel(
        kernel, collective,
        [out(D), out(inner), out(hidden), jax.ShapeDtypeStruct((8, hidden), jnp.float32)],
        [VMEM, ANY, ANY, ANY],
        [ANY, ANY, ANY, VMEM],
        gather_scratch(sizes, rows)
        + [
            pltpu.VMEM(out_flat.shape, jnp.bfloat16),
            pltpu.VMEM(down_weight.shape, jnp.bfloat16),
            pltpu.SemaphoreType.DMA((2,)),
            pltpu.VMEM((shards, rows, hidden), jnp.bfloat16),
            pltpu.SemaphoreType.DMA,
            pltpu.VMEM((2, rows, inner), jnp.bfloat16),
            pltpu.VMEM((2, rows, hidden), jnp.bfloat16),
            pltpu.SemaphoreType.DMA((2, 2)),
            pltpu.SemaphoreType.DMA((shards,)),
        ],
        2 * BLOCK * D * (inner + hidden),
    )(own, out_flat, down_weight, slope)


class SmallSum:
    def __init__(self, shards, replicas, sums, bias, total, bias_total, scratch):
        self.shards, self.replicas = shards, replicas
        self.sums, self.bias, self.total, self.bias_total = sums, bias, total, bias_total
        (
            self.came, self.block, self.blocks, self.biases, self.spread_send, self.spread_recv, self.cross_send,
            self.cross_recv, self.back_send, self.back_recv,
        ) = scratch
        self.seq, self.dp = lax.axis_index("seq"), lax.axis_index("dp")
        self.width = D // shards

    @staticmethod
    def scratch(shards, replicas):
        width = D // shards
        dma = pltpu.SemaphoreType.DMA
        return [
            pltpu.VMEM((shards, 8, width), jnp.float32),
            pltpu.VMEM((8, width), jnp.float32),
            pltpu.VMEM((replicas, 8, width), jnp.float32),
            pltpu.VMEM((replicas, 8, D), jnp.float32),
            dma((shards,)), dma((shards,)), dma((2, replicas)), dma((2, replicas)), dma((shards,)), dma((shards,)),
        ]

    def others(self, axis):
        count, here = (self.shards, self.seq) if axis == "seq" else (self.replicas, self.dp)
        return [(step, lax.rem(here + step, count)) for step in range(1, count)]

    def barrier(self):
        sem = pltpu.get_barrier_semaphore()
        amount = 0
        for axis in ("seq", "dp"):
            for _, place in self.others(axis):
                pl.semaphore_signal(sem, inc=1, device_id={axis: place}, device_id_type=MESH)
                amount += 1
        pl.semaphore_wait(sem, amount)

    def copy(self, axis, place, src, dst, send, recv):
        return pltpu.make_async_remote_copy(
            src_ref=src, dst_ref=dst, send_sem=send, recv_sem=recv, device_id={axis: place}, device_id_type=MESH
        )

    def columns(self, place):
        return pl.ds(pl.multiple_of(place * self.width, self.width), self.width)

    def spread(self):
        self.first = [
            self.copy(
                "seq", place, self.sums.at[:, self.columns(place)], self.came.at[step], self.spread_send.at[step],
                self.spread_recv.at[step],
            )
            for step, place in self.others("seq")
        ]
        self.second = [
            self.copy(
                "dp", place, self.bias, self.biases.at[self.dp], self.cross_send.at[1, step],
                self.cross_recv.at[1, step],
            )
            for step, place in self.others("dp")
        ]
        for copy in self.first + self.second:
            copy.start()

    def cross(self):
        total = self.sums[:, self.columns(self.seq)]
        for (step, _), copy in zip(self.others("seq"), self.first):
            copy.wait_recv()
            total = total + self.came[step]
        self.block[...] = total
        self.blocks[self.dp] = total
        self.third = [
            self.copy(
                "dp", place, self.block, self.blocks.at[self.dp], self.cross_send.at[0, step],
                self.cross_recv.at[0, step],
            )
            for step, place in self.others("dp")
        ]
        for copy in self.third:
            copy.start()

    def collect(self):
        for copy in self.third + self.second:
            copy.wait_recv()
        self.biases[self.dp] = self.bias[...]
        total, bias = self.blocks[0], self.biases[0]
        for place in range(1, self.replicas):
            total, bias = total + self.blocks[place], bias + self.biases[place]
        self.bias_total[...] = bias
        here = self.columns(self.seq)
        self.total[:, here] = total
        self.fourth = [
            self.copy(
                "seq", place, self.total.at[:, here], self.total.at[:, here], self.back_send.at[step],
                self.back_recv.at[step],
            )
            for step, place in self.others("seq")
        ]
        for copy in self.fourth:
            copy.start()

    def finish(self):
        for (step, _), copy in zip(self.others("seq"), self.fourth):
            source = lax.rem(self.seq + self.shards - step, self.shards)
            there = self.total.at[:, self.columns(source)]
            self.copy("seq", source, there, there, self.back_send.at[step], self.back_recv.at[step]).wait_recv()
        for copy in self.first + self.second + self.third + self.fourth:
            copy.wait_send()


def score_rows(stats, seg_row, examples, sizes, replicas, collective):
    shards = sizes[0] * sizes[1]
    width = BLOCK // shards

    def kernel(
        stats_ref, seg_ref, examples_ref, coef_ref, losses_ref,
        came, full, ratio, ratios, spread_send, spread_recv, back_send, back_recv, cross_send, cross_recv,
    ):
        seq, dp = lax.axis_index("seq"), lax.axis_index("dp")
        peers = {
            "seq": [(step, lax.rem(seq + step, shards)) for step in range(1, shards)],
            "dp": [(step, lax.rem(dp + step, replicas)) for step in range(1, replicas)],
        }
        barrier = pltpu.get_barrier_semaphore()
        for axis in peers:
            for _, place in peers[axis]:
                pl.semaphore_signal(barrier, inc=1, device_id={axis: place}, device_id_type=MESH)
        pl.semaphore_wait(barrier, shards + replicas - 2)

        def columns(place):
            return pl.ds(pl.multiple_of(place * width, width), width)

        def copy(axis, place, src, dst, send, recv):
            return pltpu.make_async_remote_copy(
                src_ref=src, dst_ref=dst, send_sem=send, recv_sem=recv, device_id={axis: place}, device_id_type=MESH
            )

        sent = [
            copy("seq", place, stats_ref.at[:, columns(place)], came.at[step], spread_send.at[step], spread_recv.at[step])
            for step, place in peers["seq"]
        ]
        for one in sent:
            one.start()
        mine = stats_ref[:, columns(seq)]
        top, total, pick = mine[0:1], mine[1:2], mine[2:3]
        for (step, _), one in zip(peers["seq"], sent):
            one.wait_recv()
            other = came[step]
            joint = jnp.maximum(top, other[0:1])
            total = total * jnp.exp(top - joint) + other[1:2] * jnp.exp(other[0:1] - joint)
            pick = pick + other[2:3]
            top = joint
        log_total = top + jnp.log(total)
        here = columns(seq)
        full[0:1, here] = log_total
        full[1:2, here] = pick - log_total
        back = [
            copy("seq", place, full.at[:, here], full.at[:, here], back_send.at[step], back_recv.at[step])
            for step, place in peers["seq"]
        ]
        for one in back:
            one.start()
        for step, _ in peers["seq"]:
            source = lax.rem(seq + shards - step, shards)
            there = full.at[:, columns(source)]
            copy("seq", source, there, there, back_send.at[step], back_recv.at[step]).wait_recv()
        member = lax.broadcasted_iota(jnp.int32, (EXB, BLOCK), 0) == seg_ref[...]
        counts, reference, sign = examples_ref[:, 0:1], examples_ref[:, 1:2], examples_ref[:, 2:3]
        mean = jnp.sum(jnp.where(member, full[1:2, :], 0.0), axis=1, keepdims=True) / counts
        log_ratio = mean - reference
        ratio[...] = jnp.broadcast_to(jnp.sum(log_ratio, axis=0, keepdims=True), ratio.shape)
        crossed = [
            copy("dp", place, ratio, ratios.at[dp], cross_send.at[step], cross_recv.at[step])
            for step, place in peers["dp"]
        ]
        for one in crossed:
            one.start()
        for one in crossed:
            one.wait_recv()
        ratios[dp] = ratio[...]
        whole = ratios[0]
        for place in range(1, replicas):
            whole = whole + ratios[place]
        center = whole[:, 0:1] / (replicas * EXB)
        squashed = jax.nn.sigmoid(BETA * sign * (log_ratio - center))
        losses_ref[...] = jnp.broadcast_to(1.0 - squashed, losses_ref.shape)
        grad = -LOSS_SCALE * BETA * sign * squashed * (1.0 - squashed) / counts
        token = jnp.sum(jnp.where(member, grad, 0.0), axis=0, keepdims=True)
        coef_ref[...] = jnp.zeros_like(coef_ref)
        coef_ref[0:1, :] = token
        coef_ref[1:2, :] = token * jnp.exp(stats_ref[0:1, :] - full[0:1, :])
        for one in sent + back + crossed:
            one.wait_send()

    dma = pltpu.SemaphoreType.DMA
    return pl.pallas_call(
        kernel,
        out_shape=[
            jax.ShapeDtypeStruct((8, BLOCK), jnp.float32),
            jax.ShapeDtypeStruct((EXB, 128), jnp.float32),
        ],
        in_specs=[VMEM] * 3,
        out_specs=[VMEM] * 2,
        scratch_shapes=[
            pltpu.VMEM((shards, 8, width), jnp.float32),
            pltpu.VMEM((8, BLOCK), jnp.float32),
            pltpu.VMEM((EXB, 128), jnp.float32),
            pltpu.VMEM((replicas, EXB, 128), jnp.float32),
            dma((shards,)), dma((shards,)), dma((shards,)), dma((shards,)), dma((replicas,)), dma((replicas,)),
        ],
        compiler_params=pltpu.CompilerParams(collective_id=collective, has_side_effects=True),
    )(stats, seg_row, examples)


def input_grad_rows(
    own, grad_stream, plain, grad_qkv, grad_up, qkv_flat, up_weight, gains, end_sums, biases, sizes, replicas,
    collective, before,
):
    shards, rows, width = grad_qkv.shape
    hidden = grad_up.shape[2]

    def kernel(
        own_ref, stream_ref, normed_any, qkv_any, up_any, qkvw_any, upw_any, gains_ref, end_ref,
        bias_ref, out_ref, total_ref, bias_total_ref,
        qkvw, upw, weight_sems, normed, qkv, up, load_sems, sums_ref, *scratch,
    ):
        grid = Grid2(sizes)
        small = SmallSum(shards, replicas, sums_ref, bias_ref, total_ref, bias_total_ref, scratch[:10])
        scratch = scratch[10:]
        parts = scratch[0]
        order = production_order(grid)

        def loads(i):
            place = order[i]
            return [
                pltpu.make_async_copy(normed_any.at[place], normed.at[i % 2], load_sems.at[i, 0]),
                pltpu.make_async_copy(qkv_any.at[place], qkv.at[i % 2], load_sems.at[i, 1]),
                pltpu.make_async_copy(up_any.at[place], up.at[i % 2], load_sems.at[i, 2]),
            ]

        copies = [loads(i) for i in range(shards)]
        weights = [
            pltpu.make_async_copy(qkvw_any, qkvw, weight_sems.at[0]),
            pltpu.make_async_copy(upw_any, upw, weight_sems.at[1]),
        ]
        for copy in copies[0] + weights:
            copy.start()
        sums_ref[...] = jnp.zeros_like(sums_ref)
        small.barrier()
        for copy in weights:
            copy.wait()
        count = [0]

        def produce(slow, fast):
            place = grid.index(slow, fast)
            i = count[0]
            count[0] += 1
            if i + 1 < shards:
                for copy in copies[i + 1]:
                    copy.start()
            for copy in copies[i]:
                copy.wait()
            slot = i % 2

            def columns(index, _):
                here = span(index, 512)
                one = dot_nt(qkv[slot], qkvw[here, :])
                two = dot_nt(up[slot], upw[here, :])
                norm = normed[slot, :, here].astype(jnp.float32)
                parts[place, :, here] = (one * gains_ref[0:1, here] + two * gains_ref[1:2, here]).astype(
                    jnp.bfloat16
                )
                sums_ref[0:1, here] += jnp.sum(one * norm, axis=0, keepdims=True)
                sums_ref[1:2, here] += jnp.sum(one, axis=0, keepdims=True)
                sums_ref[2:3, here] += jnp.sum(two * norm, axis=0, keepdims=True)
                sums_ref[3:4, here] += jnp.sum(two, axis=0, keepdims=True)
                return _

            lax.fori_loop(0, D // 512, columns, 0)

        def made():
            sums_ref[4:8] = end_ref[0:4]
            small.spread()

        run_scatter(grid, sizes, rows, scratch, produce, made, small.cross, small.collect)
        mine = grid.index(*grid.me)

        def norm_tile(index, _):
            here = span(index, ROW_TILE)
            grad = parts[mine, here].astype(jnp.float32)
            centered, inverse = tile_stats(own_ref[here].astype(jnp.float32))
            normed = centered * inverse
            out_ref[here] = stream_ref[here] + inverse * (
                grad
                - jnp.mean(grad, axis=1, keepdims=True)
                - normed * jnp.mean(grad * normed, axis=1, keepdims=True)
            )
            return _

        lax.fori_loop(0, rows // ROW_TILE, norm_tile, 0)
        small.finish()

    return row_kernel(
        kernel, collective,
        [jax.ShapeDtypeStruct((rows, D), jnp.float32), jax.ShapeDtypeStruct((8, D), jnp.float32), jax.ShapeDtypeStruct((8, D), jnp.float32)],
        [VMEM, VMEM, ANY, ANY, ANY, ANY, ANY, VMEM, VMEM, VMEM],
        [VMEM, VMEM, VMEM],
        [
            pltpu.VMEM(qkv_flat.shape, jnp.bfloat16),
            pltpu.VMEM(up_weight.shape, jnp.bfloat16),
            pltpu.SemaphoreType.DMA((2,)),
            pltpu.VMEM((2, rows, D), jnp.bfloat16),
            pltpu.VMEM((2, rows, width), jnp.bfloat16),
            pltpu.VMEM((2, rows, hidden), jnp.bfloat16),
            pltpu.SemaphoreType.DMA((shards, 3)),
            pltpu.VMEM((8, D), jnp.float32),
        ]
        + SmallSum.scratch(shards, replicas)
        + sum_scratch(sizes, rows),
        2 * BLOCK * D * (width + hidden),
        before,
    )(own, grad_stream, plain, grad_qkv, grad_up, qkv_flat, up_weight, gains, end_sums, biases)


def segment_rows(block_lengths):
    row_ends = jnp.cumsum(block_lengths)
    row_ids = jnp.arange(BLOCK, dtype=jnp.int32)
    passed = (row_ids[:, None] >= row_ends[None, :]).astype(jnp.int32)
    segment = jnp.sum(passed, axis=1)
    position = row_ids - jnp.sum(passed * block_lengths[None, :], axis=1)
    return (segment, position)


def row_of(vector):
    return vector.astype(jnp.float32)[None, :]


PAIR = [(0, 1), (1, 0), (2, 3), (3, 2)]
CROSS = [(0, 2), (2, 0), (1, 3), (3, 1)]


def held(values):
    return lax.optimization_barrier(values)


def half_of(values, which):
    half = values.shape[1] // 2
    return lax.dynamic_slice_in_dim(values, which * half, half, 1)


class PairSum:
    def __init__(self, product):
        self.plain = lax.axis_size("dp") != 4
        if self.plain:
            self.sum = jnp.stack([product(0), product(1)]).astype(jnp.bfloat16)
            return
        self.core = lax.rem(lax.axis_index("dp"), 2)
        away = product(1 - self.core).astype(jnp.bfloat16)
        came = lax.ppermute(away, "dp", PAIR)
        mine = held(product(self.core))
        self.sum = (mine + came.astype(jnp.float32)).astype(jnp.bfloat16)

    def cross(self):
        self.other = lax.psum(self.sum, "dp") if self.plain else lax.ppermute(self.sum, "dp", CROSS)
        return self

    def join(self):
        if self.plain:
            self.total = self.other
        else:
            self.total = (self.sum.astype(jnp.float32) + self.other.astype(jnp.float32)).astype(jnp.bfloat16)
        return self

    def settle(self):
        if self.plain:
            first, second = self.total[0], self.total[1]
        else:
            back = lax.ppermute(self.total, "dp", PAIR)
            first = jnp.where(self.core == 0, self.total, back)
            second = jnp.where(self.core == 0, back, self.total)
        return first.astype(jnp.float32), second.astype(jnp.float32)


def after(values, earlier):
    def kernel(*refs):
        del refs

    return pl.pallas_call(
        kernel,
        out_shape=[jax.ShapeDtypeStruct(v.shape, v.dtype) for v in values],
        in_specs=[ANY] * (len(values) + 1),
        out_specs=[ANY] * len(values),
        input_output_aliases={i: i for i in range(len(values))},
    )(*values, earlier)


def per_device(
    hidden, targets, lengths, labels, ref_logps, ln1_gain, ln1_bias, ln2_gain, ln2_bias, qkv_weight, qv_bias,
    out_weight, up_weight, up_bias, down_weight, branch_bias, lnf_gain, lnf_bias, head_weight,
):
    sizes = lines_of(lax.axis_size("seq"))
    own = hidden[0]
    local_heads = qkv_weight.shape[1]
    local_vocab = head_weight.shape[1]
    local_hidden = up_weight.shape[1]
    width = local_heads * 3 * HEAD_DIM
    inner = local_heads * HEAD_DIM
    qv_float = qv_bias.astype(jnp.float32)
    full_bias = jnp.concatenate(
        [qv_float[:, :HEAD_DIM], jnp.zeros_like(qv_float[:, :HEAD_DIM]), qv_float[:, HEAD_DIM:]], axis=-1
    ).reshape(1, width)
    qkv_flat = qkv_weight.reshape(D, width)
    out_flat = out_weight.reshape(inner, D)
    block_lengths = lengths[0]
    segment, position = segment_rows(block_lengths)
    start = jnp.arange(BLOCK, dtype=jnp.int32) - position
    start_col = start[:, None]
    first_tile = start[::ATT_TILE] // ATT_TILE
    planes = rotary_planes(position)

    norms = jnp.concatenate([row_of(v) for v in (ln1_gain, ln1_bias, ln2_gain, ln2_bias)], axis=0)
    plain, first_full, second_full, qkv, act, slope = open_rows(
        own, sizes, 0, norms, qkv_flat, full_bias, up_weight, row_of(up_bias), planes
    )
    flat_qkv = qkv.reshape(BLOCK, width)
    ctx, lse = attention_forward(flat_qkv, start_col, first_tile, local_heads)
    shards, rows = plain.shape[0], plain.shape[1]
    end_norms = jnp.concatenate([row_of(v) for v in (lnf_gain, lnf_bias, branch_bias)], axis=0)
    output, final, normed, inverse = branch_rows(
        own, ctx.reshape(shards, rows, inner), act, out_flat, down_weight, end_norms, sizes, 1
    )
    final_full, weights, stats = logit_rows(final, head_weight, targets[0][:, None], sizes, 2)

    examples = jnp.stack(
        [block_lengths.astype(jnp.float32), ref_logps[0], (2 * labels[0] - 1).astype(jnp.float32)], axis=1
    )
    coef, losses = score_rows(
        stats, segment[None, :], jnp.pad(examples, ((0, 0), (0, 125))), sizes, lax.axis_size("dp"), 6
    )
    vocab_ids = lax.axis_index("seq") * local_vocab + jnp.arange(local_vocab, dtype=jnp.int32)
    grad_logits = held((
        jnp.where(vocab_ids[None, :] == targets[0][:, None], coef[0][:, None], 0.0)
        - weights.reshape(BLOCK, local_vocab).astype(jnp.float32) * coef[1][:, None]
    ).astype(jnp.bfloat16))
    final_rows = final_full.reshape(BLOCK, D)
    head_sum = PairSum(lambda which: dot_tn(half_of(final_rows, which), grad_logits)).cross()

    grad_stream, grad_own, end_sums = final_grad_rows(
        grad_logits.reshape(shards, rows, local_vocab), head_weight, normed, inverse, row_of(lnf_gain), sizes, 3,
        (head_sum.sum,),
    )
    grad_full, grad_ctx, grad_up, up_sums = branch_grad_rows(
        grad_own, out_flat, down_weight, slope, sizes, 4
    )
    grad_rows = grad_full.reshape(BLOCK, D)
    act_rows = act.reshape(BLOCK, local_hidden)
    second_rows = second_full.reshape(BLOCK, D)
    up_rows = grad_up.reshape(BLOCK, local_hidden)
    sums = [
        PairSum(lambda which: dot_tn(ctx, half_of(grad_rows, which))),
        PairSum(lambda which: dot_tn(act_rows, half_of(grad_rows, which))),
        PairSum(lambda which: dot_tn(half_of(second_rows, which), up_rows)),
    ]
    for one in sums:
        one.cross()
    made = [one.sum for one in sums]
    grad_qkv, qkv_sums = attention_backward(
        flat_qkv, start_col, first_tile, local_heads, ctx, lse, grad_ctx.reshape(BLOCK, inner), planes,
        made,
    )
    first_rows = first_full.reshape(BLOCK, D)
    sums.append(PairSum(lambda which: dot_tn(half_of(first_rows, which), grad_qkv)))
    sums[-1].cross()
    qkv_sums = qkv_sums[:, 0]
    qv_grad = jnp.concatenate([qkv_sums[:, :HEAD_DIM], qkv_sums[:, 2 * HEAD_DIM :]], axis=-1)
    split = local_heads * 2 * HEAD_DIM
    biases = jnp.concatenate([qv_grad.reshape(-1), up_sums[0]])
    biases = jnp.pad(biases[None, :], ((0, 7), (0, D - biases.shape[0])))
    gains = jnp.concatenate([row_of(ln1_gain), row_of(ln2_gain)], axis=0)
    grad_input, small, biases = input_grad_rows(
        own, grad_stream, plain, grad_qkv.reshape(shards, rows, width), grad_up, qkv_flat, up_weight, gains,
        end_sums, biases, sizes, lax.axis_size("dp"), 5, (sums[-1].sum, head_sum.join().total),
    )
    for one, other in zip(sums, after([one.other for one in sums], small)):
        one.other = other
        one.join()
    out_grad, down_grad, up_grad, qkv_grad = [one.settle() for one in sums]
    head_grad = head_sum.settle()
    return (
        losses[:, 0][None],
        output[None],
        grad_input[None],
        small[0],
        small[1],
        small[2],
        small[3],
        jnp.concatenate(qkv_grad, axis=0).reshape(qkv_weight.shape),
        biases[0, :split].reshape(local_heads, 2 * HEAD_DIM),
        jnp.concatenate(out_grad, axis=1).reshape(out_weight.shape),
        jnp.concatenate(up_grad, axis=0),
        biases[0, split : split + local_hidden],
        jnp.concatenate(down_grad, axis=1),
        small[6],
        small[4],
        small[5],
        jnp.concatenate(head_grad, axis=0),
    )


def solution(mesh):
    return jax.shard_map(
        per_device,
        mesh=mesh,
        in_specs=(
            P("dp", "seq", None),
            P("dp", None),
            P("dp", None),
            P("dp", None),
            P("dp", None),
            P(),
            P(),
            P(),
            P(),
            P(None, "seq", None),
            P("seq", None),
            P("seq", None, None),
            P(None, "seq"),
            P("seq"),
            P("seq", None),
            P(),
            P(),
            P(),
            P(None, "seq"),
        ),
        out_specs=(
            P("dp", None),
            P("dp", "seq", None),
            P("dp", "seq", None),
            P(),
            P(),
            P(),
            P(),
            P(None, "seq", None),
            P("seq", None),
            P("seq", None, None),
            P(None, "seq"),
            P("seq"),
            P("seq", None),
            P(),
            P(),
            P(),
            P(None, "seq"),
        ),
        check_vma=False,
    )
```

```python
import jax
import jax.numpy as jnp
from jax import lax
from jax.experimental import pallas as pl
from jax.experimental.pallas import tpu as pltpu
from jax.sharding import PartitionSpec as P

D = 2048
HEAD_DIM = 128
ROT = 32
BLOCK = 2048
EXB = 8
EPSILON = 1e-05
BETA = 0.25
LOSS_SCALE = 65536.0
HALVES = 2
VMEM_LIMIT = 62 * 2**20

MESH = pl.DeviceIdType.MESH


class Grid2:
    def __init__(self, sizes):
        self.n = sizes
        place = lax.axis_index("seq")
        self.me = (place // sizes[1], lax.rem(place, sizes[1]))

    def index(self, slow, fast):
        return slow * self.n[1] + fast

    def device(self, axis, spot):
        here = list(self.me)
        here[axis] = spot
        return {"seq": self.index(*here)}

    def nearest(self, axis, rank):
        n, m = self.n[axis], self.me[axis]
        if rank == 0:
            return m
        if n == 2:
            return 1 - m
        after = n - 1 - m
        both = jnp.minimum(m, after)
        dist = (rank + 1) // 2
        near = m - dist if rank % 2 else m + dist
        far = jnp.where(m < after, m + (rank - both), m - (rank - both))
        return jnp.where(rank <= 2 * both, near, far)

    def neighbours(self):
        found = []
        for axis in (0, 1):
            m, n = self.me[axis], self.n[axis]
            if n == 2:
                found.append((None, self.device(axis, 1 - m)))
            elif n > 2:
                found.append((m > 0, self.device(axis, m - 1)))
                found.append((m < n - 1, self.device(axis, m + 1)))
        return found

    def barrier(self):
        sem = pltpu.get_barrier_semaphore()
        amount = jnp.int32(0)
        for there, device in self.neighbours():
            def tell(device=device):
                pl.semaphore_signal(sem, inc=1, device_id=device, device_id_type=MESH)
            if there is None:
                tell()
                amount = amount + 1
            else:
                pl.when(there)(tell)
                amount = amount + there.astype(jnp.int32)
        pl.semaphore_wait(sem, amount)


class Sender:
    def __init__(self, send_sems):
        self.sems = send_sems
        self.used = 0
        self.open = []

    def send(self, src, dst, recv_sem, device, when=None):
        copy = pltpu.make_async_remote_copy(
            src_ref=src, dst_ref=dst, send_sem=self.sems.at[self.used], recv_sem=recv_sem,
            device_id=device, device_id_type=MESH)
        self.used += 1
        if when is None:
            copy.start()
        else:
            pl.when(when)(copy.start)
        self.open.append((when, copy))

    def finish(self):
        for when, copy in self.open:
            if when is None:
                copy.wait_send()
            else:
                pl.when(when)(copy.wait_send)
        self.open = []


def gather_sends(sizes, halves):
    return halves * 2 * (sizes[0] * sizes[1] * 5 + 8)


def gather_rounds(grid, sender, piece, recv_sems, halves, cut, ready):
    n, me = grid.n, grid.me

    def arrived(slow, fast, half, kind, when):
        ref = piece(grid.index(slow, fast), half, kind)
        sem = recv_sems.at[kind, half, grid.index(slow, fast)]
        wait = pltpu.make_async_copy(ref, ref, sem).wait
        if when is None:
            wait()
        else:
            pl.when(when)(wait)

    def push(slow, fast, half, kind, axis, spot, *conditions):
        ref = piece(grid.index(slow, fast), half, kind)
        sem = recv_sems.at[kind, half, grid.index(slow, fast)]
        when = None
        for condition in conditions:
            if condition is not None:
                when = condition if when is None else when & condition
        sender.send(ref, ref, sem, grid.device(axis, spot), when)

    def spread(slow, fast, half, kind, axis, when):
        m, size = me[axis], n[axis]
        if size == 2:
            push(slow, fast, half, kind, axis, 1 - m, when)
        elif size > 2:
            push(slow, fast, half, kind, axis, m + 1, when, m < size - 1)
            push(slow, fast, half, kind, axis, m - 1, when, m > 0)

    def onward(slow, fast, half, kind, axis, when):
        m, size = me[axis], n[axis]
        if size <= 2:
            return
        below = (slow, fast)[axis] < m
        more = (below & (m < size - 1)) | (jnp.logical_not(below) & (m > 0))
        push(slow, fast, half, kind, axis, jnp.where(below, m + 1, m - 1), when, more)

    def sides(d):
        if d == 0:
            return [(me[0], None)]
        if n[0] == 2:
            return [(1 - me[0], None)]
        return [(me[0] - d, me[0] >= d), (me[0] + d, me[0] + d < n[0])]

    def settle(d):
        for half in range(halves):
            for slow, when in sides(d):
                for l in range(n[1]):
                    fast = grid.nearest(1, l)
                    if d > 0:
                        arrived(slow, fast, half, 1, when)
                        onward(slow, fast, half, 1, 0, when)
                    else:
                        spread(slow, fast, half, 1, 0, when)

    def complete(d):
        for l in range(1, n[1]):
            fast = grid.nearest(1, l)
            for half in range(halves):
                for slow, when in sides(d):
                    arrived(slow, fast, half, 0, when)
                    onward(slow, fast, half, 0, 1, when)

    def work(k, l):
        ready(grid.nearest(0, k), grid.nearest(1, l), k * n[1] + l)

    for half in range(halves):
        for kind in (1, 0):
            if cut[kind]:
                spread(me[0], me[1], half, kind, kind, None)
        if cut[0]:
            spread(me[0], me[1], half, 0, 1, None)
    work(0, 0)
    if cut[1]:
        for half in range(halves):
            for l in range(1, n[1]):
                fast = grid.nearest(1, l)
                arrived(me[0], fast, half, 1, None)
                onward(me[0], fast, half, 1, 1, None)
        settle(0)
    for d in range(1, n[0]):
        if cut[0]:
            for half in range(halves):
                for slow, when in sides(d):
                    arrived(slow, me[1], half, 0, when)
                    onward(slow, me[1], half, 0, 0, when)
                    spread(slow, me[1], half, 0, 1, when)
            complete(d - 1)
        for l in range(1, n[1]):
            work(d - 1, l)
        if cut[1]:
            settle(d)
        work(d, 0)
    if cut[0]:
        complete(n[0] - 1)
    for l in range(1, n[1]):
        work(n[0] - 1, l)


def scatter_slots(n):
    return 1 if n == 2 else n + 1


def scatter_plan(n):
    if n == (4, 2):
        return [
            ("make", 3, 1), ("make", 2, 1), ("make", 3, 0), ("make", 1, 1), ("first", 3), ("make", 2, 0),
            ("make", 0, 1), ("later", 3, 0), ("make", 1, 0), ("later", 3, 1), ("first", 2), ("make", 0, 0), ("made",),
            ("later", 2, 0), ("later", 2, 1), ("first", 1), ("later", 1, 0), ("later", 1, 1),
        ]
    far = n[0] - 1
    plan = [("make", k, l) for k in range(far, -1, -1) for l in range(n[1] - 1, -1, -1)] + [("made",)]
    for k in range(far, 0, -1):
        plan += [("first", k), ("later", k, 0), ("later", k, 1)]
    return plan


class Scatter:
    def __init__(self, grid, sender, part, bufs, sems, halves, cut):
        self.grid, self.sender, self.part = grid, sender, part
        self.bufs, self.sems, self.halves, self.cut = bufs, sems, halves, cut

    def slot(self, axis, target, from_below):
        if self.grid.n[axis] == 2:
            return 0
        return target + jnp.where(from_below, 1, 0)

    def take(self, kind, stage, axis, other, target, from_below, half, when, slot_index):
        buf, sem = self.bufs[kind][stage], self.sems[kind][stage]
        slot = self.slot(axis, target, from_below)

        def add():
            ref = buf.at[other, slot, half]
            pltpu.make_async_copy(ref, ref, sem.at[other, slot, half]).wait()
            mine = self.part(slot_index, half, kind)
            mine[...] = (mine[...].astype(jnp.float32) + ref[...].astype(jnp.float32)).astype(mine.dtype)

        if when is None:
            add()
        else:
            pl.when(when)(add)

    def incoming(self, axis, target):
        m, n = self.grid.me[axis], self.grid.n[axis]
        if n == 2:
            return None
        up = target > m
        return (up & (m > 0)) | (jnp.logical_not(up) & (m < n - 1))

    def toward(self, kind, stage, axis, other, target, half, slow, fast, when=None):
        grid = self.grid
        m, n = grid.me[axis], grid.n[axis]
        up = target > m
        index = grid.index(slow, fast)
        if n > 2:
            incoming = self.incoming(axis, target)
            self.take(kind, stage, axis, other, target, up, half, incoming if when is None else incoming & when, index)
        buf, sem = self.bufs[kind][stage], self.sems[kind][stage]
        slot = self.slot(axis, target, up)
        spot = 1 - m if n == 2 else jnp.where(up, m + 1, m - 1)
        self.sender.send(
            self.part(index, half, kind), buf.at[other, slot, half], sem.at[other, slot, half],
            grid.device(axis, spot), when)

    def last(self, kind, stage, axis, other, half, slow, fast):
        grid = self.grid
        m, n = grid.me[axis], grid.n[axis]
        index = grid.index(slow, fast)
        if n == 2:
            self.take(kind, stage, axis, other, m, m > 0, half, None, index)
        elif n > 2:
            self.take(kind, stage, axis, other, m, jnp.bool_(True), half, m > 0, index)
            self.take(kind, stage, axis, other, m, jnp.bool_(False), half, m < n - 1, index)

    def run(self, produce, made=lambda: None, between=lambda: None, late=lambda: None):
        grid, n, me = self.grid, self.grid.n, self.grid.me
        lagging = []

        def chain(k, half, begins):
            slow = grid.nearest(0, k)
            incoming = self.incoming(0, slow)
            if incoming is None:
                if begins:
                    self.last(0, 0, 1, slow, half, slow, me[1])
                    self.toward(0, 1, 0, 0, slow, half, slow, me[1])
                return
            when = jnp.logical_not(incoming) if begins else incoming
            pl.when(when)(lambda: self.last(0, 0, 1, slow, half, slow, me[1]))
            self.toward(0, 1, 0, 0, slow, half, slow, me[1], when)

        def catch_up():
            for step in lagging:
                self.toward(*step)
            lagging.clear()

        def make(k, l):
            slow, fast = grid.nearest(0, k), grid.nearest(1, l)
            produce(slow, fast)
            if self.cut[0] and l > 0:
                for half in range(self.halves):
                    self.toward(0, 0, 1, slow, fast, half, slow, fast)
            catch_up()
            if self.cut[1] and k > 0:
                for half in range(self.halves):
                    lagging.append((1, 0, 0, fast, slow, half, slow, fast))

        for step in scatter_plan(n):
            if step[0] == "make":
                make(*step[1:])
            elif step[0] == "made":
                catch_up()
                made()
            elif step[0] == "first" and self.cut[0]:
                for half in range(self.halves):
                    chain(step[1], half, True)
            elif self.cut[0]:
                chain(step[1], step[2], False)
        between()
        if self.cut[1]:
            for half in range(self.halves):
                for l in reversed(range(n[1])):
                    fast = grid.nearest(1, l)
                    self.last(1, 0, 0, fast, half, me[0], fast)
                    if l > 0:
                        self.toward(1, 1, 1, 0, fast, half, me[0], fast)
        late()
        if self.cut[0]:
            for half in range(self.halves):
                self.last(0, 0, 1, me[0], half, me[0], me[1])
        for half in range(self.halves):
            if self.cut[1]:
                self.last(1, 1, 1, 0, half, me[0], me[1])
            if self.cut[0]:
                self.last(0, 1, 0, 0, half, me[0], me[1])


def scatter_scratch(sizes, halves, rows, cols, cut):
    bufs, sems = [], []
    for kind, stages in ((0, (1, 0)), (1, (0, 1))):
        for stage, axis in enumerate(stages):
            lead = (sizes[1 - axis] if stage == 0 else 1, scatter_slots(sizes[axis]), halves)
            width = max(cut[kind], 128)
            bufs.append(pltpu.VMEM(lead + (rows // halves, width), jnp.bfloat16))
            sems.append(pltpu.SemaphoreType.DMA(lead))
    return bufs, sems


def scatter_sends(sizes, halves):
    return halves * 2 * (sizes[0] * sizes[1] + sizes[0] + sizes[1])


def lines_of(seq):
    fast = 2 if seq <= 8 else 4
    return (seq // fast, fast)


ATT_TILE = 256
SCALE = HEAD_DIM ** (-0.5)


def dot_nt(left, right):
    return lax.dot_general(left, right, (((1,), (1,)), ((), ())), preferred_element_type=jnp.float32)


def dot_tn(left, right):
    return lax.dot_general(left, right, (((0,), (0,)), ((), ())), preferred_element_type=jnp.float32)


def rotary_frequencies():
    half_rot = ROT // 2
    frequency = 10000.0 ** (-2.0 * jnp.arange(half_rot, dtype=jnp.float32) / ROT)
    return jnp.tile(frequency, HEAD_DIM // half_rot)[None, :]


def first_rows(lengths, row):
    start, end = jnp.zeros_like(row), jnp.int32(0)
    for example in range(EXB):
        end = end + lengths[example]
        start = jnp.where(row >= end, end, start)
    return start


def rotary_planes(position, frequencies):
    half_rot = ROT // 2
    angles = position.astype(jnp.float32) * frequencies
    cos, sin = jnp.cos(angles), jnp.sin(angles)
    lane = lax.broadcasted_iota(jnp.int32, angles.shape, 1)
    return (
        jnp.where(lane < ROT, cos, 1.0),
        jnp.where((lane >= half_rot) & (lane < ROT), sin, 0.0),
        jnp.where(lane < half_rot, -sin, 0.0),
    )


def turn(vector, cos, from_below, from_above):
    half_rot = ROT // 2
    return (
        vector * cos
        + pltpu.roll(vector, half_rot, 1) * from_below
        + pltpu.roll(vector, HEAD_DIM - half_rot, 1) * from_above
    )


def tile_mask(start_col, query_tile, key_tile):
    shape = (ATT_TILE, ATT_TILE)
    query_ids = query_tile * ATT_TILE + lax.broadcasted_iota(jnp.int32, shape, 0)
    key_ids = key_tile * ATT_TILE + lax.broadcasted_iota(jnp.int32, shape, 1)
    return (key_ids >= start_col) & (key_ids <= query_ids)


def tile_starts(lengths, tile):
    rows = tile * ATT_TILE + lax.broadcasted_iota(jnp.int32, (ATT_TILE, 1), 0)
    return first_rows(lengths, rows), first_rows(lengths, tile * ATT_TILE) // ATT_TILE


def attention_forward(qkv, lengths, heads):
    tiles = BLOCK // ATT_TILE

    def kernel(lengths_ref, q_ref, k_ref, v_ref, ctx_ref, lse_ref):
        tile = pl.program_id(1)
        queries = q_ref[...]
        start, first = tile_starts(lengths_ref, tile)

        def step(key_tile, carry):
            top, total, acc = carry
            rows = pl.ds(pl.multiple_of(key_tile * ATT_TILE, ATT_TILE), ATT_TILE)
            scores = dot_nt(queries, k_ref[rows, :]) * SCALE
            scores = jnp.where(tile_mask(start, tile, key_tile), scores, -1e30)
            new_top = jnp.maximum(top, jnp.max(scores, axis=1, keepdims=True))
            shrink = jnp.exp(top - new_top)
            weights = jnp.exp(scores - new_top)
            total = total * shrink + jnp.sum(weights, axis=1, keepdims=True)
            acc = acc * shrink + jnp.dot(
                weights.astype(jnp.bfloat16), v_ref[rows, :], preferred_element_type=jnp.float32
            )
            return (new_top, total, acc)

        begin = (
            jnp.full((ATT_TILE, 1), -1e30, jnp.float32),
            jnp.zeros((ATT_TILE, 1), jnp.float32),
            jnp.zeros((ATT_TILE, HEAD_DIM), jnp.float32),
        )
        begin = step(tile, begin)
        top, total, acc = lax.fori_loop(first, tile, step, begin)
        ctx_ref[...] = (acc / total).astype(jnp.bfloat16)
        lse_ref[...] = top + jnp.log(total)

    return pl.pallas_call(
        kernel,
        grid_spec=pltpu.PrefetchScalarGridSpec(
            num_scalar_prefetch=1,
            grid=(heads, tiles),
            in_specs=[
                pl.BlockSpec((ATT_TILE, HEAD_DIM), lambda h, i, first: (i, 3 * h)),
                pl.BlockSpec((BLOCK, HEAD_DIM), lambda h, i, first: (0, 3 * h + 1)),
                pl.BlockSpec((BLOCK, HEAD_DIM), lambda h, i, first: (0, 3 * h + 2)),
            ],
            out_specs=[
                pl.BlockSpec((ATT_TILE, HEAD_DIM), lambda h, i, first: (i, h)),
                pl.BlockSpec((pl.squeezed, ATT_TILE, 1), lambda h, i, first: (h, i, 0)),
            ],
        ),
        out_shape=[
            jax.ShapeDtypeStruct((BLOCK, heads * HEAD_DIM), jnp.bfloat16),
            jax.ShapeDtypeStruct((heads, BLOCK, 1), jnp.float32),
        ],
        compiler_params=pltpu.CompilerParams(vmem_limit_bytes=VMEM_LIMIT),
    )(lengths, qkv, qkv, qkv)


def attention_backward(qkv, lengths, heads, ctx, lse, grad_ctx, planes, before):
    tiles = BLOCK // ATT_TILE

    def kernel(
        lengths_ref, q_ref, k_ref, v_ref, ctx_ref, lse_ref, do_ref, cos_ref, below_ref,
        above_ref, *rest,
    ):
        out_ref, sums_ref, dk_ref, dv_ref = rest[len(before) :]
        tile = pl.program_id(1)

        @pl.when(tile == 0)
        def _():
            dk_ref[...] = jnp.zeros_like(dk_ref)
            dv_ref[...] = jnp.zeros_like(dv_ref)

        queries = q_ref[...]
        start, first = tile_starts(lengths_ref, tile)
        grads = do_ref[...]
        lse_rows = lse_ref[...]
        inner = jnp.sum(
            grads.astype(jnp.float32) * ctx_ref[...].astype(jnp.float32), axis=1, keepdims=True
        )

        def step(key_tile, dq):
            rows = pl.ds(pl.multiple_of(key_tile * ATT_TILE, ATT_TILE), ATT_TILE)
            keys = k_ref[rows, :]
            scores = dot_nt(queries, keys) * SCALE
            probs = jnp.where(
                tile_mask(start, tile, key_tile), jnp.exp(scores - lse_rows), 0.0
            )
            grad_probs = dot_nt(grads, v_ref[rows, :])
            grad_scores = (probs * (grad_probs - inner)).astype(jnp.bfloat16)
            dv_ref[rows, :] += dot_tn(probs.astype(jnp.bfloat16), grads)
            dk_ref[rows, :] += dot_tn(grad_scores, queries)
            return dq + jnp.dot(grad_scores, keys, preferred_element_type=jnp.float32)

        dq = lax.fori_loop(
            first, tile + 1, step, jnp.zeros((ATT_TILE, HEAD_DIM), jnp.float32)
        )
        here = pl.ds(pl.multiple_of(tile * ATT_TILE, ATT_TILE), ATT_TILE)
        out_ref[here, :HEAD_DIM] = turn(
            dq * SCALE, cos_ref[here, :], -below_ref[here, :], -above_ref[here, :]
        ).astype(jnp.bfloat16)

        @pl.when(tile == tiles - 1)
        def _():
            def finish(index, sums):
                rows = pl.ds(pl.multiple_of(index * ATT_TILE, ATT_TILE), ATT_TILE)
                out_ref[rows, HEAD_DIM : 2 * HEAD_DIM] = turn(
                    dk_ref[rows, :] * SCALE, cos_ref[rows, :], -below_ref[rows, :], -above_ref[rows, :]
                ).astype(jnp.bfloat16)
                out_ref[rows, 2 * HEAD_DIM :] = dv_ref[rows, :].astype(jnp.bfloat16)
                return sums + jnp.sum(out_ref[rows, :].astype(jnp.float32), axis=0, keepdims=True)

            sums_ref[...] = lax.fori_loop(
                0, tiles, finish, jnp.zeros((1, 3 * HEAD_DIM), jnp.float32)
            )

    whole = pl.BlockSpec((BLOCK, HEAD_DIM), lambda h, i, first: (0, 0))
    return pl.pallas_call(
        kernel,
        grid_spec=pltpu.PrefetchScalarGridSpec(
            num_scalar_prefetch=1,
            grid=(heads, tiles),
            in_specs=[
                pl.BlockSpec((ATT_TILE, HEAD_DIM), lambda h, i, first: (i, 3 * h)),
                pl.BlockSpec((BLOCK, HEAD_DIM), lambda h, i, first: (0, 3 * h + 1)),
                pl.BlockSpec((BLOCK, HEAD_DIM), lambda h, i, first: (0, 3 * h + 2)),
                pl.BlockSpec((ATT_TILE, HEAD_DIM), lambda h, i, first: (i, h)),
                pl.BlockSpec((pl.squeezed, ATT_TILE, 1), lambda h, i, first: (h, i, 0)),
                pl.BlockSpec((ATT_TILE, HEAD_DIM), lambda h, i, first: (i, h)),
                whole,
                whole,
                whole,
            ]
            + [pl.BlockSpec(memory_space=pl.ANY)] * len(before),
            out_specs=[
                pl.BlockSpec((BLOCK, 3 * HEAD_DIM), lambda h, i, first: (0, h)),
                pl.BlockSpec((pl.squeezed, 1, 3 * HEAD_DIM), lambda h, i, first: (h, 0, 0)),
            ],
            scratch_shapes=[
                pltpu.VMEM((BLOCK, HEAD_DIM), jnp.float32),
                pltpu.VMEM((BLOCK, HEAD_DIM), jnp.float32),
            ],
        ),
        out_shape=[
            jax.ShapeDtypeStruct((BLOCK, heads * 3 * HEAD_DIM), jnp.bfloat16),
            jax.ShapeDtypeStruct((heads, 1, 3 * HEAD_DIM), jnp.float32),
        ],
        compiler_params=pltpu.CompilerParams(vmem_limit_bytes=VMEM_LIMIT),
    )(lengths, qkv, qkv, qkv, ctx, lse, grad_ctx, *planes, *before)


def gather_cut(sizes):
    return (1792, 256) if sizes == (4, 2) else (D // 2, D // 2)


def scatter_cut(sizes):
    return (1664, 384) if sizes == (4, 2) else (D // 2, D // 2)


def columns_of(cut, kind):
    return pl.ds(0, cut[0]) if kind == 0 else pl.ds(cut[0], cut[1])


def tile_of(width):
    return 512 if width % 512 == 0 else 256 if width % 256 == 0 else 128


def span(index, size):
    return pl.ds(pl.multiple_of(index * size, size), size)


ANY = pl.BlockSpec(memory_space=pl.ANY)
VMEM = pl.BlockSpec(memory_space=pltpu.VMEM)
SMEM = pl.BlockSpec(memory_space=pltpu.SMEM)


def row_kernel(kernel, collective, out_shape, in_specs, out_specs, scratch, cost, before=()):
    def body(*refs):
        kernel(*refs[len(before):])

    def call(*args):
        return pl.pallas_call(
            body,
            out_shape=out_shape,
            in_specs=[ANY] * len(before) + in_specs,
            out_specs=out_specs,
            scratch_shapes=scratch,
            cost_estimate=pl.CostEstimate(flops=cost, bytes_accessed=2**28, transcendentals=0),
            compiler_params=pltpu.CompilerParams(
                collective_id=collective, has_side_effects=True, vmem_limit_bytes=VMEM_LIMIT
            ),
        )(*before, *args)

    return call


def gather_scratch(sizes, rows):
    shards = sizes[0] * sizes[1]
    return [
        pltpu.VMEM((shards, rows, D), jnp.bfloat16),
        pltpu.SemaphoreType.DMA((gather_sends(sizes, HALVES),)),
        pltpu.SemaphoreType.DMA((2, HALVES, shards)),
    ]


def run_gather(grid, sizes, rows, full, send_sems, recv_sems, ready):
    cut = gather_cut(sizes)
    step = rows // HALVES
    sender = Sender(send_sems)

    def piece(slot, half, kind):
        return full.at[slot, pl.ds(half * step, step), columns_of(cut, kind)]

    gather_rounds(grid, sender, piece, recv_sems, HALVES, cut, ready)
    sender.finish()


def sum_scratch(sizes, rows):
    shards = sizes[0] * sizes[1]
    bufs, sems = scatter_scratch(sizes, HALVES, rows, D, scatter_cut(sizes))
    return (
        [pltpu.VMEM((shards, rows, D), jnp.bfloat16)]
        + bufs
        + sems
        + [pltpu.SemaphoreType.DMA((scatter_sends(sizes, HALVES),))]
    )


def run_scatter(grid, sizes, rows, scratch, produce, *hooks):
    cut = scatter_cut(sizes)
    step = rows // HALVES
    parts, b0, b1, b2, b3, s0, s1, s2, s3, send_sems = scratch
    sender = Sender(send_sems)

    def part(slot, half, kind):
        return parts.at[slot, pl.ds(half * step, step), columns_of(cut, kind)]

    scatter = Scatter(
        grid, sender, part, ((b0, b1), (b2, b3)), ((s0, s1), (s2, s3)), HALVES, cut
    )
    scatter.run(produce, *hooks)
    sender.finish()


def production_order(grid):
    return [
        grid.index(grid.nearest(0, k), grid.nearest(1, l))
        for action, k, l in [step for step in scatter_plan(grid.n) if step[0] == "make"]
    ]


ROW_TILE = 64


def tile_stats(values):
    centered = values - jnp.mean(values, axis=1, keepdims=True)
    inverse = lax.rsqrt(jnp.mean(centered * centered, axis=1, keepdims=True) + EPSILON)
    return centered, inverse


def open_rows(own, sizes, collective, norms, qkv_flat, qkv_bias, up_weight, up_bias, lengths):
    rows = own.shape[0]
    shards = sizes[0] * sizes[1]
    width, hidden = qkv_flat.shape[1], up_weight.shape[1]
    heads = width // (3 * HEAD_DIM)

    def kernel(
        own_ref, norms_ref, qkvw_any, qkvb_ref, upw_any, upb_ref, lengths_ref, freq_ref,
        plain_any, one_any, two_any, qkv_any, act_any, slope_any, cos_ref, below_ref, above_ref,
        full, send_sems, recv_sems, qkvw, upw, load_sems, plain, one, two, qkv, act, slope, out_sems,
    ):
        grid = Grid2(sizes)
        loads = [
            pltpu.make_async_copy(qkvw_any, qkvw, load_sems.at[0]),
            pltpu.make_async_copy(upw_any, upw, load_sems.at[1]),
        ]
        for copy in loads:
            copy.start()
        full[grid.index(*grid.me)] = own_ref[...]
        grid.barrier()
        open_copies = []

        def outs(place, slot):
            pairs = ((plain, plain_any), (one, one_any), (two, two_any), (qkv, qkv_any), (act, act_any), (slope, slope_any))
            return [
                pltpu.make_async_copy(here.at[slot], there.at[place], out_sems.at[slot, i])
                for i, (here, there) in enumerate(pairs)
            ]

        def ready(slow, fast, order):
            place = grid.index(slow, fast)
            slot = order % 2
            if order == 0:
                for copy in loads:
                    copy.wait()
            if order >= 2:
                for copy in open_copies.pop(0):
                    copy.wait()

            def norm_tile(index, _):
                here = span(index, ROW_TILE)
                centered, inverse = tile_stats(full[place, here].astype(jnp.float32))
                normed = centered * inverse
                plain[slot, here] = normed.astype(jnp.bfloat16)
                one[slot, here] = (normed * norms_ref[0:1] + norms_ref[1:2]).astype(jnp.bfloat16)
                two[slot, here] = (normed * norms_ref[2:3] + norms_ref[3:4]).astype(jnp.bfloat16)
                return _

            lax.fori_loop(0, rows // ROW_TILE, norm_tile, 0)
            places = pl.ds(pl.multiple_of(place * rows, rows), rows)
            row = place * rows + lax.broadcasted_iota(jnp.int32, (rows, 1), 0)
            cos, below, above = rotary_planes(row - first_rows(lengths_ref, row), freq_ref[...])
            cos_ref[places, :], below_ref[places, :], above_ref[places, :] = cos, below, above
            whole = jnp.dot(one[slot], qkvw[...], preferred_element_type=jnp.float32) + qkvb_ref[...]
            for head in range(heads):
                first = head * 3 * HEAD_DIM
                found = whole[:, first : first + 3 * HEAD_DIM]
                qkv[slot, :, first : first + HEAD_DIM] = turn(
                    found[:, :HEAD_DIM], cos, below, above
                ).astype(jnp.bfloat16)
                qkv[slot, :, first + HEAD_DIM : first + 2 * HEAD_DIM] = turn(
                    found[:, HEAD_DIM : 2 * HEAD_DIM], cos, below, above
                ).astype(jnp.bfloat16)
                qkv[slot, :, first + 2 * HEAD_DIM : first + 3 * HEAD_DIM] = found[
                    :, 2 * HEAD_DIM :
                ].astype(jnp.bfloat16)
            tile = tile_of(hidden)

            def up_tile(index, _):
                here = span(index, tile)
                pre = jnp.dot(two[slot], upw[:, here], preferred_element_type=jnp.float32) + upb_ref[:, here]
                share = 0.5 * (1.0 + lax.erf(pre * 0.7071067811865476))
                act[slot, :, here] = (pre * share).astype(jnp.bfloat16)
                slope[slot, :, here] = (
                    share + pre * (jnp.exp(-0.5 * pre * pre) * 0.3989422804014327)
                ).astype(jnp.bfloat16)
                return _

            lax.fori_loop(0, hidden // tile, up_tile, 0)
            copies = outs(place, slot)
            for copy in copies:
                copy.start()
            open_copies.append(copies)

        run_gather(grid, sizes, rows, full, send_sems, recv_sems, ready)
        for copies in open_copies:
            for copy in copies:
                copy.wait()

    def out(columns):
        return jax.ShapeDtypeStruct((shards, rows, columns), jnp.bfloat16)

    def staged(columns):
        return pltpu.VMEM((2, rows, columns), jnp.bfloat16)

    return row_kernel(
        kernel, collective,
        [out(D), out(D), out(D), out(width), out(hidden), out(hidden)]
        + [jax.ShapeDtypeStruct((shards * rows, HEAD_DIM), jnp.float32)] * 3,
        [VMEM, VMEM, ANY, VMEM, ANY, VMEM, SMEM, VMEM],
        [ANY] * 6 + [VMEM] * 3,
        gather_scratch(sizes, rows)
        + [
            pltpu.VMEM(qkv_flat.shape, jnp.bfloat16),
            pltpu.VMEM(up_weight.shape, jnp.bfloat16),
            pltpu.SemaphoreType.DMA((2,)),
            staged(D), staged(D), staged(D), staged(width), staged(hidden), staged(hidden),
            pltpu.SemaphoreType.DMA((2, 6)),
        ],
        2 * BLOCK * D * (width + hidden),
    )(own, norms, qkv_flat, qkv_bias, up_weight, up_bias, lengths, rotary_frequencies())


def branch_rows(own, ctx, act, out_flat, down_weight, norms, sizes, collective):
    rows = own.shape[0]
    shards = sizes[0] * sizes[1]
    inner, hidden = out_flat.shape[0], down_weight.shape[0]

    def kernel(
        own_ref, ctx_any, act_any, outw_any, downw_any, norms_ref, out_ref, final_ref, normed_ref, inverse_ref,
        ctx, act, outw, downw, load_sems, *scratch,
    ):
        grid = Grid2(sizes)
        parts = scratch[0]
        weights = [
            pltpu.make_async_copy(outw_any, outw, load_sems.at[0, 0]),
            pltpu.make_async_copy(downw_any, downw, load_sems.at[0, 1]),
        ]
        order = production_order(grid)
        loads = [
            [
                pltpu.make_async_copy(ctx_any.at[place], ctx.at[place], load_sems.at[1 + i, 0]),
                pltpu.make_async_copy(act_any.at[place], act.at[place], load_sems.at[1 + i, 1]),
            ]
            for i, place in enumerate(order)
        ]
        for copy in loads[0] + weights:
            copy.start()
        for copies in loads[1:]:
            for copy in copies:
                copy.start()
        grid.barrier()
        for copy in weights:
            copy.wait()

        def produce(slow, fast):
            place = grid.index(slow, fast)
            for copy in loads.pop(0):
                copy.wait()

            def columns(index, _):
                here = span(index, 512)
                parts[place, :, here] = (
                    jnp.dot(ctx[place], outw[:, here], preferred_element_type=jnp.float32)
                    + jnp.dot(act[place], downw[:, here], preferred_element_type=jnp.float32)
                ).astype(jnp.bfloat16)
                return _

            lax.fori_loop(0, D // 512, columns, 0)

        run_scatter(grid, sizes, rows, scratch, produce)
        mine = grid.index(*grid.me)

        def norm_tile(index, _):
            here = span(index, ROW_TILE)
            stream = own_ref[here].astype(jnp.float32) + parts[mine, here].astype(jnp.float32) + norms_ref[2:3]
            out_ref[here] = stream.astype(jnp.bfloat16)
            centered, inverse = tile_stats(stream)
            normed = centered * inverse
            final_ref[here] = (normed * norms_ref[0:1] + norms_ref[1:2]).astype(jnp.bfloat16)
            normed_ref[here] = normed
            inverse_ref[here] = inverse
            return _

        lax.fori_loop(0, rows // ROW_TILE, norm_tile, 0)

    return row_kernel(
        kernel, collective,
        [
            jax.ShapeDtypeStruct((rows, D), jnp.bfloat16),
            jax.ShapeDtypeStruct((rows, D), jnp.bfloat16),
            jax.ShapeDtypeStruct((rows, D), jnp.float32),
            jax.ShapeDtypeStruct((rows, 1), jnp.float32),
        ],
        [VMEM, ANY, ANY, ANY, ANY, VMEM],
        [VMEM] * 4,
        [
            pltpu.VMEM(ctx.shape, jnp.bfloat16),
            pltpu.VMEM(act.shape, jnp.bfloat16),
            pltpu.VMEM(out_flat.shape, jnp.bfloat16),
            pltpu.VMEM(down_weight.shape, jnp.bfloat16),
            pltpu.SemaphoreType.DMA((1 + shards, 2)),
        ]
        + sum_scratch(sizes, rows),
        2 * BLOCK * D * (inner + hidden),
    )(own, ctx, act, out_flat, down_weight, norms)


def logit_rows(final, head_weight, targets_col, sizes, collective):
    rows = final.shape[0]
    shards = sizes[0] * sizes[1]
    vocab = head_weight.shape[1]

    def kernel(
        own_ref, headw_any, target_ref, final_any, weights_any, stats_ref,
        full, send_sems, recv_sems, headw, load_sem, logits, weights, out_sems, row_sems,
    ):
        grid = Grid2(sizes)
        load = pltpu.make_async_copy(headw_any, headw, load_sem)
        load.start()
        full[grid.index(*grid.me)] = own_ref[...]
        grid.barrier()
        base = lax.axis_index("seq") * vocab
        open_copies, raw_copies = [], []

        def ready(slow, fast, order):
            place = grid.index(slow, fast)
            slot = order % 2
            if order == 0:
                load.wait()
            if order >= 2:
                open_copies.pop(0).wait()
            places = pl.ds(pl.multiple_of(place * rows, rows), rows)
            target = target_ref[places, :] - base

            def fold(values, join):
                total = values[:, :128]
                for first in range(128, values.shape[1], 128):
                    total = join(total, values[:, first : first + 128])
                return total

            def logit_tile(start, size, carry):
                top, pick = carry
                here = pl.ds(start, size)
                found = jnp.dot(full[place], headw[:, here], preferred_element_type=jnp.float32)
                logits[:, here] = found
                ids = start + lax.broadcasted_iota(jnp.int32, (rows, size), 1)
                top = jnp.maximum(top, fold(found, jnp.maximum))
                pick = pick + fold(jnp.where(ids == target, found, 0.0), jnp.add)
                return (top, pick)

            def tiled(step, carry):
                count = vocab // 512
                carry = lax.fori_loop(
                    0, count, lambda i, c: step(pl.multiple_of(i * 512, 512), 512, c), carry
                )
                if vocab % 512:
                    carry = step(count * 512, vocab % 512, carry)
                return carry

            top, pick = tiled(
                logit_tile,
                (jnp.full((rows, 128), -jnp.inf, jnp.float32), jnp.zeros((rows, 128), jnp.float32)),
            )
            top = jnp.max(top, axis=1, keepdims=True)
            pick = jnp.sum(pick, axis=1, keepdims=True)

            def weight_tile(start, size, total):
                here = pl.ds(start, size)
                found = jnp.exp(logits[:, here] - top)
                weights[slot, :, here] = found.astype(jnp.bfloat16)
                return total + fold(found, jnp.add)

            total = tiled(weight_tile, jnp.zeros((rows, 128), jnp.float32))
            total = jnp.sum(total, axis=1, keepdims=True)
            lane = lax.broadcasted_iota(jnp.int32, (rows, 128), 1)
            found = jnp.where(lane == 0, top, jnp.where(lane == 1, total, pick))
            stats_ref[:, places] = found.T[0:8]
            copy = pltpu.make_async_copy(weights.at[slot], weights_any.at[place], out_sems.at[slot])
            copy.start()
            open_copies.append(copy)
            raw = pltpu.make_async_copy(full.at[place], final_any.at[place], row_sems.at[order])
            raw.start()
            raw_copies.append(raw)

        run_gather(grid, sizes, rows, full, send_sems, recv_sems, ready)
        for copy in open_copies + raw_copies:
            copy.wait()

    return row_kernel(
        kernel, collective,
        [
            jax.ShapeDtypeStruct((shards, rows, D), jnp.bfloat16),
            jax.ShapeDtypeStruct((shards, rows, vocab), jnp.bfloat16),
            jax.ShapeDtypeStruct((8, shards * rows), jnp.float32),
        ],
        [VMEM, ANY, VMEM],
        [ANY, ANY, VMEM],
        gather_scratch(sizes, rows)
        + [
            pltpu.VMEM(head_weight.shape, jnp.bfloat16),
            pltpu.SemaphoreType.DMA,
            pltpu.VMEM((rows, vocab), jnp.float32),
            pltpu.VMEM((2, rows, vocab), jnp.bfloat16),
            pltpu.SemaphoreType.DMA((2,)),
            pltpu.SemaphoreType.DMA((shards,)),
        ],
        2 * BLOCK * D * vocab,
    )(final, head_weight, targets_col)


def final_grad_rows(grad_logits, head_weight, normed, inverse, gain, sizes, collective, before):
    shards, rows, vocab = grad_logits.shape

    def kernel(
        grads_any, headw_any, normed_ref, inverse_ref, gain_ref, stream_ref, down_ref, sums_ref,
        headw, grads, load_sems, *scratch,
    ):
        grid = Grid2(sizes)
        parts = scratch[0]
        order = production_order(grid)
        loads = [
            pltpu.make_async_copy(grads_any.at[place], grads.at[i % 2], load_sems.at[i])
            for i, place in enumerate(order)
        ]
        tile = 512
        weights = [
            pltpu.make_async_copy(
                headw_any.at[pl.ds(i * tile, tile)], headw.at[pl.ds(i * tile, tile)], load_sems.at[1 + shards + i]
            )
            for i in range(D // tile)
        ]
        loads[0].start()
        for copy in weights:
            copy.start()
        grid.barrier()
        count = [0]

        def produce(slow, fast):
            place = grid.index(slow, fast)
            i = count[0]
            count[0] += 1
            if i + 1 < shards:
                loads[i + 1].start()
            loads[i].wait()

            def columns(index, _):
                here = span(index, tile)
                parts[place, :, here] = dot_nt(grads[i % 2], headw[here, :]).astype(jnp.bfloat16)
                return _

            if i == 0:
                for index, copy in enumerate(weights):
                    copy.wait()
                    columns(index, 0)
            else:
                lax.fori_loop(0, D // tile, columns, 0)

        run_scatter(grid, sizes, rows, scratch, produce)
        mine = grid.index(*grid.me)
        sums_ref[...] = jnp.zeros_like(sums_ref)

        def norm_tile(index, _):
            here = span(index, ROW_TILE)
            grad = parts[mine, here].astype(jnp.float32)
            norm = normed_ref[here]
            scaled = grad * gain_ref[...]
            stream = inverse_ref[here] * (
                scaled
                - jnp.mean(scaled, axis=1, keepdims=True)
                - norm * jnp.mean(scaled * norm, axis=1, keepdims=True)
            )
            stream_ref[here] = stream
            down_ref[here] = stream.astype(jnp.bfloat16)
            sums_ref[0:1] += jnp.sum(grad * norm, axis=0, keepdims=True)
            sums_ref[1:2] += jnp.sum(grad, axis=0, keepdims=True)
            sums_ref[2:3] += jnp.sum(stream, axis=0, keepdims=True)
            return _

        lax.fori_loop(0, rows // ROW_TILE, norm_tile, 0)

    return row_kernel(
        kernel, collective,
        [
            jax.ShapeDtypeStruct((rows, D), jnp.float32),
            jax.ShapeDtypeStruct((rows, D), jnp.bfloat16),
            jax.ShapeDtypeStruct((8, D), jnp.float32),
        ],
        [ANY, ANY, VMEM, VMEM, VMEM],
        [VMEM] * 3,
        [
            pltpu.VMEM(head_weight.shape, jnp.bfloat16),
            pltpu.VMEM((2, rows, vocab), jnp.bfloat16),
            pltpu.SemaphoreType.DMA((1 + shards + D // 512,)),
        ]
        + sum_scratch(sizes, rows),
        2 * BLOCK * D * vocab,
        before,
    )(grad_logits, head_weight, normed, inverse, gain)


def branch_grad_rows(own, out_flat, down_weight, slope, sizes, collective):
    rows = own.shape[0]
    shards = sizes[0] * sizes[1]
    inner, hidden = out_flat.shape[0], down_weight.shape[0]

    def kernel(
        own_ref, outw_any, downw_any, slope_any, rows_any, ctx_any, up_any, sums_ref,
        full, send_sems, recv_sems, outw, downw, load_sems, slope, slope_sems, ctx, up, out_sems, row_sems,
    ):
        grid = Grid2(sizes)
        loads = [
            pltpu.make_async_copy(outw_any, outw, load_sems.at[0]),
            pltpu.make_async_copy(downw_any, downw, load_sems.at[1]),
        ]
        for copy in loads:
            copy.start()
        slopes = pltpu.make_async_copy(slope_any, slope, slope_sems)
        slopes.start()
        full[grid.index(*grid.me)] = own_ref[...]
        sums_ref[...] = jnp.zeros_like(sums_ref)
        grid.barrier()
        open_copies, raw_copies = [], []

        def ready(slow, fast, order):
            place = grid.index(slow, fast)
            slot = order % 2
            if order == 0:
                for copy in loads + [slopes]:
                    copy.wait()
            if order >= 2:
                for copy in open_copies.pop(0):
                    copy.wait()
            ctx[slot] = dot_nt(full[place], outw[...]).astype(jnp.bfloat16)
            tile = tile_of(hidden)

            def up_tile(index, _):
                here = span(index, tile)
                found = dot_nt(full[place], downw[here, :]) * slope[place, :, here].astype(jnp.float32)
                rounded = found.astype(jnp.bfloat16)
                up[slot, :, here] = rounded
                sums_ref[0:1, here] += jnp.sum(rounded.astype(jnp.float32), axis=0, keepdims=True)
                return _

            lax.fori_loop(0, hidden // tile, up_tile, 0)
            copies = [
                pltpu.make_async_copy(ctx.at[slot], ctx_any.at[place], out_sems.at[slot, 0]),
                pltpu.make_async_copy(up.at[slot], up_any.at[place], out_sems.at[slot, 1]),
            ]
            for copy in copies:
                copy.start()
            open_copies.append(copies)
            raw = pltpu.make_async_copy(full.at[place], rows_any.at[place], row_sems.at[order])
            raw.start()
            raw_copies.append(raw)

        run_gather(grid, sizes, rows, full, send_sems, recv_sems, ready)
        for copies in open_copies:
            for copy in copies:
                copy.wait()
        for copy in raw_copies:
            copy.wait()

    def out(columns):
        return jax.ShapeDtypeStruct((shards, rows, columns), jnp.bfloat16)

    return row_kernel(
        kernel, collective,
        [out(D), out(inner), out(hidden), jax.ShapeDtypeStruct((8, hidden), jnp.float32)],
        [VMEM, ANY, ANY, ANY],
        [ANY, ANY, ANY, VMEM],
        gather_scratch(sizes, rows)
        + [
            pltpu.VMEM(out_flat.shape, jnp.bfloat16),
            pltpu.VMEM(down_weight.shape, jnp.bfloat16),
            pltpu.SemaphoreType.DMA((2,)),
            pltpu.VMEM((shards, rows, hidden), jnp.bfloat16),
            pltpu.SemaphoreType.DMA,
            pltpu.VMEM((2, rows, inner), jnp.bfloat16),
            pltpu.VMEM((2, rows, hidden), jnp.bfloat16),
            pltpu.SemaphoreType.DMA((2, 2)),
            pltpu.SemaphoreType.DMA((shards,)),
        ],
        2 * BLOCK * D * (inner + hidden),
    )(own, out_flat, down_weight, slope)


class SmallSum:
    def __init__(self, shards, replicas, sums, bias, total, bias_total, scratch):
        self.shards, self.replicas = shards, replicas
        self.sums, self.bias, self.total, self.bias_total = sums, bias, total, bias_total
        (
            self.came, self.block, self.blocks, self.biases, self.spread_send, self.spread_recv, self.cross_send,
            self.cross_recv, self.back_send, self.back_recv,
        ) = scratch
        self.seq, self.dp = lax.axis_index("seq"), lax.axis_index("dp")
        self.width = D // shards

    @staticmethod
    def scratch(shards, replicas):
        width = D // shards
        dma = pltpu.SemaphoreType.DMA
        return [
            pltpu.VMEM((shards, 8, width), jnp.float32),
            pltpu.VMEM((8, width), jnp.float32),
            pltpu.VMEM((replicas, 8, width), jnp.float32),
            pltpu.VMEM((replicas, 8, D), jnp.float32),
            dma((shards,)), dma((shards,)), dma((2, replicas)), dma((2, replicas)), dma((shards,)), dma((shards,)),
        ]

    def others(self, axis):
        count, here = (self.shards, self.seq) if axis == "seq" else (self.replicas, self.dp)
        return [(step, lax.rem(here + step, count)) for step in range(1, count)]

    def barrier(self):
        sem = pltpu.get_barrier_semaphore()
        amount = 0
        for axis in ("seq", "dp"):
            for _, place in self.others(axis):
                pl.semaphore_signal(sem, inc=1, device_id={axis: place}, device_id_type=MESH)
                amount += 1
        pl.semaphore_wait(sem, amount)

    def copy(self, axis, place, src, dst, send, recv):
        return pltpu.make_async_remote_copy(
            src_ref=src, dst_ref=dst, send_sem=send, recv_sem=recv, device_id={axis: place}, device_id_type=MESH
        )

    def columns(self, place):
        return pl.ds(pl.multiple_of(place * self.width, self.width), self.width)

    def spread(self):
        self.first = [
            self.copy(
                "seq", place, self.sums.at[:, self.columns(place)], self.came.at[step], self.spread_send.at[step],
                self.spread_recv.at[step],
            )
            for step, place in self.others("seq")
        ]
        self.second = [
            self.copy(
                "dp", place, self.bias, self.biases.at[self.dp], self.cross_send.at[1, step],
                self.cross_recv.at[1, step],
            )
            for step, place in self.others("dp")
        ]
        for copy in self.first + self.second:
            copy.start()

    def cross(self):
        total = self.sums[:, self.columns(self.seq)]
        for (step, _), copy in zip(self.others("seq"), self.first):
            copy.wait_recv()
            total = total + self.came[step]
        self.block[...] = total
        self.blocks[self.dp] = total
        self.third = [
            self.copy(
                "dp", place, self.block, self.blocks.at[self.dp], self.cross_send.at[0, step],
                self.cross_recv.at[0, step],
            )
            for step, place in self.others("dp")
        ]
        for copy in self.third:
            copy.start()

    def collect(self):
        for copy in self.third + self.second:
            copy.wait_recv()
        self.biases[self.dp] = self.bias[...]
        total, bias = self.blocks[0], self.biases[0]
        for place in range(1, self.replicas):
            total, bias = total + self.blocks[place], bias + self.biases[place]
        self.bias_total[...] = bias
        here = self.columns(self.seq)
        self.total[:, here] = total
        self.fourth = [
            self.copy(
                "seq", place, self.total.at[:, here], self.total.at[:, here], self.back_send.at[step],
                self.back_recv.at[step],
            )
            for step, place in self.others("seq")
        ]
        for copy in self.fourth:
            copy.start()

    def finish(self):
        for (step, _), copy in zip(self.others("seq"), self.fourth):
            source = lax.rem(self.seq + self.shards - step, self.shards)
            there = self.total.at[:, self.columns(source)]
            self.copy("seq", source, there, there, self.back_send.at[step], self.back_recv.at[step]).wait_recv()
        for copy in self.first + self.second + self.third + self.fourth:
            copy.wait_send()


def score_rows(stats, lengths, labels, reference, sizes, replicas, collective):
    shards = sizes[0] * sizes[1]
    width = BLOCK // shards

    def kernel(
        stats_ref, lengths_ref, labels_ref, reference_ref, coef_ref, losses_ref,
        came, full, ratio, ratios, spread_send, spread_recv, back_send, back_recv, cross_send, cross_recv,
    ):
        seq, dp = lax.axis_index("seq"), lax.axis_index("dp")
        peers = {
            "seq": [(step, lax.rem(seq + step, shards)) for step in range(1, shards)],
            "dp": [(step, lax.rem(dp + step, replicas)) for step in range(1, replicas)],
        }
        barrier = pltpu.get_barrier_semaphore()
        for axis in peers:
            for _, place in peers[axis]:
                pl.semaphore_signal(barrier, inc=1, device_id={axis: place}, device_id_type=MESH)
        pl.semaphore_wait(barrier, shards + replicas - 2)

        def columns(place):
            return pl.ds(pl.multiple_of(place * width, width), width)

        def copy(axis, place, src, dst, send, recv):
            return pltpu.make_async_remote_copy(
                src_ref=src, dst_ref=dst, send_sem=send, recv_sem=recv, device_id={axis: place}, device_id_type=MESH
            )

        sent = [
            copy("seq", place, stats_ref.at[:, columns(place)], came.at[step], spread_send.at[step], spread_recv.at[step])
            for step, place in peers["seq"]
        ]
        for one in sent:
            one.start()
        mine = stats_ref[:, columns(seq)]
        top, total, pick = mine[0:1], mine[1:2], mine[2:3]
        for (step, _), one in zip(peers["seq"], sent):
            one.wait_recv()
            other = came[step]
            joint = jnp.maximum(top, other[0:1])
            total = total * jnp.exp(top - joint) + other[1:2] * jnp.exp(other[0:1] - joint)
            pick = pick + other[2:3]
            top = joint
        log_total = top + jnp.log(total)
        here = columns(seq)
        full[0:1, here] = log_total
        full[1:2, here] = pick - log_total
        back = [
            copy("seq", place, full.at[:, here], full.at[:, here], back_send.at[step], back_recv.at[step])
            for step, place in peers["seq"]
        ]
        for one in back:
            one.start()
        for step, _ in peers["seq"]:
            source = lax.rem(seq + shards - step, shards)
            there = full.at[:, columns(source)]
            copy("seq", source, there, there, back_send.at[step], back_recv.at[step]).wait_recv()
        example = lax.broadcasted_iota(jnp.int32, (EXB, 1), 0)
        start, end = jnp.zeros_like(example), jnp.zeros_like(example)
        sign, reference = jnp.zeros((EXB, 1), jnp.float32), jnp.zeros((EXB, 1), jnp.float32)
        reached = jnp.int32(0)
        for index in range(EXB):
            start = jnp.where(example == index, reached, start)
            reached = reached + lengths_ref[index]
            end = jnp.where(example == index, reached, end)
            sign = jnp.where(example == index, (2 * labels_ref[index] - 1).astype(jnp.float32), sign)
            reference = jnp.where(example == index, reference_ref[index], reference)
        counts = (end - start).astype(jnp.float32)
        row = lax.broadcasted_iota(jnp.int32, (EXB, BLOCK), 1)
        member = (row >= start) & (row < end)
        mean = jnp.sum(jnp.where(member, full[1:2, :], 0.0), axis=1, keepdims=True) / counts
        log_ratio = mean - reference
        ratio[...] = jnp.broadcast_to(jnp.sum(log_ratio, axis=0, keepdims=True), ratio.shape)
        crossed = [
            copy("dp", place, ratio, ratios.at[dp], cross_send.at[step], cross_recv.at[step])
            for step, place in peers["dp"]
        ]
        for one in crossed:
            one.start()
        for one in crossed:
            one.wait_recv()
        ratios[dp] = ratio[...]
        whole = ratios[0]
        for place in range(1, replicas):
            whole = whole + ratios[place]
        center = whole[:, 0:1] / (replicas * EXB)
        squashed = jax.nn.sigmoid(BETA * sign * (log_ratio - center))
        losses_ref[...] = jnp.broadcast_to(1.0 - squashed, losses_ref.shape)
        grad = -LOSS_SCALE * BETA * sign * squashed * (1.0 - squashed) / counts
        token = jnp.sum(jnp.where(member, grad, 0.0), axis=0, keepdims=True)
        coef_ref[...] = jnp.zeros_like(coef_ref)
        coef_ref[0:1, :] = token
        coef_ref[1:2, :] = token * jnp.exp(stats_ref[0:1, :] - full[0:1, :])
        for one in sent + back + crossed:
            one.wait_send()

    dma = pltpu.SemaphoreType.DMA
    return pl.pallas_call(
        kernel,
        out_shape=[
            jax.ShapeDtypeStruct((8, BLOCK), jnp.float32),
            jax.ShapeDtypeStruct((EXB, 128), jnp.float32),
        ],
        in_specs=[VMEM] + [SMEM] * 3,
        out_specs=[VMEM] * 2,
        scratch_shapes=[
            pltpu.VMEM((shards, 8, width), jnp.float32),
            pltpu.VMEM((8, BLOCK), jnp.float32),
            pltpu.VMEM((EXB, 128), jnp.float32),
            pltpu.VMEM((replicas, EXB, 128), jnp.float32),
            dma((shards,)), dma((shards,)), dma((shards,)), dma((shards,)), dma((replicas,)), dma((replicas,)),
        ],
        compiler_params=pltpu.CompilerParams(collective_id=collective, has_side_effects=True),
    )(stats, lengths, labels, reference)


def input_grad_rows(
    own, grad_stream, plain, grad_qkv, grad_up, qkv_flat, up_weight, gains, end_sums, biases, sizes, replicas,
    collective, before,
):
    shards, rows, width = grad_qkv.shape
    hidden = grad_up.shape[2]

    def kernel(
        own_ref, stream_ref, normed_any, qkv_any, up_any, qkvw_any, upw_any, gains_ref, end_ref,
        bias_ref, out_ref, total_ref, bias_total_ref,
        qkvw, upw, weight_sems, normed, qkv, up, load_sems, sums_ref, *scratch,
    ):
        grid = Grid2(sizes)
        small = SmallSum(shards, replicas, sums_ref, bias_ref, total_ref, bias_total_ref, scratch[:10])
        scratch = scratch[10:]
        parts = scratch[0]
        order = production_order(grid)

        def loads(i):
            place = order[i]
            return [
                pltpu.make_async_copy(normed_any.at[place], normed.at[i % 2], load_sems.at[i, 0]),
                pltpu.make_async_copy(qkv_any.at[place], qkv.at[i % 2], load_sems.at[i, 1]),
                pltpu.make_async_copy(up_any.at[place], up.at[i % 2], load_sems.at[i, 2]),
            ]

        copies = [loads(i) for i in range(shards)]
        weights = [
            pltpu.make_async_copy(qkvw_any, qkvw, weight_sems.at[0]),
            pltpu.make_async_copy(upw_any, upw, weight_sems.at[1]),
        ]
        for copy in copies[0] + weights:
            copy.start()
        sums_ref[...] = jnp.zeros_like(sums_ref)
        small.barrier()
        for copy in weights:
            copy.wait()
        count = [0]

        def produce(slow, fast):
            place = grid.index(slow, fast)
            i = count[0]
            count[0] += 1
            if i + 1 < shards:
                for copy in copies[i + 1]:
                    copy.start()
            for copy in copies[i]:
                copy.wait()
            slot = i % 2

            def columns(index, _):
                here = span(index, 512)
                one = dot_nt(qkv[slot], qkvw[here, :])
                two = dot_nt(up[slot], upw[here, :])
                norm = normed[slot, :, here].astype(jnp.float32)
                parts[place, :, here] = (one * gains_ref[0:1, here] + two * gains_ref[1:2, here]).astype(
                    jnp.bfloat16
                )
                sums_ref[0:1, here] += jnp.sum(one * norm, axis=0, keepdims=True)
                sums_ref[1:2, here] += jnp.sum(one, axis=0, keepdims=True)
                sums_ref[2:3, here] += jnp.sum(two * norm, axis=0, keepdims=True)
                sums_ref[3:4, here] += jnp.sum(two, axis=0, keepdims=True)
                return _

            lax.fori_loop(0, D // 512, columns, 0)

        def made():
            sums_ref[4:8] = end_ref[0:4]
            small.spread()

        run_scatter(grid, sizes, rows, scratch, produce, made, small.cross, small.collect)
        mine = grid.index(*grid.me)

        def norm_tile(index, _):
            here = span(index, ROW_TILE)
            grad = parts[mine, here].astype(jnp.float32)
            centered, inverse = tile_stats(own_ref[here].astype(jnp.float32))
            normed = centered * inverse
            out_ref[here] = stream_ref[here] + inverse * (
                grad
                - jnp.mean(grad, axis=1, keepdims=True)
                - normed * jnp.mean(grad * normed, axis=1, keepdims=True)
            )
            return _

        lax.fori_loop(0, rows // ROW_TILE, norm_tile, 0)
        small.finish()

    return row_kernel(
        kernel, collective,
        [jax.ShapeDtypeStruct((rows, D), jnp.float32), jax.ShapeDtypeStruct((8, D), jnp.float32), jax.ShapeDtypeStruct((8, D), jnp.float32)],
        [VMEM, VMEM, ANY, ANY, ANY, ANY, ANY, VMEM, VMEM, VMEM],
        [VMEM, VMEM, VMEM],
        [
            pltpu.VMEM(qkv_flat.shape, jnp.bfloat16),
            pltpu.VMEM(up_weight.shape, jnp.bfloat16),
            pltpu.SemaphoreType.DMA((2,)),
            pltpu.VMEM((2, rows, D), jnp.bfloat16),
            pltpu.VMEM((2, rows, width), jnp.bfloat16),
            pltpu.VMEM((2, rows, hidden), jnp.bfloat16),
            pltpu.SemaphoreType.DMA((shards, 3)),
            pltpu.VMEM((8, D), jnp.float32),
        ]
        + SmallSum.scratch(shards, replicas)
        + sum_scratch(sizes, rows),
        2 * BLOCK * D * (width + hidden),
        before,
    )(own, grad_stream, plain, grad_qkv, grad_up, qkv_flat, up_weight, gains, end_sums, biases)


def join_halves(sums, others, earlier):
    steps, count = 8, len(sums)

    def kernel(*refs):
        for i in range(count):
            refs[2 * count + 1 + i][...] = (
                refs[i][...].astype(jnp.float32) + refs[count + i][...].astype(jnp.float32)
            ).astype(jnp.bfloat16)

    specs = [pl.BlockSpec((v.shape[0] // steps, v.shape[1]), lambda i: (i, 0)) for v in sums]
    return pl.pallas_call(
        kernel,
        grid=(steps,),
        out_shape=[jax.ShapeDtypeStruct(v.shape, jnp.bfloat16) for v in sums],
        in_specs=specs + specs + [ANY],
        out_specs=specs,
        compiler_params=pltpu.CompilerParams(vmem_limit_bytes=VMEM_LIMIT),
    )(*sums, *others, earlier)


def settle_halves(core, totals, backs, shapes, before=()):
    steps = 8

    def kernel(core_ref, *refs):
        count = len(totals)
        mine = pl.program_id(0) == 0
        for i in range(count):
            found = jnp.where(mine, refs[i][...].astype(jnp.float32), refs[count + i][...].astype(jnp.float32))
            out = refs[2 * count + len(before) + i]
            if len(out.shape) == 3:
                for head in range(out.shape[1]):
                    out[:, head, :] = found[:, head * out.shape[2] : (head + 1) * out.shape[2]]
            else:
                out[...] = found

    def place(half, core_ref):
        return jnp.where(half == 0, core_ref[0], 1 - core_ref[0])

    ins, outs = [], []
    for which in (0, 1):
        for value in totals:
            ins.append(
                pl.BlockSpec(
                    (value.shape[0] // steps, value.shape[1]),
                    (lambda h, i, core_ref: (jnp.where(h == 0, i, steps - 1), 0))
                    if which == 0
                    else (lambda h, i, core_ref: (jnp.where(h == 0, 0, i), 0)),
                )
            )
    for value, shape in zip(totals, shapes):
        rows = value.shape[0] // steps
        if len(shape) == 3:
            outs.append(
                pl.BlockSpec((rows,) + shape[1:], lambda h, i, core_ref: (place(h, core_ref) * steps + i, 0, 0))
            )
        elif shape[0] == value.shape[0]:
            outs.append(pl.BlockSpec((rows, value.shape[1]), lambda h, i, core_ref: (i, place(h, core_ref))))
        else:
            outs.append(pl.BlockSpec((rows, shape[1]), lambda h, i, core_ref: (place(h, core_ref) * steps + i, 0)))
    return pl.pallas_call(
        kernel,
        grid_spec=pltpu.PrefetchScalarGridSpec(
            num_scalar_prefetch=1, grid=(2, steps), in_specs=ins + [ANY] * len(before), out_specs=outs
        ),
        out_shape=[jax.ShapeDtypeStruct(shape, jnp.float32) for shape in shapes],
        compiler_params=pltpu.CompilerParams(vmem_limit_bytes=VMEM_LIMIT),
    )(core, *totals, *backs, *before)


def row_of(vector):
    return vector.astype(jnp.float32)[None, :]


PAIR = [(0, 1), (1, 0), (2, 3), (3, 2)]
CROSS = [(0, 2), (2, 0), (1, 3), (3, 1)]


def held(values):
    return lax.optimization_barrier(values)


def half_of(values, which):
    half = values.shape[1] // 2
    return lax.dynamic_slice_in_dim(values, which * half, half, 1)


class PairSum:
    def __init__(self, product):
        self.plain = lax.axis_size("dp") != 4
        if self.plain:
            self.sum = jnp.stack([product(0), product(1)]).astype(jnp.bfloat16)
            return
        self.core = lax.rem(lax.axis_index("dp"), 2)
        away = product(1 - self.core).astype(jnp.bfloat16)
        came = lax.ppermute(away, "dp", PAIR)
        mine = held(product(self.core))
        self.sum = (mine + came.astype(jnp.float32)).astype(jnp.bfloat16)

    def cross(self):
        self.other = lax.psum(self.sum, "dp") if self.plain else lax.ppermute(self.sum, "dp", CROSS)
        return self

    def join(self):
        self.total = self.other if self.plain else join_halves([self.sum], [self.other], self.other)[0]
        return self


def join_all(sums, earlier):
    if not sums[0].plain:
        totals = join_halves([one.sum for one in sums], [one.other for one in sums], earlier)
        for one, total in zip(sums, totals):
            one.total = total


def settle_all(sums, shapes, before=()):
    if sums[0].plain:
        core = jnp.zeros((1,), jnp.int32)
        return settle_halves(core, [s.other[0] for s in sums], [s.other[1] for s in sums], shapes, before)
    backs = [lax.ppermute(one.total, "dp", PAIR) for one in sums]
    return settle_halves(sums[0].core[None], [one.total for one in sums], backs, shapes, before)


def per_device(
    hidden, targets, lengths, labels, ref_logps, ln1_gain, ln1_bias, ln2_gain, ln2_bias, qkv_weight, qv_bias,
    out_weight, up_weight, up_bias, down_weight, branch_bias, lnf_gain, lnf_bias, head_weight,
):
    sizes = lines_of(lax.axis_size("seq"))
    own = hidden[0]
    local_heads = qkv_weight.shape[1]
    local_vocab = head_weight.shape[1]
    local_hidden = up_weight.shape[1]
    width = local_heads * 3 * HEAD_DIM
    inner = local_heads * HEAD_DIM
    qv_float = qv_bias.astype(jnp.float32)
    full_bias = jnp.concatenate(
        [qv_float[:, :HEAD_DIM], jnp.zeros_like(qv_float[:, :HEAD_DIM]), qv_float[:, HEAD_DIM:]], axis=-1
    ).reshape(1, width)
    qkv_flat = qkv_weight.reshape(D, width)
    out_flat = out_weight.reshape(inner, D)
    block_lengths = lengths[0]
    norms = jnp.concatenate([row_of(v) for v in (ln1_gain, ln1_bias, ln2_gain, ln2_bias)], axis=0)
    plain, first_full, second_full, qkv, act, slope, *planes = open_rows(
        own, sizes, 0, norms, qkv_flat, full_bias, up_weight, row_of(up_bias), block_lengths
    )
    flat_qkv = qkv.reshape(BLOCK, width)
    ctx, lse = attention_forward(flat_qkv, block_lengths, local_heads)
    shards, rows = plain.shape[0], plain.shape[1]
    end_norms = jnp.concatenate([row_of(v) for v in (lnf_gain, lnf_bias, branch_bias)], axis=0)
    output, final, normed, inverse = branch_rows(
        own, ctx.reshape(shards, rows, inner), act, out_flat, down_weight, end_norms, sizes, 1
    )
    final_full, weights, stats = logit_rows(final, head_weight, targets[0][:, None], sizes, 2)

    coef, losses = score_rows(
        stats, block_lengths, labels[0], ref_logps[0], sizes, lax.axis_size("dp"), 6
    )
    vocab_ids = lax.axis_index("seq") * local_vocab + jnp.arange(local_vocab, dtype=jnp.int32)
    grad_logits = held((
        jnp.where(vocab_ids[None, :] == targets[0][:, None], coef[0][:, None], 0.0)
        - weights.reshape(BLOCK, local_vocab).astype(jnp.float32) * coef[1][:, None]
    ).astype(jnp.bfloat16))
    final_rows = final_full.reshape(BLOCK, D)
    head_sum = PairSum(lambda which: dot_tn(half_of(final_rows, which), grad_logits)).cross()

    grad_stream, grad_own, end_sums = final_grad_rows(
        grad_logits.reshape(shards, rows, local_vocab), head_weight, normed, inverse, row_of(lnf_gain), sizes, 3,
        (head_sum.sum,),
    )
    grad_full, grad_ctx, grad_up, up_sums = branch_grad_rows(
        grad_own, out_flat, down_weight, slope, sizes, 4
    )
    grad_rows = grad_full.reshape(BLOCK, D)
    act_rows = act.reshape(BLOCK, local_hidden)
    second_rows = second_full.reshape(BLOCK, D)
    up_rows = grad_up.reshape(BLOCK, local_hidden)
    sums = [
        PairSum(lambda which: dot_tn(ctx, half_of(grad_rows, which))),
        PairSum(lambda which: dot_tn(act_rows, half_of(grad_rows, which))),
        PairSum(lambda which: dot_tn(half_of(second_rows, which), up_rows)),
    ]
    for one in sums:
        one.cross()
    made = [one.sum for one in sums]
    grad_qkv, qkv_sums = attention_backward(
        flat_qkv, block_lengths, local_heads, ctx, lse, grad_ctx.reshape(BLOCK, inner), planes,
        made,
    )
    first_rows = first_full.reshape(BLOCK, D)
    sums.append(PairSum(lambda which: dot_tn(half_of(first_rows, which), grad_qkv)))
    sums[-1].cross()
    qkv_sums = qkv_sums[:, 0]
    qv_grad = jnp.concatenate([qkv_sums[:, :HEAD_DIM], qkv_sums[:, 2 * HEAD_DIM :]], axis=-1)
    split = local_heads * 2 * HEAD_DIM
    biases = jnp.concatenate([qv_grad.reshape(-1), up_sums[0]])
    biases = jnp.pad(biases[None, :], ((0, 7), (0, D - biases.shape[0])))
    gains = jnp.concatenate([row_of(ln1_gain), row_of(ln2_gain)], axis=0)
    grad_input, small, biases = input_grad_rows(
        own, grad_stream, plain, grad_qkv.reshape(shards, rows, width), grad_up, qkv_flat, up_weight, gains,
        end_sums, biases, sizes, lax.axis_size("dp"), 5, (sums[-1].sum, head_sum.join().total),
    )
    join_all(sums, small)
    (head_grad,) = settle_all([head_sum], [(D, local_vocab)])
    out_grad, down_grad, up_grad, qkv_grad = settle_all(
        sums, [(inner, D), (local_hidden, D), (D, local_hidden), qkv_weight.shape], (head_grad,)
    )
    return (
        losses[:, 0][None],
        output[None],
        grad_input[None],
        small[0],
        small[1],
        small[2],
        small[3],
        qkv_grad,
        biases[0, :split].reshape(local_heads, 2 * HEAD_DIM),
        out_grad.reshape(out_weight.shape),
        up_grad,
        biases[0, split : split + local_hidden],
        down_grad,
        small[6],
        small[4],
        small[5],
        head_grad,
    )


def solution(mesh):
    return jax.shard_map(
        per_device,
        mesh=mesh,
        in_specs=(
            P("dp", "seq", None),
            P("dp", None),
            P("dp", None),
            P("dp", None),
            P("dp", None),
            P(),
            P(),
            P(),
            P(),
            P(None, "seq", None),
            P("seq", None),
            P("seq", None, None),
            P(None, "seq"),
            P("seq"),
            P("seq", None),
            P(),
            P(),
            P(),
            P(None, "seq"),
        ),
        out_specs=(
            P("dp", None),
            P("dp", "seq", None),
            P("dp", "seq", None),
            P(),
            P(),
            P(),
            P(),
            P(None, "seq", None),
            P("seq", None),
            P("seq", None, None),
            P(None, "seq"),
            P("seq"),
            P("seq", None),
            P(),
            P(),
            P(),
            P(None, "seq"),
        ),
        check_vma=False,
    )
```

```python
import jax
import jax.numpy as jnp
from jax import lax
from jax.experimental import pallas as pl
from jax.experimental.pallas import tpu as pltpu
from jax.sharding import PartitionSpec as P

D = 2048
HEAD_DIM = 128
ROT = 32
BLOCK = 2048
EXB = 8
EPSILON = 1e-05
BETA = 0.25
LOSS_SCALE = 65536.0
HALVES = 2
VMEM_LIMIT = 62 * 2**20

MESH = pl.DeviceIdType.MESH


class Grid2:
    def __init__(self, sizes):
        self.n = sizes
        place = lax.axis_index("seq")
        self.me = (place // sizes[1], lax.rem(place, sizes[1]))

    def index(self, slow, fast):
        return slow * self.n[1] + fast

    def device(self, axis, spot):
        here = list(self.me)
        here[axis] = spot
        return {"seq": self.index(*here)}

    def nearest(self, axis, rank):
        n, m = self.n[axis], self.me[axis]
        if rank == 0:
            return m
        if n == 2:
            return 1 - m
        after = n - 1 - m
        both = jnp.minimum(m, after)
        dist = (rank + 1) // 2
        near = m - dist if rank % 2 else m + dist
        far = jnp.where(m < after, m + (rank - both), m - (rank - both))
        return jnp.where(rank <= 2 * both, near, far)

    def neighbours(self):
        found = []
        for axis in (0, 1):
            m, n = self.me[axis], self.n[axis]
            if n == 2:
                found.append((None, self.device(axis, 1 - m)))
            elif n > 2:
                found.append((m > 0, self.device(axis, m - 1)))
                found.append((m < n - 1, self.device(axis, m + 1)))
        return found

    def barrier(self, *others):
        sem = pltpu.get_barrier_semaphore()
        amount = jnp.int32(0)
        for there, device in self.neighbours() + [(None, device) for device in others]:
            def tell(device=device):
                pl.semaphore_signal(sem, inc=1, device_id=device, device_id_type=MESH)
            if there is None:
                tell()
                amount = amount + 1
            else:
                pl.when(there)(tell)
                amount = amount + there.astype(jnp.int32)
        pl.semaphore_wait(sem, amount)


class Sender:
    def __init__(self, send_sems):
        self.sems = send_sems
        self.used = 0
        self.open = []

    def send(self, src, dst, recv_sem, device, when=None):
        copy = pltpu.make_async_remote_copy(
            src_ref=src, dst_ref=dst, send_sem=self.sems.at[self.used], recv_sem=recv_sem,
            device_id=device, device_id_type=MESH)
        self.used += 1
        if when is None:
            copy.start()
        else:
            pl.when(when)(copy.start)
        self.open.append((when, copy))

    def finish(self):
        for when, copy in self.open:
            if when is None:
                copy.wait_send()
            else:
                pl.when(when)(copy.wait_send)
        self.open = []


def gather_sends(sizes, halves):
    return halves * 2 * (sizes[0] * sizes[1] * 5 + 8)


def gather_rounds(grid, sender, piece, recv_sems, halves, cut, ready):
    n, me = grid.n, grid.me

    def arrived(slow, fast, half, kind, when):
        ref = piece(grid.index(slow, fast), half, kind)
        sem = recv_sems.at[kind, half, grid.index(slow, fast)]
        wait = pltpu.make_async_copy(ref, ref, sem).wait
        if when is None:
            wait()
        else:
            pl.when(when)(wait)

    def push(slow, fast, half, kind, axis, spot, *conditions):
        ref = piece(grid.index(slow, fast), half, kind)
        sem = recv_sems.at[kind, half, grid.index(slow, fast)]
        when = None
        for condition in conditions:
            if condition is not None:
                when = condition if when is None else when & condition
        sender.send(ref, ref, sem, grid.device(axis, spot), when)

    def spread(slow, fast, half, kind, axis, when):
        m, size = me[axis], n[axis]
        if size == 2:
            push(slow, fast, half, kind, axis, 1 - m, when)
        elif size > 2:
            push(slow, fast, half, kind, axis, m + 1, when, m < size - 1)
            push(slow, fast, half, kind, axis, m - 1, when, m > 0)

    def onward(slow, fast, half, kind, axis, when):
        m, size = me[axis], n[axis]
        if size <= 2:
            return
        below = (slow, fast)[axis] < m
        more = (below & (m < size - 1)) | (jnp.logical_not(below) & (m > 0))
        push(slow, fast, half, kind, axis, jnp.where(below, m + 1, m - 1), when, more)

    def sides(d):
        if d == 0:
            return [(me[0], None)]
        if n[0] == 2:
            return [(1 - me[0], None)]
        return [(me[0] - d, me[0] >= d), (me[0] + d, me[0] + d < n[0])]

    def settle(d):
        for half in range(halves):
            for slow, when in sides(d):
                for l in range(n[1]):
                    fast = grid.nearest(1, l)
                    if d > 0:
                        arrived(slow, fast, half, 1, when)
                        onward(slow, fast, half, 1, 0, when)
                    else:
                        spread(slow, fast, half, 1, 0, when)

    def complete(d):
        for l in range(1, n[1]):
            fast = grid.nearest(1, l)
            for half in range(halves):
                for slow, when in sides(d):
                    arrived(slow, fast, half, 0, when)
                    onward(slow, fast, half, 0, 1, when)

    def work(k, l):
        ready(grid.nearest(0, k), grid.nearest(1, l), k * n[1] + l)

    for half in range(halves):
        for kind in (1, 0):
            if cut[kind]:
                spread(me[0], me[1], half, kind, kind, None)
        if cut[0]:
            spread(me[0], me[1], half, 0, 1, None)
    work(0, 0)
    if cut[1]:
        for half in range(halves):
            for l in range(1, n[1]):
                fast = grid.nearest(1, l)
                arrived(me[0], fast, half, 1, None)
                onward(me[0], fast, half, 1, 1, None)
        settle(0)
    for d in range(1, n[0]):
        if cut[0]:
            for half in range(halves):
                for slow, when in sides(d):
                    arrived(slow, me[1], half, 0, when)
                    onward(slow, me[1], half, 0, 0, when)
                    spread(slow, me[1], half, 0, 1, when)
            complete(d - 1)
        for l in range(1, n[1]):
            work(d - 1, l)
        if cut[1]:
            settle(d)
        work(d, 0)
    if cut[0]:
        complete(n[0] - 1)
    for l in range(1, n[1]):
        work(n[0] - 1, l)


def scatter_slots(n):
    return 1 if n == 2 else n + 1


def scatter_plan(n):
    if n == (4, 2):
        return [
            ("make", 3, 1), ("make", 2, 1), ("make", 3, 0), ("make", 1, 1), ("first", 3), ("make", 2, 0),
            ("make", 0, 1), ("later", 3, 0), ("make", 1, 0), ("later", 3, 1), ("first", 2), ("make", 0, 0), ("made",),
            ("later", 2, 0), ("later", 2, 1), ("first", 1), ("later", 1, 0), ("later", 1, 1),
        ]
    far = n[0] - 1
    plan = [("make", k, l) for k in range(far, -1, -1) for l in range(n[1] - 1, -1, -1)] + [("made",)]
    for k in range(far, 0, -1):
        plan += [("first", k), ("later", k, 0), ("later", k, 1)]
    return plan


class Scatter:
    def __init__(self, grid, sender, part, bufs, sems, halves, cut):
        self.grid, self.sender, self.part = grid, sender, part
        self.bufs, self.sems, self.halves, self.cut = bufs, sems, halves, cut

    def slot(self, axis, target, from_below):
        if self.grid.n[axis] == 2:
            return 0
        return target + jnp.where(from_below, 1, 0)

    def take(self, kind, stage, axis, other, target, from_below, half, when, slot_index):
        buf, sem = self.bufs[kind][stage], self.sems[kind][stage]
        slot = self.slot(axis, target, from_below)

        def add():
            ref = buf.at[other, slot, half]
            pltpu.make_async_copy(ref, ref, sem.at[other, slot, half]).wait()
            mine = self.part(slot_index, half, kind)
            mine[...] = (mine[...].astype(jnp.float32) + ref[...].astype(jnp.float32)).astype(mine.dtype)

        if when is None:
            add()
        else:
            pl.when(when)(add)

    def incoming(self, axis, target):
        m, n = self.grid.me[axis], self.grid.n[axis]
        if n == 2:
            return None
        up = target > m
        return (up & (m > 0)) | (jnp.logical_not(up) & (m < n - 1))

    def toward(self, kind, stage, axis, other, target, half, slow, fast, when=None):
        grid = self.grid
        m, n = grid.me[axis], grid.n[axis]
        up = target > m
        index = grid.index(slow, fast)
        if n > 2:
            incoming = self.incoming(axis, target)
            self.take(kind, stage, axis, other, target, up, half, incoming if when is None else incoming & when, index)
        buf, sem = self.bufs[kind][stage], self.sems[kind][stage]
        slot = self.slot(axis, target, up)
        spot = 1 - m if n == 2 else jnp.where(up, m + 1, m - 1)
        self.sender.send(
            self.part(index, half, kind), buf.at[other, slot, half], sem.at[other, slot, half],
            grid.device(axis, spot), when)

    def last(self, kind, stage, axis, other, half, slow, fast):
        grid = self.grid
        m, n = grid.me[axis], grid.n[axis]
        index = grid.index(slow, fast)
        if n == 2:
            self.take(kind, stage, axis, other, m, m > 0, half, None, index)
        elif n > 2:
            self.take(kind, stage, axis, other, m, jnp.bool_(True), half, m > 0, index)
            self.take(kind, stage, axis, other, m, jnp.bool_(False), half, m < n - 1, index)

    def run(self, produce, made=lambda: None, between=lambda: None, late=lambda: None, fill=lambda: None):
        grid, n, me = self.grid, self.grid.n, self.grid.me
        lagging, filling = [], []

        def chain(k, half, begins):
            slow = grid.nearest(0, k)
            incoming = self.incoming(0, slow)
            if incoming is None:
                if begins:
                    self.last(0, 0, 1, slow, half, slow, me[1])
                    self.toward(0, 1, 0, 0, slow, half, slow, me[1])
                return
            when = jnp.logical_not(incoming) if begins else incoming
            pl.when(when)(lambda: self.last(0, 0, 1, slow, half, slow, me[1]))
            self.toward(0, 1, 0, 0, slow, half, slow, me[1], when)

        def catch_up():
            for step in lagging:
                self.toward(*step)
            lagging.clear()

        def make(k, l):
            slow, fast = grid.nearest(0, k), grid.nearest(1, l)
            produce(slow, fast)
            if self.cut[0] and l > 0:
                for half in range(self.halves):
                    self.toward(0, 0, 1, slow, fast, half, slow, fast)
            catch_up()
            if self.cut[1] and k > 0:
                for half in range(self.halves):
                    lagging.append((1, 0, 0, fast, slow, half, slow, fast))

        for step in scatter_plan(n):
            if step[0] == "make":
                make(*step[1:])
            elif step[0] == "made":
                catch_up()
                made()
                filling.append(fill)
            elif step[0] == "first" and self.cut[0]:
                for more in filling:
                    more()
                for half in range(self.halves):
                    chain(step[1], half, True)
            elif self.cut[0]:
                for more in filling:
                    more()
                chain(step[1], step[2], False)
        between()
        fill()
        if self.cut[1]:
            for half in range(self.halves):
                for l in reversed(range(n[1])):
                    fast = grid.nearest(1, l)
                    self.last(1, 0, 0, fast, half, me[0], fast)
                    if l > 0:
                        self.toward(1, 1, 1, 0, fast, half, me[0], fast)
        late()
        if self.cut[0]:
            for half in range(self.halves):
                fill()
                self.last(0, 0, 1, me[0], half, me[0], me[1])
        for half in range(self.halves):
            if self.cut[1]:
                self.last(1, 1, 1, 0, half, me[0], me[1])
            if self.cut[0]:
                self.last(0, 1, 0, 0, half, me[0], me[1])


def scatter_scratch(sizes, halves, rows, cols, cut):
    bufs, sems = [], []
    for kind, stages in ((0, (1, 0)), (1, (0, 1))):
        for stage, axis in enumerate(stages):
            lead = (sizes[1 - axis] if stage == 0 else 1, scatter_slots(sizes[axis]), halves)
            width = max(cut[kind], 128)
            bufs.append(pltpu.VMEM(lead + (rows // halves, width), jnp.bfloat16))
            sems.append(pltpu.SemaphoreType.DMA(lead))
    return bufs, sems


def scatter_sends(sizes, halves):
    return halves * 2 * (sizes[0] * sizes[1] + sizes[0] + sizes[1])


def lines_of(seq):
    fast = 2 if seq <= 8 else 4
    return (seq // fast, fast)


ATT_TILE = 256
SCALE = HEAD_DIM ** (-0.5)


def dot_nt(left, right):
    return lax.dot_general(left, right, (((1,), (1,)), ((), ())), preferred_element_type=jnp.float32)


def dot_tn(left, right):
    return lax.dot_general(left, right, (((0,), (0,)), ((), ())), preferred_element_type=jnp.float32)


def rotary_frequencies():
    half_rot = ROT // 2
    frequency = 10000.0 ** (-2.0 * jnp.arange(half_rot, dtype=jnp.float32) / ROT)
    return jnp.tile(frequency, HEAD_DIM // half_rot)[None, :]


def first_rows(lengths, row):
    start, end = jnp.zeros_like(row), jnp.int32(0)
    for example in range(EXB):
        end = end + lengths[example]
        start = jnp.where(row >= end, end, start)
    return start


def rotary_planes(position, frequencies):
    half_rot = ROT // 2
    angles = position.astype(jnp.float32) * frequencies
    cos, sin = jnp.cos(angles), jnp.sin(angles)
    lane = lax.broadcasted_iota(jnp.int32, angles.shape, 1)
    return (
        jnp.where(lane < ROT, cos, 1.0),
        jnp.where((lane >= half_rot) & (lane < ROT), sin, 0.0),
        jnp.where(lane < half_rot, -sin, 0.0),
    )


def turn(vector, cos, from_below, from_above):
    half_rot = ROT // 2
    return (
        vector * cos
        + pltpu.roll(vector, half_rot, 1) * from_below
        + pltpu.roll(vector, HEAD_DIM - half_rot, 1) * from_above
    )


def tile_mask(start_col, query_tile, key_tile):
    shape = (ATT_TILE, ATT_TILE)
    query_ids = query_tile * ATT_TILE + lax.broadcasted_iota(jnp.int32, shape, 0)
    key_ids = key_tile * ATT_TILE + lax.broadcasted_iota(jnp.int32, shape, 1)
    return (key_ids >= start_col) & (key_ids <= query_ids)


def tile_starts(lengths, tile):
    rows = tile * ATT_TILE + lax.broadcasted_iota(jnp.int32, (ATT_TILE, 1), 0)
    return first_rows(lengths, rows), first_rows(lengths, tile * ATT_TILE) // ATT_TILE


def attention_forward(qkv, lengths, heads):
    tiles = BLOCK // ATT_TILE

    def kernel(lengths_ref, q_ref, k_ref, v_ref, ctx_ref, lse_ref):
        tile = pl.program_id(1)
        queries = q_ref[...]
        start, first = tile_starts(lengths_ref, tile)

        def step(key_tile, carry):
            top, total, acc = carry
            rows = pl.ds(pl.multiple_of(key_tile * ATT_TILE, ATT_TILE), ATT_TILE)
            scores = dot_nt(queries, k_ref[rows, :]) * SCALE
            scores = jnp.where(tile_mask(start, tile, key_tile), scores, -1e30)
            new_top = jnp.maximum(top, jnp.max(scores, axis=1, keepdims=True))
            shrink = jnp.exp(top - new_top)
            weights = jnp.exp(scores - new_top)
            total = total * shrink + jnp.sum(weights, axis=1, keepdims=True)
            acc = acc * shrink + jnp.dot(
                weights.astype(jnp.bfloat16), v_ref[rows, :], preferred_element_type=jnp.float32
            )
            return (new_top, total, acc)

        begin = (
            jnp.full((ATT_TILE, 1), -1e30, jnp.float32),
            jnp.zeros((ATT_TILE, 1), jnp.float32),
            jnp.zeros((ATT_TILE, HEAD_DIM), jnp.float32),
        )
        begin = step(tile, begin)
        top, total, acc = lax.fori_loop(first, tile, step, begin)
        ctx_ref[...] = (acc / total).astype(jnp.bfloat16)
        lse_ref[...] = top + jnp.log(total)

    return pl.pallas_call(
        kernel,
        grid_spec=pltpu.PrefetchScalarGridSpec(
            num_scalar_prefetch=1,
            grid=(heads, tiles),
            in_specs=[
                pl.BlockSpec((ATT_TILE, HEAD_DIM), lambda h, i, first: (i, 3 * h)),
                pl.BlockSpec((BLOCK, HEAD_DIM), lambda h, i, first: (0, 3 * h + 1)),
                pl.BlockSpec((BLOCK, HEAD_DIM), lambda h, i, first: (0, 3 * h + 2)),
            ],
            out_specs=[
                pl.BlockSpec((ATT_TILE, HEAD_DIM), lambda h, i, first: (i, h)),
                pl.BlockSpec((pl.squeezed, ATT_TILE, 1), lambda h, i, first: (h, i, 0)),
            ],
        ),
        out_shape=[
            jax.ShapeDtypeStruct((BLOCK, heads * HEAD_DIM), jnp.bfloat16),
            jax.ShapeDtypeStruct((heads, BLOCK, 1), jnp.float32),
        ],
        compiler_params=pltpu.CompilerParams(vmem_limit_bytes=VMEM_LIMIT),
    )(lengths, qkv, qkv, qkv)


def attention_backward(qkv, lengths, heads, ctx, lse, grad_ctx, planes, before):
    tiles = BLOCK // ATT_TILE

    def kernel(
        lengths_ref, q_ref, k_ref, v_ref, ctx_ref, lse_ref, do_ref, cos_ref, below_ref,
        above_ref, *rest,
    ):
        out_ref, sums_ref, dk_ref, dv_ref = rest[len(before) :]
        tile = pl.program_id(1)

        @pl.when(tile == 0)
        def _():
            dk_ref[...] = jnp.zeros_like(dk_ref)
            dv_ref[...] = jnp.zeros_like(dv_ref)

        queries = q_ref[...]
        start, first = tile_starts(lengths_ref, tile)
        grads = do_ref[...]
        lse_rows = lse_ref[...]
        inner = jnp.sum(
            grads.astype(jnp.float32) * ctx_ref[...].astype(jnp.float32), axis=1, keepdims=True
        )

        def step(key_tile, dq):
            rows = pl.ds(pl.multiple_of(key_tile * ATT_TILE, ATT_TILE), ATT_TILE)
            keys = k_ref[rows, :]
            scores = dot_nt(queries, keys) * SCALE
            probs = jnp.where(
                tile_mask(start, tile, key_tile), jnp.exp(scores - lse_rows), 0.0
            )
            grad_probs = dot_nt(grads, v_ref[rows, :])
            grad_scores = (probs * (grad_probs - inner)).astype(jnp.bfloat16)
            dv_ref[rows, :] += dot_tn(probs.astype(jnp.bfloat16), grads)
            dk_ref[rows, :] += dot_tn(grad_scores, queries)
            return dq + jnp.dot(grad_scores, keys, preferred_element_type=jnp.float32)

        dq = lax.fori_loop(
            first, tile + 1, step, jnp.zeros((ATT_TILE, HEAD_DIM), jnp.float32)
        )
        here = pl.ds(pl.multiple_of(tile * ATT_TILE, ATT_TILE), ATT_TILE)
        out_ref[here, :HEAD_DIM] = turn(
            dq * SCALE, cos_ref[here, :], -below_ref[here, :], -above_ref[here, :]
        ).astype(jnp.bfloat16)

        @pl.when(tile == tiles - 1)
        def _():
            def finish(index, sums):
                rows = pl.ds(pl.multiple_of(index * ATT_TILE, ATT_TILE), ATT_TILE)
                out_ref[rows, HEAD_DIM : 2 * HEAD_DIM] = turn(
                    dk_ref[rows, :] * SCALE, cos_ref[rows, :], -below_ref[rows, :], -above_ref[rows, :]
                ).astype(jnp.bfloat16)
                out_ref[rows, 2 * HEAD_DIM :] = dv_ref[rows, :].astype(jnp.bfloat16)
                return sums + jnp.sum(out_ref[rows, :].astype(jnp.float32), axis=0, keepdims=True)

            sums_ref[...] = lax.fori_loop(
                0, tiles, finish, jnp.zeros((1, 3 * HEAD_DIM), jnp.float32)
            )

    whole = pl.BlockSpec((BLOCK, HEAD_DIM), lambda h, i, first: (0, 0))
    return pl.pallas_call(
        kernel,
        grid_spec=pltpu.PrefetchScalarGridSpec(
            num_scalar_prefetch=1,
            grid=(heads, tiles),
            in_specs=[
                pl.BlockSpec((ATT_TILE, HEAD_DIM), lambda h, i, first: (i, 3 * h)),
                pl.BlockSpec((BLOCK, HEAD_DIM), lambda h, i, first: (0, 3 * h + 1)),
                pl.BlockSpec((BLOCK, HEAD_DIM), lambda h, i, first: (0, 3 * h + 2)),
                pl.BlockSpec((ATT_TILE, HEAD_DIM), lambda h, i, first: (i, h)),
                pl.BlockSpec((pl.squeezed, ATT_TILE, 1), lambda h, i, first: (h, i, 0)),
                pl.BlockSpec((ATT_TILE, HEAD_DIM), lambda h, i, first: (i, h)),
                whole,
                whole,
                whole,
            ]
            + [pl.BlockSpec(memory_space=pl.ANY)] * len(before),
            out_specs=[
                pl.BlockSpec((BLOCK, 3 * HEAD_DIM), lambda h, i, first: (0, h)),
                pl.BlockSpec((pl.squeezed, 1, 3 * HEAD_DIM), lambda h, i, first: (h, 0, 0)),
            ],
            scratch_shapes=[
                pltpu.VMEM((BLOCK, HEAD_DIM), jnp.float32),
                pltpu.VMEM((BLOCK, HEAD_DIM), jnp.float32),
            ],
        ),
        out_shape=[
            jax.ShapeDtypeStruct((BLOCK, heads * 3 * HEAD_DIM), jnp.bfloat16),
            jax.ShapeDtypeStruct((heads, 1, 3 * HEAD_DIM), jnp.float32),
        ],
        compiler_params=pltpu.CompilerParams(vmem_limit_bytes=VMEM_LIMIT),
    )(lengths, qkv, qkv, qkv, ctx, lse, grad_ctx, *planes, *before)


def gather_cut(sizes):
    return (1792, 256) if sizes == (4, 2) else (D // 2, D // 2)


def scatter_cut(sizes):
    return (1664, 384) if sizes == (4, 2) else (D // 2, D // 2)


def columns_of(cut, kind):
    return pl.ds(0, cut[0]) if kind == 0 else pl.ds(cut[0], cut[1])


def tile_of(width):
    return 512 if width % 512 == 0 else 256 if width % 256 == 0 else 128


def span(index, size):
    return pl.ds(pl.multiple_of(index * size, size), size)


ANY = pl.BlockSpec(memory_space=pl.ANY)
VMEM = pl.BlockSpec(memory_space=pltpu.VMEM)
SMEM = pl.BlockSpec(memory_space=pltpu.SMEM)


def row_kernel(kernel, collective, out_shape, in_specs, out_specs, scratch, cost, before=()):
    def body(*refs):
        kernel(*refs[len(before):])

    def call(*args):
        return pl.pallas_call(
            body,
            out_shape=out_shape,
            in_specs=[ANY] * len(before) + in_specs,
            out_specs=out_specs,
            scratch_shapes=scratch,
            cost_estimate=pl.CostEstimate(flops=cost, bytes_accessed=2**28 if cost > 1 else 1, transcendentals=0),
            compiler_params=pltpu.CompilerParams(
                collective_id=collective, has_side_effects=True, vmem_limit_bytes=VMEM_LIMIT
            ),
        )(*before, *args)

    return call


def gather_scratch(sizes, rows):
    shards = sizes[0] * sizes[1]
    return [
        pltpu.VMEM((shards, rows, D), jnp.bfloat16),
        pltpu.SemaphoreType.DMA((gather_sends(sizes, HALVES),)),
        pltpu.SemaphoreType.DMA((2, HALVES, shards)),
    ]


def run_gather(grid, sizes, rows, full, send_sems, recv_sems, ready):
    cut = gather_cut(sizes)
    step = rows // HALVES
    sender = Sender(send_sems)

    def piece(slot, half, kind):
        return full.at[slot, pl.ds(half * step, step), columns_of(cut, kind)]

    gather_rounds(grid, sender, piece, recv_sems, HALVES, cut, ready)
    sender.finish()


def sum_scratch(sizes, rows):
    shards = sizes[0] * sizes[1]
    bufs, sems = scatter_scratch(sizes, HALVES, rows, D, scatter_cut(sizes))
    return (
        [pltpu.VMEM((shards, rows, D), jnp.bfloat16)]
        + bufs
        + sems
        + [pltpu.SemaphoreType.DMA((scatter_sends(sizes, HALVES),))]
    )


def run_scatter(grid, sizes, rows, scratch, produce, *hooks):
    cut = scatter_cut(sizes)
    step = rows // HALVES
    parts, b0, b1, b2, b3, s0, s1, s2, s3, send_sems = scratch
    sender = Sender(send_sems)

    def part(slot, half, kind):
        return parts.at[slot, pl.ds(half * step, step), columns_of(cut, kind)]

    scatter = Scatter(
        grid, sender, part, ((b0, b1), (b2, b3)), ((s0, s1), (s2, s3)), HALVES, cut
    )
    scatter.run(produce, *hooks)
    sender.finish()


def production_order(grid):
    return [
        grid.index(grid.nearest(0, k), grid.nearest(1, l))
        for action, k, l in [step for step in scatter_plan(grid.n) if step[0] == "make"]
    ]


ROW_TILE = 64


def tile_stats(values):
    centered = values - jnp.mean(values, axis=1, keepdims=True)
    inverse = lax.rsqrt(jnp.mean(centered * centered, axis=1, keepdims=True) + EPSILON)
    return centered, inverse


def open_rows(own, sizes, collective, norms, qkv_flat, qkv_bias, up_weight, up_bias, lengths):
    rows = own.shape[0]
    shards = sizes[0] * sizes[1]
    width, hidden = qkv_flat.shape[1], up_weight.shape[1]
    heads = width // (3 * HEAD_DIM)

    def kernel(
        own_ref, norms_ref, qkvw_any, qkvb_ref, upw_any, upb_ref, lengths_ref, freq_ref,
        plain_any, one_any, two_any, qkv_any, act_any, slope_any, cos_ref, below_ref, above_ref,
        full, send_sems, recv_sems, qkvw, upw, load_sems, plain, one, two, qkv, act, slope, out_sems,
    ):
        grid = Grid2(sizes)
        loads = [
            pltpu.make_async_copy(qkvw_any, qkvw, load_sems.at[0]),
            pltpu.make_async_copy(upw_any, upw, load_sems.at[1]),
        ]
        for copy in loads:
            copy.start()
        full[grid.index(*grid.me)] = own_ref[...]
        grid.barrier()
        open_copies = []

        def outs(place, slot):
            pairs = ((plain, plain_any), (one, one_any), (two, two_any), (qkv, qkv_any), (act, act_any), (slope, slope_any))
            return [
                pltpu.make_async_copy(here.at[slot], there.at[place], out_sems.at[slot, i])
                for i, (here, there) in enumerate(pairs)
            ]

        def ready(slow, fast, order):
            place = grid.index(slow, fast)
            slot = order % 2
            if order == 0:
                for copy in loads:
                    copy.wait()
            if order >= 2:
                for copy in open_copies.pop(0):
                    copy.wait()

            def norm_tile(index, _):
                here = span(index, ROW_TILE)
                centered, inverse = tile_stats(full[place, here].astype(jnp.float32))
                normed = centered * inverse
                plain[slot, here] = normed.astype(jnp.bfloat16)
                one[slot, here] = (normed * norms_ref[0:1] + norms_ref[1:2]).astype(jnp.bfloat16)
                two[slot, here] = (normed * norms_ref[2:3] + norms_ref[3:4]).astype(jnp.bfloat16)
                return _

            lax.fori_loop(0, rows // ROW_TILE, norm_tile, 0)
            places = pl.ds(pl.multiple_of(place * rows, rows), rows)
            row = place * rows + lax.broadcasted_iota(jnp.int32, (rows, 1), 0)
            cos, below, above = rotary_planes(row - first_rows(lengths_ref, row), freq_ref[...])
            cos_ref[places, :], below_ref[places, :], above_ref[places, :] = cos, below, above
            whole = jnp.dot(one[slot], qkvw[...], preferred_element_type=jnp.float32) + qkvb_ref[...]
            for head in range(heads):
                first = head * 3 * HEAD_DIM
                found = whole[:, first : first + 3 * HEAD_DIM]
                qkv[slot, :, first : first + HEAD_DIM] = turn(
                    found[:, :HEAD_DIM], cos, below, above
                ).astype(jnp.bfloat16)
                qkv[slot, :, first + HEAD_DIM : first + 2 * HEAD_DIM] = turn(
                    found[:, HEAD_DIM : 2 * HEAD_DIM], cos, below, above
                ).astype(jnp.bfloat16)
                qkv[slot, :, first + 2 * HEAD_DIM : first + 3 * HEAD_DIM] = found[
                    :, 2 * HEAD_DIM :
                ].astype(jnp.bfloat16)
            tile = tile_of(hidden)

            def up_tile(index, _):
                here = span(index, tile)
                pre = jnp.dot(two[slot], upw[:, here], preferred_element_type=jnp.float32) + upb_ref[:, here]
                share = 0.5 * (1.0 + lax.erf(pre * 0.7071067811865476))
                act[slot, :, here] = (pre * share).astype(jnp.bfloat16)
                slope[slot, :, here] = (
                    share + pre * (jnp.exp(-0.5 * pre * pre) * 0.3989422804014327)
                ).astype(jnp.bfloat16)
                return _

            lax.fori_loop(0, hidden // tile, up_tile, 0)
            copies = outs(place, slot)
            for copy in copies:
                copy.start()
            open_copies.append(copies)

        run_gather(grid, sizes, rows, full, send_sems, recv_sems, ready)
        for copies in open_copies:
            for copy in copies:
                copy.wait()

    def out(columns):
        return jax.ShapeDtypeStruct((shards, rows, columns), jnp.bfloat16)

    def staged(columns):
        return pltpu.VMEM((2, rows, columns), jnp.bfloat16)

    return row_kernel(
        kernel, collective,
        [out(D), out(D), out(D), out(width), out(hidden), out(hidden)]
        + [jax.ShapeDtypeStruct((shards * rows, HEAD_DIM), jnp.float32)] * 3,
        [VMEM, VMEM, ANY, VMEM, ANY, VMEM, SMEM, VMEM],
        [ANY] * 6 + [VMEM] * 3,
        gather_scratch(sizes, rows)
        + [
            pltpu.VMEM(qkv_flat.shape, jnp.bfloat16),
            pltpu.VMEM(up_weight.shape, jnp.bfloat16),
            pltpu.SemaphoreType.DMA((2,)),
            staged(D), staged(D), staged(D), staged(width), staged(hidden), staged(hidden),
            pltpu.SemaphoreType.DMA((2, 6)),
        ],
        2 * BLOCK * D * (width + hidden),
    )(own, norms, qkv_flat, qkv_bias, up_weight, up_bias, lengths, rotary_frequencies())


def branch_rows(own, ctx, act, out_flat, down_weight, norms, sizes, collective):
    rows = own.shape[0]
    shards = sizes[0] * sizes[1]
    inner, hidden = out_flat.shape[0], down_weight.shape[0]

    def kernel(
        own_ref, ctx_any, act_any, outw_any, downw_any, norms_ref, out_ref, final_ref, normed_ref, inverse_ref,
        ctx, act, outw, downw, load_sems, *scratch,
    ):
        grid = Grid2(sizes)
        parts = scratch[0]
        weights = [
            pltpu.make_async_copy(outw_any, outw, load_sems.at[0, 0]),
            pltpu.make_async_copy(downw_any, downw, load_sems.at[0, 1]),
        ]
        order = production_order(grid)
        loads = [
            [
                pltpu.make_async_copy(ctx_any.at[place], ctx.at[place], load_sems.at[1 + i, 0]),
                pltpu.make_async_copy(act_any.at[place], act.at[place], load_sems.at[1 + i, 1]),
            ]
            for i, place in enumerate(order)
        ]
        for copy in loads[0] + weights:
            copy.start()
        for copies in loads[1:]:
            for copy in copies:
                copy.start()
        grid.barrier()
        for copy in weights:
            copy.wait()

        def produce(slow, fast):
            place = grid.index(slow, fast)
            for copy in loads.pop(0):
                copy.wait()

            def columns(index, _):
                here = span(index, 512)
                parts[place, :, here] = (
                    jnp.dot(ctx[place], outw[:, here], preferred_element_type=jnp.float32)
                    + jnp.dot(act[place], downw[:, here], preferred_element_type=jnp.float32)
                ).astype(jnp.bfloat16)
                return _

            lax.fori_loop(0, D // 512, columns, 0)

        run_scatter(grid, sizes, rows, scratch, produce)
        mine = grid.index(*grid.me)

        def norm_tile(index, _):
            here = span(index, ROW_TILE)
            stream = own_ref[here].astype(jnp.float32) + parts[mine, here].astype(jnp.float32) + norms_ref[2:3]
            out_ref[here] = stream.astype(jnp.bfloat16)
            centered, inverse = tile_stats(stream)
            normed = centered * inverse
            final_ref[here] = (normed * norms_ref[0:1] + norms_ref[1:2]).astype(jnp.bfloat16)
            normed_ref[here] = normed
            inverse_ref[here] = inverse
            return _

        lax.fori_loop(0, rows // ROW_TILE, norm_tile, 0)

    return row_kernel(
        kernel, collective,
        [
            jax.ShapeDtypeStruct((rows, D), jnp.bfloat16),
            jax.ShapeDtypeStruct((rows, D), jnp.bfloat16),
            jax.ShapeDtypeStruct((rows, D), jnp.float32),
            jax.ShapeDtypeStruct((rows, 1), jnp.float32),
        ],
        [VMEM, ANY, ANY, ANY, ANY, VMEM],
        [VMEM] * 4,
        [
            pltpu.VMEM(ctx.shape, jnp.bfloat16),
            pltpu.VMEM(act.shape, jnp.bfloat16),
            pltpu.VMEM(out_flat.shape, jnp.bfloat16),
            pltpu.VMEM(down_weight.shape, jnp.bfloat16),
            pltpu.SemaphoreType.DMA((1 + shards, 2)),
        ]
        + sum_scratch(sizes, rows),
        2 * BLOCK * D * (inner + hidden),
    )(own, ctx, act, out_flat, down_weight, norms)


def logit_rows(final, head_weight, targets_col, sizes, collective):
    rows = final.shape[0]
    shards = sizes[0] * sizes[1]
    vocab = head_weight.shape[1]

    def kernel(
        own_ref, headw_any, target_ref, final_any, weights_any, stats_ref,
        full, send_sems, recv_sems, headw, load_sem, logits, weights, out_sems, row_sems,
    ):
        grid = Grid2(sizes)
        load = pltpu.make_async_copy(headw_any, headw, load_sem)
        load.start()
        full[grid.index(*grid.me)] = own_ref[...]
        grid.barrier()
        base = lax.axis_index("seq") * vocab
        open_copies, raw_copies = [], []

        def ready(slow, fast, order):
            place = grid.index(slow, fast)
            slot = order % 2
            if order == 0:
                load.wait()
            if order >= 2:
                open_copies.pop(0).wait()
            places = pl.ds(pl.multiple_of(place * rows, rows), rows)
            target = target_ref[places, :] - base

            def fold(values, join):
                total = values[:, :128]
                for first in range(128, values.shape[1], 128):
                    total = join(total, values[:, first : first + 128])
                return total

            def logit_tile(start, size, carry):
                top, pick = carry
                here = pl.ds(start, size)
                found = jnp.dot(full[place], headw[:, here], preferred_element_type=jnp.float32)
                logits[:, here] = found
                ids = start + lax.broadcasted_iota(jnp.int32, (rows, size), 1)
                top = jnp.maximum(top, fold(found, jnp.maximum))
                pick = pick + fold(jnp.where(ids == target, found, 0.0), jnp.add)
                return (top, pick)

            def tiled(step, carry):
                count = vocab // 512
                carry = lax.fori_loop(
                    0, count, lambda i, c: step(pl.multiple_of(i * 512, 512), 512, c), carry
                )
                if vocab % 512:
                    carry = step(count * 512, vocab % 512, carry)
                return carry

            top, pick = tiled(
                logit_tile,
                (jnp.full((rows, 128), -jnp.inf, jnp.float32), jnp.zeros((rows, 128), jnp.float32)),
            )
            top = jnp.max(top, axis=1, keepdims=True)
            pick = jnp.sum(pick, axis=1, keepdims=True)

            def weight_tile(start, size, total):
                here = pl.ds(start, size)
                found = jnp.exp(logits[:, here] - top)
                weights[slot, :, here] = found.astype(jnp.bfloat16)
                return total + fold(found, jnp.add)

            total = tiled(weight_tile, jnp.zeros((rows, 128), jnp.float32))
            total = jnp.sum(total, axis=1, keepdims=True)
            lane = lax.broadcasted_iota(jnp.int32, (rows, 128), 1)
            found = jnp.where(lane == 0, top, jnp.where(lane == 1, total, pick))
            stats_ref[:, places] = found.T[0:8]
            copy = pltpu.make_async_copy(weights.at[slot], weights_any.at[place], out_sems.at[slot])
            copy.start()
            open_copies.append(copy)
            raw = pltpu.make_async_copy(full.at[place], final_any.at[place], row_sems.at[order])
            raw.start()
            raw_copies.append(raw)

        run_gather(grid, sizes, rows, full, send_sems, recv_sems, ready)
        for copy in open_copies + raw_copies:
            copy.wait()

    return row_kernel(
        kernel, collective,
        [
            jax.ShapeDtypeStruct((shards, rows, D), jnp.bfloat16),
            jax.ShapeDtypeStruct((shards, rows, vocab), jnp.bfloat16),
            jax.ShapeDtypeStruct((8, shards * rows), jnp.float32),
        ],
        [VMEM, ANY, VMEM],
        [ANY, ANY, VMEM],
        gather_scratch(sizes, rows)
        + [
            pltpu.VMEM(head_weight.shape, jnp.bfloat16),
            pltpu.SemaphoreType.DMA,
            pltpu.VMEM((rows, vocab), jnp.float32),
            pltpu.VMEM((2, rows, vocab), jnp.bfloat16),
            pltpu.SemaphoreType.DMA((2,)),
            pltpu.SemaphoreType.DMA((shards,)),
        ],
        2 * BLOCK * D * vocab,
    )(final, head_weight, targets_col)


def final_grad_rows(grad_logits, head_weight, normed, inverse, gain, sizes, collective, before):
    shards, rows, vocab = grad_logits.shape

    def kernel(
        grads_any, headw_any, normed_ref, inverse_ref, gain_ref, stream_ref, down_ref, sums_ref,
        headw, grads, load_sems, *scratch,
    ):
        grid = Grid2(sizes)
        parts = scratch[0]
        order = production_order(grid)
        loads = [
            pltpu.make_async_copy(grads_any.at[place], grads.at[i % 2], load_sems.at[i])
            for i, place in enumerate(order)
        ]
        tile = 512
        weights = [
            pltpu.make_async_copy(
                headw_any.at[pl.ds(i * tile, tile)], headw.at[pl.ds(i * tile, tile)], load_sems.at[1 + shards + i]
            )
            for i in range(D // tile)
        ]
        loads[0].start()
        for copy in weights:
            copy.start()
        grid.barrier()
        count = [0]

        def produce(slow, fast):
            place = grid.index(slow, fast)
            i = count[0]
            count[0] += 1
            if i + 1 < shards:
                loads[i + 1].start()
            loads[i].wait()

            def columns(index, _):
                here = span(index, tile)
                parts[place, :, here] = dot_nt(grads[i % 2], headw[here, :]).astype(jnp.bfloat16)
                return _

            if i == 0:
                for index, copy in enumerate(weights):
                    copy.wait()
                    columns(index, 0)
            else:
                lax.fori_loop(0, D // tile, columns, 0)

        run_scatter(grid, sizes, rows, scratch, produce)
        mine = grid.index(*grid.me)
        sums_ref[...] = jnp.zeros_like(sums_ref)

        def norm_tile(index, _):
            here = span(index, ROW_TILE)
            grad = parts[mine, here].astype(jnp.float32)
            norm = normed_ref[here]
            scaled = grad * gain_ref[...]
            stream = inverse_ref[here] * (
                scaled
                - jnp.mean(scaled, axis=1, keepdims=True)
                - norm * jnp.mean(scaled * norm, axis=1, keepdims=True)
            )
            stream_ref[here] = stream
            down_ref[here] = stream.astype(jnp.bfloat16)
            sums_ref[0:1] += jnp.sum(grad * norm, axis=0, keepdims=True)
            sums_ref[1:2] += jnp.sum(grad, axis=0, keepdims=True)
            sums_ref[2:3] += jnp.sum(stream, axis=0, keepdims=True)
            return _

        lax.fori_loop(0, rows // ROW_TILE, norm_tile, 0)

    return row_kernel(
        kernel, collective,
        [
            jax.ShapeDtypeStruct((rows, D), jnp.float32),
            jax.ShapeDtypeStruct((rows, D), jnp.bfloat16),
            jax.ShapeDtypeStruct((8, D), jnp.float32),
        ],
        [ANY, ANY, VMEM, VMEM, VMEM],
        [VMEM] * 3,
        [
            pltpu.VMEM(head_weight.shape, jnp.bfloat16),
            pltpu.VMEM((2, rows, vocab), jnp.bfloat16),
            pltpu.SemaphoreType.DMA((1 + shards + D // 512,)),
        ]
        + sum_scratch(sizes, rows),
        2 * BLOCK * D * vocab,
        before,
    )(grad_logits, head_weight, normed, inverse, gain)


def branch_grad_rows(own, out_flat, down_weight, slope, sizes, collective):
    rows = own.shape[0]
    shards = sizes[0] * sizes[1]
    inner, hidden = out_flat.shape[0], down_weight.shape[0]

    def kernel(
        own_ref, outw_any, downw_any, slope_any, rows_any, ctx_any, up_any, sums_ref,
        full, send_sems, recv_sems, outw, downw, load_sems, slope, slope_sems, ctx, up, out_sems, row_sems,
    ):
        grid = Grid2(sizes)
        loads = [
            pltpu.make_async_copy(outw_any, outw, load_sems.at[0]),
            pltpu.make_async_copy(downw_any, downw, load_sems.at[1]),
        ]
        for copy in loads:
            copy.start()
        slopes = pltpu.make_async_copy(slope_any, slope, slope_sems)
        slopes.start()
        full[grid.index(*grid.me)] = own_ref[...]
        sums_ref[...] = jnp.zeros_like(sums_ref)
        grid.barrier()
        open_copies, raw_copies = [], []

        def ready(slow, fast, order):
            place = grid.index(slow, fast)
            slot = order % 2
            if order == 0:
                for copy in loads + [slopes]:
                    copy.wait()
            if order >= 2:
                for copy in open_copies.pop(0):
                    copy.wait()
            ctx[slot] = dot_nt(full[place], outw[...]).astype(jnp.bfloat16)
            tile = tile_of(hidden)

            def up_tile(index, _):
                here = span(index, tile)
                found = dot_nt(full[place], downw[here, :]) * slope[place, :, here].astype(jnp.float32)
                rounded = found.astype(jnp.bfloat16)
                up[slot, :, here] = rounded
                sums_ref[0:1, here] += jnp.sum(rounded.astype(jnp.float32), axis=0, keepdims=True)
                return _

            lax.fori_loop(0, hidden // tile, up_tile, 0)
            copies = [
                pltpu.make_async_copy(ctx.at[slot], ctx_any.at[place], out_sems.at[slot, 0]),
                pltpu.make_async_copy(up.at[slot], up_any.at[place], out_sems.at[slot, 1]),
            ]
            for copy in copies:
                copy.start()
            open_copies.append(copies)
            raw = pltpu.make_async_copy(full.at[place], rows_any.at[place], row_sems.at[order])
            raw.start()
            raw_copies.append(raw)

        run_gather(grid, sizes, rows, full, send_sems, recv_sems, ready)
        for copies in open_copies:
            for copy in copies:
                copy.wait()
        for copy in raw_copies:
            copy.wait()

    def out(columns):
        return jax.ShapeDtypeStruct((shards, rows, columns), jnp.bfloat16)

    return row_kernel(
        kernel, collective,
        [out(D), out(inner), out(hidden), jax.ShapeDtypeStruct((8, hidden), jnp.float32)],
        [VMEM, ANY, ANY, ANY],
        [ANY, ANY, ANY, VMEM],
        gather_scratch(sizes, rows)
        + [
            pltpu.VMEM(out_flat.shape, jnp.bfloat16),
            pltpu.VMEM(down_weight.shape, jnp.bfloat16),
            pltpu.SemaphoreType.DMA((2,)),
            pltpu.VMEM((shards, rows, hidden), jnp.bfloat16),
            pltpu.SemaphoreType.DMA,
            pltpu.VMEM((2, rows, inner), jnp.bfloat16),
            pltpu.VMEM((2, rows, hidden), jnp.bfloat16),
            pltpu.SemaphoreType.DMA((2, 2)),
            pltpu.SemaphoreType.DMA((shards,)),
        ],
        2 * BLOCK * D * (inner + hidden),
    )(own, out_flat, down_weight, slope)


class SmallSum:
    def __init__(self, shards, sums, total, scratch):
        self.shards, self.sums, self.total = shards, sums, total
        self.came, self.spread_send, self.spread_recv, self.back_send, self.back_recv = scratch
        self.here = lax.axis_index("seq")
        self.width = D // shards
        self.others = [(step, lax.rem(self.here + step, shards)) for step in range(1, shards)]

    @staticmethod
    def scratch(shards):
        dma = pltpu.SemaphoreType.DMA
        return [pltpu.VMEM((shards, 8, D // shards), jnp.float32)] + [dma((shards,))] * 4

    def barrier(self):
        sem = pltpu.get_barrier_semaphore()
        for _, place in self.others:
            pl.semaphore_signal(sem, inc=1, device_id={"seq": place}, device_id_type=MESH)
        pl.semaphore_wait(sem, self.shards - 1)

    def copy(self, place, src, dst, send, recv):
        return pltpu.make_async_remote_copy(
            src_ref=src, dst_ref=dst, send_sem=send, recv_sem=recv, device_id={"seq": place}, device_id_type=MESH
        )

    def columns(self, place):
        return pl.ds(pl.multiple_of(place * self.width, self.width), self.width)

    def spread(self):
        self.first = [
            self.copy(
                place, self.sums.at[:, self.columns(place)], self.came.at[step], self.spread_send.at[step],
                self.spread_recv.at[step],
            )
            for step, place in self.others
        ]
        for copy in self.first:
            copy.start()

    def collect(self):
        here = self.columns(self.here)
        total = self.sums[:, here]
        for (step, _), copy in zip(self.others, self.first):
            copy.wait_recv()
            total = total + self.came[step]
        self.total[:, here] = total
        self.second = [
            self.copy(
                place, self.total.at[:, here], self.total.at[:, here], self.back_send.at[step], self.back_recv.at[step]
            )
            for step, place in self.others
        ]
        for copy in self.second:
            copy.start()

    def finish(self):
        for step, _ in self.others:
            source = lax.rem(self.here + self.shards - step, self.shards)
            there = self.total.at[:, self.columns(source)]
            self.copy(source, there, there, self.back_send.at[step], self.back_recv.at[step]).wait_recv()
        for copy in self.first + self.second:
            copy.wait_send()


def score_rows(stats, lengths, labels, reference, sizes, replicas, collective):
    shards = sizes[0] * sizes[1]
    width = BLOCK // shards

    def kernel(
        stats_ref, lengths_ref, labels_ref, reference_ref, coef_ref, losses_ref,
        came, full, ratio, ratios, spread_send, spread_recv, back_send, back_recv, cross_send, cross_recv,
    ):
        seq, dp = lax.axis_index("seq"), lax.axis_index("dp")
        peers = {
            "seq": [(step, lax.rem(seq + step, shards)) for step in range(1, shards)],
            "dp": [(step, lax.rem(dp + step, replicas)) for step in range(1, replicas)],
        }
        barrier = pltpu.get_barrier_semaphore()
        for axis in peers:
            for _, place in peers[axis]:
                pl.semaphore_signal(barrier, inc=1, device_id={axis: place}, device_id_type=MESH)
        pl.semaphore_wait(barrier, shards + replicas - 2)

        def columns(place):
            return pl.ds(pl.multiple_of(place * width, width), width)

        def copy(axis, place, src, dst, send, recv):
            return pltpu.make_async_remote_copy(
                src_ref=src, dst_ref=dst, send_sem=send, recv_sem=recv, device_id={axis: place}, device_id_type=MESH
            )

        sent = [
            copy("seq", place, stats_ref.at[:, columns(place)], came.at[step], spread_send.at[step], spread_recv.at[step])
            for step, place in peers["seq"]
        ]
        for one in sent:
            one.start()
        mine = stats_ref[:, columns(seq)]
        top, total, pick = mine[0:1], mine[1:2], mine[2:3]
        for (step, _), one in zip(peers["seq"], sent):
            one.wait_recv()
            other = came[step]
            joint = jnp.maximum(top, other[0:1])
            total = total * jnp.exp(top - joint) + other[1:2] * jnp.exp(other[0:1] - joint)
            pick = pick + other[2:3]
            top = joint
        log_total = top + jnp.log(total)
        here = columns(seq)
        full[0:1, here] = log_total
        full[1:2, here] = pick - log_total
        back = [
            copy("seq", place, full.at[:, here], full.at[:, here], back_send.at[step], back_recv.at[step])
            for step, place in peers["seq"]
        ]
        for one in back:
            one.start()
        for step, _ in peers["seq"]:
            source = lax.rem(seq + shards - step, shards)
            there = full.at[:, columns(source)]
            copy("seq", source, there, there, back_send.at[step], back_recv.at[step]).wait_recv()
        example = lax.broadcasted_iota(jnp.int32, (EXB, 1), 0)
        start, end = jnp.zeros_like(example), jnp.zeros_like(example)
        sign, reference = jnp.zeros((EXB, 1), jnp.float32), jnp.zeros((EXB, 1), jnp.float32)
        reached = jnp.int32(0)
        for index in range(EXB):
            start = jnp.where(example == index, reached, start)
            reached = reached + lengths_ref[index]
            end = jnp.where(example == index, reached, end)
            sign = jnp.where(example == index, (2 * labels_ref[index] - 1).astype(jnp.float32), sign)
            reference = jnp.where(example == index, reference_ref[index], reference)
        counts = (end - start).astype(jnp.float32)
        row = lax.broadcasted_iota(jnp.int32, (EXB, BLOCK), 1)
        member = (row >= start) & (row < end)
        mean = jnp.sum(jnp.where(member, full[1:2, :], 0.0), axis=1, keepdims=True) / counts
        log_ratio = mean - reference
        ratio[...] = jnp.broadcast_to(jnp.sum(log_ratio, axis=0, keepdims=True), ratio.shape)
        crossed = [
            copy("dp", place, ratio, ratios.at[dp], cross_send.at[step], cross_recv.at[step])
            for step, place in peers["dp"]
        ]
        for one in crossed:
            one.start()
        for one in crossed:
            one.wait_recv()
        ratios[dp] = ratio[...]
        whole = ratios[0]
        for place in range(1, replicas):
            whole = whole + ratios[place]
        center = whole[:, 0:1] / (replicas * EXB)
        squashed = jax.nn.sigmoid(BETA * sign * (log_ratio - center))
        losses_ref[...] = jnp.broadcast_to(1.0 - squashed, losses_ref.shape)
        grad = -LOSS_SCALE * BETA * sign * squashed * (1.0 - squashed) / counts
        token = jnp.sum(jnp.where(member, grad, 0.0), axis=0, keepdims=True)
        coef_ref[...] = jnp.zeros_like(coef_ref)
        coef_ref[0:1, :] = token
        coef_ref[1:2, :] = token * jnp.exp(stats_ref[0:1, :] - full[0:1, :])
        for one in sent + back + crossed:
            one.wait_send()

    dma = pltpu.SemaphoreType.DMA
    return pl.pallas_call(
        kernel,
        out_shape=[
            jax.ShapeDtypeStruct((8, BLOCK), jnp.float32),
            jax.ShapeDtypeStruct((EXB, 128), jnp.float32),
        ],
        in_specs=[VMEM] + [SMEM] * 3,
        out_specs=[VMEM] * 2,
        scratch_shapes=[
            pltpu.VMEM((shards, 8, width), jnp.float32),
            pltpu.VMEM((8, BLOCK), jnp.float32),
            pltpu.VMEM((EXB, 128), jnp.float32),
            pltpu.VMEM((replicas, EXB, 128), jnp.float32),
            dma((shards,)), dma((shards,)), dma((shards,)), dma((shards,)), dma((replicas,)), dma((replicas,)),
        ],
        compiler_params=pltpu.CompilerParams(collective_id=collective, has_side_effects=True),
    )(stats, lengths, labels, reference)


def input_grad_rows(
    own, grad_stream, plain, grad_qkv, grad_up, qkv_flat, up_weight, gains, end_sums, sizes, collective,
    before,
):
    shards, rows, width = grad_qkv.shape
    hidden = grad_up.shape[2]

    def kernel(
        own_ref, stream_ref, normed_any, qkv_any, up_any, qkvw_any, upw_any, gains_ref, end_ref,
        out_ref, total_ref,
        qkvw, upw, weight_sems, normed, qkv, up, load_sems, sums_ref, *scratch,
    ):
        grid = Grid2(sizes)
        small = SmallSum(shards, sums_ref, total_ref, scratch[:5])
        scratch = scratch[5:]
        parts = scratch[0]
        order = production_order(grid)

        def loads(i):
            place = order[i]
            return [
                pltpu.make_async_copy(normed_any.at[place], normed.at[i % 2], load_sems.at[i, 0]),
                pltpu.make_async_copy(qkv_any.at[place], qkv.at[i % 2], load_sems.at[i, 1]),
                pltpu.make_async_copy(up_any.at[place], up.at[i % 2], load_sems.at[i, 2]),
            ]

        copies = [loads(i) for i in range(shards)]
        weights = [
            pltpu.make_async_copy(qkvw_any, qkvw, weight_sems.at[0]),
            pltpu.make_async_copy(upw_any, upw, weight_sems.at[1]),
        ]
        for copy in copies[0] + weights:
            copy.start()
        sums_ref[...] = jnp.zeros_like(sums_ref)
        small.barrier()
        for copy in weights:
            copy.wait()
        count = [0]

        def produce(slow, fast):
            place = grid.index(slow, fast)
            i = count[0]
            count[0] += 1
            if i + 1 < shards:
                for copy in copies[i + 1]:
                    copy.start()
            for copy in copies[i]:
                copy.wait()
            slot = i % 2

            def columns(index, _):
                here = span(index, 512)
                one = dot_nt(qkv[slot], qkvw[here, :])
                two = dot_nt(up[slot], upw[here, :])
                norm = normed[slot, :, here].astype(jnp.float32)
                parts[place, :, here] = (one * gains_ref[0:1, here] + two * gains_ref[1:2, here]).astype(
                    jnp.bfloat16
                )
                sums_ref[0:1, here] += jnp.sum(one * norm, axis=0, keepdims=True)
                sums_ref[1:2, here] += jnp.sum(one, axis=0, keepdims=True)
                sums_ref[2:3, here] += jnp.sum(two * norm, axis=0, keepdims=True)
                sums_ref[3:4, here] += jnp.sum(two, axis=0, keepdims=True)
                return _

            lax.fori_loop(0, D // 512, columns, 0)

        def made():
            sums_ref[4:8] = end_ref[0:4]
            small.spread()

        run_scatter(grid, sizes, rows, scratch, produce, made, lambda: None, small.collect)
        mine = grid.index(*grid.me)

        def norm_tile(index, _):
            here = span(index, ROW_TILE)
            grad = parts[mine, here].astype(jnp.float32)
            centered, inverse = tile_stats(own_ref[here].astype(jnp.float32))
            normed = centered * inverse
            out_ref[here] = stream_ref[here] + inverse * (
                grad
                - jnp.mean(grad, axis=1, keepdims=True)
                - normed * jnp.mean(grad * normed, axis=1, keepdims=True)
            )
            return _

        lax.fori_loop(0, rows // ROW_TILE, norm_tile, 0)
        small.finish()

    return row_kernel(
        kernel, collective,
        [jax.ShapeDtypeStruct((rows, D), jnp.float32), jax.ShapeDtypeStruct((8, D), jnp.float32)],
        [VMEM, VMEM, ANY, ANY, ANY, ANY, ANY, VMEM, VMEM],
        [VMEM, VMEM],
        [
            pltpu.VMEM(qkv_flat.shape, jnp.bfloat16),
            pltpu.VMEM(up_weight.shape, jnp.bfloat16),
            pltpu.SemaphoreType.DMA((2,)),
            pltpu.VMEM((2, rows, D), jnp.bfloat16),
            pltpu.VMEM((2, rows, width), jnp.bfloat16),
            pltpu.VMEM((2, rows, hidden), jnp.bfloat16),
            pltpu.SemaphoreType.DMA((shards, 3)),
            pltpu.VMEM((8, D), jnp.float32),
        ]
        + SmallSum.scratch(shards)
        + sum_scratch(sizes, rows),
        1,
        before,
    )(own, grad_stream, plain, grad_qkv, grad_up, qkv_flat, up_weight, gains, end_sums)


def join_halves(sums, others, earlier):
    steps, count = 8, len(sums)

    def kernel(*refs):
        for i in range(count):
            refs[2 * count + 1 + i][...] = (
                refs[i][...].astype(jnp.float32) + refs[count + i][...].astype(jnp.float32)
            ).astype(jnp.bfloat16)

    specs = [pl.BlockSpec((v.shape[0] // steps, v.shape[1]), lambda i: (i, 0)) for v in sums]
    return pl.pallas_call(
        kernel,
        grid=(steps,),
        out_shape=[jax.ShapeDtypeStruct(v.shape, jnp.bfloat16) for v in sums],
        in_specs=specs + specs + [ANY],
        out_specs=specs,
        compiler_params=pltpu.CompilerParams(vmem_limit_bytes=VMEM_LIMIT),
    )(*sums, *others, earlier)


def settle_halves(core, totals, backs, shapes, before=()):
    steps = 8

    def kernel(core_ref, *refs):
        count = len(totals)
        mine = pl.program_id(0) == 0
        for i in range(count):
            found = jnp.where(mine, refs[i][...].astype(jnp.float32), refs[count + i][...].astype(jnp.float32))
            out = refs[2 * count + len(before) + i]
            if len(out.shape) == 3:
                for head in range(out.shape[1]):
                    out[:, head, :] = found[:, head * out.shape[2] : (head + 1) * out.shape[2]]
            else:
                out[...] = found

    def place(half, core_ref):
        return jnp.where(half == 0, core_ref[0], 1 - core_ref[0])

    ins, outs = [], []
    for which in (0, 1):
        for value in totals:
            ins.append(
                pl.BlockSpec(
                    (value.shape[0] // steps, value.shape[1]),
                    (lambda h, i, core_ref: (jnp.where(h == 0, i, steps - 1), 0))
                    if which == 0
                    else (lambda h, i, core_ref: (jnp.where(h == 0, 0, i), 0)),
                )
            )
    for value, shape in zip(totals, shapes):
        rows = value.shape[0] // steps
        if len(shape) == 3:
            outs.append(
                pl.BlockSpec((rows,) + shape[1:], lambda h, i, core_ref: (place(h, core_ref) * steps + i, 0, 0))
            )
        elif shape[0] == value.shape[0]:
            outs.append(pl.BlockSpec((rows, value.shape[1]), lambda h, i, core_ref: (i, place(h, core_ref))))
        else:
            outs.append(pl.BlockSpec((rows, shape[1]), lambda h, i, core_ref: (place(h, core_ref) * steps + i, 0)))
    return pl.pallas_call(
        kernel,
        grid_spec=pltpu.PrefetchScalarGridSpec(
            num_scalar_prefetch=1, grid=(2, steps), in_specs=ins + [ANY] * len(before), out_specs=outs
        ),
        out_shape=[jax.ShapeDtypeStruct(shape, jnp.float32) for shape in shapes],
        compiler_params=pltpu.CompilerParams(vmem_limit_bytes=VMEM_LIMIT),
    )(core, *totals, *backs, *before)


def row_of(vector):
    return vector.astype(jnp.float32)[None, :]


def held(values):
    return lax.optimization_barrier(values)


def half_of(values, which):
    half = values.shape[1] // 2
    return lax.dynamic_slice_in_dim(values, which * half, half, 1)


def pairs(step):
    return [(place, place ^ step) for place in range(lax.axis_size("dp"))]


class PairSum:
    def __init__(self, product=None, made=None):
        self.plain = lax.axis_size("dp") != 4
        self.core = lax.rem(lax.axis_index("dp"), 2)
        if made is None:
            away = product(1 - self.core).astype(jnp.bfloat16)
            came = lax.ppermute(away, "dp", pairs(1))
            mine = held(product(self.core))
            made = (mine + came.astype(jnp.float32)).astype(jnp.bfloat16)
        self.sum = made

    def cross(self):
        if self.plain:
            none = jnp.zeros_like(self.sum)
            both = jnp.stack([jnp.where(self.core == which, self.sum, none) for which in (0, 1)])
            self.other = lax.psum(both, "dp")
        else:
            self.other = lax.ppermute(self.sum, "dp", pairs(2))
        return self

    def join(self):
        if self.plain:
            self.total = self.other
        else:
            self.total = (self.sum.astype(jnp.float32) + self.other.astype(jnp.float32)).astype(jnp.bfloat16)
        return self


def sum_over_dp(values):
    if lax.axis_size("dp") != 4:
        return lax.psum(values, "dp")
    for step in (1, 2):
        values = values + lax.ppermute(values, "dp", pairs(step))
    return values


def join_all(sums, earlier):
    if not sums[0].plain:
        totals = join_halves([one.sum for one in sums], [one.other for one in sums], earlier)
        for one, total in zip(sums, totals):
            one.total = total


def settle_all(sums, shapes, before=()):
    if sums[0].plain:
        core = jnp.zeros((1,), jnp.int32)
        return settle_halves(core, [s.other[0] for s in sums], [s.other[1] for s in sums], shapes, before)
    backs = [lax.ppermute(one.total, "dp", pairs(1)) for one in sums]
    return settle_halves(sums[0].core[None], [one.total for one in sums], backs, shapes, before)


def per_device(
    hidden, targets, lengths, labels, ref_logps, ln1_gain, ln1_bias, ln2_gain, ln2_bias, qkv_weight, qv_bias,
    out_weight, up_weight, up_bias, down_weight, branch_bias, lnf_gain, lnf_bias, head_weight,
):
    sizes = lines_of(lax.axis_size("seq"))
    own = hidden[0]
    local_heads = qkv_weight.shape[1]
    local_vocab = head_weight.shape[1]
    local_hidden = up_weight.shape[1]
    width = local_heads * 3 * HEAD_DIM
    inner = local_heads * HEAD_DIM
    qv_float = qv_bias.astype(jnp.float32)
    full_bias = jnp.concatenate(
        [qv_float[:, :HEAD_DIM], jnp.zeros_like(qv_float[:, :HEAD_DIM]), qv_float[:, HEAD_DIM:]], axis=-1
    ).reshape(1, width)
    qkv_flat = qkv_weight.reshape(D, width)
    out_flat = out_weight.reshape(inner, D)
    block_lengths = lengths[0]
    norms = jnp.concatenate([row_of(v) for v in (ln1_gain, ln1_bias, ln2_gain, ln2_bias)], axis=0)
    plain, first_full, second_full, qkv, act, slope, *planes = open_rows(
        own, sizes, 0, norms, qkv_flat, full_bias, up_weight, row_of(up_bias), block_lengths
    )
    flat_qkv = qkv.reshape(BLOCK, width)
    ctx, lse = attention_forward(flat_qkv, block_lengths, local_heads)
    shards, rows = plain.shape[0], plain.shape[1]
    end_norms = jnp.concatenate([row_of(v) for v in (lnf_gain, lnf_bias, branch_bias)], axis=0)
    output, final, normed, inverse = branch_rows(
        own, ctx.reshape(shards, rows, inner), act, out_flat, down_weight, end_norms, sizes, 1
    )
    targets_col = targets[0][:, None]
    final_full, weights, stats = logit_rows(final, head_weight, targets_col, sizes, 2)

    coef, losses = score_rows(
        stats, block_lengths, labels[0], ref_logps[0], sizes, lax.axis_size("dp"), 6
    )
    vocab_ids = lax.axis_index("seq") * local_vocab + jnp.arange(local_vocab, dtype=jnp.int32)
    grad_logits = held((
        jnp.where(vocab_ids[None, :] == targets[0][:, None], coef[0][:, None], 0.0)
        - weights.reshape(BLOCK, local_vocab).astype(jnp.float32) * coef[1][:, None]
    ).astype(jnp.bfloat16))
    final_rows = final_full.reshape(BLOCK, D)
    head_sum = PairSum(lambda which: dot_tn(half_of(final_rows, which), grad_logits)).cross()

    grad_stream, grad_own, end_sums = final_grad_rows(
        grad_logits.reshape(shards, rows, local_vocab), head_weight, normed, inverse, row_of(lnf_gain), sizes, 3,
        (head_sum.sum,),
    )
    grad_full, grad_ctx, grad_up, up_sums = branch_grad_rows(
        grad_own, out_flat, down_weight, slope, sizes, 4
    )
    grad_rows = grad_full.reshape(BLOCK, D)
    act_rows = act.reshape(BLOCK, local_hidden)
    second_rows = second_full.reshape(BLOCK, D)
    up_rows = grad_up.reshape(BLOCK, local_hidden)
    sums = [
        PairSum(lambda which: dot_tn(ctx, half_of(grad_rows, which))),
        PairSum(lambda which: dot_tn(act_rows, half_of(grad_rows, which))),
        PairSum(lambda which: dot_tn(half_of(second_rows, which), up_rows)),
    ]
    for one in sums:
        one.cross()
    made = [one.sum for one in sums]
    grad_qkv, qkv_sums = attention_backward(
        flat_qkv, block_lengths, local_heads, ctx, lse, grad_ctx.reshape(BLOCK, inner), planes,
        made,
    )
    first_rows = first_full.reshape(BLOCK, D)
    sums.append(PairSum(lambda which: dot_tn(half_of(first_rows, which), grad_qkv)))
    sums[-1].cross()
    qkv_sums = qkv_sums[:, 0]
    qv_grad = jnp.concatenate([qkv_sums[:, :HEAD_DIM], qkv_sums[:, 2 * HEAD_DIM :]], axis=-1)
    split = local_heads * 2 * HEAD_DIM
    biases = jnp.concatenate([qv_grad.reshape(-1), up_sums[0]])
    biases = jnp.pad(biases[None, :], ((0, 0), (0, D - biases.shape[0])))
    gains = jnp.concatenate([row_of(ln1_gain), row_of(ln2_gain)], axis=0)
    grad_input, group_sums = input_grad_rows(
        own, grad_stream, plain, grad_qkv.reshape(shards, rows, width), grad_up, qkv_flat, up_weight, gains,
        end_sums, sizes, 5, (sums[-1].sum, head_sum.join().total),
    )
    (head_grad,) = settle_all([head_sum], [(D, local_vocab)], (group_sums,))
    join_all(sums, head_grad)
    small = sum_over_dp(jnp.concatenate([group_sums[:7], biases], axis=0))
    out_grad, down_grad, up_grad, qkv_grad = settle_all(
        sums, [(inner, D), (local_hidden, D), (D, local_hidden), qkv_weight.shape]
    )
    return (
        losses[:, 0][None],
        output[None],
        grad_input[None],
        small[0],
        small[1],
        small[2],
        small[3],
        qkv_grad,
        small[7, :split].reshape(local_heads, 2 * HEAD_DIM),
        out_grad.reshape(out_weight.shape),
        up_grad,
        small[7, split : split + local_hidden],
        down_grad,
        small[6],
        small[4],
        small[5],
        head_grad,
    )


def solution(mesh):
    return jax.shard_map(
        per_device,
        mesh=mesh,
        in_specs=(
            P("dp", "seq", None),
            P("dp", None),
            P("dp", None),
            P("dp", None),
            P("dp", None),
            P(),
            P(),
            P(),
            P(),
            P(None, "seq", None),
            P("seq", None),
            P("seq", None, None),
            P(None, "seq"),
            P("seq"),
            P("seq", None),
            P(),
            P(),
            P(),
            P(None, "seq"),
        ),
        out_specs=(
            P("dp", None),
            P("dp", "seq", None),
            P("dp", "seq", None),
            P(),
            P(),
            P(),
            P(),
            P(None, "seq", None),
            P("seq", None),
            P("seq", None, None),
            P(None, "seq"),
            P("seq"),
            P("seq", None),
            P(),
            P(),
            P(),
            P(None, "seq"),
        ),
        check_vma=False,
    )
```

```python
import jax
import jax.numpy as jnp
from jax import lax
from jax.experimental import pallas as pl
from jax.experimental.pallas import tpu as pltpu
from jax.sharding import PartitionSpec as P

D = 2048
HEAD_DIM = 128
ROT = 32
BLOCK = 2048
EXB = 8
EPSILON = 1e-05
BETA = 0.25
LOSS_SCALE = 65536.0
HALVES = 2
VMEM_LIMIT = 62 * 2**20

MESH = pl.DeviceIdType.MESH


class Grid2:
    def __init__(self, sizes):
        self.n = sizes
        place = lax.axis_index("seq")
        self.me = (place // sizes[1], lax.rem(place, sizes[1]))

    def index(self, slow, fast):
        return slow * self.n[1] + fast

    def device(self, axis, spot):
        here = list(self.me)
        here[axis] = spot
        return {"seq": self.index(*here)}

    def nearest(self, axis, rank):
        n, m = self.n[axis], self.me[axis]
        if rank == 0:
            return m
        if n == 2:
            return 1 - m
        after = n - 1 - m
        both = jnp.minimum(m, after)
        dist = (rank + 1) // 2
        near = m - dist if rank % 2 else m + dist
        far = jnp.where(m < after, m + (rank - both), m - (rank - both))
        return jnp.where(rank <= 2 * both, near, far)

    def neighbours(self):
        found = []
        for axis in (0, 1):
            m, n = self.me[axis], self.n[axis]
            if n == 2:
                found.append((None, self.device(axis, 1 - m)))
            elif n > 2:
                found.append((m > 0, self.device(axis, m - 1)))
                found.append((m < n - 1, self.device(axis, m + 1)))
        return found

    def barrier(self, *others):
        sem = pltpu.get_barrier_semaphore()
        amount = jnp.int32(0)
        for there, device in self.neighbours() + [(None, device) for device in others]:
            def tell(device=device):
                pl.semaphore_signal(sem, inc=1, device_id=device, device_id_type=MESH)
            if there is None:
                tell()
                amount = amount + 1
            else:
                pl.when(there)(tell)
                amount = amount + there.astype(jnp.int32)
        pl.semaphore_wait(sem, amount)


class Sender:
    def __init__(self, send_sems):
        self.sems = send_sems
        self.used = 0
        self.open = []

    def send(self, src, dst, recv_sem, device, when=None):
        copy = pltpu.make_async_remote_copy(
            src_ref=src, dst_ref=dst, send_sem=self.sems.at[self.used], recv_sem=recv_sem,
            device_id=device, device_id_type=MESH)
        self.used += 1
        if when is None:
            copy.start()
        else:
            pl.when(when)(copy.start)
        self.open.append((when, copy))

    def finish(self):
        for when, copy in self.open:
            if when is None:
                copy.wait_send()
            else:
                pl.when(when)(copy.wait_send)
        self.open = []


def gather_sends(sizes, halves):
    return halves * 2 * (sizes[0] * sizes[1] * 5 + 8)


def gather_rounds(grid, sender, piece, recv_sems, halves, cut, ready):
    n, me = grid.n, grid.me

    def arrived(slow, fast, half, kind, when):
        ref = piece(grid.index(slow, fast), half, kind)
        sem = recv_sems.at[kind, half, grid.index(slow, fast)]
        wait = pltpu.make_async_copy(ref, ref, sem).wait
        if when is None:
            wait()
        else:
            pl.when(when)(wait)

    def push(slow, fast, half, kind, axis, spot, *conditions):
        ref = piece(grid.index(slow, fast), half, kind)
        sem = recv_sems.at[kind, half, grid.index(slow, fast)]
        when = None
        for condition in conditions:
            if condition is not None:
                when = condition if when is None else when & condition
        sender.send(ref, ref, sem, grid.device(axis, spot), when)

    def spread(slow, fast, half, kind, axis, when):
        m, size = me[axis], n[axis]
        if size == 2:
            push(slow, fast, half, kind, axis, 1 - m, when)
        elif size > 2:
            push(slow, fast, half, kind, axis, m + 1, when, m < size - 1)
            push(slow, fast, half, kind, axis, m - 1, when, m > 0)

    def onward(slow, fast, half, kind, axis, when):
        m, size = me[axis], n[axis]
        if size <= 2:
            return
        below = (slow, fast)[axis] < m
        more = (below & (m < size - 1)) | (jnp.logical_not(below) & (m > 0))
        push(slow, fast, half, kind, axis, jnp.where(below, m + 1, m - 1), when, more)

    def sides(d):
        if d == 0:
            return [(me[0], None)]
        if n[0] == 2:
            return [(1 - me[0], None)]
        return [(me[0] - d, me[0] >= d), (me[0] + d, me[0] + d < n[0])]

    def settle(d):
        for half in range(halves):
            for slow, when in sides(d):
                for l in range(n[1]):
                    fast = grid.nearest(1, l)
                    if d > 0:
                        arrived(slow, fast, half, 1, when)
                        onward(slow, fast, half, 1, 0, when)
                    else:
                        spread(slow, fast, half, 1, 0, when)

    def complete(d):
        for l in range(1, n[1]):
            fast = grid.nearest(1, l)
            for half in range(halves):
                for slow, when in sides(d):
                    arrived(slow, fast, half, 0, when)
                    onward(slow, fast, half, 0, 1, when)

    def work(k, l):
        ready(grid.nearest(0, k), grid.nearest(1, l), k * n[1] + l)

    for half in range(halves):
        for kind in (1, 0):
            if cut[kind]:
                spread(me[0], me[1], half, kind, kind, None)
        if cut[0]:
            spread(me[0], me[1], half, 0, 1, None)
    work(0, 0)
    if cut[1]:
        for half in range(halves):
            for l in range(1, n[1]):
                fast = grid.nearest(1, l)
                arrived(me[0], fast, half, 1, None)
                onward(me[0], fast, half, 1, 1, None)
        settle(0)
    for d in range(1, n[0]):
        if cut[0]:
            for half in range(halves):
                for slow, when in sides(d):
                    arrived(slow, me[1], half, 0, when)
                    onward(slow, me[1], half, 0, 0, when)
                    spread(slow, me[1], half, 0, 1, when)
            complete(d - 1)
        for l in range(1, n[1]):
            work(d - 1, l)
        if cut[1]:
            settle(d)
        work(d, 0)
    if cut[0]:
        complete(n[0] - 1)
    for l in range(1, n[1]):
        work(n[0] - 1, l)


def scatter_slots(n):
    return 1 if n == 2 else n + 1


def scatter_plan(n, quick):
    if n == (4, 2) and not quick:
        return [
            ("make", 3, 1), ("make", 2, 1), ("make", 3, 0), ("make", 1, 1), ("first", 3), ("make", 2, 0),
            ("make", 0, 1), ("later", 3, 0), ("make", 1, 0), ("later", 3, 1), ("first", 2), ("make", 0, 0), ("made",),
            ("later", 2, 0), ("later", 2, 1), ("first", 1), ("later", 1, 0), ("later", 1, 1),
        ]
    far = n[0] - 1
    plan = [("make", k, l) for l in range(n[1] - 1, -1, -1) for k in range(far, -1, -1)] + [("made",)]
    for k in range(far, 0, -1):
        plan += [("first", k), ("later", k, 0), ("later", k, 1)]
    return plan


class Scatter:
    def __init__(self, grid, sender, part, bufs, sems, halves, cut, quick):
        self.grid, self.sender, self.part, self.quick = grid, sender, part, quick
        self.bufs, self.sems, self.halves, self.cut = bufs, sems, halves, cut

    def slot(self, axis, target, from_below):
        if self.grid.n[axis] == 2:
            return 0
        return target + jnp.where(from_below, 1, 0)

    def take(self, kind, stage, axis, other, target, from_below, half, when, slot_index):
        buf, sem = self.bufs[kind][stage], self.sems[kind][stage]
        slot = self.slot(axis, target, from_below)

        def add():
            ref = buf.at[other, slot, half]
            pltpu.make_async_copy(ref, ref, sem.at[other, slot, half]).wait()
            mine = self.part(slot_index, half, kind)
            mine[...] = (mine[...].astype(jnp.float32) + ref[...].astype(jnp.float32)).astype(mine.dtype)

        if when is None:
            add()
        else:
            pl.when(when)(add)

    def incoming(self, axis, target):
        m, n = self.grid.me[axis], self.grid.n[axis]
        if n == 2:
            return None
        up = target > m
        return (up & (m > 0)) | (jnp.logical_not(up) & (m < n - 1))

    def toward(self, kind, stage, axis, other, target, half, slow, fast, when=None):
        grid = self.grid
        m, n = grid.me[axis], grid.n[axis]
        up = target > m
        index = grid.index(slow, fast)
        if n > 2:
            incoming = self.incoming(axis, target)
            self.take(kind, stage, axis, other, target, up, half, incoming if when is None else incoming & when, index)
        buf, sem = self.bufs[kind][stage], self.sems[kind][stage]
        slot = self.slot(axis, target, up)
        spot = 1 - m if n == 2 else jnp.where(up, m + 1, m - 1)
        self.sender.send(
            self.part(index, half, kind), buf.at[other, slot, half], sem.at[other, slot, half],
            grid.device(axis, spot), when)

    def last(self, kind, stage, axis, other, half, slow, fast):
        grid = self.grid
        m, n = grid.me[axis], grid.n[axis]
        index = grid.index(slow, fast)
        if n == 2:
            self.take(kind, stage, axis, other, m, m > 0, half, None, index)
        elif n > 2:
            self.take(kind, stage, axis, other, m, jnp.bool_(True), half, m > 0, index)
            self.take(kind, stage, axis, other, m, jnp.bool_(False), half, m < n - 1, index)

    def run(self, produce, made=lambda: None, late=lambda: None):
        grid, n, me = self.grid, self.grid.n, self.grid.me
        lagging = []

        def chain(k, half, begins):
            slow = grid.nearest(0, k)
            incoming = self.incoming(0, slow)
            if incoming is None:
                if begins:
                    self.last(0, 0, 1, slow, half, slow, me[1])
                    self.toward(0, 1, 0, 0, slow, half, slow, me[1])
                return
            when = jnp.logical_not(incoming) if begins else incoming
            pl.when(when)(lambda: self.last(0, 0, 1, slow, half, slow, me[1]))
            self.toward(0, 1, 0, 0, slow, half, slow, me[1], when)

        def catch_up():
            for step in lagging:
                self.toward(*step)
            lagging.clear()

        def make(k, l):
            slow, fast = grid.nearest(0, k), grid.nearest(1, l)
            produce(slow, fast)
            if self.cut[0] and l > 0:
                for half in range(self.halves):
                    self.toward(0, 0, 1, slow, fast, half, slow, fast)
            catch_up()
            if self.cut[1] and k > 0:
                for half in range(self.halves):
                    lagging.append((1, 0, 0, fast, slow, half, slow, fast))

        for step in scatter_plan(n, self.quick):
            if step[0] == "make":
                make(*step[1:])
            elif step[0] == "made":
                catch_up()
                made()
            elif step[0] == "first" and self.cut[0]:
                for half in range(self.halves):
                    chain(step[1], half, True)
            elif self.cut[0]:
                chain(step[1], step[2], False)
        if self.cut[1]:
            for half in range(self.halves):
                for l in reversed(range(n[1])):
                    fast = grid.nearest(1, l)
                    self.last(1, 0, 0, fast, half, me[0], fast)
                    if l > 0:
                        self.toward(1, 1, 1, 0, fast, half, me[0], fast)
        late()
        if self.cut[0]:
            for half in range(self.halves):
                self.last(0, 0, 1, me[0], half, me[0], me[1])
        for half in range(self.halves):
            if self.cut[1]:
                self.last(1, 1, 1, 0, half, me[0], me[1])
            if self.cut[0]:
                self.last(0, 1, 0, 0, half, me[0], me[1])


def scatter_scratch(sizes, halves, rows, cols, cut):
    bufs, sems = [], []
    for kind, stages in ((0, (1, 0)), (1, (0, 1))):
        for stage, axis in enumerate(stages):
            lead = (sizes[1 - axis] if stage == 0 else 1, scatter_slots(sizes[axis]), halves)
            width = max(cut[kind], 128)
            bufs.append(pltpu.VMEM(lead + (rows // halves, width), jnp.bfloat16))
            sems.append(pltpu.SemaphoreType.DMA(lead))
    return bufs, sems


def scatter_sends(sizes, halves):
    return halves * 2 * (sizes[0] * sizes[1] + sizes[0] + sizes[1])


def lines_of(seq):
    fast = 2 if seq <= 8 else 4
    return (seq // fast, fast)


ATT_TILE = 256
SCALE = HEAD_DIM ** (-0.5)


def dot_nt(left, right):
    return lax.dot_general(left, right, (((1,), (1,)), ((), ())), preferred_element_type=jnp.float32)


def dot_tn(left, right):
    return lax.dot_general(left, right, (((0,), (0,)), ((), ())), preferred_element_type=jnp.float32)


def rotary_frequencies():
    half_rot = ROT // 2
    frequency = 10000.0 ** (-2.0 * jnp.arange(half_rot, dtype=jnp.float32) / ROT)
    return jnp.tile(frequency, HEAD_DIM // half_rot)[None, :]


def first_rows(lengths, row):
    start, end = jnp.zeros_like(row), jnp.int32(0)
    for example in range(EXB):
        end = end + lengths[example]
        start = jnp.where(row >= end, end, start)
    return start


def rotary_planes(position, frequencies):
    half_rot = ROT // 2
    angles = position.astype(jnp.float32) * frequencies
    cos, sin = jnp.cos(angles), jnp.sin(angles)
    lane = lax.broadcasted_iota(jnp.int32, angles.shape, 1)
    return (
        jnp.where(lane < ROT, cos, 1.0),
        jnp.where((lane >= half_rot) & (lane < ROT), sin, 0.0),
        jnp.where(lane < half_rot, -sin, 0.0),
    )


def turn(vector, cos, from_below, from_above):
    half_rot = ROT // 2
    return (
        vector * cos
        + pltpu.roll(vector, half_rot, 1) * from_below
        + pltpu.roll(vector, HEAD_DIM - half_rot, 1) * from_above
    )


def tile_mask(start_col, query_tile, key_tile):
    shape = (ATT_TILE, ATT_TILE)
    query_ids = query_tile * ATT_TILE + lax.broadcasted_iota(jnp.int32, shape, 0)
    key_ids = key_tile * ATT_TILE + lax.broadcasted_iota(jnp.int32, shape, 1)
    return (key_ids >= start_col) & (key_ids <= query_ids)


def tile_starts(lengths, tile):
    rows = tile * ATT_TILE + lax.broadcasted_iota(jnp.int32, (ATT_TILE, 1), 0)
    return first_rows(lengths, rows), first_rows(lengths, tile * ATT_TILE) // ATT_TILE


def attention_forward(qkv, lengths, heads):
    tiles = BLOCK // ATT_TILE

    def kernel(lengths_ref, q_ref, k_ref, v_ref, ctx_ref, lse_ref):
        tile = pl.program_id(1)
        queries = q_ref[...]
        start, first = tile_starts(lengths_ref, tile)

        def step(key_tile, carry):
            top, total, acc = carry
            rows = pl.ds(pl.multiple_of(key_tile * ATT_TILE, ATT_TILE), ATT_TILE)
            scores = dot_nt(queries, k_ref[rows, :]) * SCALE
            scores = jnp.where(tile_mask(start, tile, key_tile), scores, -1e30)
            new_top = jnp.maximum(top, jnp.max(scores, axis=1, keepdims=True))
            shrink = jnp.exp(top - new_top)
            weights = jnp.exp(scores - new_top)
            total = total * shrink + jnp.sum(weights, axis=1, keepdims=True)
            acc = acc * shrink + jnp.dot(
                weights.astype(jnp.bfloat16), v_ref[rows, :], preferred_element_type=jnp.float32
            )
            return (new_top, total, acc)

        begin = (
            jnp.full((ATT_TILE, 1), -1e30, jnp.float32),
            jnp.zeros((ATT_TILE, 1), jnp.float32),
            jnp.zeros((ATT_TILE, HEAD_DIM), jnp.float32),
        )
        begin = step(tile, begin)
        top, total, acc = lax.fori_loop(first, tile, step, begin)
        ctx_ref[...] = (acc / total).astype(jnp.bfloat16)
        lse_ref[...] = top + jnp.log(total)

    return pl.pallas_call(
        kernel,
        grid_spec=pltpu.PrefetchScalarGridSpec(
            num_scalar_prefetch=1,
            grid=(heads, tiles),
            in_specs=[
                pl.BlockSpec((ATT_TILE, HEAD_DIM), lambda h, i, first: (i, 3 * h)),
                pl.BlockSpec((BLOCK, HEAD_DIM), lambda h, i, first: (0, 3 * h + 1)),
                pl.BlockSpec((BLOCK, HEAD_DIM), lambda h, i, first: (0, 3 * h + 2)),
            ],
            out_specs=[
                pl.BlockSpec((ATT_TILE, HEAD_DIM), lambda h, i, first: (i, h)),
                pl.BlockSpec((pl.squeezed, ATT_TILE, 1), lambda h, i, first: (h, i, 0)),
            ],
        ),
        out_shape=[
            jax.ShapeDtypeStruct((BLOCK, heads * HEAD_DIM), jnp.bfloat16),
            jax.ShapeDtypeStruct((heads, BLOCK, 1), jnp.float32),
        ],
        compiler_params=pltpu.CompilerParams(vmem_limit_bytes=VMEM_LIMIT),
    )(lengths, qkv, qkv, qkv)


def attention_backward(qkv, lengths, heads, ctx, lse, grad_ctx, planes, before):
    tiles = BLOCK // ATT_TILE

    def kernel(
        lengths_ref, q_ref, k_ref, v_ref, ctx_ref, lse_ref, do_ref, cos_ref, below_ref,
        above_ref, *rest,
    ):
        out_ref, sums_ref, dk_ref, dv_ref = rest[len(before) :]
        tile = pl.program_id(1)

        @pl.when(tile == 0)
        def _():
            dk_ref[...] = jnp.zeros_like(dk_ref)
            dv_ref[...] = jnp.zeros_like(dv_ref)

        queries = q_ref[...]
        start, first = tile_starts(lengths_ref, tile)
        grads = do_ref[...]
        lse_rows = lse_ref[...]
        inner = jnp.sum(
            grads.astype(jnp.float32) * ctx_ref[...].astype(jnp.float32), axis=1, keepdims=True
        )

        def step(key_tile, dq):
            rows = pl.ds(pl.multiple_of(key_tile * ATT_TILE, ATT_TILE), ATT_TILE)
            keys = k_ref[rows, :]
            scores = dot_nt(queries, keys) * SCALE
            probs = jnp.where(
                tile_mask(start, tile, key_tile), jnp.exp(scores - lse_rows), 0.0
            )
            grad_probs = dot_nt(grads, v_ref[rows, :])
            grad_scores = (probs * (grad_probs - inner)).astype(jnp.bfloat16)
            dv_ref[rows, :] += dot_tn(probs.astype(jnp.bfloat16), grads)
            dk_ref[rows, :] += dot_tn(grad_scores, queries)
            return dq + jnp.dot(grad_scores, keys, preferred_element_type=jnp.float32)

        dq = lax.fori_loop(
            first, tile + 1, step, jnp.zeros((ATT_TILE, HEAD_DIM), jnp.float32)
        )
        here = pl.ds(pl.multiple_of(tile * ATT_TILE, ATT_TILE), ATT_TILE)
        out_ref[here, :HEAD_DIM] = turn(
            dq * SCALE, cos_ref[here, :], -below_ref[here, :], -above_ref[here, :]
        ).astype(jnp.bfloat16)

        @pl.when(tile == tiles - 1)
        def _():
            def finish(index, sums):
                rows = pl.ds(pl.multiple_of(index * ATT_TILE, ATT_TILE), ATT_TILE)
                out_ref[rows, HEAD_DIM : 2 * HEAD_DIM] = turn(
                    dk_ref[rows, :] * SCALE, cos_ref[rows, :], -below_ref[rows, :], -above_ref[rows, :]
                ).astype(jnp.bfloat16)
                out_ref[rows, 2 * HEAD_DIM :] = dv_ref[rows, :].astype(jnp.bfloat16)
                return sums + jnp.sum(out_ref[rows, :].astype(jnp.float32), axis=0, keepdims=True)

            sums_ref[...] = lax.fori_loop(
                0, tiles, finish, jnp.zeros((1, 3 * HEAD_DIM), jnp.float32)
            )

    whole = pl.BlockSpec((BLOCK, HEAD_DIM), lambda h, i, first: (0, 0))
    return pl.pallas_call(
        kernel,
        grid_spec=pltpu.PrefetchScalarGridSpec(
            num_scalar_prefetch=1,
            grid=(heads, tiles),
            in_specs=[
                pl.BlockSpec((ATT_TILE, HEAD_DIM), lambda h, i, first: (i, 3 * h)),
                pl.BlockSpec((BLOCK, HEAD_DIM), lambda h, i, first: (0, 3 * h + 1)),
                pl.BlockSpec((BLOCK, HEAD_DIM), lambda h, i, first: (0, 3 * h + 2)),
                pl.BlockSpec((ATT_TILE, HEAD_DIM), lambda h, i, first: (i, h)),
                pl.BlockSpec((pl.squeezed, ATT_TILE, 1), lambda h, i, first: (h, i, 0)),
                pl.BlockSpec((ATT_TILE, HEAD_DIM), lambda h, i, first: (i, h)),
                whole,
                whole,
                whole,
            ]
            + [pl.BlockSpec(memory_space=pl.ANY)] * len(before),
            out_specs=[
                pl.BlockSpec((BLOCK, 3 * HEAD_DIM), lambda h, i, first: (0, h)),
                pl.BlockSpec((pl.squeezed, 1, 3 * HEAD_DIM), lambda h, i, first: (h, 0, 0)),
            ],
            scratch_shapes=[
                pltpu.VMEM((BLOCK, HEAD_DIM), jnp.float32),
                pltpu.VMEM((BLOCK, HEAD_DIM), jnp.float32),
            ],
        ),
        out_shape=[
            jax.ShapeDtypeStruct((BLOCK, heads * 3 * HEAD_DIM), jnp.bfloat16),
            jax.ShapeDtypeStruct((heads, 1, 3 * HEAD_DIM), jnp.float32),
        ],
        compiler_params=pltpu.CompilerParams(vmem_limit_bytes=VMEM_LIMIT),
    )(lengths, qkv, qkv, qkv, ctx, lse, grad_ctx, *planes, *before)


def gather_cut(sizes):
    return (1792, 256) if sizes == (4, 2) else (D // 2, D // 2)


def scatter_cut(sizes):
    return (1664, 384) if sizes == (4, 2) else (D // 2, D // 2)


def columns_of(cut, kind):
    return pl.ds(0, cut[0]) if kind == 0 else pl.ds(cut[0], cut[1])


def tile_of(width):
    return 512 if width % 512 == 0 else 256 if width % 256 == 0 else 128


def span(index, size):
    return pl.ds(pl.multiple_of(index * size, size), size)


ANY = pl.BlockSpec(memory_space=pl.ANY)
VMEM = pl.BlockSpec(memory_space=pltpu.VMEM)
SMEM = pl.BlockSpec(memory_space=pltpu.SMEM)


def row_kernel(kernel, collective, out_shape, in_specs, out_specs, scratch, cost, before=()):
    def body(*refs):
        kernel(*refs[len(before):])

    def call(*args):
        return pl.pallas_call(
            body,
            out_shape=out_shape,
            in_specs=[ANY] * len(before) + in_specs,
            out_specs=out_specs,
            scratch_shapes=scratch,
            cost_estimate=pl.CostEstimate(flops=cost, bytes_accessed=2**28 if cost > 1 else 1, transcendentals=0),
            compiler_params=pltpu.CompilerParams(
                collective_id=collective, has_side_effects=True, vmem_limit_bytes=VMEM_LIMIT
            ),
        )(*before, *args)

    return call


def gather_scratch(sizes, rows):
    shards = sizes[0] * sizes[1]
    return [
        pltpu.VMEM((shards, rows, D), jnp.bfloat16),
        pltpu.SemaphoreType.DMA((gather_sends(sizes, HALVES),)),
        pltpu.SemaphoreType.DMA((2, HALVES, shards)),
    ]


def run_gather(grid, sizes, rows, full, send_sems, recv_sems, ready):
    cut = gather_cut(sizes)
    step = rows // HALVES
    sender = Sender(send_sems)

    def piece(slot, half, kind):
        return full.at[slot, pl.ds(half * step, step), columns_of(cut, kind)]

    gather_rounds(grid, sender, piece, recv_sems, HALVES, cut, ready)
    sender.finish()


def sum_scratch(sizes, rows):
    shards = sizes[0] * sizes[1]
    bufs, sems = scatter_scratch(sizes, HALVES, rows, D, scatter_cut(sizes))
    return (
        [pltpu.VMEM((shards, rows, D), jnp.bfloat16)]
        + bufs
        + sems
        + [pltpu.SemaphoreType.DMA((scatter_sends(sizes, HALVES),))]
    )


def run_scatter(grid, sizes, rows, scratch, produce, *hooks, quick=False):
    cut = scatter_cut(sizes)
    step = rows // HALVES
    parts, b0, b1, b2, b3, s0, s1, s2, s3, send_sems = scratch
    sender = Sender(send_sems)

    def part(slot, half, kind):
        return parts.at[slot, pl.ds(half * step, step), columns_of(cut, kind)]

    scatter = Scatter(
        grid, sender, part, ((b0, b1), (b2, b3)), ((s0, s1), (s2, s3)), HALVES, cut, quick
    )
    scatter.run(produce, *hooks)
    sender.finish()


def production_order(grid, quick=False):
    return [
        grid.index(grid.nearest(0, k), grid.nearest(1, l))
        for action, k, l in [step for step in scatter_plan(grid.n, quick) if step[0] == "make"]
    ]


ROW_TILE = 64


def tile_stats(values):
    centered = values - jnp.mean(values, axis=1, keepdims=True)
    inverse = lax.rsqrt(jnp.mean(centered * centered, axis=1, keepdims=True) + EPSILON)
    return centered, inverse


def open_rows(own, sizes, collective, norms, qkv_flat, qkv_bias, up_weight, up_bias, lengths):
    rows = own.shape[0]
    shards = sizes[0] * sizes[1]
    width, hidden = qkv_flat.shape[1], up_weight.shape[1]
    heads = width // (3 * HEAD_DIM)

    def kernel(
        own_ref, norms_ref, qkvw_any, qkvb_ref, upw_any, upb_ref, lengths_ref, freq_ref,
        plain_any, one_any, two_any, qkv_any, act_any, slope_any, cos_ref, below_ref, above_ref,
        full, send_sems, recv_sems, qkvw, upw, load_sems, plain, one, two, qkv, act, slope, out_sems,
    ):
        grid = Grid2(sizes)
        loads = [
            pltpu.make_async_copy(qkvw_any, qkvw, load_sems.at[0]),
            pltpu.make_async_copy(upw_any, upw, load_sems.at[1]),
        ]
        for copy in loads:
            copy.start()
        full[grid.index(*grid.me)] = own_ref[...]
        grid.barrier()
        open_copies = []

        def outs(place, slot):
            pairs = ((plain, plain_any), (one, one_any), (two, two_any), (qkv, qkv_any), (act, act_any), (slope, slope_any))
            return [
                pltpu.make_async_copy(here.at[slot], there.at[place], out_sems.at[slot, i])
                for i, (here, there) in enumerate(pairs)
            ]

        def ready(slow, fast, order):
            place = grid.index(slow, fast)
            slot = order % 2
            if order == 0:
                for copy in loads:
                    copy.wait()
            if order >= 2:
                for copy in open_copies.pop(0):
                    copy.wait()

            def norm_tile(index, _):
                here = span(index, ROW_TILE)
                centered, inverse = tile_stats(full[place, here].astype(jnp.float32))
                normed = centered * inverse
                plain[slot, here] = normed.astype(jnp.bfloat16)
                one[slot, here] = (normed * norms_ref[0:1] + norms_ref[1:2]).astype(jnp.bfloat16)
                two[slot, here] = (normed * norms_ref[2:3] + norms_ref[3:4]).astype(jnp.bfloat16)
                return _

            lax.fori_loop(0, rows // ROW_TILE, norm_tile, 0)
            places = pl.ds(pl.multiple_of(place * rows, rows), rows)
            row = place * rows + lax.broadcasted_iota(jnp.int32, (rows, 1), 0)
            cos, below, above = rotary_planes(row - first_rows(lengths_ref, row), freq_ref[...])
            cos_ref[places, :], below_ref[places, :], above_ref[places, :] = cos, below, above
            whole = jnp.dot(one[slot], qkvw[...], preferred_element_type=jnp.float32) + qkvb_ref[...]
            for head in range(heads):
                first = head * 3 * HEAD_DIM
                found = whole[:, first : first + 3 * HEAD_DIM]
                qkv[slot, :, first : first + HEAD_DIM] = turn(
                    found[:, :HEAD_DIM], cos, below, above
                ).astype(jnp.bfloat16)
                qkv[slot, :, first + HEAD_DIM : first + 2 * HEAD_DIM] = turn(
                    found[:, HEAD_DIM : 2 * HEAD_DIM], cos, below, above
                ).astype(jnp.bfloat16)
                qkv[slot, :, first + 2 * HEAD_DIM : first + 3 * HEAD_DIM] = found[
                    :, 2 * HEAD_DIM :
                ].astype(jnp.bfloat16)
            tile = tile_of(hidden)

            def up_tile(index, _):
                here = span(index, tile)
                pre = jnp.dot(two[slot], upw[:, here], preferred_element_type=jnp.float32) + upb_ref[:, here]
                share = 0.5 * (1.0 + lax.erf(pre * 0.7071067811865476))
                act[slot, :, here] = (pre * share).astype(jnp.bfloat16)
                slope[slot, :, here] = (
                    share + pre * (jnp.exp(-0.5 * pre * pre) * 0.3989422804014327)
                ).astype(jnp.bfloat16)
                return _

            lax.fori_loop(0, hidden // tile, up_tile, 0)
            copies = outs(place, slot)
            for copy in copies:
                copy.start()
            open_copies.append(copies)

        run_gather(grid, sizes, rows, full, send_sems, recv_sems, ready)
        for copies in open_copies:
            for copy in copies:
                copy.wait()

    def out(columns):
        return jax.ShapeDtypeStruct((shards, rows, columns), jnp.bfloat16)

    def staged(columns):
        return pltpu.VMEM((2, rows, columns), jnp.bfloat16)

    return row_kernel(
        kernel, collective,
        [out(D), out(D), out(D), out(width), out(hidden), out(hidden)]
        + [jax.ShapeDtypeStruct((shards * rows, HEAD_DIM), jnp.float32)] * 3,
        [VMEM, VMEM, ANY, VMEM, ANY, VMEM, SMEM, VMEM],
        [ANY] * 6 + [VMEM] * 3,
        gather_scratch(sizes, rows)
        + [
            pltpu.VMEM(qkv_flat.shape, jnp.bfloat16),
            pltpu.VMEM(up_weight.shape, jnp.bfloat16),
            pltpu.SemaphoreType.DMA((2,)),
            staged(D), staged(D), staged(D), staged(width), staged(hidden), staged(hidden),
            pltpu.SemaphoreType.DMA((2, 6)),
        ],
        2 * BLOCK * D * (width + hidden),
    )(own, norms, qkv_flat, qkv_bias, up_weight, up_bias, lengths, rotary_frequencies())


def branch_rows(own, ctx, act, out_flat, down_weight, norms, sizes, collective):
    rows = own.shape[0]
    shards = sizes[0] * sizes[1]
    inner, hidden = out_flat.shape[0], down_weight.shape[0]

    def kernel(
        own_ref, ctx_any, act_any, outw_any, downw_any, norms_ref, out_ref, final_ref, normed_ref, inverse_ref,
        ctx, act, outw, downw, load_sems, *scratch,
    ):
        grid = Grid2(sizes)
        parts = scratch[0]
        weights = [
            pltpu.make_async_copy(outw_any, outw, load_sems.at[0, 0]),
            pltpu.make_async_copy(downw_any, downw, load_sems.at[0, 1]),
        ]
        order = production_order(grid)
        loads = [
            [
                pltpu.make_async_copy(ctx_any.at[place], ctx.at[place], load_sems.at[1 + i, 0]),
                pltpu.make_async_copy(act_any.at[place], act.at[place], load_sems.at[1 + i, 1]),
            ]
            for i, place in enumerate(order)
        ]
        for copy in loads[0] + weights:
            copy.start()
        for copies in loads[1:]:
            for copy in copies:
                copy.start()
        grid.barrier()
        for copy in weights:
            copy.wait()

        def produce(slow, fast):
            place = grid.index(slow, fast)
            for copy in loads.pop(0):
                copy.wait()

            def columns(index, _):
                here = span(index, 512)
                parts[place, :, here] = (
                    jnp.dot(ctx[place], outw[:, here], preferred_element_type=jnp.float32)
                    + jnp.dot(act[place], downw[:, here], preferred_element_type=jnp.float32)
                ).astype(jnp.bfloat16)
                return _

            lax.fori_loop(0, D // 512, columns, 0)

        run_scatter(grid, sizes, rows, scratch, produce)
        mine = grid.index(*grid.me)

        def norm_tile(index, _):
            here = span(index, ROW_TILE)
            stream = own_ref[here].astype(jnp.float32) + parts[mine, here].astype(jnp.float32) + norms_ref[2:3]
            out_ref[here] = stream.astype(jnp.bfloat16)
            centered, inverse = tile_stats(stream)
            normed = centered * inverse
            final_ref[here] = (normed * norms_ref[0:1] + norms_ref[1:2]).astype(jnp.bfloat16)
            normed_ref[here] = normed
            inverse_ref[here] = inverse
            return _

        lax.fori_loop(0, rows // ROW_TILE, norm_tile, 0)

    return row_kernel(
        kernel, collective,
        [
            jax.ShapeDtypeStruct((rows, D), jnp.bfloat16),
            jax.ShapeDtypeStruct((rows, D), jnp.bfloat16),
            jax.ShapeDtypeStruct((rows, D), jnp.float32),
            jax.ShapeDtypeStruct((rows, 1), jnp.float32),
        ],
        [VMEM, ANY, ANY, ANY, ANY, VMEM],
        [VMEM] * 4,
        [
            pltpu.VMEM(ctx.shape, jnp.bfloat16),
            pltpu.VMEM(act.shape, jnp.bfloat16),
            pltpu.VMEM(out_flat.shape, jnp.bfloat16),
            pltpu.VMEM(down_weight.shape, jnp.bfloat16),
            pltpu.SemaphoreType.DMA((1 + shards, 2)),
        ]
        + sum_scratch(sizes, rows),
        2 * BLOCK * D * (inner + hidden),
    )(own, ctx, act, out_flat, down_weight, norms)


def logit_rows(final, head_weight, targets_col, sizes, collective):
    rows = final.shape[0]
    shards = sizes[0] * sizes[1]
    vocab = head_weight.shape[1]

    def kernel(
        own_ref, headw_any, target_ref, final_any, weights_any, stats_ref,
        full, send_sems, recv_sems, headw, load_sem, logits, weights, out_sems, row_sems,
    ):
        grid = Grid2(sizes)
        load = pltpu.make_async_copy(headw_any, headw, load_sem)
        load.start()
        full[grid.index(*grid.me)] = own_ref[...]
        grid.barrier()
        base = lax.axis_index("seq") * vocab
        open_copies, raw_copies = [], []

        def ready(slow, fast, order):
            place = grid.index(slow, fast)
            slot = order % 2
            if order == 0:
                load.wait()
            if order >= 2:
                open_copies.pop(0).wait()
            places = pl.ds(pl.multiple_of(place * rows, rows), rows)
            target = target_ref[places, :] - base

            def fold(values, join):
                total = values[:, :128]
                for first in range(128, values.shape[1], 128):
                    total = join(total, values[:, first : first + 128])
                return total

            def logit_tile(start, size, carry):
                top, pick = carry
                here = pl.ds(start, size)
                found = jnp.dot(full[place], headw[:, here], preferred_element_type=jnp.float32)
                logits[:, here] = found
                ids = start + lax.broadcasted_iota(jnp.int32, (rows, size), 1)
                top = jnp.maximum(top, fold(found, jnp.maximum))
                pick = pick + fold(jnp.where(ids == target, found, 0.0), jnp.add)
                return (top, pick)

            def tiled(step, carry):
                count = vocab // 512
                carry = lax.fori_loop(
                    0, count, lambda i, c: step(pl.multiple_of(i * 512, 512), 512, c), carry
                )
                if vocab % 512:
                    carry = step(count * 512, vocab % 512, carry)
                return carry

            top, pick = tiled(
                logit_tile,
                (jnp.full((rows, 128), -jnp.inf, jnp.float32), jnp.zeros((rows, 128), jnp.float32)),
            )
            top = jnp.max(top, axis=1, keepdims=True)
            pick = jnp.sum(pick, axis=1, keepdims=True)

            def weight_tile(start, size, total):
                here = pl.ds(start, size)
                found = jnp.exp(logits[:, here] - top)
                weights[slot, :, here] = found.astype(jnp.bfloat16)
                return total + fold(found, jnp.add)

            total = tiled(weight_tile, jnp.zeros((rows, 128), jnp.float32))
            total = jnp.sum(total, axis=1, keepdims=True)
            lane = lax.broadcasted_iota(jnp.int32, (rows, 128), 1)
            found = jnp.where(lane == 0, top, jnp.where(lane == 1, total, pick))
            stats_ref[:, places] = found.T[0:8]
            copy = pltpu.make_async_copy(weights.at[slot], weights_any.at[place], out_sems.at[slot])
            copy.start()
            open_copies.append(copy)
            raw = pltpu.make_async_copy(full.at[place], final_any.at[place], row_sems.at[order])
            raw.start()
            raw_copies.append(raw)

        run_gather(grid, sizes, rows, full, send_sems, recv_sems, ready)
        for copy in open_copies + raw_copies:
            copy.wait()

    return row_kernel(
        kernel, collective,
        [
            jax.ShapeDtypeStruct((shards, rows, D), jnp.bfloat16),
            jax.ShapeDtypeStruct((shards, rows, vocab), jnp.bfloat16),
            jax.ShapeDtypeStruct((8, shards * rows), jnp.float32),
        ],
        [VMEM, ANY, VMEM],
        [ANY, ANY, VMEM],
        gather_scratch(sizes, rows)
        + [
            pltpu.VMEM(head_weight.shape, jnp.bfloat16),
            pltpu.SemaphoreType.DMA,
            pltpu.VMEM((rows, vocab), jnp.float32),
            pltpu.VMEM((2, rows, vocab), jnp.bfloat16),
            pltpu.SemaphoreType.DMA((2,)),
            pltpu.SemaphoreType.DMA((shards,)),
        ],
        2 * BLOCK * D * vocab,
    )(final, head_weight, targets_col)


def final_grad_rows(grad_logits, head_weight, normed, inverse, gain, sizes, collective, before):
    shards, rows, vocab = grad_logits.shape

    def kernel(
        grads_any, headw_any, normed_ref, inverse_ref, gain_ref, stream_ref, down_ref, sums_ref,
        headw, grads, load_sems, *scratch,
    ):
        grid = Grid2(sizes)
        parts = scratch[0]
        order = production_order(grid)
        loads = [
            pltpu.make_async_copy(grads_any.at[place], grads.at[i % 2], load_sems.at[i])
            for i, place in enumerate(order)
        ]
        tile = 512
        weights = [
            pltpu.make_async_copy(
                headw_any.at[pl.ds(i * tile, tile)], headw.at[pl.ds(i * tile, tile)], load_sems.at[1 + shards + i]
            )
            for i in range(D // tile)
        ]
        loads[0].start()
        for copy in weights:
            copy.start()
        grid.barrier()
        count = [0]

        def produce(slow, fast):
            place = grid.index(slow, fast)
            i = count[0]
            count[0] += 1
            if i + 1 < shards:
                loads[i + 1].start()
            loads[i].wait()

            def columns(index, _):
                here = span(index, tile)
                parts[place, :, here] = dot_nt(grads[i % 2], headw[here, :]).astype(jnp.bfloat16)
                return _

            if i == 0:
                for index, copy in enumerate(weights):
                    copy.wait()
                    columns(index, 0)
            else:
                lax.fori_loop(0, D // tile, columns, 0)

        run_scatter(grid, sizes, rows, scratch, produce)
        mine = grid.index(*grid.me)
        sums_ref[...] = jnp.zeros_like(sums_ref)

        def norm_tile(index, _):
            here = span(index, ROW_TILE)
            grad = parts[mine, here].astype(jnp.float32)
            norm = normed_ref[here]
            scaled = grad * gain_ref[...]
            stream = inverse_ref[here] * (
                scaled
                - jnp.mean(scaled, axis=1, keepdims=True)
                - norm * jnp.mean(scaled * norm, axis=1, keepdims=True)
            )
            stream_ref[here] = stream
            down_ref[here] = stream.astype(jnp.bfloat16)
            sums_ref[0:1] += jnp.sum(grad * norm, axis=0, keepdims=True)
            sums_ref[1:2] += jnp.sum(grad, axis=0, keepdims=True)
            sums_ref[2:3] += jnp.sum(stream, axis=0, keepdims=True)
            return _

        lax.fori_loop(0, rows // ROW_TILE, norm_tile, 0)

    return row_kernel(
        kernel, collective,
        [
            jax.ShapeDtypeStruct((rows, D), jnp.float32),
            jax.ShapeDtypeStruct((rows, D), jnp.bfloat16),
            jax.ShapeDtypeStruct((8, D), jnp.float32),
        ],
        [ANY, ANY, VMEM, VMEM, VMEM],
        [VMEM] * 3,
        [
            pltpu.VMEM(head_weight.shape, jnp.bfloat16),
            pltpu.VMEM((2, rows, vocab), jnp.bfloat16),
            pltpu.SemaphoreType.DMA((1 + shards + D // 512,)),
        ]
        + sum_scratch(sizes, rows),
        2 * BLOCK * D * vocab,
        before,
    )(grad_logits, head_weight, normed, inverse, gain)


def branch_grad_rows(own, out_flat, down_weight, slope, ctx, act, second, sizes, collective):
    rows = own.shape[0]
    shards = sizes[0] * sizes[1]
    inner, hidden = out_flat.shape[0], down_weight.shape[0]
    half_width = D // 2

    def kernel(
        own_ref, outw_any, downw_any, slope_any, ctx_any, act_any, second_any,
        grad_ctx_any, grad_up_any, sums_ref, out_away, out_mine, down_away, down_mine, up_away, up_mine,
        full, send_sems, recv_sems, outw, downw, load_sems, slope, slope_sem, grad_ctx, grad_up, out_sems,
        ctx, act, second, row_sems, out_total, down_total, up_total, part_sems,
    ):
        grid = Grid2(sizes)
        core = lax.rem(lax.axis_index("dp"), 2)
        loads = [
            pltpu.make_async_copy(outw_any, outw, load_sems.at[0]),
            pltpu.make_async_copy(downw_any, downw, load_sems.at[1]),
        ]
        for copy in loads:
            copy.start()
        slopes = pltpu.make_async_copy(slope_any, slope, slope_sem)
        slopes.start()
        order_of = [
            grid.index(grid.nearest(0, k), grid.nearest(1, l)) for k in range(sizes[0]) for l in range(sizes[1])
        ]
        row_loads = [
            [
                pltpu.make_async_copy(there.at[place], here.at[i % 2], row_sems.at[i % 2, j])
                for j, (there, here) in enumerate(((ctx_any, ctx), (act_any, act), (second_any, second)))
            ]
            for i, place in enumerate(order_of)
        ]
        for copy in row_loads[0]:
            copy.start()
        full[grid.index(*grid.me)] = own_ref[...]
        sums_ref[...] = jnp.zeros_like(sums_ref)
        grid.barrier()
        open_copies = []

        def ready(slow, fast, order):
            place = grid.index(slow, fast)
            slot = order % 2
            if order == 0:
                for copy in loads + [slopes]:
                    copy.wait()
            if order >= 2:
                for copy in open_copies.pop(0):
                    copy.wait()
            if order + 1 < shards:
                for copy in row_loads[order + 1]:
                    copy.start()
            grad_ctx[slot] = dot_nt(full[place], outw[...]).astype(jnp.bfloat16)
            tile = tile_of(hidden)

            def up_tile(index, _):
                here = span(index, tile)
                found = dot_nt(full[place], downw[here, :]) * slope[place, :, here].astype(jnp.float32)
                rounded = found.astype(jnp.bfloat16)
                grad_up[slot, :, here] = rounded
                sums_ref[0:1, here] += jnp.sum(rounded.astype(jnp.float32), axis=0, keepdims=True)
                return _

            lax.fori_loop(0, hidden // tile, up_tile, 0)
            copies = [
                pltpu.make_async_copy(grad_ctx.at[slot], grad_ctx_any.at[place], out_sems.at[slot, 0]),
                pltpu.make_async_copy(grad_up.at[slot], grad_up_any.at[place], out_sems.at[slot, 1]),
            ]
            for copy in copies:
                copy.start()
            open_copies.append(copies)
            for copy in row_loads[order]:
                copy.wait()

            def add(total, here, found):
                if order == 0:
                    total[:, here] = found
                else:
                    total[:, here] += found

            def stream_tile(index, _):
                here = span(index, 512)
                grads = full[place, :, here]
                add(out_total, here, dot_tn(ctx[slot], grads))
                add(down_total, here, dot_tn(act[slot], grads))
                return _

            lax.fori_loop(0, D // 512, stream_tile, 0)

            def up_grad_tile(index, _):
                here = span(index, tile)
                add(up_total, here, dot_tn(second[slot], grad_up[slot, :, here]))
                return _

            lax.fori_loop(0, hidden // tile, up_grad_tile, 0)

        run_gather(grid, sizes, rows, full, send_sems, recv_sems, ready)
        for copies in open_copies:
            for copy in copies:
                copy.wait()
        stores = []

        def store(total, there, row, column, height, width):
            index = len(stores)
            if index < 2 * shards:
                here = full.at[index // 2, :, pl.ds((index % 2) * half_width, width)]
            else:
                here = slope.at[index - 2 * shards, :, pl.ds(0, width)]
            here[...] = total[
                pl.ds(pl.multiple_of(row, rows), rows), pl.ds(pl.multiple_of(column, 128), width)
            ].astype(jnp.bfloat16)
            copy = pltpu.make_async_copy(here, there.at[pl.ds(height, rows)], part_sems.at[index])
            copy.start()
            stores.append(copy)

        for which, wide in ((1 - core, (out_away, down_away, up_away)), (core, (out_mine, down_mine, up_mine))):
            for total, there, count in ((out_total, wide[0], inner), (down_total, wide[1], hidden)):
                for height in range(0, count, rows):
                    store(total, there, height, which * half_width, height, half_width)
            for height in range(0, half_width, rows):
                store(up_total, wide[2], which * half_width + height, 0, height, hidden)
        for copy in stores:
            copy.wait()

    def out(columns):
        return jax.ShapeDtypeStruct((shards, rows, columns), jnp.bfloat16)

    parts = [
        jax.ShapeDtypeStruct(shape, jnp.bfloat16)
        for shape in ((inner, half_width), (hidden, half_width), (half_width, hidden))
        for _ in range(2)
    ]
    stores = 2 * (inner // rows + hidden // rows + half_width // rows)
    return row_kernel(
        kernel, collective,
        [out(inner), out(hidden), jax.ShapeDtypeStruct((8, hidden), jnp.float32)] + parts,
        [VMEM] + [ANY] * 6,
        [ANY, ANY, VMEM] + [ANY] * 6,
        gather_scratch(sizes, rows)
        + [
            pltpu.VMEM(out_flat.shape, jnp.bfloat16),
            pltpu.VMEM(down_weight.shape, jnp.bfloat16),
            pltpu.SemaphoreType.DMA((2,)),
            pltpu.VMEM((shards, rows, hidden), jnp.bfloat16),
            pltpu.SemaphoreType.DMA,
            pltpu.VMEM((2, rows, inner), jnp.bfloat16),
            pltpu.VMEM((2, rows, hidden), jnp.bfloat16),
            pltpu.SemaphoreType.DMA((2, 2)),
            pltpu.VMEM((2, rows, inner), jnp.bfloat16),
            pltpu.VMEM((2, rows, hidden), jnp.bfloat16),
            pltpu.VMEM((2, rows, D), jnp.bfloat16),
            pltpu.SemaphoreType.DMA((2, 3)),
            pltpu.VMEM((inner, D), jnp.float32),
            pltpu.VMEM((hidden, D), jnp.float32),
            pltpu.VMEM((D, hidden), jnp.float32),
            pltpu.SemaphoreType.DMA((stores,)),
        ],
        4 * BLOCK * D * (inner + hidden) + 2 * BLOCK * D * hidden,
    )(own, out_flat, down_weight, slope, ctx, act, second)


class SmallSum:
    def __init__(self, shards, sums, total, scratch):
        self.shards, self.sums, self.total = shards, sums, total
        self.came, self.spread_send, self.spread_recv, self.back_send, self.back_recv = scratch
        self.here = lax.axis_index("seq")
        self.width = D // shards
        self.others = [(step, lax.rem(self.here + step, shards)) for step in range(1, shards)]

    @staticmethod
    def scratch(shards):
        dma = pltpu.SemaphoreType.DMA
        return [pltpu.VMEM((shards, 8, D // shards), jnp.float32)] + [dma((shards,))] * 4

    def barrier(self):
        sem = pltpu.get_barrier_semaphore()
        for _, place in self.others:
            pl.semaphore_signal(sem, inc=1, device_id={"seq": place}, device_id_type=MESH)
        pl.semaphore_wait(sem, self.shards - 1)

    def copy(self, place, src, dst, send, recv):
        return pltpu.make_async_remote_copy(
            src_ref=src, dst_ref=dst, send_sem=send, recv_sem=recv, device_id={"seq": place}, device_id_type=MESH
        )

    def columns(self, place):
        return pl.ds(pl.multiple_of(place * self.width, self.width), self.width)

    def spread(self):
        self.first = [
            self.copy(
                place, self.sums.at[:, self.columns(place)], self.came.at[step], self.spread_send.at[step],
                self.spread_recv.at[step],
            )
            for step, place in self.others
        ]
        for copy in self.first:
            copy.start()

    def collect(self):
        here = self.columns(self.here)
        total = self.sums[:, here]
        for (step, _), copy in zip(self.others, self.first):
            copy.wait_recv()
            total = total + self.came[step]
        self.total[:, here] = total
        self.second = [
            self.copy(
                place, self.total.at[:, here], self.total.at[:, here], self.back_send.at[step], self.back_recv.at[step]
            )
            for step, place in self.others
        ]
        for copy in self.second:
            copy.start()

    def finish(self):
        for step, _ in self.others:
            source = lax.rem(self.here + self.shards - step, self.shards)
            there = self.total.at[:, self.columns(source)]
            self.copy(source, there, there, self.back_send.at[step], self.back_recv.at[step]).wait_recv()
        for copy in self.first + self.second:
            copy.wait_send()


def score_rows(stats, lengths, labels, reference, sizes, replicas, collective):
    shards = sizes[0] * sizes[1]
    width = BLOCK // shards

    def kernel(
        stats_ref, lengths_ref, labels_ref, reference_ref, coef_ref, losses_ref,
        came, full, ratio, ratios, spread_send, spread_recv, back_send, back_recv, cross_send, cross_recv,
    ):
        seq, dp = lax.axis_index("seq"), lax.axis_index("dp")
        peers = {
            "seq": [(step, lax.rem(seq + step, shards)) for step in range(1, shards)],
            "dp": [(step, lax.rem(dp + step, replicas)) for step in range(1, replicas)],
        }
        barrier = pltpu.get_barrier_semaphore()
        for axis in peers:
            for _, place in peers[axis]:
                pl.semaphore_signal(barrier, inc=1, device_id={axis: place}, device_id_type=MESH)
        pl.semaphore_wait(barrier, shards + replicas - 2)

        def columns(place):
            return pl.ds(pl.multiple_of(place * width, width), width)

        def copy(axis, place, src, dst, send, recv):
            return pltpu.make_async_remote_copy(
                src_ref=src, dst_ref=dst, send_sem=send, recv_sem=recv, device_id={axis: place}, device_id_type=MESH
            )

        sent = [
            copy("seq", place, stats_ref.at[:, columns(place)], came.at[step], spread_send.at[step], spread_recv.at[step])
            for step, place in peers["seq"]
        ]
        for one in sent:
            one.start()
        mine = stats_ref[:, columns(seq)]
        top, total, pick = mine[0:1], mine[1:2], mine[2:3]
        for (step, _), one in zip(peers["seq"], sent):
            one.wait_recv()
            other = came[step]
            joint = jnp.maximum(top, other[0:1])
            total = total * jnp.exp(top - joint) + other[1:2] * jnp.exp(other[0:1] - joint)
            pick = pick + other[2:3]
            top = joint
        log_total = top + jnp.log(total)
        here = columns(seq)
        full[0:1, here] = log_total
        full[1:2, here] = pick - log_total
        back = [
            copy("seq", place, full.at[:, here], full.at[:, here], back_send.at[step], back_recv.at[step])
            for step, place in peers["seq"]
        ]
        for one in back:
            one.start()
        for step, _ in peers["seq"]:
            source = lax.rem(seq + shards - step, shards)
            there = full.at[:, columns(source)]
            copy("seq", source, there, there, back_send.at[step], back_recv.at[step]).wait_recv()
        example = lax.broadcasted_iota(jnp.int32, (EXB, 1), 0)
        start, end = jnp.zeros_like(example), jnp.zeros_like(example)
        sign, reference = jnp.zeros((EXB, 1), jnp.float32), jnp.zeros((EXB, 1), jnp.float32)
        reached = jnp.int32(0)
        for index in range(EXB):
            start = jnp.where(example == index, reached, start)
            reached = reached + lengths_ref[index]
            end = jnp.where(example == index, reached, end)
            sign = jnp.where(example == index, (2 * labels_ref[index] - 1).astype(jnp.float32), sign)
            reference = jnp.where(example == index, reference_ref[index], reference)
        counts = (end - start).astype(jnp.float32)
        row = lax.broadcasted_iota(jnp.int32, (EXB, BLOCK), 1)
        member = (row >= start) & (row < end)
        mean = jnp.sum(jnp.where(member, full[1:2, :], 0.0), axis=1, keepdims=True) / counts
        log_ratio = mean - reference
        ratio[...] = jnp.broadcast_to(jnp.sum(log_ratio, axis=0, keepdims=True), ratio.shape)
        crossed = [
            copy("dp", place, ratio, ratios.at[dp], cross_send.at[step], cross_recv.at[step])
            for step, place in peers["dp"]
        ]
        for one in crossed:
            one.start()
        for one in crossed:
            one.wait_recv()
        ratios[dp] = ratio[...]
        whole = ratios[0]
        for place in range(1, replicas):
            whole = whole + ratios[place]
        center = whole[:, 0:1] / (replicas * EXB)
        squashed = jax.nn.sigmoid(BETA * sign * (log_ratio - center))
        losses_ref[...] = jnp.broadcast_to(1.0 - squashed, losses_ref.shape)
        grad = -LOSS_SCALE * BETA * sign * squashed * (1.0 - squashed) / counts
        token = jnp.sum(jnp.where(member, grad, 0.0), axis=0, keepdims=True)
        coef_ref[...] = jnp.zeros_like(coef_ref)
        coef_ref[0:1, :] = token
        coef_ref[1:2, :] = token * jnp.exp(stats_ref[0:1, :] - full[0:1, :])
        for one in sent + back + crossed:
            one.wait_send()

    dma = pltpu.SemaphoreType.DMA
    return pl.pallas_call(
        kernel,
        out_shape=[
            jax.ShapeDtypeStruct((8, BLOCK), jnp.float32),
            jax.ShapeDtypeStruct((EXB, 128), jnp.float32),
        ],
        in_specs=[VMEM] + [SMEM] * 3,
        out_specs=[VMEM] * 2,
        scratch_shapes=[
            pltpu.VMEM((shards, 8, width), jnp.float32),
            pltpu.VMEM((8, BLOCK), jnp.float32),
            pltpu.VMEM((EXB, 128), jnp.float32),
            pltpu.VMEM((replicas, EXB, 128), jnp.float32),
            dma((shards,)), dma((shards,)), dma((shards,)), dma((shards,)), dma((replicas,)), dma((replicas,)),
        ],
        compiler_params=pltpu.CompilerParams(collective_id=collective, has_side_effects=True),
    )(stats, lengths, labels, reference)


def input_grad_rows(
    own, grad_stream, plain, grad_qkv, grad_up, qkv_flat, up_weight, gains, end_sums, sizes, collective,
    before,
):
    shards, rows, width = grad_qkv.shape
    hidden = grad_up.shape[2]

    def kernel(
        own_ref, stream_ref, normed_any, qkv_any, up_any, qkvw_any, upw_any, gains_ref, end_ref,
        out_ref, total_ref,
        qkvw, upw, weight_sems, normed, qkv, up, load_sems, sums_ref, *scratch,
    ):
        grid = Grid2(sizes)
        small = SmallSum(shards, sums_ref, total_ref, scratch[:5])
        scratch = scratch[5:]
        parts = scratch[0]
        order = production_order(grid)

        def loads(i):
            place = order[i]
            return [
                pltpu.make_async_copy(normed_any.at[place], normed.at[i % 2], load_sems.at[i, 0]),
                pltpu.make_async_copy(qkv_any.at[place], qkv.at[i % 2], load_sems.at[i, 1]),
                pltpu.make_async_copy(up_any.at[place], up.at[i % 2], load_sems.at[i, 2]),
            ]

        copies = [loads(i) for i in range(shards)]
        weights = [
            pltpu.make_async_copy(qkvw_any, qkvw, weight_sems.at[0]),
            pltpu.make_async_copy(upw_any, upw, weight_sems.at[1]),
        ]
        for copy in copies[0] + weights:
            copy.start()
        sums_ref[...] = jnp.zeros_like(sums_ref)
        small.barrier()
        for copy in weights:
            copy.wait()
        count = [0]

        def produce(slow, fast):
            place = grid.index(slow, fast)
            i = count[0]
            count[0] += 1
            if i + 1 < shards:
                for copy in copies[i + 1]:
                    copy.start()
            for copy in copies[i]:
                copy.wait()
            slot = i % 2

            def columns(index, _):
                here = span(index, 512)
                one = dot_nt(qkv[slot], qkvw[here, :])
                two = dot_nt(up[slot], upw[here, :])
                norm = normed[slot, :, here].astype(jnp.float32)
                parts[place, :, here] = (one * gains_ref[0:1, here] + two * gains_ref[1:2, here]).astype(
                    jnp.bfloat16
                )
                sums_ref[0:1, here] += jnp.sum(one * norm, axis=0, keepdims=True)
                sums_ref[1:2, here] += jnp.sum(one, axis=0, keepdims=True)
                sums_ref[2:3, here] += jnp.sum(two * norm, axis=0, keepdims=True)
                sums_ref[3:4, here] += jnp.sum(two, axis=0, keepdims=True)
                return _

            lax.fori_loop(0, D // 512, columns, 0)

        def made():
            sums_ref[4:8] = end_ref[0:4]
            small.spread()

        run_scatter(grid, sizes, rows, scratch, produce, made, small.collect)
        mine = grid.index(*grid.me)

        def norm_tile(index, _):
            here = span(index, ROW_TILE)
            grad = parts[mine, here].astype(jnp.float32)
            centered, inverse = tile_stats(own_ref[here].astype(jnp.float32))
            normed = centered * inverse
            out_ref[here] = stream_ref[here] + inverse * (
                grad
                - jnp.mean(grad, axis=1, keepdims=True)
                - normed * jnp.mean(grad * normed, axis=1, keepdims=True)
            )
            return _

        lax.fori_loop(0, rows // ROW_TILE, norm_tile, 0)
        small.finish()

    return row_kernel(
        kernel, collective,
        [jax.ShapeDtypeStruct((rows, D), jnp.float32), jax.ShapeDtypeStruct((8, D), jnp.float32)],
        [VMEM, VMEM, ANY, ANY, ANY, ANY, ANY, VMEM, VMEM],
        [VMEM, VMEM],
        [
            pltpu.VMEM(qkv_flat.shape, jnp.bfloat16),
            pltpu.VMEM(up_weight.shape, jnp.bfloat16),
            pltpu.SemaphoreType.DMA((2,)),
            pltpu.VMEM((2, rows, D), jnp.bfloat16),
            pltpu.VMEM((2, rows, width), jnp.bfloat16),
            pltpu.VMEM((2, rows, hidden), jnp.bfloat16),
            pltpu.SemaphoreType.DMA((shards, 3)),
            pltpu.VMEM((8, D), jnp.float32),
        ]
        + SmallSum.scratch(shards)
        + sum_scratch(sizes, rows),
        1,
        before,
    )(own, grad_stream, plain, grad_qkv, grad_up, qkv_flat, up_weight, gains, end_sums)


def join_halves(sums, others, earlier):
    steps, count = 8, len(sums)

    def kernel(*refs):
        for i in range(count):
            refs[2 * count + 1 + i][...] = (
                refs[i][...].astype(jnp.float32) + refs[count + i][...].astype(jnp.float32)
            ).astype(jnp.bfloat16)

    specs = [pl.BlockSpec((v.shape[0] // steps, v.shape[1]), lambda i: (i, 0)) for v in sums]
    return pl.pallas_call(
        kernel,
        grid=(steps,),
        out_shape=[jax.ShapeDtypeStruct(v.shape, jnp.bfloat16) for v in sums],
        in_specs=specs + specs + [ANY],
        out_specs=specs,
        compiler_params=pltpu.CompilerParams(vmem_limit_bytes=VMEM_LIMIT),
    )(*sums, *others, earlier)


def settle_halves(core, totals, backs, shapes, before=()):
    steps = 8

    def kernel(core_ref, *refs):
        count = len(totals)
        mine = pl.program_id(0) == 0
        for i in range(count):
            found = jnp.where(mine, refs[i][...].astype(jnp.float32), refs[count + i][...].astype(jnp.float32))
            out = refs[2 * count + len(before) + i]
            if len(out.shape) == 3:
                for head in range(out.shape[1]):
                    out[:, head, :] = found[:, head * out.shape[2] : (head + 1) * out.shape[2]]
            else:
                out[...] = found

    def place(half, core_ref):
        return jnp.where(half == 0, core_ref[0], 1 - core_ref[0])

    ins, outs = [], []
    for which in (0, 1):
        for value in totals:
            ins.append(
                pl.BlockSpec(
                    (value.shape[0] // steps, value.shape[1]),
                    (lambda h, i, core_ref: (jnp.where(h == 0, i, steps - 1), 0))
                    if which == 0
                    else (lambda h, i, core_ref: (jnp.where(h == 0, 0, i), 0)),
                )
            )
    for value, shape in zip(totals, shapes):
        rows = value.shape[0] // steps
        if len(shape) == 3:
            outs.append(
                pl.BlockSpec((rows,) + shape[1:], lambda h, i, core_ref: (place(h, core_ref) * steps + i, 0, 0))
            )
        elif shape[0] == value.shape[0]:
            outs.append(pl.BlockSpec((rows, value.shape[1]), lambda h, i, core_ref: (i, place(h, core_ref))))
        else:
            outs.append(pl.BlockSpec((rows, shape[1]), lambda h, i, core_ref: (place(h, core_ref) * steps + i, 0)))
    return pl.pallas_call(
        kernel,
        grid_spec=pltpu.PrefetchScalarGridSpec(
            num_scalar_prefetch=1, grid=(2, steps), in_specs=ins + [ANY] * len(before), out_specs=outs
        ),
        out_shape=[jax.ShapeDtypeStruct(shape, jnp.float32) for shape in shapes],
        compiler_params=pltpu.CompilerParams(vmem_limit_bytes=VMEM_LIMIT),
    )(core, *totals, *backs, *before)


def row_of(vector):
    return vector.astype(jnp.float32)[None, :]


def held(values):
    return lax.optimization_barrier(values)


def half_of(values, which):
    half = values.shape[1] // 2
    return lax.dynamic_slice_in_dim(values, which * half, half, 1)


def pairs(step):
    return [(place, place ^ step) for place in range(lax.axis_size("dp"))]


class PairSum:
    def __init__(self, away, mine):
        self.plain = lax.axis_size("dp") != 4
        self.core = lax.rem(lax.axis_index("dp"), 2)
        came = lax.ppermute(away, "dp", pairs(1))
        self.sum = (mine.astype(jnp.float32) + came.astype(jnp.float32)).astype(jnp.bfloat16)

    def cross(self):
        if self.plain:
            none = jnp.zeros_like(self.sum)
            both = jnp.stack([jnp.where(self.core == which, self.sum, none) for which in (0, 1)])
            self.other = lax.psum(both, "dp")
        else:
            self.other = lax.ppermute(self.sum, "dp", pairs(2))
        return self

    def join(self, earlier):
        self.total = self.other if self.plain else join_halves([self.sum], [self.other], earlier)[0]
        return self


def sum_over_dp(values):
    if lax.axis_size("dp") != 4:
        return lax.psum(values, "dp")
    for step in (1, 2):
        values = values + lax.ppermute(values, "dp", pairs(step))
    return values


def pair_product(product):
    core = lax.rem(lax.axis_index("dp"), 2)
    return PairSum(product(1 - core).astype(jnp.bfloat16), held(product(core)))


def join_all(sums, earlier):
    if not sums[0].plain:
        totals = join_halves([one.sum for one in sums], [one.other for one in sums], earlier)
        for one, total in zip(sums, totals):
            one.total = total


def settle_all(sums, shapes, before=()):
    if sums[0].plain:
        core = jnp.zeros((1,), jnp.int32)
        return settle_halves(core, [s.other[0] for s in sums], [s.other[1] for s in sums], shapes, before)
    backs = [lax.ppermute(one.total, "dp", pairs(1)) for one in sums]
    return settle_halves(sums[0].core[None], [one.total for one in sums], backs, shapes, before)


def per_device(
    hidden, targets, lengths, labels, ref_logps, ln1_gain, ln1_bias, ln2_gain, ln2_bias, qkv_weight, qv_bias,
    out_weight, up_weight, up_bias, down_weight, branch_bias, lnf_gain, lnf_bias, head_weight,
):
    sizes = lines_of(lax.axis_size("seq"))
    own = hidden[0]
    local_heads = qkv_weight.shape[1]
    local_vocab = head_weight.shape[1]
    local_hidden = up_weight.shape[1]
    width = local_heads * 3 * HEAD_DIM
    inner = local_heads * HEAD_DIM
    qv_float = qv_bias.astype(jnp.float32)
    full_bias = jnp.concatenate(
        [qv_float[:, :HEAD_DIM], jnp.zeros_like(qv_float[:, :HEAD_DIM]), qv_float[:, HEAD_DIM:]], axis=-1
    ).reshape(1, width)
    qkv_flat = qkv_weight.reshape(D, width)
    out_flat = out_weight.reshape(inner, D)
    block_lengths = lengths[0]
    norms = jnp.concatenate([row_of(v) for v in (ln1_gain, ln1_bias, ln2_gain, ln2_bias)], axis=0)
    plain, first_full, second_full, qkv, act, slope, *planes = open_rows(
        own, sizes, 0, norms, qkv_flat, full_bias, up_weight, row_of(up_bias), block_lengths
    )
    flat_qkv = qkv.reshape(BLOCK, width)
    ctx, lse = attention_forward(flat_qkv, block_lengths, local_heads)
    shards, rows = plain.shape[0], plain.shape[1]
    end_norms = jnp.concatenate([row_of(v) for v in (lnf_gain, lnf_bias, branch_bias)], axis=0)
    output, final, normed, inverse = branch_rows(
        own, ctx.reshape(shards, rows, inner), act, out_flat, down_weight, end_norms, sizes, 1
    )
    targets_col = targets[0][:, None]
    final_full, weights, stats = logit_rows(final, head_weight, targets_col, sizes, 2)

    coef, losses = score_rows(
        stats, block_lengths, labels[0], ref_logps[0], sizes, lax.axis_size("dp"), 6
    )
    vocab_ids = lax.axis_index("seq") * local_vocab + jnp.arange(local_vocab, dtype=jnp.int32)
    grad_logits = held((
        jnp.where(vocab_ids[None, :] == targets[0][:, None], coef[0][:, None], 0.0)
        - weights.reshape(BLOCK, local_vocab).astype(jnp.float32) * coef[1][:, None]
    ).astype(jnp.bfloat16))
    final_rows = final_full.reshape(BLOCK, D)
    head_sum = pair_product(lambda which: dot_tn(half_of(final_rows, which), grad_logits)).cross()

    grad_stream, grad_own, end_sums = final_grad_rows(
        grad_logits.reshape(shards, rows, local_vocab), head_weight, normed, inverse, row_of(lnf_gain), sizes, 3,
        (head_sum.sum,),
    )
    grad_ctx, grad_up, up_sums, *halves = branch_grad_rows(
        grad_own, out_flat, down_weight, slope, ctx.reshape(shards, rows, inner), act, second_full, sizes, 4
    )
    sums = [PairSum(*halves[2 * i : 2 * i + 2]).cross() for i in range(3)]
    grad_qkv, qkv_sums = attention_backward(
        flat_qkv, block_lengths, local_heads, ctx, lse, grad_ctx.reshape(BLOCK, inner), planes,
        (),
    )
    first_rows = first_full.reshape(BLOCK, D)
    sums.append(pair_product(lambda which: dot_tn(half_of(first_rows, which), grad_qkv)).cross())
    qkv_sums = qkv_sums[:, 0]
    qv_grad = jnp.concatenate([qkv_sums[:, :HEAD_DIM], qkv_sums[:, 2 * HEAD_DIM :]], axis=-1)
    split = local_heads * 2 * HEAD_DIM
    biases = jnp.concatenate([qv_grad.reshape(-1), up_sums[0]])
    biases = jnp.pad(biases[None, :], ((0, 0), (0, D - biases.shape[0])))
    gains = jnp.concatenate([row_of(ln1_gain), row_of(ln2_gain)], axis=0)
    grad_input, group_sums = input_grad_rows(
        own, grad_stream, plain, grad_qkv.reshape(shards, rows, width), grad_up, qkv_flat, up_weight, gains,
        end_sums, sizes, 5, (sums[-1].sum, head_sum.join(up_sums).total),
    )
    (head_grad,) = settle_all([head_sum], [(D, local_vocab)], (group_sums,))
    join_all(sums, head_grad)
    small = sum_over_dp(jnp.concatenate([group_sums[:7], biases], axis=0))
    out_grad, down_grad, up_grad, qkv_grad = settle_all(
        sums, [(inner, D), (local_hidden, D), (D, local_hidden), qkv_weight.shape]
    )
    return (
        losses[:, 0][None],
        output[None],
        grad_input[None],
        small[0],
        small[1],
        small[2],
        small[3],
        qkv_grad,
        small[7, :split].reshape(local_heads, 2 * HEAD_DIM),
        out_grad.reshape(out_weight.shape),
        up_grad,
        small[7, split : split + local_hidden],
        down_grad,
        small[6],
        small[4],
        small[5],
        head_grad,
    )


def solution(mesh):
    return jax.shard_map(
        per_device,
        mesh=mesh,
        in_specs=(
            P("dp", "seq", None),
            P("dp", None),
            P("dp", None),
            P("dp", None),
            P("dp", None),
            P(),
            P(),
            P(),
            P(),
            P(None, "seq", None),
            P("seq", None),
            P("seq", None, None),
            P(None, "seq"),
            P("seq"),
            P("seq", None),
            P(),
            P(),
            P(),
            P(None, "seq"),
        ),
        out_specs=(
            P("dp", None),
            P("dp", "seq", None),
            P("dp", "seq", None),
            P(),
            P(),
            P(),
            P(),
            P(None, "seq", None),
            P("seq", None),
            P("seq", None, None),
            P(None, "seq"),
            P("seq"),
            P("seq", None),
            P(),
            P(),
            P(),
            P(None, "seq"),
        ),
        check_vma=False,
    )
```

```python
import jax
import jax.numpy as jnp
from jax import lax
from jax.experimental import pallas as pl
from jax.experimental.pallas import tpu as pltpu
from jax.sharding import PartitionSpec as P

D = 2048
HEAD_DIM = 128
ROT = 32
BLOCK = 2048
EXB = 8
EPSILON = 1e-05
BETA = 0.25
LOSS_SCALE = 65536.0
HALVES = 2
VMEM_LIMIT = 62 * 2**20

MESH = pl.DeviceIdType.MESH


class Grid2:
    def __init__(self, sizes):
        self.n = sizes
        place = lax.axis_index("seq")
        self.me = (place // sizes[1], lax.rem(place, sizes[1]))

    def index(self, slow, fast):
        return slow * self.n[1] + fast

    def device(self, axis, spot):
        here = list(self.me)
        here[axis] = spot
        return {"seq": self.index(*here)}

    def nearest(self, axis, rank):
        n, m = self.n[axis], self.me[axis]
        if rank == 0:
            return m
        if n == 2:
            return 1 - m
        after = n - 1 - m
        both = jnp.minimum(m, after)
        dist = (rank + 1) // 2
        near = m - dist if rank % 2 else m + dist
        far = jnp.where(m < after, m + (rank - both), m - (rank - both))
        return jnp.where(rank <= 2 * both, near, far)

    def neighbours(self):
        found = []
        for axis in (0, 1):
            m, n = self.me[axis], self.n[axis]
            if n == 2:
                found.append((None, self.device(axis, 1 - m)))
            elif n > 2:
                found.append((m > 0, self.device(axis, m - 1)))
                found.append((m < n - 1, self.device(axis, m + 1)))
        return found

    def barrier(self, *others):
        sem = pltpu.get_barrier_semaphore()
        amount = jnp.int32(0)
        for there, device in self.neighbours() + [(None, device) for device in others]:
            def tell(device=device):
                pl.semaphore_signal(sem, inc=1, device_id=device, device_id_type=MESH)
            if there is None:
                tell()
                amount = amount + 1
            else:
                pl.when(there)(tell)
                amount = amount + there.astype(jnp.int32)
        pl.semaphore_wait(sem, amount)


class Sender:
    def __init__(self, send_sems):
        self.sems = send_sems
        self.used = 0
        self.open = []

    def send(self, src, dst, recv_sem, device, when=None):
        copy = pltpu.make_async_remote_copy(
            src_ref=src, dst_ref=dst, send_sem=self.sems.at[self.used], recv_sem=recv_sem,
            device_id=device, device_id_type=MESH)
        self.used += 1
        if when is None:
            copy.start()
        else:
            pl.when(when)(copy.start)
        self.open.append((when, copy))

    def finish(self):
        for when, copy in self.open:
            if when is None:
                copy.wait_send()
            else:
                pl.when(when)(copy.wait_send)
        self.open = []


def gather_sends(sizes, halves):
    return halves * 2 * (sizes[0] * sizes[1] * 5 + 8)


def gather_rounds(grid, sender, piece, recv_sems, halves, cut, ready):
    n, me = grid.n, grid.me

    def arrived(slow, fast, half, kind, when):
        ref = piece(grid.index(slow, fast), half, kind)
        sem = recv_sems.at[kind, half, grid.index(slow, fast)]
        wait = pltpu.make_async_copy(ref, ref, sem).wait
        if when is None:
            wait()
        else:
            pl.when(when)(wait)

    def push(slow, fast, half, kind, axis, spot, *conditions):
        ref = piece(grid.index(slow, fast), half, kind)
        sem = recv_sems.at[kind, half, grid.index(slow, fast)]
        when = None
        for condition in conditions:
            if condition is not None:
                when = condition if when is None else when & condition
        sender.send(ref, ref, sem, grid.device(axis, spot), when)

    def spread(slow, fast, half, kind, axis, when):
        m, size = me[axis], n[axis]
        if size == 2:
            push(slow, fast, half, kind, axis, 1 - m, when)
        elif size > 2:
            push(slow, fast, half, kind, axis, m + 1, when, m < size - 1)
            push(slow, fast, half, kind, axis, m - 1, when, m > 0)

    def onward(slow, fast, half, kind, axis, when):
        m, size = me[axis], n[axis]
        if size <= 2:
            return
        below = (slow, fast)[axis] < m
        more = (below & (m < size - 1)) | (jnp.logical_not(below) & (m > 0))
        push(slow, fast, half, kind, axis, jnp.where(below, m + 1, m - 1), when, more)

    def sides(d):
        if d == 0:
            return [(me[0], None)]
        if n[0] == 2:
            return [(1 - me[0], None)]
        return [(me[0] - d, me[0] >= d), (me[0] + d, me[0] + d < n[0])]

    def settle(d):
        for half in range(halves):
            for slow, when in sides(d):
                for l in range(n[1]):
                    fast = grid.nearest(1, l)
                    if d > 0:
                        arrived(slow, fast, half, 1, when)
                        onward(slow, fast, half, 1, 0, when)
                    else:
                        spread(slow, fast, half, 1, 0, when)

    def complete(d):
        for l in range(1, n[1]):
            fast = grid.nearest(1, l)
            for half in range(halves):
                for slow, when in sides(d):
                    arrived(slow, fast, half, 0, when)
                    onward(slow, fast, half, 0, 1, when)

    def work(k, l):
        ready(grid.nearest(0, k), grid.nearest(1, l), k * n[1] + l)

    for half in range(halves):
        for kind in (1, 0):
            if cut[kind]:
                spread(me[0], me[1], half, kind, kind, None)
        if cut[0]:
            spread(me[0], me[1], half, 0, 1, None)
    work(0, 0)
    if cut[1]:
        for half in range(halves):
            for l in range(1, n[1]):
                fast = grid.nearest(1, l)
                arrived(me[0], fast, half, 1, None)
                onward(me[0], fast, half, 1, 1, None)
        settle(0)
    for d in range(1, n[0]):
        if cut[0]:
            for half in range(halves):
                for slow, when in sides(d):
                    arrived(slow, me[1], half, 0, when)
                    onward(slow, me[1], half, 0, 0, when)
                    spread(slow, me[1], half, 0, 1, when)
            complete(d - 1)
        for l in range(1, n[1]):
            work(d - 1, l)
        if cut[1]:
            settle(d)
        work(d, 0)
    if cut[0]:
        complete(n[0] - 1)
    for l in range(1, n[1]):
        work(n[0] - 1, l)


def scatter_slots(n):
    return 1 if n == 2 else n + 1


def scatter_plan(n, quick):
    if n == (4, 2) and not quick:
        return [
            ("make", 3, 1), ("make", 2, 1), ("make", 3, 0), ("make", 1, 1), ("first", 3), ("make", 2, 0),
            ("make", 0, 1), ("later", 3, 0), ("make", 1, 0), ("later", 3, 1), ("first", 2), ("make", 0, 0), ("made",),
            ("later", 2, 0), ("later", 2, 1), ("first", 1), ("later", 1, 0), ("later", 1, 1),
        ]
    far = n[0] - 1
    plan = [("make", k, l) for l in range(n[1] - 1, -1, -1) for k in range(far, -1, -1)] + [("made",)]
    for k in range(far, 0, -1):
        plan += [("first", k), ("later", k, 0), ("later", k, 1)]
    return plan


class Scatter:
    def __init__(self, grid, sender, part, bufs, sems, halves, cut, quick):
        self.grid, self.sender, self.part, self.quick = grid, sender, part, quick
        self.bufs, self.sems, self.halves, self.cut = bufs, sems, halves, cut

    def slot(self, axis, target, from_below):
        if self.grid.n[axis] == 2:
            return 0
        return target + jnp.where(from_below, 1, 0)

    def take(self, kind, stage, axis, other, target, from_below, half, when, slot_index):
        buf, sem = self.bufs[kind][stage], self.sems[kind][stage]
        slot = self.slot(axis, target, from_below)

        def add():
            ref = buf.at[other, slot, half]
            pltpu.make_async_copy(ref, ref, sem.at[other, slot, half]).wait()
            mine = self.part(slot_index, half, kind)
            mine[...] = (mine[...].astype(jnp.float32) + ref[...].astype(jnp.float32)).astype(mine.dtype)

        if when is None:
            add()
        else:
            pl.when(when)(add)

    def incoming(self, axis, target):
        m, n = self.grid.me[axis], self.grid.n[axis]
        if n == 2:
            return None
        up = target > m
        return (up & (m > 0)) | (jnp.logical_not(up) & (m < n - 1))

    def toward(self, kind, stage, axis, other, target, half, slow, fast, when=None):
        grid = self.grid
        m, n = grid.me[axis], grid.n[axis]
        up = target > m
        index = grid.index(slow, fast)
        if n > 2:
            incoming = self.incoming(axis, target)
            self.take(kind, stage, axis, other, target, up, half, incoming if when is None else incoming & when, index)
        buf, sem = self.bufs[kind][stage], self.sems[kind][stage]
        slot = self.slot(axis, target, up)
        spot = 1 - m if n == 2 else jnp.where(up, m + 1, m - 1)
        self.sender.send(
            self.part(index, half, kind), buf.at[other, slot, half], sem.at[other, slot, half],
            grid.device(axis, spot), when)

    def last(self, kind, stage, axis, other, half, slow, fast):
        grid = self.grid
        m, n = grid.me[axis], grid.n[axis]
        index = grid.index(slow, fast)
        if n == 2:
            self.take(kind, stage, axis, other, m, m > 0, half, None, index)
        elif n > 2:
            self.take(kind, stage, axis, other, m, jnp.bool_(True), half, m > 0, index)
            self.take(kind, stage, axis, other, m, jnp.bool_(False), half, m < n - 1, index)

    def run(self, produce, made=lambda: None, late=lambda: None):
        grid, n, me = self.grid, self.grid.n, self.grid.me
        lagging = []

        def chain(k, half, begins):
            slow = grid.nearest(0, k)
            incoming = self.incoming(0, slow)
            if incoming is None:
                if begins:
                    self.last(0, 0, 1, slow, half, slow, me[1])
                    self.toward(0, 1, 0, 0, slow, half, slow, me[1])
                return
            when = jnp.logical_not(incoming) if begins else incoming
            pl.when(when)(lambda: self.last(0, 0, 1, slow, half, slow, me[1]))
            self.toward(0, 1, 0, 0, slow, half, slow, me[1], when)

        def catch_up():
            for step in lagging:
                self.toward(*step)
            lagging.clear()

        def make(k, l):
            slow, fast = grid.nearest(0, k), grid.nearest(1, l)
            produce(slow, fast)
            if self.cut[0] and l > 0:
                for half in range(self.halves):
                    self.toward(0, 0, 1, slow, fast, half, slow, fast)
            catch_up()
            if self.cut[1] and k > 0:
                for half in range(self.halves):
                    lagging.append((1, 0, 0, fast, slow, half, slow, fast))

        for step in scatter_plan(n, self.quick):
            if step[0] == "make":
                make(*step[1:])
            elif step[0] == "made":
                catch_up()
                made()
            elif step[0] == "first" and self.cut[0]:
                for half in range(self.halves):
                    chain(step[1], half, True)
            elif self.cut[0]:
                chain(step[1], step[2], False)
        if self.cut[1]:
            for half in range(self.halves):
                for l in reversed(range(n[1])):
                    fast = grid.nearest(1, l)
                    self.last(1, 0, 0, fast, half, me[0], fast)
                    if l > 0:
                        self.toward(1, 1, 1, 0, fast, half, me[0], fast)
        late()
        if self.cut[0]:
            for half in range(self.halves):
                self.last(0, 0, 1, me[0], half, me[0], me[1])
        for half in range(self.halves):
            if self.cut[1]:
                self.last(1, 1, 1, 0, half, me[0], me[1])
            if self.cut[0]:
                self.last(0, 1, 0, 0, half, me[0], me[1])


def scatter_scratch(sizes, halves, rows, cols, cut):
    bufs, sems = [], []
    for kind, stages in ((0, (1, 0)), (1, (0, 1))):
        for stage, axis in enumerate(stages):
            lead = (sizes[1 - axis] if stage == 0 else 1, scatter_slots(sizes[axis]), halves)
            width = max(cut[kind], 128)
            bufs.append(pltpu.VMEM(lead + (rows // halves, width), jnp.bfloat16))
            sems.append(pltpu.SemaphoreType.DMA(lead))
    return bufs, sems


def scatter_sends(sizes, halves):
    return halves * 2 * (sizes[0] * sizes[1] + sizes[0] + sizes[1])


def lines_of(seq):
    fast = 2 if seq <= 8 else 4
    return (seq // fast, fast)


ATT_TILE = 256


def span(index, size):
    return pl.ds(pl.multiple_of(index * size, size), size)


SCALE = HEAD_DIM ** (-0.5)


def dot_nt(left, right):
    return lax.dot_general(left, right, (((1,), (1,)), ((), ())), preferred_element_type=jnp.float32)


def dot_tn(left, right):
    return lax.dot_general(left, right, (((0,), (0,)), ((), ())), preferred_element_type=jnp.float32)


def rotary_frequencies():
    half_rot = ROT // 2
    frequency = 10000.0 ** (-2.0 * jnp.arange(half_rot, dtype=jnp.float32) / ROT)
    return jnp.tile(frequency, HEAD_DIM // half_rot)[None, :]


def first_rows(lengths, row):
    start, end = jnp.zeros_like(row), jnp.int32(0)
    for example in range(EXB):
        end = end + lengths[example]
        start = jnp.where(row >= end, end, start)
    return start


def rotary_planes(position, frequencies):
    half_rot = ROT // 2
    angles = position.astype(jnp.float32) * frequencies
    cos, sin = jnp.cos(angles), jnp.sin(angles)
    lane = lax.broadcasted_iota(jnp.int32, angles.shape, 1)
    return (
        jnp.where(lane < ROT, cos, 1.0),
        jnp.where((lane >= half_rot) & (lane < ROT), sin, 0.0),
        jnp.where(lane < half_rot, -sin, 0.0),
    )


def turn(vector, cos, from_below, from_above):
    half_rot = ROT // 2
    return (
        vector * cos
        + pltpu.roll(vector, half_rot, 1) * from_below
        + pltpu.roll(vector, HEAD_DIM - half_rot, 1) * from_above
    )


def tile_mask(start_col, query_tile, key_tile):
    shape = (ATT_TILE, ATT_TILE)
    query_ids = query_tile * ATT_TILE + lax.broadcasted_iota(jnp.int32, shape, 0)
    key_ids = key_tile * ATT_TILE + lax.broadcasted_iota(jnp.int32, shape, 1)
    return (key_ids >= start_col) & (key_ids <= query_ids)


def tile_starts(lengths, tile):
    rows = tile * ATT_TILE + lax.broadcasted_iota(jnp.int32, (ATT_TILE, 1), 0)
    return first_rows(lengths, rows), first_rows(lengths, tile * ATT_TILE) // ATT_TILE


def attention_forward(qkv, lengths, heads):
    tiles = BLOCK // ATT_TILE

    def kernel(lengths_ref, qkv_ref, ctx_ref, lse_ref):
        tile = pl.program_id(0)
        start, first = tile_starts(lengths_ref, tile)
        here = span(tile, ATT_TILE)
        queries = [qkv_ref[here, 3 * head * HEAD_DIM : (3 * head + 1) * HEAD_DIM] for head in range(heads)]

        def step(key_tile, carry):
            rows = span(key_tile, ATT_TILE)
            allowed = tile_mask(start, tile, key_tile)
            found = []
            for head in range(heads):
                top, total, acc = carry[head]
                keys = qkv_ref[rows, (3 * head + 1) * HEAD_DIM : (3 * head + 2) * HEAD_DIM]
                values = qkv_ref[rows, (3 * head + 2) * HEAD_DIM : (3 * head + 3) * HEAD_DIM]
                scores = jnp.where(allowed, dot_nt(queries[head], keys) * SCALE, -1e30)
                new_top = jnp.maximum(top, jnp.max(scores, axis=1, keepdims=True))
                shrink = jnp.exp(top - new_top)
                weights = jnp.exp(scores - new_top)
                total = total * shrink + jnp.sum(weights, axis=1, keepdims=True)
                acc = acc * shrink + jnp.dot(
                    weights.astype(jnp.bfloat16), values, preferred_element_type=jnp.float32
                )
                found.append((new_top, total, acc))
            return tuple(found)

        begin = (
            jnp.full((ATT_TILE, 1), -1e30, jnp.float32),
            jnp.zeros((ATT_TILE, 1), jnp.float32),
            jnp.zeros((ATT_TILE, HEAD_DIM), jnp.float32),
        )
        result = lax.fori_loop(first, tile, step, step(tile, (begin,) * heads))
        for head in range(heads):
            top, total, acc = result[head]
            ctx_ref[:, head * HEAD_DIM : (head + 1) * HEAD_DIM] = (acc / total).astype(jnp.bfloat16)
            lse_ref[head] = top + jnp.log(total)

    return pl.pallas_call(
        kernel,
        grid_spec=pltpu.PrefetchScalarGridSpec(
            num_scalar_prefetch=1,
            grid=(tiles,),
            in_specs=[pl.BlockSpec(qkv.shape, lambda i, lengths: (0, 0))],
            out_specs=[
                pl.BlockSpec((ATT_TILE, heads * HEAD_DIM), lambda i, lengths: (i, 0)),
                pl.BlockSpec((heads, ATT_TILE, 1), lambda i, lengths: (0, i, 0)),
            ],
        ),
        out_shape=[
            jax.ShapeDtypeStruct((BLOCK, heads * HEAD_DIM), jnp.bfloat16),
            jax.ShapeDtypeStruct((heads, BLOCK, 1), jnp.float32),
        ],
        compiler_params=pltpu.CompilerParams(vmem_limit_bytes=VMEM_LIMIT),
    )(lengths, qkv)


def attention_backward(qkv, lengths, heads, ctx, lse, grad_ctx, planes):
    tiles = BLOCK // ATT_TILE

    def kernel(
        lengths_ref, qkv_ref, ctx_ref, lse_ref, do_ref, cos_ref, below_ref, above_ref, out_ref, sums_ref, dk_ref,
        dv_ref,
    ):
        tile = pl.program_id(0)

        @pl.when(tile == 0)
        def _():
            dk_ref[...] = jnp.zeros_like(dk_ref)
            dv_ref[...] = jnp.zeros_like(dv_ref)

        start, first = tile_starts(lengths_ref, tile)
        here = span(tile, ATT_TILE)
        fixed = []
        for head in range(heads):
            lanes = slice(head * HEAD_DIM, (head + 1) * HEAD_DIM)
            grads = do_ref[:, lanes]
            inner = jnp.sum(
                grads.astype(jnp.float32) * ctx_ref[:, lanes].astype(jnp.float32), axis=1, keepdims=True
            )
            queries = qkv_ref[here, 3 * head * HEAD_DIM : (3 * head + 1) * HEAD_DIM]
            fixed.append((queries, grads, inner, lse_ref[head]))

        def step(key_tile, carry):
            rows = span(key_tile, ATT_TILE)
            allowed = tile_mask(start, tile, key_tile)
            found = []
            for head in range(heads):
                queries, grads, inner, lse_rows = fixed[head]
                lanes = slice(head * HEAD_DIM, (head + 1) * HEAD_DIM)
                keys = qkv_ref[rows, (3 * head + 1) * HEAD_DIM : (3 * head + 2) * HEAD_DIM]
                values = qkv_ref[rows, (3 * head + 2) * HEAD_DIM : (3 * head + 3) * HEAD_DIM]
                scores = dot_nt(queries, keys) * SCALE
                probs = jnp.where(allowed, jnp.exp(scores - lse_rows), 0.0)
                grad_scores = (probs * (dot_nt(grads, values) - inner)).astype(jnp.bfloat16)
                dv_ref[rows, lanes] += dot_tn(probs.astype(jnp.bfloat16), grads)
                dk_ref[rows, lanes] += dot_tn(grad_scores, queries)
                found.append(carry[head] + jnp.dot(grad_scores, keys, preferred_element_type=jnp.float32))
            return tuple(found)

        none = jnp.zeros((ATT_TILE, HEAD_DIM), jnp.float32)
        result = lax.fori_loop(first, tile + 1, step, (none,) * heads)
        for head in range(heads):
            out_ref[here, 3 * head * HEAD_DIM : (3 * head + 1) * HEAD_DIM] = turn(
                result[head] * SCALE, cos_ref[here, :], -below_ref[here, :], -above_ref[here, :]
            ).astype(jnp.bfloat16)

        @pl.when(tile == tiles - 1)
        def _():
            def finish(index, sums):
                rows = span(index, ATT_TILE)
                for head in range(heads):
                    lanes = slice(head * HEAD_DIM, (head + 1) * HEAD_DIM)
                    out_ref[rows, (3 * head + 1) * HEAD_DIM : (3 * head + 2) * HEAD_DIM] = turn(
                        dk_ref[rows, lanes] * SCALE, cos_ref[rows, :], -below_ref[rows, :], -above_ref[rows, :]
                    ).astype(jnp.bfloat16)
                    out_ref[rows, (3 * head + 2) * HEAD_DIM : (3 * head + 3) * HEAD_DIM] = dv_ref[rows, lanes].astype(
                        jnp.bfloat16
                    )
                return sums + jnp.sum(out_ref[rows, :].astype(jnp.float32), axis=0, keepdims=True)

            sums_ref[...] = lax.fori_loop(
                0, tiles, finish, jnp.zeros((1, 3 * heads * HEAD_DIM), jnp.float32)
            )

    def whole(shape):
        return pl.BlockSpec(shape, lambda i, lengths: (0,) * len(shape))

    return pl.pallas_call(
        kernel,
        grid_spec=pltpu.PrefetchScalarGridSpec(
            num_scalar_prefetch=1,
            grid=(tiles,),
            in_specs=[
                whole(qkv.shape),
                pl.BlockSpec((ATT_TILE, heads * HEAD_DIM), lambda i, lengths: (i, 0)),
                pl.BlockSpec((heads, ATT_TILE, 1), lambda i, lengths: (0, i, 0)),
                pl.BlockSpec((ATT_TILE, heads * HEAD_DIM), lambda i, lengths: (i, 0)),
                whole((BLOCK, HEAD_DIM)),
                whole((BLOCK, HEAD_DIM)),
                whole((BLOCK, HEAD_DIM)),
            ],
            out_specs=[whole(qkv.shape), whole((1, qkv.shape[1]))],
            scratch_shapes=[
                pltpu.VMEM((BLOCK, heads * HEAD_DIM), jnp.float32),
                pltpu.VMEM((BLOCK, heads * HEAD_DIM), jnp.float32),
            ],
        ),
        out_shape=[
            jax.ShapeDtypeStruct(qkv.shape, jnp.bfloat16),
            jax.ShapeDtypeStruct((1, qkv.shape[1]), jnp.float32),
        ],
        compiler_params=pltpu.CompilerParams(vmem_limit_bytes=VMEM_LIMIT),
    )(lengths, qkv, ctx, lse, grad_ctx, *planes)


def gather_cut(sizes):
    return (1792, 256) if sizes == (4, 2) else (D // 2, D // 2)


def scatter_cut(sizes):
    return (1664, 384) if sizes == (4, 2) else (D // 2, D // 2)


def columns_of(cut, kind):
    return pl.ds(0, cut[0]) if kind == 0 else pl.ds(cut[0], cut[1])


def tile_of(width):
    return 512 if width % 512 == 0 else 256 if width % 256 == 0 else 128


ANY = pl.BlockSpec(memory_space=pl.ANY)
VMEM = pl.BlockSpec(memory_space=pltpu.VMEM)
SMEM = pl.BlockSpec(memory_space=pltpu.SMEM)


def row_kernel(kernel, collective, out_shape, in_specs, out_specs, scratch, cost, before=()):
    def body(*refs):
        kernel(*refs[len(before):])

    def call(*args):
        return pl.pallas_call(
            body,
            out_shape=out_shape,
            in_specs=[ANY] * len(before) + in_specs,
            out_specs=out_specs,
            scratch_shapes=scratch,
            cost_estimate=pl.CostEstimate(flops=cost, bytes_accessed=2**28 if cost > 1 else 1, transcendentals=0),
            compiler_params=pltpu.CompilerParams(
                collective_id=collective, has_side_effects=True, vmem_limit_bytes=VMEM_LIMIT
            ),
        )(*before, *args)

    return call


def gather_scratch(sizes, rows):
    shards = sizes[0] * sizes[1]
    return [
        pltpu.VMEM((shards, rows, D), jnp.bfloat16),
        pltpu.SemaphoreType.DMA((gather_sends(sizes, HALVES),)),
        pltpu.SemaphoreType.DMA((2, HALVES, shards)),
    ]


def run_gather(grid, sizes, rows, full, send_sems, recv_sems, ready):
    cut = gather_cut(sizes)
    step = rows // HALVES
    sender = Sender(send_sems)

    def piece(slot, half, kind):
        return full.at[slot, pl.ds(half * step, step), columns_of(cut, kind)]

    gather_rounds(grid, sender, piece, recv_sems, HALVES, cut, ready)
    sender.finish()


def sum_scratch(sizes, rows):
    shards = sizes[0] * sizes[1]
    bufs, sems = scatter_scratch(sizes, HALVES, rows, D, scatter_cut(sizes))
    return (
        [pltpu.VMEM((shards, rows, D), jnp.bfloat16)]
        + bufs
        + sems
        + [pltpu.SemaphoreType.DMA((scatter_sends(sizes, HALVES),))]
    )


def run_scatter(grid, sizes, rows, scratch, produce, *hooks, quick=False):
    cut = scatter_cut(sizes)
    step = rows // HALVES
    parts, b0, b1, b2, b3, s0, s1, s2, s3, send_sems = scratch
    sender = Sender(send_sems)

    def part(slot, half, kind):
        return parts.at[slot, pl.ds(half * step, step), columns_of(cut, kind)]

    scatter = Scatter(
        grid, sender, part, ((b0, b1), (b2, b3)), ((s0, s1), (s2, s3)), HALVES, cut, quick
    )
    scatter.run(produce, *hooks)
    sender.finish()


def production_order(grid, quick=False):
    return [
        grid.index(grid.nearest(0, k), grid.nearest(1, l))
        for action, k, l in [step for step in scatter_plan(grid.n, quick) if step[0] == "make"]
    ]


ROW_TILE = 64


def tile_stats(values):
    centered = values - jnp.mean(values, axis=1, keepdims=True)
    inverse = lax.rsqrt(jnp.mean(centered * centered, axis=1, keepdims=True) + EPSILON)
    return centered, inverse


def open_rows(own, sizes, collective, norms, qkv_flat, qkv_bias, up_weight, up_bias, lengths):
    rows = own.shape[0]
    shards = sizes[0] * sizes[1]
    width, hidden = qkv_flat.shape[1], up_weight.shape[1]
    heads = width // (3 * HEAD_DIM)

    def kernel(
        own_ref, norms_ref, qkvw_any, qkvb_ref, upw_any, upb_ref, lengths_ref, freq_ref,
        plain_any, one_any, two_any, qkv_any, act_any, slope_any, cos_ref, below_ref, above_ref,
        full, send_sems, recv_sems, qkvw, upw, load_sems, plain, one, two, qkv, act, slope, out_sems,
    ):
        grid = Grid2(sizes)
        loads = [
            pltpu.make_async_copy(qkvw_any, qkvw, load_sems.at[0]),
            pltpu.make_async_copy(upw_any, upw, load_sems.at[1]),
        ]
        for copy in loads:
            copy.start()
        full[grid.index(*grid.me)] = own_ref[...]
        grid.barrier()
        open_copies = []

        def outs(place, slot):
            pairs = ((plain, plain_any), (one, one_any), (two, two_any), (qkv, qkv_any), (act, act_any), (slope, slope_any))
            return [
                pltpu.make_async_copy(here.at[slot], there.at[place], out_sems.at[slot, i])
                for i, (here, there) in enumerate(pairs)
            ]

        def ready(slow, fast, order):
            place = grid.index(slow, fast)
            slot = order % 2
            if order == 0:
                for copy in loads:
                    copy.wait()
            if order >= 2:
                for copy in open_copies.pop(0):
                    copy.wait()

            def norm_tile(index, _):
                here = span(index, ROW_TILE)
                centered, inverse = tile_stats(full[place, here].astype(jnp.float32))
                normed = centered * inverse
                plain[slot, here] = normed.astype(jnp.bfloat16)
                one[slot, here] = (normed * norms_ref[0:1] + norms_ref[1:2]).astype(jnp.bfloat16)
                two[slot, here] = (normed * norms_ref[2:3] + norms_ref[3:4]).astype(jnp.bfloat16)
                return _

            lax.fori_loop(0, rows // ROW_TILE, norm_tile, 0)
            places = pl.ds(pl.multiple_of(place * rows, rows), rows)
            row = place * rows + lax.broadcasted_iota(jnp.int32, (rows, 1), 0)
            cos, below, above = rotary_planes(row - first_rows(lengths_ref, row), freq_ref[...])
            cos_ref[places, :], below_ref[places, :], above_ref[places, :] = cos, below, above
            whole = jnp.dot(one[slot], qkvw[...], preferred_element_type=jnp.float32) + qkvb_ref[...]
            for head in range(heads):
                first = head * 3 * HEAD_DIM
                found = whole[:, first : first + 3 * HEAD_DIM]
                qkv[slot, :, first : first + HEAD_DIM] = turn(
                    found[:, :HEAD_DIM], cos, below, above
                ).astype(jnp.bfloat16)
                qkv[slot, :, first + HEAD_DIM : first + 2 * HEAD_DIM] = turn(
                    found[:, HEAD_DIM : 2 * HEAD_DIM], cos, below, above
                ).astype(jnp.bfloat16)
                qkv[slot, :, first + 2 * HEAD_DIM : first + 3 * HEAD_DIM] = found[
                    :, 2 * HEAD_DIM :
                ].astype(jnp.bfloat16)
            tile = tile_of(hidden)

            def up_tile(index, _):
                here = span(index, tile)
                pre = jnp.dot(two[slot], upw[:, here], preferred_element_type=jnp.float32) + upb_ref[:, here]
                share = 0.5 * (1.0 + lax.erf(pre * 0.7071067811865476))
                act[slot, :, here] = (pre * share).astype(jnp.bfloat16)
                slope[slot, :, here] = (
                    share + pre * (jnp.exp(-0.5 * pre * pre) * 0.3989422804014327)
                ).astype(jnp.bfloat16)
                return _

            lax.fori_loop(0, hidden // tile, up_tile, 0)
            copies = outs(place, slot)
            for copy in copies:
                copy.start()
            open_copies.append(copies)

        run_gather(grid, sizes, rows, full, send_sems, recv_sems, ready)
        for copies in open_copies:
            for copy in copies:
                copy.wait()

    def out(columns):
        return jax.ShapeDtypeStruct((shards, rows, columns), jnp.bfloat16)

    def staged(columns):
        return pltpu.VMEM((2, rows, columns), jnp.bfloat16)

    return row_kernel(
        kernel, collective,
        [out(D), out(D), out(D), out(width), out(hidden), out(hidden)]
        + [jax.ShapeDtypeStruct((shards * rows, HEAD_DIM), jnp.float32)] * 3,
        [VMEM, VMEM, ANY, VMEM, ANY, VMEM, SMEM, VMEM],
        [ANY] * 6 + [VMEM] * 3,
        gather_scratch(sizes, rows)
        + [
            pltpu.VMEM(qkv_flat.shape, jnp.bfloat16),
            pltpu.VMEM(up_weight.shape, jnp.bfloat16),
            pltpu.SemaphoreType.DMA((2,)),
            staged(D), staged(D), staged(D), staged(width), staged(hidden), staged(hidden),
            pltpu.SemaphoreType.DMA((2, 6)),
        ],
        2 * BLOCK * D * (width + hidden),
    )(own, norms, qkv_flat, qkv_bias, up_weight, up_bias, lengths, rotary_frequencies())


def branch_rows(own, ctx, act, out_flat, down_weight, norms, sizes, collective):
    rows = own.shape[0]
    shards = sizes[0] * sizes[1]
    inner, hidden = out_flat.shape[0], down_weight.shape[0]

    def kernel(
        own_ref, ctx_any, act_any, outw_any, downw_any, norms_ref, out_ref, final_ref, normed_ref, inverse_ref,
        ctx, act, outw, downw, load_sems, *scratch,
    ):
        grid = Grid2(sizes)
        parts = scratch[0]
        weights = [
            pltpu.make_async_copy(outw_any, outw, load_sems.at[0, 0]),
            pltpu.make_async_copy(downw_any, downw, load_sems.at[0, 1]),
        ]
        order = production_order(grid)
        loads = [
            [
                pltpu.make_async_copy(ctx_any.at[place], ctx.at[place], load_sems.at[1 + i, 0]),
                pltpu.make_async_copy(act_any.at[place], act.at[place], load_sems.at[1 + i, 1]),
            ]
            for i, place in enumerate(order)
        ]
        for copy in loads[0] + weights:
            copy.start()
        for copies in loads[1:]:
            for copy in copies:
                copy.start()
        grid.barrier()
        for copy in weights:
            copy.wait()

        def produce(slow, fast):
            place = grid.index(slow, fast)
            for copy in loads.pop(0):
                copy.wait()

            def columns(index, _):
                here = span(index, 512)
                parts[place, :, here] = (
                    jnp.dot(ctx[place], outw[:, here], preferred_element_type=jnp.float32)
                    + jnp.dot(act[place], downw[:, here], preferred_element_type=jnp.float32)
                ).astype(jnp.bfloat16)
                return _

            lax.fori_loop(0, D // 512, columns, 0)

        run_scatter(grid, sizes, rows, scratch, produce)
        mine = grid.index(*grid.me)

        def norm_tile(index, _):
            here = span(index, ROW_TILE)
            stream = own_ref[here].astype(jnp.float32) + parts[mine, here].astype(jnp.float32) + norms_ref[2:3]
            out_ref[here] = stream.astype(jnp.bfloat16)
            centered, inverse = tile_stats(stream)
            normed = centered * inverse
            final_ref[here] = (normed * norms_ref[0:1] + norms_ref[1:2]).astype(jnp.bfloat16)
            normed_ref[here] = normed
            inverse_ref[here] = inverse
            return _

        lax.fori_loop(0, rows // ROW_TILE, norm_tile, 0)

    return row_kernel(
        kernel, collective,
        [
            jax.ShapeDtypeStruct((rows, D), jnp.bfloat16),
            jax.ShapeDtypeStruct((rows, D), jnp.bfloat16),
            jax.ShapeDtypeStruct((rows, D), jnp.float32),
            jax.ShapeDtypeStruct((rows, 1), jnp.float32),
        ],
        [VMEM, ANY, ANY, ANY, ANY, VMEM],
        [VMEM] * 4,
        [
            pltpu.VMEM(ctx.shape, jnp.bfloat16),
            pltpu.VMEM(act.shape, jnp.bfloat16),
            pltpu.VMEM(out_flat.shape, jnp.bfloat16),
            pltpu.VMEM(down_weight.shape, jnp.bfloat16),
            pltpu.SemaphoreType.DMA((1 + shards, 2)),
        ]
        + sum_scratch(sizes, rows),
        2 * BLOCK * D * (inner + hidden),
    )(own, ctx, act, out_flat, down_weight, norms)


def logit_rows(final, head_weight, targets_col, sizes, collective):
    rows = final.shape[0]
    shards = sizes[0] * sizes[1]
    vocab = head_weight.shape[1]

    def kernel(
        own_ref, headw_any, target_ref, final_any, weights_any, stats_ref,
        full, send_sems, recv_sems, headw, load_sem, logits, weights, out_sems, row_sems,
    ):
        grid = Grid2(sizes)
        load = pltpu.make_async_copy(headw_any, headw, load_sem)
        load.start()
        full[grid.index(*grid.me)] = own_ref[...]
        grid.barrier()
        base = lax.axis_index("seq") * vocab
        open_copies, raw_copies = [], []

        def ready(slow, fast, order):
            place = grid.index(slow, fast)
            slot = order % 2
            if order == 0:
                load.wait()
            if order >= 2:
                open_copies.pop(0).wait()
            places = pl.ds(pl.multiple_of(place * rows, rows), rows)
            target = target_ref[places, :] - base

            def fold(values, join):
                total = values[:, :128]
                for first in range(128, values.shape[1], 128):
                    total = join(total, values[:, first : first + 128])
                return total

            def logit_tile(start, size, carry):
                top, pick = carry
                here = pl.ds(start, size)
                found = jnp.dot(full[place], headw[:, here], preferred_element_type=jnp.float32)
                logits[:, here] = found
                ids = start + lax.broadcasted_iota(jnp.int32, (rows, size), 1)
                top = jnp.maximum(top, fold(found, jnp.maximum))
                pick = pick + fold(jnp.where(ids == target, found, 0.0), jnp.add)
                return (top, pick)

            def tiled(step, carry):
                count = vocab // 512
                carry = lax.fori_loop(
                    0, count, lambda i, c: step(pl.multiple_of(i * 512, 512), 512, c), carry
                )
                if vocab % 512:
                    carry = step(count * 512, vocab % 512, carry)
                return carry

            top, pick = tiled(
                logit_tile,
                (jnp.full((rows, 128), -jnp.inf, jnp.float32), jnp.zeros((rows, 128), jnp.float32)),
            )
            top = jnp.max(top, axis=1, keepdims=True)
            pick = jnp.sum(pick, axis=1, keepdims=True)

            def weight_tile(start, size, total):
                here = pl.ds(start, size)
                found = jnp.exp(logits[:, here] - top)
                weights[slot, :, here] = found.astype(jnp.bfloat16)
                return total + fold(found, jnp.add)

            total = tiled(weight_tile, jnp.zeros((rows, 128), jnp.float32))
            total = jnp.sum(total, axis=1, keepdims=True)
            lane = lax.broadcasted_iota(jnp.int32, (rows, 128), 1)
            found = jnp.where(lane == 0, top, jnp.where(lane == 1, total, pick))
            stats_ref[:, places] = found.T[0:8]
            copy = pltpu.make_async_copy(weights.at[slot], weights_any.at[place], out_sems.at[slot])
            copy.start()
            open_copies.append(copy)
            raw = pltpu.make_async_copy(full.at[place], final_any.at[place], row_sems.at[order])
            raw.start()
            raw_copies.append(raw)

        run_gather(grid, sizes, rows, full, send_sems, recv_sems, ready)
        for copy in open_copies + raw_copies:
            copy.wait()

    return row_kernel(
        kernel, collective,
        [
            jax.ShapeDtypeStruct((shards, rows, D), jnp.bfloat16),
            jax.ShapeDtypeStruct((shards, rows, vocab), jnp.bfloat16),
            jax.ShapeDtypeStruct((8, shards * rows), jnp.float32),
        ],
        [VMEM, ANY, VMEM],
        [ANY, ANY, VMEM],
        gather_scratch(sizes, rows)
        + [
            pltpu.VMEM(head_weight.shape, jnp.bfloat16),
            pltpu.SemaphoreType.DMA,
            pltpu.VMEM((rows, vocab), jnp.float32),
            pltpu.VMEM((2, rows, vocab), jnp.bfloat16),
            pltpu.SemaphoreType.DMA((2,)),
            pltpu.SemaphoreType.DMA((shards,)),
        ],
        2 * BLOCK * D * vocab,
    )(final, head_weight, targets_col)


def final_grad_rows(grad_logits, head_weight, normed, inverse, gain, sizes, collective, before):
    shards, rows, vocab = grad_logits.shape

    def kernel(
        grads_any, headw_any, normed_ref, inverse_ref, gain_ref, stream_ref, down_ref, sums_ref,
        headw, grads, load_sems, *scratch,
    ):
        grid = Grid2(sizes)
        parts = scratch[0]
        order = production_order(grid)
        loads = [
            pltpu.make_async_copy(grads_any.at[place], grads.at[i % 2], load_sems.at[i])
            for i, place in enumerate(order)
        ]
        tile = 512
        weights = [
            pltpu.make_async_copy(
                headw_any.at[pl.ds(i * tile, tile)], headw.at[pl.ds(i * tile, tile)], load_sems.at[1 + shards + i]
            )
            for i in range(D // tile)
        ]
        loads[0].start()
        for copy in weights:
            copy.start()
        grid.barrier()
        count = [0]

        def produce(slow, fast):
            place = grid.index(slow, fast)
            i = count[0]
            count[0] += 1
            if i + 1 < shards:
                loads[i + 1].start()
            loads[i].wait()

            def columns(index, _):
                here = span(index, tile)
                parts[place, :, here] = dot_nt(grads[i % 2], headw[here, :]).astype(jnp.bfloat16)
                return _

            if i == 0:
                for index, copy in enumerate(weights):
                    copy.wait()
                    columns(index, 0)
            else:
                lax.fori_loop(0, D // tile, columns, 0)

        run_scatter(grid, sizes, rows, scratch, produce)
        mine = grid.index(*grid.me)
        sums_ref[...] = jnp.zeros_like(sums_ref)

        def norm_tile(index, _):
            here = span(index, ROW_TILE)
            grad = parts[mine, here].astype(jnp.float32)
            norm = normed_ref[here]
            scaled = grad * gain_ref[...]
            stream = inverse_ref[here] * (
                scaled
                - jnp.mean(scaled, axis=1, keepdims=True)
                - norm * jnp.mean(scaled * norm, axis=1, keepdims=True)
            )
            stream_ref[here] = stream
            down_ref[here] = stream.astype(jnp.bfloat16)
            sums_ref[0:1] += jnp.sum(grad * norm, axis=0, keepdims=True)
            sums_ref[1:2] += jnp.sum(grad, axis=0, keepdims=True)
            sums_ref[2:3] += jnp.sum(stream, axis=0, keepdims=True)
            return _

        lax.fori_loop(0, rows // ROW_TILE, norm_tile, 0)

    return row_kernel(
        kernel, collective,
        [
            jax.ShapeDtypeStruct((rows, D), jnp.float32),
            jax.ShapeDtypeStruct((rows, D), jnp.bfloat16),
            jax.ShapeDtypeStruct((8, D), jnp.float32),
        ],
        [ANY, ANY, VMEM, VMEM, VMEM],
        [VMEM] * 3,
        [
            pltpu.VMEM(head_weight.shape, jnp.bfloat16),
            pltpu.VMEM((2, rows, vocab), jnp.bfloat16),
            pltpu.SemaphoreType.DMA((1 + shards + D // 512,)),
        ]
        + sum_scratch(sizes, rows),
        2 * BLOCK * D * vocab,
        before,
    )(grad_logits, head_weight, normed, inverse, gain)


def branch_grad_rows(own, out_flat, down_weight, slope, ctx, act, second, sizes, collective, before):
    rows = own.shape[0]
    shards = sizes[0] * sizes[1]
    inner, hidden = out_flat.shape[0], down_weight.shape[0]
    half_width = D // 2

    def kernel(
        own_ref, outw_any, downw_any, slope_any, ctx_any, act_any, second_any,
        grad_ctx_any, grad_up_any, sums_ref, stream_away, stream_mine, up_away, up_mine,
        full, send_sems, recv_sems, outw, downw, load_sems, slope, slope_sem, grad_ctx, grad_up, out_sems,
        ctx, act, second, row_sems, out_total, down_total, up_total, part_sems,
    ):
        grid = Grid2(sizes)
        core = lax.rem(lax.axis_index("dp"), 2)
        loads = [
            pltpu.make_async_copy(outw_any, outw, load_sems.at[0]),
            pltpu.make_async_copy(downw_any, downw, load_sems.at[1]),
        ]
        for copy in loads:
            copy.start()
        slopes = pltpu.make_async_copy(slope_any, slope, slope_sem)
        slopes.start()
        order_of = [
            grid.index(grid.nearest(0, k), grid.nearest(1, l)) for k in range(sizes[0]) for l in range(sizes[1])
        ]
        row_loads = [
            [
                pltpu.make_async_copy(there.at[place], here.at[i % 2], row_sems.at[i % 2, j])
                for j, (there, here) in enumerate(((ctx_any, ctx), (act_any, act), (second_any, second)))
            ]
            for i, place in enumerate(order_of)
        ]
        for copy in row_loads[0]:
            copy.start()
        full[grid.index(*grid.me)] = own_ref[...]
        sums_ref[...] = jnp.zeros_like(sums_ref)
        grid.barrier()
        open_copies = []

        def ready(slow, fast, order):
            place = grid.index(slow, fast)
            slot = order % 2
            if order == 0:
                for copy in loads + [slopes]:
                    copy.wait()
            if order >= 2:
                for copy in open_copies.pop(0):
                    copy.wait()
            if order + 1 < shards:
                for copy in row_loads[order + 1]:
                    copy.start()
            grad_ctx[slot] = dot_nt(full[place], outw[...]).astype(jnp.bfloat16)
            tile = tile_of(hidden)

            def up_tile(index, _):
                here = span(index, tile)
                found = dot_nt(full[place], downw[here, :]) * slope[place, :, here].astype(jnp.float32)
                rounded = found.astype(jnp.bfloat16)
                grad_up[slot, :, here] = rounded
                sums_ref[0:1, here] += jnp.sum(rounded.astype(jnp.float32), axis=0, keepdims=True)
                return _

            lax.fori_loop(0, hidden // tile, up_tile, 0)
            copies = [
                pltpu.make_async_copy(grad_ctx.at[slot], grad_ctx_any.at[place], out_sems.at[slot, 0]),
                pltpu.make_async_copy(grad_up.at[slot], grad_up_any.at[place], out_sems.at[slot, 1]),
            ]
            for copy in copies:
                copy.start()
            open_copies.append(copies)
            for copy in row_loads[order]:
                copy.wait()

            def add(total, here, found):
                if order == 0:
                    total[:, here] = found
                else:
                    total[:, here] += found

            def stream_tile(index, _):
                here = span(index, 512)
                grads = full[place, :, here]
                add(out_total, here, dot_tn(ctx[slot], grads))
                add(down_total, here, dot_tn(act[slot], grads))
                return _

            lax.fori_loop(0, D // 512, stream_tile, 0)

            def up_grad_tile(index, _):
                here = span(index, tile)
                add(up_total, here, dot_tn(second[slot], grad_up[slot, :, here]))
                return _

            lax.fori_loop(0, hidden // tile, up_grad_tile, 0)

        run_gather(grid, sizes, rows, full, send_sems, recv_sems, ready)
        for copies in open_copies:
            for copy in copies:
                copy.wait()
        stores = []

        def store(total, there, row, column, height, width):
            index = len(stores)
            if index < 2 * shards:
                here = full.at[index // 2, :, pl.ds((index % 2) * half_width, width)]
            else:
                here = slope.at[index - 2 * shards, :, pl.ds(0, width)]
            here[...] = total[
                pl.ds(pl.multiple_of(row, rows), rows), pl.ds(pl.multiple_of(column, 128), width)
            ].astype(jnp.bfloat16)
            copy = pltpu.make_async_copy(here, there.at[pl.ds(height, rows)], part_sems.at[index])
            copy.start()
            stores.append(copy)

        for which, wide in ((1 - core, (stream_away, up_away)), (core, (stream_mine, up_mine))):
            for total, begin, count in ((out_total, 0, inner), (down_total, inner, hidden)):
                for height in range(0, count, rows):
                    store(total, wide[0], height, which * half_width, begin + height, half_width)
            for height in range(0, half_width, rows):
                store(up_total, wide[1], which * half_width + height, 0, height, hidden)
        for copy in stores:
            copy.wait()

    def out(columns):
        return jax.ShapeDtypeStruct((shards, rows, columns), jnp.bfloat16)

    parts = [
        jax.ShapeDtypeStruct(shape, jnp.bfloat16)
        for shape in ((inner + hidden, half_width), (half_width, hidden))
        for _ in range(2)
    ]
    stores = 2 * (inner // rows + hidden // rows + half_width // rows)
    return row_kernel(
        kernel, collective,
        [out(inner), out(hidden), jax.ShapeDtypeStruct((8, hidden), jnp.float32)] + parts,
        [VMEM] + [ANY] * 6,
        [ANY, ANY, VMEM] + [ANY] * 4,
        gather_scratch(sizes, rows)
        + [
            pltpu.VMEM(out_flat.shape, jnp.bfloat16),
            pltpu.VMEM(down_weight.shape, jnp.bfloat16),
            pltpu.SemaphoreType.DMA((2,)),
            pltpu.VMEM((shards, rows, hidden), jnp.bfloat16),
            pltpu.SemaphoreType.DMA,
            pltpu.VMEM((2, rows, inner), jnp.bfloat16),
            pltpu.VMEM((2, rows, hidden), jnp.bfloat16),
            pltpu.SemaphoreType.DMA((2, 2)),
            pltpu.VMEM((2, rows, inner), jnp.bfloat16),
            pltpu.VMEM((2, rows, hidden), jnp.bfloat16),
            pltpu.VMEM((2, rows, D), jnp.bfloat16),
            pltpu.SemaphoreType.DMA((2, 3)),
            pltpu.VMEM((inner, D), jnp.float32),
            pltpu.VMEM((hidden, D), jnp.float32),
            pltpu.VMEM((D, hidden), jnp.float32),
            pltpu.SemaphoreType.DMA((stores,)),
        ],
        4 * BLOCK * D * (inner + hidden) + 2 * BLOCK * D * hidden,
        before,
    )(own, out_flat, down_weight, slope, ctx, act, second)


class SmallSum:
    def __init__(self, shards, sums, total, scratch):
        self.shards, self.sums, self.total = shards, sums, total
        self.came, self.spread_send, self.spread_recv, self.back_send, self.back_recv = scratch
        self.here = lax.axis_index("seq")
        self.width = D // shards
        self.others = [(step, lax.rem(self.here + step, shards)) for step in range(1, shards)]

    @staticmethod
    def scratch(shards):
        dma = pltpu.SemaphoreType.DMA
        return [pltpu.VMEM((shards, 8, D // shards), jnp.float32)] + [dma((shards,))] * 4

    def barrier(self):
        sem = pltpu.get_barrier_semaphore()
        for _, place in self.others:
            pl.semaphore_signal(sem, inc=1, device_id={"seq": place}, device_id_type=MESH)
        pl.semaphore_wait(sem, self.shards - 1)

    def copy(self, place, src, dst, send, recv):
        return pltpu.make_async_remote_copy(
            src_ref=src, dst_ref=dst, send_sem=send, recv_sem=recv, device_id={"seq": place}, device_id_type=MESH
        )

    def columns(self, place):
        return pl.ds(pl.multiple_of(place * self.width, self.width), self.width)

    def spread(self):
        self.first = [
            self.copy(
                place, self.sums.at[:, self.columns(place)], self.came.at[step], self.spread_send.at[step],
                self.spread_recv.at[step],
            )
            for step, place in self.others
        ]
        for copy in self.first:
            copy.start()

    def collect(self):
        here = self.columns(self.here)
        total = self.sums[:, here]
        for (step, _), copy in zip(self.others, self.first):
            copy.wait_recv()
            total = total + self.came[step]
        self.total[:, here] = total
        self.second = [
            self.copy(
                place, self.total.at[:, here], self.total.at[:, here], self.back_send.at[step], self.back_recv.at[step]
            )
            for step, place in self.others
        ]
        for copy in self.second:
            copy.start()

    def finish(self):
        for step, _ in self.others:
            source = lax.rem(self.here + self.shards - step, self.shards)
            there = self.total.at[:, self.columns(source)]
            self.copy(source, there, there, self.back_send.at[step], self.back_recv.at[step]).wait_recv()
        for copy in self.first + self.second:
            copy.wait_send()


def score_rows(stats, lengths, labels, reference, sizes, replicas, collective):
    shards = sizes[0] * sizes[1]
    width = BLOCK // shards

    def kernel(
        stats_ref, lengths_ref, labels_ref, reference_ref, coef_ref, losses_ref,
        came, full, ratio, ratios, spread_send, spread_recv, back_send, back_recv, cross_send, cross_recv,
    ):
        seq, dp = lax.axis_index("seq"), lax.axis_index("dp")
        peers = {
            "seq": [(step, lax.rem(seq + step, shards)) for step in range(1, shards)],
            "dp": [(step, lax.rem(dp + step, replicas)) for step in range(1, replicas)],
        }
        barrier = pltpu.get_barrier_semaphore()
        for axis in peers:
            for _, place in peers[axis]:
                pl.semaphore_signal(barrier, inc=1, device_id={axis: place}, device_id_type=MESH)
        pl.semaphore_wait(barrier, shards + replicas - 2)

        def columns(place):
            return pl.ds(pl.multiple_of(place * width, width), width)

        def copy(axis, place, src, dst, send, recv):
            return pltpu.make_async_remote_copy(
                src_ref=src, dst_ref=dst, send_sem=send, recv_sem=recv, device_id={axis: place}, device_id_type=MESH
            )

        sent = [
            copy("seq", place, stats_ref.at[:, columns(place)], came.at[step], spread_send.at[step], spread_recv.at[step])
            for step, place in peers["seq"]
        ]
        for one in sent:
            one.start()
        mine = stats_ref[:, columns(seq)]
        top, total, pick = mine[0:1], mine[1:2], mine[2:3]
        for (step, _), one in zip(peers["seq"], sent):
            one.wait_recv()
            other = came[step]
            joint = jnp.maximum(top, other[0:1])
            total = total * jnp.exp(top - joint) + other[1:2] * jnp.exp(other[0:1] - joint)
            pick = pick + other[2:3]
            top = joint
        log_total = top + jnp.log(total)
        here = columns(seq)
        full[0:1, here] = log_total
        full[1:2, here] = pick - log_total
        back = [
            copy("seq", place, full.at[:, here], full.at[:, here], back_send.at[step], back_recv.at[step])
            for step, place in peers["seq"]
        ]
        for one in back:
            one.start()
        for step, _ in peers["seq"]:
            source = lax.rem(seq + shards - step, shards)
            there = full.at[:, columns(source)]
            copy("seq", source, there, there, back_send.at[step], back_recv.at[step]).wait_recv()
        example = lax.broadcasted_iota(jnp.int32, (EXB, 1), 0)
        start, end = jnp.zeros_like(example), jnp.zeros_like(example)
        sign, reference = jnp.zeros((EXB, 1), jnp.float32), jnp.zeros((EXB, 1), jnp.float32)
        reached = jnp.int32(0)
        for index in range(EXB):
            start = jnp.where(example == index, reached, start)
            reached = reached + lengths_ref[index]
            end = jnp.where(example == index, reached, end)
            sign = jnp.where(example == index, (2 * labels_ref[index] - 1).astype(jnp.float32), sign)
            reference = jnp.where(example == index, reference_ref[index], reference)
        counts = (end - start).astype(jnp.float32)
        row = lax.broadcasted_iota(jnp.int32, (EXB, BLOCK), 1)
        member = (row >= start) & (row < end)
        mean = jnp.sum(jnp.where(member, full[1:2, :], 0.0), axis=1, keepdims=True) / counts
        log_ratio = mean - reference
        ratio[...] = jnp.broadcast_to(jnp.sum(log_ratio, axis=0, keepdims=True), ratio.shape)
        crossed = [
            copy("dp", place, ratio, ratios.at[dp], cross_send.at[step], cross_recv.at[step])
            for step, place in peers["dp"]
        ]
        for one in crossed:
            one.start()
        for one in crossed:
            one.wait_recv()
        ratios[dp] = ratio[...]
        whole = ratios[0]
        for place in range(1, replicas):
            whole = whole + ratios[place]
        center = whole[:, 0:1] / (replicas * EXB)
        squashed = jax.nn.sigmoid(BETA * sign * (log_ratio - center))
        losses_ref[...] = jnp.broadcast_to(1.0 - squashed, losses_ref.shape)
        grad = -LOSS_SCALE * BETA * sign * squashed * (1.0 - squashed) / counts
        token = jnp.sum(jnp.where(member, grad, 0.0), axis=0, keepdims=True)
        coef_ref[...] = jnp.zeros_like(coef_ref)
        coef_ref[0:1, :] = token
        coef_ref[1:2, :] = token * jnp.exp(stats_ref[0:1, :] - full[0:1, :])
        for one in sent + back + crossed:
            one.wait_send()

    dma = pltpu.SemaphoreType.DMA
    return pl.pallas_call(
        kernel,
        out_shape=[
            jax.ShapeDtypeStruct((8, BLOCK), jnp.float32),
            jax.ShapeDtypeStruct((EXB, 128), jnp.float32),
        ],
        in_specs=[VMEM] + [SMEM] * 3,
        out_specs=[VMEM] * 2,
        scratch_shapes=[
            pltpu.VMEM((shards, 8, width), jnp.float32),
            pltpu.VMEM((8, BLOCK), jnp.float32),
            pltpu.VMEM((EXB, 128), jnp.float32),
            pltpu.VMEM((replicas, EXB, 128), jnp.float32),
            dma((shards,)), dma((shards,)), dma((shards,)), dma((shards,)), dma((replicas,)), dma((replicas,)),
        ],
        compiler_params=pltpu.CompilerParams(collective_id=collective, has_side_effects=True),
    )(stats, lengths, labels, reference)


def input_grad_rows(
    own, grad_stream, plain, grad_qkv, grad_up, qkv_flat, up_weight, gains, end_sums, sizes, collective,
    before,
):
    shards, rows, width = grad_qkv.shape
    hidden = grad_up.shape[2]

    def kernel(
        own_ref, stream_ref, normed_any, qkv_any, up_any, qkvw_any, upw_any, gains_ref, end_ref,
        out_ref, total_ref,
        qkvw, upw, weight_sems, normed, qkv, up, load_sems, sums_ref, *scratch,
    ):
        grid = Grid2(sizes)
        small = SmallSum(shards, sums_ref, total_ref, scratch[:5])
        scratch = scratch[5:]
        parts = scratch[0]
        order = production_order(grid)

        def loads(i):
            place = order[i]
            return [
                pltpu.make_async_copy(normed_any.at[place], normed.at[i % 2], load_sems.at[i, 0]),
                pltpu.make_async_copy(qkv_any.at[place], qkv.at[i % 2], load_sems.at[i, 1]),
                pltpu.make_async_copy(up_any.at[place], up.at[i % 2], load_sems.at[i, 2]),
            ]

        copies = [loads(i) for i in range(shards)]
        weights = [
            pltpu.make_async_copy(qkvw_any, qkvw, weight_sems.at[0]),
            pltpu.make_async_copy(upw_any, upw, weight_sems.at[1]),
        ]
        for copy in copies[0] + weights:
            copy.start()
        sums_ref[...] = jnp.zeros_like(sums_ref)
        small.barrier()
        for copy in weights:
            copy.wait()
        count = [0]

        def produce(slow, fast):
            place = grid.index(slow, fast)
            i = count[0]
            count[0] += 1
            if i + 1 < shards:
                for copy in copies[i + 1]:
                    copy.start()
            for copy in copies[i]:
                copy.wait()
            slot = i % 2

            def columns(index, _):
                here = span(index, 512)
                one = dot_nt(qkv[slot], qkvw[here, :])
                two = dot_nt(up[slot], upw[here, :])
                norm = normed[slot, :, here].astype(jnp.float32)
                parts[place, :, here] = (one * gains_ref[0:1, here] + two * gains_ref[1:2, here]).astype(
                    jnp.bfloat16
                )
                sums_ref[0:1, here] += jnp.sum(one * norm, axis=0, keepdims=True)
                sums_ref[1:2, here] += jnp.sum(one, axis=0, keepdims=True)
                sums_ref[2:3, here] += jnp.sum(two * norm, axis=0, keepdims=True)
                sums_ref[3:4, here] += jnp.sum(two, axis=0, keepdims=True)
                return _

            lax.fori_loop(0, D // 512, columns, 0)

        def made():
            sums_ref[4:8] = end_ref[0:4]
            small.spread()

        run_scatter(grid, sizes, rows, scratch, produce, made, small.collect)
        mine = grid.index(*grid.me)

        def norm_tile(index, _):
            here = span(index, ROW_TILE)
            grad = parts[mine, here].astype(jnp.float32)
            centered, inverse = tile_stats(own_ref[here].astype(jnp.float32))
            normed = centered * inverse
            out_ref[here] = stream_ref[here] + inverse * (
                grad
                - jnp.mean(grad, axis=1, keepdims=True)
                - normed * jnp.mean(grad * normed, axis=1, keepdims=True)
            )
            return _

        lax.fori_loop(0, rows // ROW_TILE, norm_tile, 0)
        small.finish()

    return row_kernel(
        kernel, collective,
        [jax.ShapeDtypeStruct((rows, D), jnp.float32), jax.ShapeDtypeStruct((8, D), jnp.float32)],
        [VMEM, VMEM, ANY, ANY, ANY, ANY, ANY, VMEM, VMEM],
        [VMEM, VMEM],
        [
            pltpu.VMEM(qkv_flat.shape, jnp.bfloat16),
            pltpu.VMEM(up_weight.shape, jnp.bfloat16),
            pltpu.SemaphoreType.DMA((2,)),
            pltpu.VMEM((2, rows, D), jnp.bfloat16),
            pltpu.VMEM((2, rows, width), jnp.bfloat16),
            pltpu.VMEM((2, rows, hidden), jnp.bfloat16),
            pltpu.SemaphoreType.DMA((shards, 3)),
            pltpu.VMEM((8, D), jnp.float32),
        ]
        + SmallSum.scratch(shards)
        + sum_scratch(sizes, rows),
        1,
        before,
    )(own, grad_stream, plain, grad_qkv, grad_up, qkv_flat, up_weight, gains, end_sums)


def settle_halves(core, mine, backs, shapes, places, before=()):
    depth, most = 4, 256
    count = len(mine[0])
    steps = []
    for index, (_, _, rows) in enumerate(places):
        size = min(most, rows)
        for which in (0, 1):
            for first in range(0, rows, size):
                steps.append((index, which, first, size))
    width = max(arrays[0].shape[1] for arrays in mine)
    deep = [shape for shape in shapes if len(shape) == 3]

    def kernel(core_ref, *refs):
        sources = [
            [refs[(index * 2 + which) * count : (index * 2 + which + 1) * count] for which in (0, 1)]
            for index, _, _ in places
        ]
        rest = refs[2 * count * len(mine) + len(before) :]
        outs, (taken, given, split, in_sems, out_sems) = rest[: len(shapes)], rest[len(shapes) :]

        def loads(i):
            index, which, first, size = steps[i]
            number, begin, _ = places[index]
            columns = mine[number][0].shape[1]
            return [
                pltpu.make_async_copy(
                    source.at[pl.ds(begin + first, size)],
                    taken.at[i % depth, j, pl.ds(0, size), pl.ds(0, columns)],
                    in_sems.at[i % depth, j],
                )
                for j, source in enumerate(sources[index][which])
            ]

        def store(i):
            index, which, first, size = steps[i]
            number, _, rows = places[index]
            columns = mine[number][0].shape[1]
            place = core_ref[0] if which == 0 else 1 - core_ref[0]
            if len(shapes[index]) == 2 and shapes[index][0] == rows:
                there = outs[index].at[pl.ds(first, size), pl.ds(pl.multiple_of(place * columns, columns), columns)]
            else:
                there = outs[index].at[pl.ds(pl.multiple_of(place * rows + first, size), size)]
            here = given.at[i % depth, pl.ds(0, size), pl.ds(0, columns)]
            if len(shapes[index]) == 3:
                here = split.at[i % depth, pl.ds(0, size)]
            return pltpu.make_async_copy(here, there, out_sems.at[i % depth])

        for i in range(min(depth - 1, len(steps))):
            for copy in loads(i):
                copy.start()
        for i, (index, which, first, size) in enumerate(steps):
            if i + depth - 1 < len(steps):
                for copy in loads(i + depth - 1):
                    copy.start()
            for copy in loads(i):
                copy.wait()
            if i >= depth:
                store(i - depth).wait()
            columns = mine[places[index][0]][0].shape[1]

            def convert(row, _, i=i, index=index, columns=columns):
                here = span(row, 32)
                found = taken[i % depth, 0, here, :columns].astype(jnp.float32)
                for j in range(1, count):
                    found = found + taken[i % depth, j, here, :columns].astype(jnp.float32)
                if len(shapes[index]) == 3:
                    for head in range(shapes[index][1]):
                        split[i % depth, here, head, :] = found[
                            :, head * shapes[index][2] : (head + 1) * shapes[index][2]
                        ]
                else:
                    given[i % depth, here, :columns] = found
                return _

            lax.fori_loop(0, size // 32, convert, 0)
            store(i).start()
        for i in range(max(len(steps) - depth, 0), len(steps)):
            store(i).wait()

    dma = pltpu.SemaphoreType.DMA
    return pl.pallas_call(
        kernel,
        out_shape=[jax.ShapeDtypeStruct(shape, jnp.float32) for shape in shapes],
        in_specs=[SMEM] + [ANY] * (2 * count * len(mine) + len(before)),
        out_specs=[ANY] * len(shapes),
        scratch_shapes=[
            pltpu.VMEM((depth, count, most, width), jnp.bfloat16),
            pltpu.VMEM((depth, most, width), jnp.float32),
            pltpu.VMEM((depth, most) + deep[0][1:] if deep else (1, 8, 128), jnp.float32),
            dma((depth, count)),
            dma((depth,)),
        ],
        compiler_params=pltpu.CompilerParams(vmem_limit_bytes=VMEM_LIMIT),
    )(core, *[array for pair in zip(mine, backs) for half in pair for array in half], *before)


def row_of(vector):
    return vector.astype(jnp.float32)[None, :]


def held(values):
    return lax.optimization_barrier(values)


def half_of(values, which):
    half = values.shape[1] // 2
    return lax.dynamic_slice_in_dim(values, which * half, half, 1)


def pairs(step):
    return [(place, place ^ step) for place in range(lax.axis_size("dp"))]


class PairSum:
    def __init__(self, away, mine):
        self.plain = lax.axis_size("dp") != 4
        self.core = lax.rem(lax.axis_index("dp"), 2)
        came = lax.ppermute(away, "dp", pairs(1))
        self.sum = (mine.astype(jnp.float32) + came.astype(jnp.float32)).astype(jnp.bfloat16)

    def cross(self):
        if self.plain:
            none = jnp.zeros_like(self.sum)
            both = jnp.stack([jnp.where(self.core == which, self.sum, none) for which in (0, 1)])
            self.other, self.first_back = lax.psum(both, "dp"), self.sum
        else:
            self.other = lax.ppermute(self.sum, "dp", pairs(2))
            self.first_back = lax.ppermute(self.sum, "dp", pairs(1))
        return self


def after(values, earlier):
    def kernel(*refs):
        del refs

    return pl.pallas_call(
        kernel,
        out_shape=[jax.ShapeDtypeStruct(v.shape, v.dtype) for v in values],
        in_specs=[ANY] * (len(values) + 1),
        out_specs=[ANY] * len(values),
        input_output_aliases={i: i for i in range(len(values))},
    )(*values, earlier)


def give_back(sums, earlier):
    if sums[0].plain:
        for one in sums:
            one.mine, one.back = [one.other[0]], [one.other[1]]
        return
    for one, other in zip(sums, after([one.other for one in sums], earlier)):
        one.mine = [one.sum, other]
        one.back = [one.first_back, lax.ppermute(other, "dp", pairs(1))]


def settle_all(sums, shapes, places, before=()):
    core = jnp.zeros((1,), jnp.int32) if sums[0].plain else sums[0].core[None]
    return settle_halves(core, [one.mine for one in sums], [one.back for one in sums], shapes, places, before)


def pair_product(product):
    core = lax.rem(lax.axis_index("dp"), 2)
    return PairSum(product(1 - core).astype(jnp.bfloat16), held(product(core)))


def sum_over_dp(values):
    if lax.axis_size("dp") != 4:
        return lax.psum(values, "dp")
    for step in (1, 2):
        values = values + lax.ppermute(values, "dp", pairs(step))
    return values


def per_device(
    hidden, targets, lengths, labels, ref_logps, ln1_gain, ln1_bias, ln2_gain, ln2_bias, qkv_weight, qv_bias,
    out_weight, up_weight, up_bias, down_weight, branch_bias, lnf_gain, lnf_bias, head_weight,
):
    sizes = lines_of(lax.axis_size("seq"))
    own = hidden[0]
    local_heads = qkv_weight.shape[1]
    local_vocab = head_weight.shape[1]
    local_hidden = up_weight.shape[1]
    width = local_heads * 3 * HEAD_DIM
    inner = local_heads * HEAD_DIM
    qv_float = qv_bias.astype(jnp.float32)
    full_bias = jnp.concatenate(
        [qv_float[:, :HEAD_DIM], jnp.zeros_like(qv_float[:, :HEAD_DIM]), qv_float[:, HEAD_DIM:]], axis=-1
    ).reshape(1, width)
    qkv_flat = qkv_weight.reshape(D, width)
    out_flat = out_weight.reshape(inner, D)
    block_lengths = lengths[0]
    norms = jnp.concatenate([row_of(v) for v in (ln1_gain, ln1_bias, ln2_gain, ln2_bias)], axis=0)
    plain, first_full, second_full, qkv, act, slope, *planes = open_rows(
        own, sizes, 0, norms, qkv_flat, full_bias, up_weight, row_of(up_bias), block_lengths
    )
    flat_qkv = qkv.reshape(BLOCK, width)
    ctx, lse = attention_forward(flat_qkv, block_lengths, local_heads)
    shards, rows = plain.shape[0], plain.shape[1]
    end_norms = jnp.concatenate([row_of(v) for v in (lnf_gain, lnf_bias, branch_bias)], axis=0)
    output, final, normed, inverse = branch_rows(
        own, ctx.reshape(shards, rows, inner), act, out_flat, down_weight, end_norms, sizes, 1
    )
    targets_col = targets[0][:, None]
    final_full, weights, stats = logit_rows(final, head_weight, targets_col, sizes, 2)

    coef, losses = score_rows(
        stats, block_lengths, labels[0], ref_logps[0], sizes, lax.axis_size("dp"), 6
    )
    vocab_ids = lax.axis_index("seq") * local_vocab + jnp.arange(local_vocab, dtype=jnp.int32)
    grad_logits = held((
        jnp.where(vocab_ids[None, :] == targets[0][:, None], coef[0][:, None], 0.0)
        - weights.reshape(BLOCK, local_vocab).astype(jnp.float32) * coef[1][:, None]
    ).astype(jnp.bfloat16))
    final_rows = final_full.reshape(BLOCK, D)
    head_sum = pair_product(lambda which: dot_tn(half_of(final_rows, which), grad_logits)).cross()

    grad_stream, grad_own, end_sums = final_grad_rows(
        grad_logits.reshape(shards, rows, local_vocab), head_weight, normed, inverse, row_of(lnf_gain), sizes, 3,
        (head_sum.sum,),
    )
    grad_ctx, grad_up, up_sums, *halves = branch_grad_rows(
        grad_own, out_flat, down_weight, slope, ctx.reshape(shards, rows, inner), act, second_full, sizes, 4,
        (head_sum.first_back,),
    )
    sums = [PairSum(*halves[2 * i : 2 * i + 2]).cross() for i in range(2)]
    grad_qkv, qkv_sums = attention_backward(
        flat_qkv, block_lengths, local_heads, ctx, lse, grad_ctx.reshape(BLOCK, inner), planes
    )
    first_rows = first_full.reshape(BLOCK, D)
    sums.append(pair_product(lambda which: dot_tn(half_of(first_rows, which), grad_qkv)).cross())
    qkv_sums = qkv_sums.reshape(local_heads, 3 * HEAD_DIM)
    qv_grad = jnp.concatenate([qkv_sums[:, :HEAD_DIM], qkv_sums[:, 2 * HEAD_DIM :]], axis=-1)
    split = local_heads * 2 * HEAD_DIM
    biases = jnp.concatenate([qv_grad.reshape(-1), up_sums[0]])
    biases = jnp.pad(biases[None, :], ((0, 0), (0, D - biases.shape[0])))
    give_back([head_sum], grad_qkv)
    gains = jnp.concatenate([row_of(ln1_gain), row_of(ln2_gain)], axis=0)
    grad_input, group_sums = input_grad_rows(
        own, grad_stream, plain, grad_qkv.reshape(shards, rows, width), grad_up, qkv_flat, up_weight, gains,
        end_sums, sizes, 5, [one.first_back for one in sums],
    )
    give_back(sums[:2], group_sums)
    (head_grad,) = settle_all([head_sum], [(D, local_vocab)], [(0, 0, D // 2)], (group_sums,))
    give_back(sums[2:], head_grad)
    small = sum_over_dp(jnp.concatenate([group_sums[:7], biases], axis=0))
    out_grad, down_grad, up_grad, qkv_grad = settle_all(
        sums,
        [(inner, D), (local_hidden, D), (D, local_hidden), qkv_weight.shape],
        [(0, 0, inner), (0, inner, local_hidden), (1, 0, D // 2), (2, 0, D // 2)],
    )
    return (
        losses[:, 0][None],
        output[None],
        grad_input[None],
        small[0],
        small[1],
        small[2],
        small[3],
        qkv_grad,
        small[7, :split].reshape(local_heads, 2 * HEAD_DIM),
        out_grad.reshape(out_weight.shape),
        up_grad,
        small[7, split : split + local_hidden],
        down_grad,
        small[6],
        small[4],
        small[5],
        head_grad,
    )


def solution(mesh):
    return jax.shard_map(
        per_device,
        mesh=mesh,
        in_specs=(
            P("dp", "seq", None),
            P("dp", None),
            P("dp", None),
            P("dp", None),
            P("dp", None),
            P(),
            P(),
            P(),
            P(),
            P(None, "seq", None),
            P("seq", None),
            P("seq", None, None),
            P(None, "seq"),
            P("seq"),
            P("seq", None),
            P(),
            P(),
            P(),
            P(None, "seq"),
        ),
        out_specs=(
            P("dp", None),
            P("dp", "seq", None),
            P("dp", "seq", None),
            P(),
            P(),
            P(),
            P(),
            P(None, "seq", None),
            P("seq", None),
            P("seq", None, None),
            P(None, "seq"),
            P("seq"),
            P("seq", None),
            P(),
            P(),
            P(),
            P(None, "seq"),
        ),
        check_vma=False,
    )
```

```python
import jax
import jax.numpy as jnp
from jax import lax
from jax.experimental import pallas as pl
from jax.experimental.pallas import tpu as pltpu
from jax.sharding import PartitionSpec as P

D = 2048
HEAD_DIM = 128
ROT = 32
BLOCK = 2048
EXB = 8
EPSILON = 1e-05
BETA = 0.25
LOSS_SCALE = 65536.0
HALVES = 2
VMEM_LIMIT = 62 * 2**20

MESH = pl.DeviceIdType.MESH


class Grid2:
    def __init__(self, sizes):
        self.n = sizes
        place = lax.axis_index("seq")
        self.me = (place // sizes[1], lax.rem(place, sizes[1]))

    def index(self, slow, fast):
        return slow * self.n[1] + fast

    def device(self, axis, spot):
        here = list(self.me)
        here[axis] = spot
        return {"seq": self.index(*here)}

    def nearest(self, axis, rank):
        n, m = self.n[axis], self.me[axis]
        if rank == 0:
            return m
        if n == 2:
            return 1 - m
        after = n - 1 - m
        both = jnp.minimum(m, after)
        dist = (rank + 1) // 2
        near = m - dist if rank % 2 else m + dist
        far = jnp.where(m < after, m + (rank - both), m - (rank - both))
        return jnp.where(rank <= 2 * both, near, far)

    def neighbours(self):
        found = []
        for axis in (0, 1):
            m, n = self.me[axis], self.n[axis]
            if n == 2:
                found.append((None, self.device(axis, 1 - m)))
            elif n > 2:
                found.append((m > 0, self.device(axis, m - 1)))
                found.append((m < n - 1, self.device(axis, m + 1)))
        return found

    def barrier(self, *others):
        sem = pltpu.get_barrier_semaphore()
        amount = jnp.int32(0)
        for there, device in self.neighbours() + [(None, device) for device in others]:
            def tell(device=device):
                pl.semaphore_signal(sem, inc=1, device_id=device, device_id_type=MESH)
            if there is None:
                tell()
                amount = amount + 1
            else:
                pl.when(there)(tell)
                amount = amount + there.astype(jnp.int32)
        pl.semaphore_wait(sem, amount)


class Sender:
    def __init__(self, send_sems):
        self.sems = send_sems
        self.used = 0
        self.open = []

    def send(self, src, dst, recv_sem, device, when=None):
        copy = pltpu.make_async_remote_copy(
            src_ref=src, dst_ref=dst, send_sem=self.sems.at[self.used], recv_sem=recv_sem,
            device_id=device, device_id_type=MESH)
        self.used += 1
        if when is None:
            copy.start()
        else:
            pl.when(when)(copy.start)
        self.open.append((when, copy))

    def finish(self):
        for when, copy in self.open:
            if when is None:
                copy.wait_send()
            else:
                pl.when(when)(copy.wait_send)
        self.open = []


def gather_sends(sizes, halves):
    return halves * 2 * (sizes[0] * sizes[1] * 5 + 8)


def gather_rounds(grid, sender, piece, recv_sems, halves, cut, ready):
    n, me = grid.n, grid.me

    def arrived(slow, fast, half, kind, when):
        ref = piece(grid.index(slow, fast), half, kind)
        sem = recv_sems.at[kind, half, grid.index(slow, fast)]
        wait = pltpu.make_async_copy(ref, ref, sem).wait
        if when is None:
            wait()
        else:
            pl.when(when)(wait)

    def push(slow, fast, half, kind, axis, spot, *conditions):
        ref = piece(grid.index(slow, fast), half, kind)
        sem = recv_sems.at[kind, half, grid.index(slow, fast)]
        when = None
        for condition in conditions:
            if condition is not None:
                when = condition if when is None else when & condition
        sender.send(ref, ref, sem, grid.device(axis, spot), when)

    def spread(slow, fast, half, kind, axis, when):
        m, size = me[axis], n[axis]
        if size == 2:
            push(slow, fast, half, kind, axis, 1 - m, when)
        elif size > 2:
            push(slow, fast, half, kind, axis, m + 1, when, m < size - 1)
            push(slow, fast, half, kind, axis, m - 1, when, m > 0)

    def onward(slow, fast, half, kind, axis, when):
        m, size = me[axis], n[axis]
        if size <= 2:
            return
        below = (slow, fast)[axis] < m
        more = (below & (m < size - 1)) | (jnp.logical_not(below) & (m > 0))
        push(slow, fast, half, kind, axis, jnp.where(below, m + 1, m - 1), when, more)

    def sides(d):
        if d == 0:
            return [(me[0], None)]
        if n[0] == 2:
            return [(1 - me[0], None)]
        return [(me[0] - d, me[0] >= d), (me[0] + d, me[0] + d < n[0])]

    def settle(d):
        for half in range(halves):
            for slow, when in sides(d):
                for l in range(n[1]):
                    fast = grid.nearest(1, l)
                    if d > 0:
                        arrived(slow, fast, half, 1, when)
                        onward(slow, fast, half, 1, 0, when)
                    else:
                        spread(slow, fast, half, 1, 0, when)

    def complete(d):
        for l in range(1, n[1]):
            fast = grid.nearest(1, l)
            for half in range(halves):
                for slow, when in sides(d):
                    arrived(slow, fast, half, 0, when)
                    onward(slow, fast, half, 0, 1, when)

    def work(k, l):
        ready(grid.nearest(0, k), grid.nearest(1, l), k * n[1] + l)

    for half in range(halves):
        for kind in (1, 0):
            if cut[kind]:
                spread(me[0], me[1], half, kind, kind, None)
        if cut[0]:
            spread(me[0], me[1], half, 0, 1, None)
    work(0, 0)
    if cut[1]:
        for half in range(halves):
            for l in range(1, n[1]):
                fast = grid.nearest(1, l)
                arrived(me[0], fast, half, 1, None)
                onward(me[0], fast, half, 1, 1, None)
        settle(0)
    for d in range(1, n[0]):
        if cut[0]:
            for half in range(halves):
                for slow, when in sides(d):
                    arrived(slow, me[1], half, 0, when)
                    onward(slow, me[1], half, 0, 0, when)
                    spread(slow, me[1], half, 0, 1, when)
            complete(d - 1)
        for l in range(1, n[1]):
            work(d - 1, l)
        if cut[1]:
            settle(d)
        work(d, 0)
    if cut[0]:
        complete(n[0] - 1)
    for l in range(1, n[1]):
        work(n[0] - 1, l)


def scatter_slots(n):
    return 1 if n == 2 else n + 1


def scatter_plan(n, quick):
    if n == (4, 2) and not quick:
        return [
            ("make", 3, 1), ("make", 2, 1), ("make", 3, 0), ("make", 1, 1), ("first", 3), ("make", 2, 0),
            ("make", 0, 1), ("later", 3, 0), ("make", 1, 0), ("later", 3, 1), ("first", 2), ("make", 0, 0), ("made",),
            ("later", 2, 0), ("later", 2, 1), ("first", 1), ("later", 1, 0), ("later", 1, 1),
        ]
    far = n[0] - 1
    plan = [("make", k, l) for l in range(n[1] - 1, -1, -1) for k in range(far, -1, -1)] + [("made",)]
    for k in range(far, 0, -1):
        plan += [("first", k), ("later", k, 0), ("later", k, 1)]
    return plan


class Scatter:
    def __init__(self, grid, sender, part, bufs, sems, halves, cut, quick):
        self.grid, self.sender, self.part, self.quick = grid, sender, part, quick
        self.bufs, self.sems, self.halves, self.cut = bufs, sems, halves, cut

    def slot(self, axis, target, from_below):
        if self.grid.n[axis] == 2:
            return 0
        return target + jnp.where(from_below, 1, 0)

    def take(self, kind, stage, axis, other, target, from_below, half, when, slot_index):
        buf, sem = self.bufs[kind][stage], self.sems[kind][stage]
        slot = self.slot(axis, target, from_below)

        def add():
            ref = buf.at[other, slot, half]
            pltpu.make_async_copy(ref, ref, sem.at[other, slot, half]).wait()
            mine = self.part(slot_index, half, kind)
            mine[...] = (mine[...].astype(jnp.float32) + ref[...].astype(jnp.float32)).astype(mine.dtype)

        if when is None:
            add()
        else:
            pl.when(when)(add)

    def incoming(self, axis, target):
        m, n = self.grid.me[axis], self.grid.n[axis]
        if n == 2:
            return None
        up = target > m
        return (up & (m > 0)) | (jnp.logical_not(up) & (m < n - 1))

    def toward(self, kind, stage, axis, other, target, half, slow, fast, when=None):
        grid = self.grid
        m, n = grid.me[axis], grid.n[axis]
        up = target > m
        index = grid.index(slow, fast)
        if n > 2:
            incoming = self.incoming(axis, target)
            self.take(kind, stage, axis, other, target, up, half, incoming if when is None else incoming & when, index)
        buf, sem = self.bufs[kind][stage], self.sems[kind][stage]
        slot = self.slot(axis, target, up)
        spot = 1 - m if n == 2 else jnp.where(up, m + 1, m - 1)
        self.sender.send(
            self.part(index, half, kind), buf.at[other, slot, half], sem.at[other, slot, half],
            grid.device(axis, spot), when)

    def last(self, kind, stage, axis, other, half, slow, fast):
        grid = self.grid
        m, n = grid.me[axis], grid.n[axis]
        index = grid.index(slow, fast)
        if n == 2:
            self.take(kind, stage, axis, other, m, m > 0, half, None, index)
        elif n > 2:
            self.take(kind, stage, axis, other, m, jnp.bool_(True), half, m > 0, index)
            self.take(kind, stage, axis, other, m, jnp.bool_(False), half, m < n - 1, index)

    def run(self, produce, made=lambda: None, late=lambda: None):
        grid, n, me = self.grid, self.grid.n, self.grid.me
        lagging = []

        def chain(k, half, begins):
            slow = grid.nearest(0, k)
            incoming = self.incoming(0, slow)
            if incoming is None:
                if begins:
                    self.last(0, 0, 1, slow, half, slow, me[1])
                    self.toward(0, 1, 0, 0, slow, half, slow, me[1])
                return
            when = jnp.logical_not(incoming) if begins else incoming
            pl.when(when)(lambda: self.last(0, 0, 1, slow, half, slow, me[1]))
            self.toward(0, 1, 0, 0, slow, half, slow, me[1], when)

        def catch_up():
            for step in lagging:
                self.toward(*step)
            lagging.clear()

        def make(k, l):
            slow, fast = grid.nearest(0, k), grid.nearest(1, l)
            produce(slow, fast)
            if self.cut[0] and l > 0:
                for half in range(self.halves):
                    self.toward(0, 0, 1, slow, fast, half, slow, fast)
            catch_up()
            if self.cut[1] and k > 0:
                for half in range(self.halves):
                    lagging.append((1, 0, 0, fast, slow, half, slow, fast))

        for step in scatter_plan(n, self.quick):
            if step[0] == "make":
                make(*step[1:])
            elif step[0] == "made":
                catch_up()
                made()
            elif step[0] == "first" and self.cut[0]:
                for half in range(self.halves):
                    chain(step[1], half, True)
            elif self.cut[0]:
                chain(step[1], step[2], False)
        if self.cut[1]:
            for half in range(self.halves):
                for l in reversed(range(n[1])):
                    fast = grid.nearest(1, l)
                    self.last(1, 0, 0, fast, half, me[0], fast)
                    if l > 0:
                        self.toward(1, 1, 1, 0, fast, half, me[0], fast)
        late()
        if self.cut[0]:
            for half in range(self.halves):
                self.last(0, 0, 1, me[0], half, me[0], me[1])
        for half in range(self.halves):
            if self.cut[1]:
                self.last(1, 1, 1, 0, half, me[0], me[1])
            if self.cut[0]:
                self.last(0, 1, 0, 0, half, me[0], me[1])


def scatter_scratch(sizes, halves, rows, cols, cut):
    bufs, sems = [], []
    for kind, stages in ((0, (1, 0)), (1, (0, 1))):
        for stage, axis in enumerate(stages):
            lead = (sizes[1 - axis] if stage == 0 else 1, scatter_slots(sizes[axis]), halves)
            width = max(cut[kind], 128)
            bufs.append(pltpu.VMEM(lead + (rows // halves, width), jnp.bfloat16))
            sems.append(pltpu.SemaphoreType.DMA(lead))
    return bufs, sems


def scatter_sends(sizes, halves):
    return halves * 2 * (sizes[0] * sizes[1] + sizes[0] + sizes[1])


def lines_of(seq):
    fast = 2 if seq <= 8 else 4
    return (seq // fast, fast)


ATT_TILE = 256


def span(index, size):
    return pl.ds(pl.multiple_of(index * size, size), size)


SCALE = HEAD_DIM ** (-0.5)


def dot_nt(left, right):
    return lax.dot_general(left, right, (((1,), (1,)), ((), ())), preferred_element_type=jnp.float32)


def dot_tn(left, right):
    return lax.dot_general(left, right, (((0,), (0,)), ((), ())), preferred_element_type=jnp.float32)


def rotary_frequencies():
    half_rot = ROT // 2
    frequency = 10000.0 ** (-2.0 * jnp.arange(half_rot, dtype=jnp.float32) / ROT)
    return jnp.tile(frequency, HEAD_DIM // half_rot)[None, :]


def first_rows(lengths, row):
    start, end = jnp.zeros_like(row), jnp.int32(0)
    for example in range(EXB):
        end = end + lengths[example]
        start = jnp.where(row >= end, end, start)
    return start


def rotary_planes(position, frequencies):
    half_rot = ROT // 2
    angles = position.astype(jnp.float32) * frequencies
    cos, sin = jnp.cos(angles), jnp.sin(angles)
    lane = lax.broadcasted_iota(jnp.int32, angles.shape, 1)
    return (
        jnp.where(lane < ROT, cos, 1.0),
        jnp.where((lane >= half_rot) & (lane < ROT), sin, 0.0),
        jnp.where(lane < half_rot, -sin, 0.0),
    )


def turn(vector, cos, from_below, from_above):
    half_rot = ROT // 2
    return (
        vector * cos
        + pltpu.roll(vector, half_rot, 1) * from_below
        + pltpu.roll(vector, HEAD_DIM - half_rot, 1) * from_above
    )


def tile_mask(start_col, query_tile, key_tile):
    shape = (ATT_TILE, ATT_TILE)
    query_ids = query_tile * ATT_TILE + lax.broadcasted_iota(jnp.int32, shape, 0)
    key_ids = key_tile * ATT_TILE + lax.broadcasted_iota(jnp.int32, shape, 1)
    return (key_ids >= start_col) & (key_ids <= query_ids)


def tile_starts(lengths, tile):
    rows = tile * ATT_TILE + lax.broadcasted_iota(jnp.int32, (ATT_TILE, 1), 0)
    return first_rows(lengths, rows), first_rows(lengths, tile * ATT_TILE) // ATT_TILE


def attention_forward(qkv, lengths, heads):
    tiles = BLOCK // ATT_TILE

    def kernel(lengths_ref, qkv_ref, ctx_ref, lse_ref):
        tile = pl.program_id(0)
        start, first = tile_starts(lengths_ref, tile)
        here = span(tile, ATT_TILE)
        queries = [qkv_ref[here, 3 * head * HEAD_DIM : (3 * head + 1) * HEAD_DIM] for head in range(heads)]

        def step(key_tile, carry):
            rows = span(key_tile, ATT_TILE)
            allowed = tile_mask(start, tile, key_tile)
            found = []
            for head in range(heads):
                top, total, acc = carry[head]
                keys = qkv_ref[rows, (3 * head + 1) * HEAD_DIM : (3 * head + 2) * HEAD_DIM]
                values = qkv_ref[rows, (3 * head + 2) * HEAD_DIM : (3 * head + 3) * HEAD_DIM]
                scores = jnp.where(allowed, dot_nt(queries[head], keys) * SCALE, -1e30)
                new_top = jnp.maximum(top, jnp.max(scores, axis=1, keepdims=True))
                shrink = jnp.exp(top - new_top)
                weights = jnp.exp(scores - new_top)
                total = total * shrink + jnp.sum(weights, axis=1, keepdims=True)
                acc = acc * shrink + jnp.dot(
                    weights.astype(jnp.bfloat16), values, preferred_element_type=jnp.float32
                )
                found.append((new_top, total, acc))
            return tuple(found)

        begin = (
            jnp.full((ATT_TILE, 1), -1e30, jnp.float32),
            jnp.zeros((ATT_TILE, 1), jnp.float32),
            jnp.zeros((ATT_TILE, HEAD_DIM), jnp.float32),
        )
        result = lax.fori_loop(first, tile, step, step(tile, (begin,) * heads))
        for head in range(heads):
            top, total, acc = result[head]
            ctx_ref[:, head * HEAD_DIM : (head + 1) * HEAD_DIM] = (acc / total).astype(jnp.bfloat16)
            lse_ref[head] = top + jnp.log(total)

    return pl.pallas_call(
        kernel,
        grid_spec=pltpu.PrefetchScalarGridSpec(
            num_scalar_prefetch=1,
            grid=(tiles,),
            in_specs=[pl.BlockSpec(qkv.shape, lambda i, lengths: (0, 0))],
            out_specs=[
                pl.BlockSpec((ATT_TILE, heads * HEAD_DIM), lambda i, lengths: (i, 0)),
                pl.BlockSpec((heads, ATT_TILE, 1), lambda i, lengths: (0, i, 0)),
            ],
        ),
        out_shape=[
            jax.ShapeDtypeStruct((BLOCK, heads * HEAD_DIM), jnp.bfloat16),
            jax.ShapeDtypeStruct((heads, BLOCK, 1), jnp.float32),
        ],
        compiler_params=pltpu.CompilerParams(vmem_limit_bytes=VMEM_LIMIT),
    )(lengths, qkv)


def attention_backward(qkv, lengths, heads, ctx, lse, grad_ctx, planes):
    tiles = BLOCK // ATT_TILE

    def kernel(
        lengths_ref, qkv_ref, ctx_ref, lse_ref, do_ref, cos_ref, below_ref, above_ref, out_ref, sums_ref, dk_ref,
        dv_ref,
    ):
        tile = pl.program_id(0)

        @pl.when(tile == 0)
        def _():
            dk_ref[...] = jnp.zeros_like(dk_ref)
            dv_ref[...] = jnp.zeros_like(dv_ref)

        start, first = tile_starts(lengths_ref, tile)
        here = span(tile, ATT_TILE)
        fixed = []
        for head in range(heads):
            lanes = slice(head * HEAD_DIM, (head + 1) * HEAD_DIM)
            grads = do_ref[:, lanes]
            inner = jnp.sum(
                grads.astype(jnp.float32) * ctx_ref[:, lanes].astype(jnp.float32), axis=1, keepdims=True
            )
            queries = qkv_ref[here, 3 * head * HEAD_DIM : (3 * head + 1) * HEAD_DIM]
            fixed.append((queries, grads, inner, lse_ref[head]))

        def step(key_tile, carry):
            rows = span(key_tile, ATT_TILE)
            allowed = tile_mask(start, tile, key_tile)
            found = []
            for head in range(heads):
                queries, grads, inner, lse_rows = fixed[head]
                lanes = slice(head * HEAD_DIM, (head + 1) * HEAD_DIM)
                keys = qkv_ref[rows, (3 * head + 1) * HEAD_DIM : (3 * head + 2) * HEAD_DIM]
                values = qkv_ref[rows, (3 * head + 2) * HEAD_DIM : (3 * head + 3) * HEAD_DIM]
                scores = dot_nt(queries, keys) * SCALE
                probs = jnp.where(allowed, jnp.exp(scores - lse_rows), 0.0)
                grad_scores = (probs * (dot_nt(grads, values) - inner)).astype(jnp.bfloat16)
                dv_ref[rows, lanes] += dot_tn(probs.astype(jnp.bfloat16), grads)
                dk_ref[rows, lanes] += dot_tn(grad_scores, queries)
                found.append(carry[head] + jnp.dot(grad_scores, keys, preferred_element_type=jnp.float32))
            return tuple(found)

        none = jnp.zeros((ATT_TILE, HEAD_DIM), jnp.float32)
        result = lax.fori_loop(first, tile + 1, step, (none,) * heads)
        for head in range(heads):
            out_ref[here, 3 * head * HEAD_DIM : (3 * head + 1) * HEAD_DIM] = turn(
                result[head] * SCALE, cos_ref[here, :], -below_ref[here, :], -above_ref[here, :]
            ).astype(jnp.bfloat16)

        @pl.when(tile == tiles - 1)
        def _():
            def finish(index, sums):
                rows = span(index, ATT_TILE)
                for head in range(heads):
                    lanes = slice(head * HEAD_DIM, (head + 1) * HEAD_DIM)
                    out_ref[rows, (3 * head + 1) * HEAD_DIM : (3 * head + 2) * HEAD_DIM] = turn(
                        dk_ref[rows, lanes] * SCALE, cos_ref[rows, :], -below_ref[rows, :], -above_ref[rows, :]
                    ).astype(jnp.bfloat16)
                    out_ref[rows, (3 * head + 2) * HEAD_DIM : (3 * head + 3) * HEAD_DIM] = dv_ref[rows, lanes].astype(
                        jnp.bfloat16
                    )
                return sums + jnp.sum(out_ref[rows, :].astype(jnp.float32), axis=0, keepdims=True)

            sums_ref[...] = lax.fori_loop(
                0, tiles, finish, jnp.zeros((1, 3 * heads * HEAD_DIM), jnp.float32)
            )

    def whole(shape):
        return pl.BlockSpec(shape, lambda i, lengths: (0,) * len(shape))

    return pl.pallas_call(
        kernel,
        grid_spec=pltpu.PrefetchScalarGridSpec(
            num_scalar_prefetch=1,
            grid=(tiles,),
            in_specs=[
                whole(qkv.shape),
                pl.BlockSpec((ATT_TILE, heads * HEAD_DIM), lambda i, lengths: (i, 0)),
                pl.BlockSpec((heads, ATT_TILE, 1), lambda i, lengths: (0, i, 0)),
                pl.BlockSpec((ATT_TILE, heads * HEAD_DIM), lambda i, lengths: (i, 0)),
                whole((BLOCK, HEAD_DIM)),
                whole((BLOCK, HEAD_DIM)),
                whole((BLOCK, HEAD_DIM)),
            ],
            out_specs=[whole(qkv.shape), whole((1, qkv.shape[1]))],
            scratch_shapes=[
                pltpu.VMEM((BLOCK, heads * HEAD_DIM), jnp.float32),
                pltpu.VMEM((BLOCK, heads * HEAD_DIM), jnp.float32),
            ],
        ),
        out_shape=[
            jax.ShapeDtypeStruct(qkv.shape, jnp.bfloat16),
            jax.ShapeDtypeStruct((1, qkv.shape[1]), jnp.float32),
        ],
        compiler_params=pltpu.CompilerParams(vmem_limit_bytes=VMEM_LIMIT),
    )(lengths, qkv, ctx, lse, grad_ctx, *planes)


def gather_cut(sizes):
    return (1792, 256) if sizes == (4, 2) else (D // 2, D // 2)


def scatter_cut(sizes):
    return (1664, 384) if sizes == (4, 2) else (D // 2, D // 2)


def columns_of(cut, kind):
    return pl.ds(0, cut[0]) if kind == 0 else pl.ds(cut[0], cut[1])


def tile_of(width):
    return 512 if width % 512 == 0 else 256 if width % 256 == 0 else 128


ANY = pl.BlockSpec(memory_space=pl.ANY)
VMEM = pl.BlockSpec(memory_space=pltpu.VMEM)
SMEM = pl.BlockSpec(memory_space=pltpu.SMEM)


def row_kernel(kernel, collective, out_shape, in_specs, out_specs, scratch, cost, before=()):
    def body(*refs):
        kernel(*refs[len(before):])

    def call(*args):
        return pl.pallas_call(
            body,
            out_shape=out_shape,
            in_specs=[ANY] * len(before) + in_specs,
            out_specs=out_specs,
            scratch_shapes=scratch,
            cost_estimate=pl.CostEstimate(flops=cost, bytes_accessed=2**28 if cost > 1 else 1, transcendentals=0),
            compiler_params=pltpu.CompilerParams(
                collective_id=collective, has_side_effects=True, vmem_limit_bytes=VMEM_LIMIT
            ),
        )(*before, *args)

    return call


def gather_scratch(sizes, rows):
    shards = sizes[0] * sizes[1]
    return [
        pltpu.VMEM((shards, rows, D), jnp.bfloat16),
        pltpu.SemaphoreType.DMA((gather_sends(sizes, HALVES),)),
        pltpu.SemaphoreType.DMA((2, HALVES, shards)),
    ]


def run_gather(grid, sizes, rows, full, send_sems, recv_sems, ready):
    cut = gather_cut(sizes)
    step = rows // HALVES
    sender = Sender(send_sems)

    def piece(slot, half, kind):
        return full.at[slot, pl.ds(half * step, step), columns_of(cut, kind)]

    gather_rounds(grid, sender, piece, recv_sems, HALVES, cut, ready)
    sender.finish()


def sum_scratch(sizes, rows):
    shards = sizes[0] * sizes[1]
    bufs, sems = scatter_scratch(sizes, HALVES, rows, D, scatter_cut(sizes))
    return (
        [pltpu.VMEM((shards, rows, D), jnp.bfloat16)]
        + bufs
        + sems
        + [pltpu.SemaphoreType.DMA((scatter_sends(sizes, HALVES),))]
    )


def run_scatter(grid, sizes, rows, scratch, produce, *hooks, quick=False):
    cut = scatter_cut(sizes)
    step = rows // HALVES
    parts, b0, b1, b2, b3, s0, s1, s2, s3, send_sems = scratch
    sender = Sender(send_sems)

    def part(slot, half, kind):
        return parts.at[slot, pl.ds(half * step, step), columns_of(cut, kind)]

    scatter = Scatter(
        grid, sender, part, ((b0, b1), (b2, b3)), ((s0, s1), (s2, s3)), HALVES, cut, quick
    )
    scatter.run(produce, *hooks)
    sender.finish()


def production_order(grid, quick=False):
    return [
        grid.index(grid.nearest(0, k), grid.nearest(1, l))
        for action, k, l in [step for step in scatter_plan(grid.n, quick) if step[0] == "make"]
    ]


ROW_TILE = 64


def tile_stats(values):
    centered = values - jnp.mean(values, axis=1, keepdims=True)
    inverse = lax.rsqrt(jnp.mean(centered * centered, axis=1, keepdims=True) + EPSILON)
    return centered, inverse


def open_rows(own, sizes, collective, norms, qkv_flat, qkv_bias, up_weight, up_bias, lengths):
    rows = own.shape[0]
    shards = sizes[0] * sizes[1]
    width, hidden = qkv_flat.shape[1], up_weight.shape[1]
    heads = width // (3 * HEAD_DIM)

    def kernel(
        own_ref, norms_ref, qkvw_any, qkvb_ref, upw_any, upb_ref, lengths_ref, freq_ref,
        plain_any, one_any, two_any, qkv_any, act_any, slope_any, cos_ref, below_ref, above_ref,
        full, send_sems, recv_sems, qkvw, upw, load_sems, plain, one, two, qkv, act, slope, out_sems,
    ):
        grid = Grid2(sizes)
        loads = [
            pltpu.make_async_copy(qkvw_any, qkvw, load_sems.at[0]),
            pltpu.make_async_copy(upw_any, upw, load_sems.at[1]),
        ]
        for copy in loads:
            copy.start()
        full[grid.index(*grid.me)] = own_ref[...]
        grid.barrier()
        open_copies = []

        def outs(place, slot):
            pairs = ((plain, plain_any), (one, one_any), (two, two_any), (qkv, qkv_any), (act, act_any), (slope, slope_any))
            return [
                pltpu.make_async_copy(here.at[slot], there.at[place], out_sems.at[slot, i])
                for i, (here, there) in enumerate(pairs)
            ]

        def ready(slow, fast, order):
            place = grid.index(slow, fast)
            slot = order % 2
            if order == 0:
                for copy in loads:
                    copy.wait()
            if order >= 2:
                for copy in open_copies.pop(0):
                    copy.wait()

            def norm_tile(index, _):
                here = span(index, ROW_TILE)
                centered, inverse = tile_stats(full[place, here].astype(jnp.float32))
                normed = centered * inverse
                plain[slot, here] = normed.astype(jnp.bfloat16)
                one[slot, here] = (normed * norms_ref[0:1] + norms_ref[1:2]).astype(jnp.bfloat16)
                two[slot, here] = (normed * norms_ref[2:3] + norms_ref[3:4]).astype(jnp.bfloat16)
                return _

            lax.fori_loop(0, rows // ROW_TILE, norm_tile, 0)
            places = pl.ds(pl.multiple_of(place * rows, rows), rows)
            row = place * rows + lax.broadcasted_iota(jnp.int32, (rows, 1), 0)
            cos, below, above = rotary_planes(row - first_rows(lengths_ref, row), freq_ref[...])
            cos_ref[places, :], below_ref[places, :], above_ref[places, :] = cos, below, above
            whole = jnp.dot(one[slot], qkvw[...], preferred_element_type=jnp.float32) + qkvb_ref[...]
            for head in range(heads):
                first = head * 3 * HEAD_DIM
                found = whole[:, first : first + 3 * HEAD_DIM]
                qkv[slot, :, first : first + HEAD_DIM] = turn(
                    found[:, :HEAD_DIM], cos, below, above
                ).astype(jnp.bfloat16)
                qkv[slot, :, first + HEAD_DIM : first + 2 * HEAD_DIM] = turn(
                    found[:, HEAD_DIM : 2 * HEAD_DIM], cos, below, above
                ).astype(jnp.bfloat16)
                qkv[slot, :, first + 2 * HEAD_DIM : first + 3 * HEAD_DIM] = found[
                    :, 2 * HEAD_DIM :
                ].astype(jnp.bfloat16)
            tile = tile_of(hidden)

            def up_tile(index, _):
                here = span(index, tile)
                pre = jnp.dot(two[slot], upw[:, here], preferred_element_type=jnp.float32) + upb_ref[:, here]
                share = 0.5 * (1.0 + lax.erf(pre * 0.7071067811865476))
                act[slot, :, here] = (pre * share).astype(jnp.bfloat16)
                slope[slot, :, here] = (
                    share + pre * (jnp.exp(-0.5 * pre * pre) * 0.3989422804014327)
                ).astype(jnp.bfloat16)
                return _

            lax.fori_loop(0, hidden // tile, up_tile, 0)
            copies = outs(place, slot)
            for copy in copies:
                copy.start()
            open_copies.append(copies)

        run_gather(grid, sizes, rows, full, send_sems, recv_sems, ready)
        for copies in open_copies:
            for copy in copies:
                copy.wait()

    def out(columns):
        return jax.ShapeDtypeStruct((shards, rows, columns), jnp.bfloat16)

    def staged(columns):
        return pltpu.VMEM((2, rows, columns), jnp.bfloat16)

    return row_kernel(
        kernel, collective,
        [out(D), out(D), out(D), out(width), out(hidden), out(hidden)]
        + [jax.ShapeDtypeStruct((shards * rows, HEAD_DIM), jnp.float32)] * 3,
        [VMEM, VMEM, ANY, VMEM, ANY, VMEM, SMEM, VMEM],
        [ANY] * 6 + [VMEM] * 3,
        gather_scratch(sizes, rows)
        + [
            pltpu.VMEM(qkv_flat.shape, jnp.bfloat16),
            pltpu.VMEM(up_weight.shape, jnp.bfloat16),
            pltpu.SemaphoreType.DMA((2,)),
            staged(D), staged(D), staged(D), staged(width), staged(hidden), staged(hidden),
            pltpu.SemaphoreType.DMA((2, 6)),
        ],
        2 * BLOCK * D * (width + hidden),
    )(own, norms, qkv_flat, qkv_bias, up_weight, up_bias, lengths, rotary_frequencies())


def branch_rows(own, ctx, act, out_flat, down_weight, norms, sizes, collective):
    rows = own.shape[0]
    shards = sizes[0] * sizes[1]
    inner, hidden = out_flat.shape[0], down_weight.shape[0]

    def kernel(
        own_ref, ctx_any, act_any, outw_any, downw_any, norms_ref, out_ref, final_ref, normed_ref, inverse_ref,
        ctx, act, outw, downw, load_sems, *scratch,
    ):
        grid = Grid2(sizes)
        parts = scratch[0]
        weights = [
            pltpu.make_async_copy(outw_any, outw, load_sems.at[0, 0]),
            pltpu.make_async_copy(downw_any, downw, load_sems.at[0, 1]),
        ]
        order = production_order(grid)
        loads = [
            [
                pltpu.make_async_copy(ctx_any.at[place], ctx.at[place], load_sems.at[1 + i, 0]),
                pltpu.make_async_copy(act_any.at[place], act.at[place], load_sems.at[1 + i, 1]),
            ]
            for i, place in enumerate(order)
        ]
        for copy in loads[0] + weights:
            copy.start()
        for copies in loads[1:]:
            for copy in copies:
                copy.start()
        grid.barrier()
        for copy in weights:
            copy.wait()

        def produce(slow, fast):
            place = grid.index(slow, fast)
            for copy in loads.pop(0):
                copy.wait()

            def columns(index, _):
                here = span(index, 512)
                parts[place, :, here] = (
                    jnp.dot(ctx[place], outw[:, here], preferred_element_type=jnp.float32)
                    + jnp.dot(act[place], downw[:, here], preferred_element_type=jnp.float32)
                ).astype(jnp.bfloat16)
                return _

            lax.fori_loop(0, D // 512, columns, 0)

        run_scatter(grid, sizes, rows, scratch, produce)
        mine = grid.index(*grid.me)

        def norm_tile(index, _):
            here = span(index, ROW_TILE)
            stream = own_ref[here].astype(jnp.float32) + parts[mine, here].astype(jnp.float32) + norms_ref[2:3]
            out_ref[here] = stream.astype(jnp.bfloat16)
            centered, inverse = tile_stats(stream)
            normed = centered * inverse
            final_ref[here] = (normed * norms_ref[0:1] + norms_ref[1:2]).astype(jnp.bfloat16)
            normed_ref[here] = normed
            inverse_ref[here] = inverse
            return _

        lax.fori_loop(0, rows // ROW_TILE, norm_tile, 0)

    return row_kernel(
        kernel, collective,
        [
            jax.ShapeDtypeStruct((rows, D), jnp.bfloat16),
            jax.ShapeDtypeStruct((rows, D), jnp.bfloat16),
            jax.ShapeDtypeStruct((rows, D), jnp.float32),
            jax.ShapeDtypeStruct((rows, 1), jnp.float32),
        ],
        [VMEM, ANY, ANY, ANY, ANY, VMEM],
        [VMEM] * 4,
        [
            pltpu.VMEM(ctx.shape, jnp.bfloat16),
            pltpu.VMEM(act.shape, jnp.bfloat16),
            pltpu.VMEM(out_flat.shape, jnp.bfloat16),
            pltpu.VMEM(down_weight.shape, jnp.bfloat16),
            pltpu.SemaphoreType.DMA((1 + shards, 2)),
        ]
        + sum_scratch(sizes, rows),
        2 * BLOCK * D * (inner + hidden),
    )(own, ctx, act, out_flat, down_weight, norms)


def logit_rows(final, head_weight, targets_col, sizes, collective):
    rows = final.shape[0]
    shards = sizes[0] * sizes[1]
    vocab = head_weight.shape[1]

    def kernel(
        own_ref, headw_any, target_ref, final_any, weights_any, stats_ref,
        full, send_sems, recv_sems, headw, load_sem, logits, weights, out_sems, row_sems,
    ):
        grid = Grid2(sizes)
        load = pltpu.make_async_copy(headw_any, headw, load_sem)
        load.start()
        full[grid.index(*grid.me)] = own_ref[...]
        grid.barrier()
        base = lax.axis_index("seq") * vocab
        open_copies, raw_copies = [], []

        def ready(slow, fast, order):
            place = grid.index(slow, fast)
            slot = order % 2
            if order == 0:
                load.wait()
            if order >= 2:
                open_copies.pop(0).wait()
            places = pl.ds(pl.multiple_of(place * rows, rows), rows)
            target = target_ref[places, :] - base

            def fold(values, join):
                total = values[:, :128]
                for first in range(128, values.shape[1], 128):
                    total = join(total, values[:, first : first + 128])
                return total

            def logit_tile(start, size, carry):
                top, pick = carry
                here = pl.ds(start, size)
                found = jnp.dot(full[place], headw[:, here], preferred_element_type=jnp.float32)
                logits[:, here] = found
                ids = start + lax.broadcasted_iota(jnp.int32, (rows, size), 1)
                top = jnp.maximum(top, fold(found, jnp.maximum))
                pick = pick + fold(jnp.where(ids == target, found, 0.0), jnp.add)
                return (top, pick)

            def tiled(step, carry):
                count = vocab // 512
                carry = lax.fori_loop(
                    0, count, lambda i, c: step(pl.multiple_of(i * 512, 512), 512, c), carry
                )
                if vocab % 512:
                    carry = step(count * 512, vocab % 512, carry)
                return carry

            top, pick = tiled(
                logit_tile,
                (jnp.full((rows, 128), -jnp.inf, jnp.float32), jnp.zeros((rows, 128), jnp.float32)),
            )
            top = jnp.max(top, axis=1, keepdims=True)
            pick = jnp.sum(pick, axis=1, keepdims=True)

            def weight_tile(start, size, total):
                here = pl.ds(start, size)
                found = jnp.exp(logits[:, here] - top)
                weights[slot, :, here] = found.astype(jnp.bfloat16)
                return total + fold(found, jnp.add)

            total = tiled(weight_tile, jnp.zeros((rows, 128), jnp.float32))
            total = jnp.sum(total, axis=1, keepdims=True)
            lane = lax.broadcasted_iota(jnp.int32, (rows, 128), 1)
            found = jnp.where(lane == 0, top, jnp.where(lane == 1, total, pick))
            stats_ref[:, places] = found.T[0:8]
            copy = pltpu.make_async_copy(weights.at[slot], weights_any.at[place], out_sems.at[slot])
            copy.start()
            open_copies.append(copy)
            raw = pltpu.make_async_copy(full.at[place], final_any.at[place], row_sems.at[order])
            raw.start()
            raw_copies.append(raw)

        run_gather(grid, sizes, rows, full, send_sems, recv_sems, ready)
        for copy in open_copies + raw_copies:
            copy.wait()

    return row_kernel(
        kernel, collective,
        [
            jax.ShapeDtypeStruct((shards, rows, D), jnp.bfloat16),
            jax.ShapeDtypeStruct((shards, rows, vocab), jnp.bfloat16),
            jax.ShapeDtypeStruct((8, shards * rows), jnp.float32),
        ],
        [VMEM, ANY, VMEM],
        [ANY, ANY, VMEM],
        gather_scratch(sizes, rows)
        + [
            pltpu.VMEM(head_weight.shape, jnp.bfloat16),
            pltpu.SemaphoreType.DMA,
            pltpu.VMEM((rows, vocab), jnp.float32),
            pltpu.VMEM((2, rows, vocab), jnp.bfloat16),
            pltpu.SemaphoreType.DMA((2,)),
            pltpu.SemaphoreType.DMA((shards,)),
        ],
        2 * BLOCK * D * vocab,
    )(final, head_weight, targets_col)


def final_grad_rows(grad_logits, head_weight, normed, inverse, gain, sizes, collective, before):
    shards, rows, vocab = grad_logits.shape

    def kernel(
        grads_any, headw_any, normed_ref, inverse_ref, gain_ref, stream_ref, down_ref, sums_ref,
        headw, grads, load_sems, *scratch,
    ):
        grid = Grid2(sizes)
        parts = scratch[0]
        order = production_order(grid)
        loads = [
            pltpu.make_async_copy(grads_any.at[place], grads.at[i % 2], load_sems.at[i])
            for i, place in enumerate(order)
        ]
        tile = 512
        weights = [
            pltpu.make_async_copy(
                headw_any.at[pl.ds(i * tile, tile)], headw.at[pl.ds(i * tile, tile)], load_sems.at[1 + shards + i]
            )
            for i in range(D // tile)
        ]
        loads[0].start()
        for copy in weights:
            copy.start()
        grid.barrier()
        count = [0]

        def produce(slow, fast):
            place = grid.index(slow, fast)
            i = count[0]
            count[0] += 1
            if i + 1 < shards:
                loads[i + 1].start()
            loads[i].wait()

            def columns(index, _):
                here = span(index, tile)
                parts[place, :, here] = dot_nt(grads[i % 2], headw[here, :]).astype(jnp.bfloat16)
                return _

            if i == 0:
                for index, copy in enumerate(weights):
                    copy.wait()
                    columns(index, 0)
            else:
                lax.fori_loop(0, D // tile, columns, 0)

        run_scatter(grid, sizes, rows, scratch, produce)
        mine = grid.index(*grid.me)
        sums_ref[...] = jnp.zeros_like(sums_ref)

        def norm_tile(index, _):
            here = span(index, ROW_TILE)
            grad = parts[mine, here].astype(jnp.float32)
            norm = normed_ref[here]
            scaled = grad * gain_ref[...]
            stream = inverse_ref[here] * (
                scaled
                - jnp.mean(scaled, axis=1, keepdims=True)
                - norm * jnp.mean(scaled * norm, axis=1, keepdims=True)
            )
            stream_ref[here] = stream
            down_ref[here] = stream.astype(jnp.bfloat16)
            sums_ref[0:1] += jnp.sum(grad * norm, axis=0, keepdims=True)
            sums_ref[1:2] += jnp.sum(grad, axis=0, keepdims=True)
            sums_ref[2:3] += jnp.sum(stream, axis=0, keepdims=True)
            return _

        lax.fori_loop(0, rows // ROW_TILE, norm_tile, 0)

    return row_kernel(
        kernel, collective,
        [
            jax.ShapeDtypeStruct((rows, D), jnp.float32),
            jax.ShapeDtypeStruct((rows, D), jnp.bfloat16),
            jax.ShapeDtypeStruct((8, D), jnp.float32),
        ],
        [ANY, ANY, VMEM, VMEM, VMEM],
        [VMEM] * 3,
        [
            pltpu.VMEM(head_weight.shape, jnp.bfloat16),
            pltpu.VMEM((2, rows, vocab), jnp.bfloat16),
            pltpu.SemaphoreType.DMA((1 + shards + D // 512,)),
        ]
        + sum_scratch(sizes, rows),
        2 * BLOCK * D * vocab,
        before,
    )(grad_logits, head_weight, normed, inverse, gain)


def branch_grad_rows(own, out_flat, down_weight, slope, ctx, act, second, sizes, collective, before):
    rows = own.shape[0]
    shards = sizes[0] * sizes[1]
    inner, hidden = out_flat.shape[0], down_weight.shape[0]
    half_width = D // 2

    def kernel(
        own_ref, outw_any, downw_any, slope_any, ctx_any, act_any, second_any,
        grad_ctx_any, grad_up_any, sums_ref, stream_away, stream_mine, up_away, up_mine,
        full, send_sems, recv_sems, outw, downw, load_sems, slope, slope_sem, grad_ctx, grad_up, out_sems,
        ctx, act, second, row_sems, out_total, down_total, up_total, part_sems,
    ):
        grid = Grid2(sizes)
        core = lax.rem(lax.axis_index("dp"), 2)
        loads = [
            pltpu.make_async_copy(outw_any, outw, load_sems.at[0]),
            pltpu.make_async_copy(downw_any, downw, load_sems.at[1]),
        ]
        for copy in loads:
            copy.start()
        slopes = pltpu.make_async_copy(slope_any, slope, slope_sem)
        slopes.start()
        order_of = [
            grid.index(grid.nearest(0, k), grid.nearest(1, l)) for k in range(sizes[0]) for l in range(sizes[1])
        ]
        row_loads = [
            [
                pltpu.make_async_copy(there.at[place], here.at[i % 2], row_sems.at[i % 2, j])
                for j, (there, here) in enumerate(((ctx_any, ctx), (act_any, act), (second_any, second)))
            ]
            for i, place in enumerate(order_of)
        ]
        for copy in row_loads[0]:
            copy.start()
        full[grid.index(*grid.me)] = own_ref[...]
        sums_ref[...] = jnp.zeros_like(sums_ref)
        grid.barrier()
        open_copies = []

        def ready(slow, fast, order):
            place = grid.index(slow, fast)
            slot = order % 2
            if order == 0:
                for copy in loads + [slopes]:
                    copy.wait()
            if order >= 2:
                for copy in open_copies.pop(0):
                    copy.wait()
            if order + 1 < shards:
                for copy in row_loads[order + 1]:
                    copy.start()
            grad_ctx[slot] = dot_nt(full[place], outw[...]).astype(jnp.bfloat16)
            tile = tile_of(hidden)

            def up_tile(index, _):
                here = span(index, tile)
                found = dot_nt(full[place], downw[here, :]) * slope[place, :, here].astype(jnp.float32)
                rounded = found.astype(jnp.bfloat16)
                grad_up[slot, :, here] = rounded
                sums_ref[0:1, here] += jnp.sum(rounded.astype(jnp.float32), axis=0, keepdims=True)
                return _

            lax.fori_loop(0, hidden // tile, up_tile, 0)
            copies = [
                pltpu.make_async_copy(grad_ctx.at[slot], grad_ctx_any.at[place], out_sems.at[slot, 0]),
                pltpu.make_async_copy(grad_up.at[slot], grad_up_any.at[place], out_sems.at[slot, 1]),
            ]
            for copy in copies:
                copy.start()
            open_copies.append(copies)
            for copy in row_loads[order]:
                copy.wait()

            def add(total, here, found):
                if order == 0:
                    total[:, here] = found
                else:
                    total[:, here] += found

            def stream_tile(index, _):
                here = span(index, 512)
                grads = full[place, :, here]
                add(out_total, here, dot_tn(ctx[slot], grads))
                add(down_total, here, dot_tn(act[slot], grads))
                return _

            lax.fori_loop(0, D // 512, stream_tile, 0)

            def up_grad_tile(index, _):
                here = span(index, tile)
                add(up_total, here, dot_tn(second[slot], grad_up[slot, :, here]))
                return _

            lax.fori_loop(0, hidden // tile, up_grad_tile, 0)

        run_gather(grid, sizes, rows, full, send_sems, recv_sems, ready)
        for copies in open_copies:
            for copy in copies:
                copy.wait()
        stores = []

        def store(total, there, row, column, height, width):
            index = len(stores)
            if index < 2 * shards:
                here = full.at[index // 2, :, pl.ds((index % 2) * half_width, width)]
            else:
                here = slope.at[index - 2 * shards, :, pl.ds(0, width)]
            here[...] = total[
                pl.ds(pl.multiple_of(row, rows), rows), pl.ds(pl.multiple_of(column, 128), width)
            ].astype(jnp.bfloat16)
            copy = pltpu.make_async_copy(here, there.at[pl.ds(height, rows)], part_sems.at[index])
            copy.start()
            stores.append(copy)

        for which, wide in ((1 - core, (stream_away, up_away)), (core, (stream_mine, up_mine))):
            for total, begin, count in ((out_total, 0, inner), (down_total, inner, hidden)):
                for height in range(0, count, rows):
                    store(total, wide[0], height, which * half_width, begin + height, half_width)
            for height in range(0, half_width, rows):
                store(up_total, wide[1], which * half_width + height, 0, height, hidden)
        for copy in stores:
            copy.wait()

    def out(columns):
        return jax.ShapeDtypeStruct((shards, rows, columns), jnp.bfloat16)

    parts = [
        jax.ShapeDtypeStruct(shape, jnp.bfloat16)
        for shape in ((inner + hidden, half_width), (half_width, hidden))
        for _ in range(2)
    ]
    stores = 2 * (inner // rows + hidden // rows + half_width // rows)
    return row_kernel(
        kernel, collective,
        [out(inner), out(hidden), jax.ShapeDtypeStruct((8, hidden), jnp.float32)] + parts,
        [VMEM] + [ANY] * 6,
        [ANY, ANY, VMEM] + [ANY] * 4,
        gather_scratch(sizes, rows)
        + [
            pltpu.VMEM(out_flat.shape, jnp.bfloat16),
            pltpu.VMEM(down_weight.shape, jnp.bfloat16),
            pltpu.SemaphoreType.DMA((2,)),
            pltpu.VMEM((shards, rows, hidden), jnp.bfloat16),
            pltpu.SemaphoreType.DMA,
            pltpu.VMEM((2, rows, inner), jnp.bfloat16),
            pltpu.VMEM((2, rows, hidden), jnp.bfloat16),
            pltpu.SemaphoreType.DMA((2, 2)),
            pltpu.VMEM((2, rows, inner), jnp.bfloat16),
            pltpu.VMEM((2, rows, hidden), jnp.bfloat16),
            pltpu.VMEM((2, rows, D), jnp.bfloat16),
            pltpu.SemaphoreType.DMA((2, 3)),
            pltpu.VMEM((inner, D), jnp.float32),
            pltpu.VMEM((hidden, D), jnp.float32),
            pltpu.VMEM((D, hidden), jnp.float32),
            pltpu.SemaphoreType.DMA((stores,)),
        ],
        4 * BLOCK * D * (inner + hidden) + 2 * BLOCK * D * hidden,
        before,
    )(own, out_flat, down_weight, slope, ctx, act, second)


class SmallSum:
    def __init__(self, shards, sums, total, scratch):
        self.shards, self.sums, self.total = shards, sums, total
        self.came, self.spread_send, self.spread_recv, self.back_send, self.back_recv = scratch
        self.here = lax.axis_index("seq")
        self.width = D // shards
        self.others = [(step, lax.rem(self.here + step, shards)) for step in range(1, shards)]

    @staticmethod
    def scratch(shards):
        dma = pltpu.SemaphoreType.DMA
        return [pltpu.VMEM((shards, 8, D // shards), jnp.float32)] + [dma((shards,))] * 4

    def barrier(self):
        sem = pltpu.get_barrier_semaphore()
        for _, place in self.others:
            pl.semaphore_signal(sem, inc=1, device_id={"seq": place}, device_id_type=MESH)
        pl.semaphore_wait(sem, self.shards - 1)

    def copy(self, place, src, dst, send, recv):
        return pltpu.make_async_remote_copy(
            src_ref=src, dst_ref=dst, send_sem=send, recv_sem=recv, device_id={"seq": place}, device_id_type=MESH
        )

    def columns(self, place):
        return pl.ds(pl.multiple_of(place * self.width, self.width), self.width)

    def spread(self):
        self.first = [
            self.copy(
                place, self.sums.at[:, self.columns(place)], self.came.at[step], self.spread_send.at[step],
                self.spread_recv.at[step],
            )
            for step, place in self.others
        ]
        for copy in self.first:
            copy.start()

    def collect(self):
        here = self.columns(self.here)
        total = self.sums[:, here]
        for (step, _), copy in zip(self.others, self.first):
            copy.wait_recv()
            total = total + self.came[step]
        self.total[:, here] = total
        self.second = [
            self.copy(
                place, self.total.at[:, here], self.total.at[:, here], self.back_send.at[step], self.back_recv.at[step]
            )
            for step, place in self.others
        ]
        for copy in self.second:
            copy.start()

    def finish(self):
        for step, _ in self.others:
            source = lax.rem(self.here + self.shards - step, self.shards)
            there = self.total.at[:, self.columns(source)]
            self.copy(source, there, there, self.back_send.at[step], self.back_recv.at[step]).wait_recv()
        for copy in self.first + self.second:
            copy.wait_send()


def score_rows(stats, lengths, labels, reference, sizes, replicas, collective):
    shards = sizes[0] * sizes[1]
    width = BLOCK // shards

    def kernel(
        stats_ref, lengths_ref, labels_ref, reference_ref, coef_ref, losses_ref,
        came, full, ratio, ratios, spread_send, spread_recv, back_send, back_recv, cross_send, cross_recv,
    ):
        seq, dp = lax.axis_index("seq"), lax.axis_index("dp")
        peers = {
            "seq": [(step, lax.rem(seq + step, shards)) for step in range(1, shards)],
            "dp": [(step, lax.rem(dp + step, replicas)) for step in range(1, replicas)],
        }
        barrier = pltpu.get_barrier_semaphore()
        for axis in peers:
            for _, place in peers[axis]:
                pl.semaphore_signal(barrier, inc=1, device_id={axis: place}, device_id_type=MESH)
        pl.semaphore_wait(barrier, shards + replicas - 2)

        def columns(place):
            return pl.ds(pl.multiple_of(place * width, width), width)

        def copy(axis, place, src, dst, send, recv):
            return pltpu.make_async_remote_copy(
                src_ref=src, dst_ref=dst, send_sem=send, recv_sem=recv, device_id={axis: place}, device_id_type=MESH
            )

        sent = [
            copy("seq", place, stats_ref.at[:, columns(place)], came.at[step], spread_send.at[step], spread_recv.at[step])
            for step, place in peers["seq"]
        ]
        for one in sent:
            one.start()
        mine = stats_ref[:, columns(seq)]
        top, total, pick = mine[0:1], mine[1:2], mine[2:3]
        for (step, _), one in zip(peers["seq"], sent):
            one.wait_recv()
            other = came[step]
            joint = jnp.maximum(top, other[0:1])
            total = total * jnp.exp(top - joint) + other[1:2] * jnp.exp(other[0:1] - joint)
            pick = pick + other[2:3]
            top = joint
        log_total = top + jnp.log(total)
        here = columns(seq)
        full[0:1, here] = log_total
        full[1:2, here] = pick - log_total
        back = [
            copy("seq", place, full.at[:, here], full.at[:, here], back_send.at[step], back_recv.at[step])
            for step, place in peers["seq"]
        ]
        for one in back:
            one.start()
        for step, _ in peers["seq"]:
            source = lax.rem(seq + shards - step, shards)
            there = full.at[:, columns(source)]
            copy("seq", source, there, there, back_send.at[step], back_recv.at[step]).wait_recv()
        example = lax.broadcasted_iota(jnp.int32, (EXB, 1), 0)
        start, end = jnp.zeros_like(example), jnp.zeros_like(example)
        sign, reference = jnp.zeros((EXB, 1), jnp.float32), jnp.zeros((EXB, 1), jnp.float32)
        reached = jnp.int32(0)
        for index in range(EXB):
            start = jnp.where(example == index, reached, start)
            reached = reached + lengths_ref[index]
            end = jnp.where(example == index, reached, end)
            sign = jnp.where(example == index, (2 * labels_ref[index] - 1).astype(jnp.float32), sign)
            reference = jnp.where(example == index, reference_ref[index], reference)
        counts = (end - start).astype(jnp.float32)
        row = lax.broadcasted_iota(jnp.int32, (EXB, BLOCK), 1)
        member = (row >= start) & (row < end)
        mean = jnp.sum(jnp.where(member, full[1:2, :], 0.0), axis=1, keepdims=True) / counts
        log_ratio = mean - reference
        ratio[...] = jnp.broadcast_to(jnp.sum(log_ratio, axis=0, keepdims=True), ratio.shape)
        crossed = [
            copy("dp", place, ratio, ratios.at[dp], cross_send.at[step], cross_recv.at[step])
            for step, place in peers["dp"]
        ]
        for one in crossed:
            one.start()
        for one in crossed:
            one.wait_recv()
        ratios[dp] = ratio[...]
        whole = ratios[0]
        for place in range(1, replicas):
            whole = whole + ratios[place]
        center = whole[:, 0:1] / (replicas * EXB)
        squashed = jax.nn.sigmoid(BETA * sign * (log_ratio - center))
        losses_ref[...] = jnp.broadcast_to(1.0 - squashed, losses_ref.shape)
        grad = -LOSS_SCALE * BETA * sign * squashed * (1.0 - squashed) / counts
        token = jnp.sum(jnp.where(member, grad, 0.0), axis=0, keepdims=True)
        coef_ref[...] = jnp.zeros_like(coef_ref)
        coef_ref[0:1, :] = token
        coef_ref[1:2, :] = token * jnp.exp(stats_ref[0:1, :] - full[0:1, :])
        for one in sent + back + crossed:
            one.wait_send()

    dma = pltpu.SemaphoreType.DMA
    return pl.pallas_call(
        kernel,
        out_shape=[
            jax.ShapeDtypeStruct((8, BLOCK), jnp.float32),
            jax.ShapeDtypeStruct((EXB, 128), jnp.float32),
        ],
        in_specs=[VMEM] + [SMEM] * 3,
        out_specs=[VMEM] * 2,
        scratch_shapes=[
            pltpu.VMEM((shards, 8, width), jnp.float32),
            pltpu.VMEM((8, BLOCK), jnp.float32),
            pltpu.VMEM((EXB, 128), jnp.float32),
            pltpu.VMEM((replicas, EXB, 128), jnp.float32),
            dma((shards,)), dma((shards,)), dma((shards,)), dma((shards,)), dma((replicas,)), dma((replicas,)),
        ],
        compiler_params=pltpu.CompilerParams(collective_id=collective, has_side_effects=True),
    )(stats, lengths, labels, reference)


def input_grad_rows(
    own, grad_stream, plain, grad_qkv, grad_up, qkv_flat, up_weight, gains, end_sums, sizes, collective,
    before,
):
    shards, rows, width = grad_qkv.shape
    hidden = grad_up.shape[2]

    def kernel(
        own_ref, stream_ref, normed_any, qkv_any, up_any, qkvw_any, upw_any, gains_ref, end_ref,
        out_ref, total_ref,
        qkvw, upw, weight_sems, normed, qkv, up, load_sems, sums_ref, *scratch,
    ):
        grid = Grid2(sizes)
        small = SmallSum(shards, sums_ref, total_ref, scratch[:5])
        scratch = scratch[5:]
        parts = scratch[0]
        order = production_order(grid)

        def loads(i):
            place = order[i]
            return [
                pltpu.make_async_copy(normed_any.at[place], normed.at[i % 2], load_sems.at[i, 0]),
                pltpu.make_async_copy(qkv_any.at[place], qkv.at[i % 2], load_sems.at[i, 1]),
                pltpu.make_async_copy(up_any.at[place], up.at[i % 2], load_sems.at[i, 2]),
            ]

        copies = [loads(i) for i in range(shards)]
        weights = [
            pltpu.make_async_copy(qkvw_any, qkvw, weight_sems.at[0]),
            pltpu.make_async_copy(upw_any, upw, weight_sems.at[1]),
        ]
        for copy in copies[0] + weights:
            copy.start()
        sums_ref[...] = jnp.zeros_like(sums_ref)
        small.barrier()
        for copy in weights:
            copy.wait()
        count = [0]

        def produce(slow, fast):
            place = grid.index(slow, fast)
            i = count[0]
            count[0] += 1
            if i + 1 < shards:
                for copy in copies[i + 1]:
                    copy.start()
            for copy in copies[i]:
                copy.wait()
            slot = i % 2

            def columns(index, _):
                here = span(index, 512)
                one = dot_nt(qkv[slot], qkvw[here, :])
                two = dot_nt(up[slot], upw[here, :])
                norm = normed[slot, :, here].astype(jnp.float32)
                parts[place, :, here] = (one * gains_ref[0:1, here] + two * gains_ref[1:2, here]).astype(
                    jnp.bfloat16
                )
                sums_ref[0:1, here] += jnp.sum(one * norm, axis=0, keepdims=True)
                sums_ref[1:2, here] += jnp.sum(one, axis=0, keepdims=True)
                sums_ref[2:3, here] += jnp.sum(two * norm, axis=0, keepdims=True)
                sums_ref[3:4, here] += jnp.sum(two, axis=0, keepdims=True)
                return _

            lax.fori_loop(0, D // 512, columns, 0)

        def made():
            sums_ref[4:8] = end_ref[0:4]
            small.spread()

        run_scatter(grid, sizes, rows, scratch, produce, made, small.collect)
        mine = grid.index(*grid.me)

        def norm_tile(index, _):
            here = span(index, ROW_TILE)
            grad = parts[mine, here].astype(jnp.float32)
            centered, inverse = tile_stats(own_ref[here].astype(jnp.float32))
            normed = centered * inverse
            out_ref[here] = stream_ref[here] + inverse * (
                grad
                - jnp.mean(grad, axis=1, keepdims=True)
                - normed * jnp.mean(grad * normed, axis=1, keepdims=True)
            )
            return _

        lax.fori_loop(0, rows // ROW_TILE, norm_tile, 0)
        small.finish()

    return row_kernel(
        kernel, collective,
        [jax.ShapeDtypeStruct((rows, D), jnp.float32), jax.ShapeDtypeStruct((8, D), jnp.float32)],
        [VMEM, VMEM, ANY, ANY, ANY, ANY, ANY, VMEM, VMEM],
        [VMEM, VMEM],
        [
            pltpu.VMEM(qkv_flat.shape, jnp.bfloat16),
            pltpu.VMEM(up_weight.shape, jnp.bfloat16),
            pltpu.SemaphoreType.DMA((2,)),
            pltpu.VMEM((2, rows, D), jnp.bfloat16),
            pltpu.VMEM((2, rows, width), jnp.bfloat16),
            pltpu.VMEM((2, rows, hidden), jnp.bfloat16),
            pltpu.SemaphoreType.DMA((shards, 3)),
            pltpu.VMEM((8, D), jnp.float32),
        ]
        + SmallSum.scratch(shards)
        + sum_scratch(sizes, rows),
        1,
        before,
    )(own, grad_stream, plain, grad_qkv, grad_up, qkv_flat, up_weight, gains, end_sums)


def head_products(weights, coef, targets_col, final, place):
    vocab = weights.shape[1]
    half_width = D // 2
    tile = 256 if vocab % 256 == 0 else 128
    chunk = 256

    def away_kernel(place_ref, weights_ref, coef_ref, target_ref, final_ref, grads_ref, away_ref, factors):
        step = pl.program_id(0)

        @pl.when(step == 0)
        def _():
            for block in range(BLOCK // 128):
                here = pl.ds(block * 128, 128)
                found = jnp.concatenate([coef_ref[:, here], jnp.zeros((120, 128), jnp.float32)], axis=0)
                factors[here, :] = found.T

        first = place_ref[1] + step * tile

        def rows_step(index, _):
            here = span(index, chunk)
            ids = first + lax.broadcasted_iota(jnp.int32, (chunk, tile), 1)
            factor = factors[here, :]
            grads_ref[here, :] = (
                jnp.where(ids == target_ref[here, :], factor[:, 0:1], 0.0)
                - weights_ref[here, :].astype(jnp.float32) * factor[:, 1:2]
            ).astype(jnp.bfloat16)
            return _

        lax.fori_loop(0, BLOCK // chunk, rows_step, 0)
        away_ref[...] = dot_tn(final_ref[...], grads_ref[...]).astype(jnp.bfloat16)

    def mine_kernel(place_ref, grads_ref, final_ref, mine_ref):
        mine_ref[...] = dot_tn(final_ref[...], grads_ref[...]).astype(jnp.bfloat16)

    wide = pl.BlockSpec((BLOCK, tile), lambda j, place_ref: (0, j))
    narrow = pl.BlockSpec((half_width, tile), lambda j, place_ref: (0, j))
    cost = pl.CostEstimate(flops=2 * BLOCK * half_width * vocab, bytes_accessed=2**25, transcendentals=0)
    half = jax.ShapeDtypeStruct((half_width, vocab), jnp.bfloat16)
    grads, away = pl.pallas_call(
        away_kernel,
        grid_spec=pltpu.PrefetchScalarGridSpec(
            num_scalar_prefetch=1,
            grid=(vocab // tile,),
            in_specs=[
                wide,
                pl.BlockSpec((8, BLOCK), lambda j, place_ref: (0, 0)),
                pl.BlockSpec((BLOCK, 1), lambda j, place_ref: (0, 0)),
                pl.BlockSpec((BLOCK, half_width), lambda j, place_ref: (0, 1 - place_ref[0])),
            ],
            out_specs=[wide, narrow],
            scratch_shapes=[pltpu.VMEM((BLOCK, 128), jnp.float32)],
        ),
        out_shape=[jax.ShapeDtypeStruct((BLOCK, vocab), jnp.bfloat16), half],
        cost_estimate=cost,
        compiler_params=pltpu.CompilerParams(vmem_limit_bytes=VMEM_LIMIT),
    )(place, weights, coef, targets_col, final)
    mine = pl.pallas_call(
        mine_kernel,
        grid_spec=pltpu.PrefetchScalarGridSpec(
            num_scalar_prefetch=1,
            grid=(vocab // tile,),
            in_specs=[wide, pl.BlockSpec((BLOCK, half_width), lambda j, place_ref: (0, place_ref[0]))],
            out_specs=narrow,
        ),
        out_shape=half,
        cost_estimate=cost,
        compiler_params=pltpu.CompilerParams(vmem_limit_bytes=VMEM_LIMIT),
    )(place, grads, final)
    return grads, away, mine


def settle_halves(core, mine, backs, shapes, places, passed=()):
    depth, most = 4, 256
    count = len(mine[0])
    steps = []
    for index, (_, _, rows) in enumerate(places):
        size = min(most, rows)
        for which in (0, 1):
            for first in range(0, rows, size):
                steps.append((index, which, first, size))
    width = max(arrays[0].shape[1] for arrays in mine)
    deep = [shape for shape in shapes if len(shape) == 3]

    def kernel(core_ref, *refs):
        sources = [
            [refs[(index * 2 + which) * count : (index * 2 + which + 1) * count] for which in (0, 1)]
            for index, _, _ in places
        ]
        rest = refs[2 * count * len(mine) :]
        through, rest = rest[: len(passed)], rest[len(passed) :]
        outs, rest = rest[: len(shapes)], rest[len(shapes) :]
        copies = [
            pltpu.make_async_copy(here, there, rest[-1].at[i])
            for i, (here, there) in enumerate(zip(through, rest[: len(passed)]))
        ]
        taken, given, split, in_sems, out_sems = rest[len(passed) : -1]
        for copy in copies:
            copy.start()

        def loads(i):
            index, which, first, size = steps[i]
            number, begin, _ = places[index]
            columns = mine[number][0].shape[1]
            return [
                pltpu.make_async_copy(
                    source.at[pl.ds(begin + first, size)],
                    taken.at[i % depth, j, pl.ds(0, size), pl.ds(0, columns)],
                    in_sems.at[i % depth, j],
                )
                for j, source in enumerate(sources[index][which])
            ]

        def store(i):
            index, which, first, size = steps[i]
            number, _, rows = places[index]
            columns = mine[number][0].shape[1]
            place = core_ref[0] if which == 0 else 1 - core_ref[0]
            if len(shapes[index]) == 2 and shapes[index][0] == rows:
                there = outs[index].at[pl.ds(first, size), pl.ds(pl.multiple_of(place * columns, columns), columns)]
            else:
                there = outs[index].at[pl.ds(pl.multiple_of(place * rows + first, size), size)]
            here = given.at[i % depth, pl.ds(0, size), pl.ds(0, columns)]
            if len(shapes[index]) == 3:
                here = split.at[i % depth, pl.ds(0, size)]
            return pltpu.make_async_copy(here, there, out_sems.at[i % depth])

        for i in range(min(depth - 1, len(steps))):
            for copy in loads(i):
                copy.start()
        for i, (index, which, first, size) in enumerate(steps):
            if i + depth - 1 < len(steps):
                for copy in loads(i + depth - 1):
                    copy.start()
            for copy in loads(i):
                copy.wait()
            if i >= depth:
                store(i - depth).wait()
            columns = mine[places[index][0]][0].shape[1]

            def convert(row, _, i=i, index=index, columns=columns):
                here = span(row, 32)
                found = taken[i % depth, 0, here, :columns].astype(jnp.float32)
                for j in range(1, count):
                    found = found + taken[i % depth, j, here, :columns].astype(jnp.float32)
                if len(shapes[index]) == 3:
                    for head in range(shapes[index][1]):
                        split[i % depth, here, head, :] = found[
                            :, head * shapes[index][2] : (head + 1) * shapes[index][2]
                        ]
                else:
                    given[i % depth, here, :columns] = found
                return _

            lax.fori_loop(0, size // 32, convert, 0)
            store(i).start()
        for i in range(max(len(steps) - depth, 0), len(steps)):
            store(i).wait()
        for copy in copies:
            copy.wait()

    dma = pltpu.SemaphoreType.DMA
    return pl.pallas_call(
        kernel,
        out_shape=[jax.ShapeDtypeStruct(shape, jnp.float32) for shape in shapes]
        + [jax.ShapeDtypeStruct(array.shape, array.dtype) for array in passed],
        in_specs=[SMEM] + [ANY] * (2 * count * len(mine) + len(passed)),
        out_specs=[ANY] * (len(shapes) + len(passed)),
        scratch_shapes=[
            pltpu.VMEM((depth, count, most, width), jnp.bfloat16),
            pltpu.VMEM((depth, most, width), jnp.float32),
            pltpu.VMEM((depth, most) + deep[0][1:] if deep else (1, 8, 128), jnp.float32),
            dma((depth, count)),
            dma((depth,)),
            dma((max(len(passed), 1),)),
        ],
        compiler_params=pltpu.CompilerParams(vmem_limit_bytes=VMEM_LIMIT),
    )(core, *[array for pair in zip(mine, backs) for half in pair for array in half], *passed)


def row_of(vector):
    return vector.astype(jnp.float32)[None, :]


def held(values):
    return lax.optimization_barrier(values)


def half_of(values, which):
    half = values.shape[1] // 2
    return lax.dynamic_slice_in_dim(values, which * half, half, 1)


def pairs(step):
    return [(place, place ^ step) for place in range(lax.axis_size("dp"))]


class PairSum:
    def __init__(self, away, mine):
        self.plain = lax.axis_size("dp") != 4
        self.core = lax.rem(lax.axis_index("dp"), 2)
        came = lax.ppermute(away, "dp", pairs(1))
        self.sum = (mine.astype(jnp.float32) + came.astype(jnp.float32)).astype(jnp.bfloat16)

    def cross(self):
        if self.plain:
            none = jnp.zeros_like(self.sum)
            both = jnp.stack([jnp.where(self.core == which, self.sum, none) for which in (0, 1)])
            self.other, self.first_back = lax.psum(both, "dp"), self.sum
        else:
            self.other = lax.ppermute(self.sum, "dp", pairs(2))
            self.first_back = lax.ppermute(self.sum, "dp", pairs(1))
        return self


def after(values, earlier):
    def kernel(*refs):
        del refs

    return pl.pallas_call(
        kernel,
        out_shape=[jax.ShapeDtypeStruct(v.shape, v.dtype) for v in values],
        in_specs=[ANY] * (len(values) + 1),
        out_specs=[ANY] * len(values),
        input_output_aliases={i: i for i in range(len(values))},
    )(*values, earlier)


def give_back(sums, earlier):
    if sums[0].plain:
        for one in sums:
            one.mine, one.back = [one.other[0]], [one.other[1]]
        return
    for one, other in zip(sums, after([one.other for one in sums], earlier)):
        one.mine = [one.sum, other]
        one.back = [one.first_back, lax.ppermute(other, "dp", pairs(1))]


def settle_all(sums, shapes, places, passed=()):
    core = jnp.zeros((1,), jnp.int32) if sums[0].plain else sums[0].core[None]
    return settle_halves(core, [one.mine for one in sums], [one.back for one in sums], shapes, places, passed)


def pair_product(product):
    core = lax.rem(lax.axis_index("dp"), 2)
    return PairSum(product(1 - core).astype(jnp.bfloat16), held(product(core)))


def sum_over_dp(values):
    if lax.axis_size("dp") != 4:
        return lax.psum(values, "dp")
    for step in (1, 2):
        values = values + lax.ppermute(values, "dp", pairs(step))
    return values


def per_device(
    hidden, targets, lengths, labels, ref_logps, ln1_gain, ln1_bias, ln2_gain, ln2_bias, qkv_weight, qv_bias,
    out_weight, up_weight, up_bias, down_weight, branch_bias, lnf_gain, lnf_bias, head_weight,
):
    sizes = lines_of(lax.axis_size("seq"))
    own = hidden[0]
    local_heads = qkv_weight.shape[1]
    local_vocab = head_weight.shape[1]
    local_hidden = up_weight.shape[1]
    width = local_heads * 3 * HEAD_DIM
    inner = local_heads * HEAD_DIM
    qv_float = qv_bias.astype(jnp.float32)
    full_bias = jnp.concatenate(
        [qv_float[:, :HEAD_DIM], jnp.zeros_like(qv_float[:, :HEAD_DIM]), qv_float[:, HEAD_DIM:]], axis=-1
    ).reshape(1, width)
    qkv_flat = qkv_weight.reshape(D, width)
    out_flat = out_weight.reshape(inner, D)
    block_lengths = lengths[0]
    norms = jnp.concatenate([row_of(v) for v in (ln1_gain, ln1_bias, ln2_gain, ln2_bias)], axis=0)
    plain, first_full, second_full, qkv, act, slope, *planes = open_rows(
        own, sizes, 0, norms, qkv_flat, full_bias, up_weight, row_of(up_bias), block_lengths
    )
    flat_qkv = qkv.reshape(BLOCK, width)
    ctx, lse = attention_forward(flat_qkv, block_lengths, local_heads)
    shards, rows = plain.shape[0], plain.shape[1]
    end_norms = jnp.concatenate([row_of(v) for v in (lnf_gain, lnf_bias, branch_bias)], axis=0)
    output, final, normed, inverse = branch_rows(
        own, ctx.reshape(shards, rows, inner), act, out_flat, down_weight, end_norms, sizes, 1
    )
    targets_col = targets[0][:, None]
    final_full, weights, stats = logit_rows(final, head_weight, targets_col, sizes, 2)

    coef, losses = score_rows(
        stats, block_lengths, labels[0], ref_logps[0], sizes, lax.axis_size("dp"), 6
    )
    core = lax.rem(lax.axis_index("dp"), 2)
    grad_logits, away, mine = head_products(
        weights.reshape(BLOCK, local_vocab), coef, targets_col, final_full.reshape(BLOCK, D),
        jnp.stack([core, lax.axis_index("seq") * local_vocab]),
    )
    head_sum = PairSum(away, mine).cross()
    grad_stream, grad_own, end_sums = final_grad_rows(
        grad_logits.reshape(shards, rows, local_vocab), head_weight, normed, inverse, row_of(lnf_gain), sizes, 3,
        (head_sum.sum,),
    )
    grad_ctx, grad_up, up_sums, *halves = branch_grad_rows(
        grad_own, out_flat, down_weight, slope, ctx.reshape(shards, rows, inner), act, second_full, sizes, 4,
        (head_sum.first_back,),
    )
    sums = [PairSum(*halves[2 * i : 2 * i + 2]).cross() for i in range(2)]
    grad_qkv, qkv_sums = attention_backward(
        flat_qkv, block_lengths, local_heads, ctx, lse, grad_ctx.reshape(BLOCK, inner), planes
    )
    first_rows = first_full.reshape(BLOCK, D)
    sums.append(pair_product(lambda which: dot_tn(half_of(first_rows, which), grad_qkv)).cross())
    qkv_sums = qkv_sums.reshape(local_heads, 3 * HEAD_DIM)
    qv_grad = jnp.concatenate([qkv_sums[:, :HEAD_DIM], qkv_sums[:, 2 * HEAD_DIM :]], axis=-1)
    split = local_heads * 2 * HEAD_DIM
    biases = jnp.concatenate([qv_grad.reshape(-1), up_sums[0]])
    biases = jnp.pad(biases[None, :], ((0, 0), (0, D - biases.shape[0])))
    give_back([head_sum], grad_qkv)
    gains = jnp.concatenate([row_of(ln1_gain), row_of(ln2_gain)], axis=0)
    grad_input, group_sums = input_grad_rows(
        own, grad_stream, plain, grad_qkv.reshape(shards, rows, width), grad_up, qkv_flat, up_weight, gains,
        end_sums, sizes, 5, [one.first_back for one in sums],
    )
    give_back(sums[:2], group_sums)
    head_grad, output, grad_input = settle_all(
        [head_sum], [(D, local_vocab)], [(0, 0, D // 2)], (output, grad_input)
    )
    give_back(sums[2:], head_grad)
    small = sum_over_dp(jnp.concatenate([group_sums[:7], biases], axis=0))
    out_grad, down_grad, up_grad, qkv_grad = settle_all(
        sums,
        [(inner, D), (local_hidden, D), (D, local_hidden), qkv_weight.shape],
        [(0, 0, inner), (0, inner, local_hidden), (1, 0, D // 2), (2, 0, D // 2)],
    )
    return (
        losses[:, 0][None],
        output[None],
        grad_input[None],
        small[0],
        small[1],
        small[2],
        small[3],
        qkv_grad,
        small[7, :split].reshape(local_heads, 2 * HEAD_DIM),
        out_grad.reshape(out_weight.shape),
        up_grad,
        small[7, split : split + local_hidden],
        down_grad,
        small[6],
        small[4],
        small[5],
        head_grad,
    )


def solution(mesh):
    return jax.shard_map(
        per_device,
        mesh=mesh,
        in_specs=(
            P("dp", "seq", None),
            P("dp", None),
            P("dp", None),
            P("dp", None),
            P("dp", None),
            P(),
            P(),
            P(),
            P(),
            P(None, "seq", None),
            P("seq", None),
            P("seq", None, None),
            P(None, "seq"),
            P("seq"),
            P("seq", None),
            P(),
            P(),
            P(),
            P(None, "seq"),
        ),
        out_specs=(
            P("dp", None),
            P("dp", "seq", None),
            P("dp", "seq", None),
            P(),
            P(),
            P(),
            P(),
            P(None, "seq", None),
            P("seq", None),
            P("seq", None, None),
            P(None, "seq"),
            P("seq"),
            P("seq", None),
            P(),
            P(),
            P(),
            P(None, "seq"),
        ),
        check_vma=False,
    )
```

```python
import jax
import jax.numpy as jnp
from jax import lax
from jax.experimental import pallas as pl
from jax.experimental.pallas import tpu as pltpu
from jax.sharding import PartitionSpec as P

D = 2048
HEAD_DIM = 128
ROT = 32
BLOCK = 2048
EXB = 8
EPSILON = 1e-05
BETA = 0.25
LOSS_SCALE = 65536.0
HALVES = 2
VMEM_LIMIT = 62 * 2**20

MESH = pl.DeviceIdType.MESH


class Grid2:
    def __init__(self, sizes):
        self.n = sizes
        place = lax.axis_index("seq")
        self.me = (place // sizes[1], lax.rem(place, sizes[1]))

    def index(self, slow, fast):
        return slow * self.n[1] + fast

    def device(self, axis, spot):
        here = list(self.me)
        here[axis] = spot
        return {"seq": self.index(*here)}

    def nearest(self, axis, rank):
        n, m = self.n[axis], self.me[axis]
        if rank == 0:
            return m
        if n == 2:
            return 1 - m
        after = n - 1 - m
        both = jnp.minimum(m, after)
        dist = (rank + 1) // 2
        near = m - dist if rank % 2 else m + dist
        far = jnp.where(m < after, m + (rank - both), m - (rank - both))
        return jnp.where(rank <= 2 * both, near, far)

    def neighbours(self):
        found = []
        for axis in (0, 1):
            m, n = self.me[axis], self.n[axis]
            if n == 2:
                found.append((None, self.device(axis, 1 - m)))
            elif n > 2:
                found.append((m > 0, self.device(axis, m - 1)))
                found.append((m < n - 1, self.device(axis, m + 1)))
        return found

    def barrier(self, *others):
        sem = pltpu.get_barrier_semaphore()
        amount = jnp.int32(0)
        for there, device in self.neighbours() + [(None, device) for device in others]:
            def tell(device=device):
                pl.semaphore_signal(sem, inc=1, device_id=device, device_id_type=MESH)
            if there is None:
                tell()
                amount = amount + 1
            else:
                pl.when(there)(tell)
                amount = amount + there.astype(jnp.int32)
        pl.semaphore_wait(sem, amount)


class Sender:
    def __init__(self, send_sems):
        self.sems = send_sems
        self.used = 0
        self.open = []

    def send(self, src, dst, recv_sem, device, when=None):
        copy = pltpu.make_async_remote_copy(
            src_ref=src, dst_ref=dst, send_sem=self.sems.at[self.used], recv_sem=recv_sem,
            device_id=device, device_id_type=MESH)
        self.used += 1
        if when is None:
            copy.start()
        else:
            pl.when(when)(copy.start)
        self.open.append((when, copy))

    def finish(self):
        for when, copy in self.open:
            if when is None:
                copy.wait_send()
            else:
                pl.when(when)(copy.wait_send)
        self.open = []


def gather_sends(sizes, halves):
    return halves * 2 * (sizes[0] * sizes[1] * 5 + 8)


def gather_rounds(grid, sender, piece, recv_sems, halves, cut, ready):
    n, me = grid.n, grid.me

    def arrived(slow, fast, half, kind, when):
        ref = piece(grid.index(slow, fast), half, kind)
        sem = recv_sems.at[kind, half, grid.index(slow, fast)]
        wait = pltpu.make_async_copy(ref, ref, sem).wait
        if when is None:
            wait()
        else:
            pl.when(when)(wait)

    def push(slow, fast, half, kind, axis, spot, *conditions):
        ref = piece(grid.index(slow, fast), half, kind)
        sem = recv_sems.at[kind, half, grid.index(slow, fast)]
        when = None
        for condition in conditions:
            if condition is not None:
                when = condition if when is None else when & condition
        sender.send(ref, ref, sem, grid.device(axis, spot), when)

    def spread(slow, fast, half, kind, axis, when):
        m, size = me[axis], n[axis]
        if size == 2:
            push(slow, fast, half, kind, axis, 1 - m, when)
        elif size > 2:
            push(slow, fast, half, kind, axis, m + 1, when, m < size - 1)
            push(slow, fast, half, kind, axis, m - 1, when, m > 0)

    def onward(slow, fast, half, kind, axis, when):
        m, size = me[axis], n[axis]
        if size <= 2:
            return
        below = (slow, fast)[axis] < m
        more = (below & (m < size - 1)) | (jnp.logical_not(below) & (m > 0))
        push(slow, fast, half, kind, axis, jnp.where(below, m + 1, m - 1), when, more)

    def sides(d):
        if d == 0:
            return [(me[0], None)]
        if n[0] == 2:
            return [(1 - me[0], None)]
        return [(me[0] - d, me[0] >= d), (me[0] + d, me[0] + d < n[0])]

    def settle(d):
        for half in range(halves):
            for slow, when in sides(d):
                for l in range(n[1]):
                    fast = grid.nearest(1, l)
                    if d > 0:
                        arrived(slow, fast, half, 1, when)
                        onward(slow, fast, half, 1, 0, when)
                    else:
                        spread(slow, fast, half, 1, 0, when)

    def complete(d):
        for l in range(1, n[1]):
            fast = grid.nearest(1, l)
            for half in range(halves):
                for slow, when in sides(d):
                    arrived(slow, fast, half, 0, when)
                    onward(slow, fast, half, 0, 1, when)

    def work(k, l):
        ready(grid.nearest(0, k), grid.nearest(1, l), k * n[1] + l)

    for half in range(halves):
        for kind in (1, 0):
            if cut[kind]:
                spread(me[0], me[1], half, kind, kind, None)
        if cut[0]:
            spread(me[0], me[1], half, 0, 1, None)
    work(0, 0)
    if cut[1]:
        for half in range(halves):
            for l in range(1, n[1]):
                fast = grid.nearest(1, l)
                arrived(me[0], fast, half, 1, None)
                onward(me[0], fast, half, 1, 1, None)
        settle(0)
    for d in range(1, n[0]):
        if cut[0]:
            for half in range(halves):
                for slow, when in sides(d):
                    arrived(slow, me[1], half, 0, when)
                    onward(slow, me[1], half, 0, 0, when)
                    spread(slow, me[1], half, 0, 1, when)
            complete(d - 1)
        for l in range(1, n[1]):
            work(d - 1, l)
        if cut[1]:
            settle(d)
        work(d, 0)
    if cut[0]:
        complete(n[0] - 1)
    for l in range(1, n[1]):
        work(n[0] - 1, l)


def scatter_slots(n):
    return 1 if n == 2 else n + 1


def scatter_plan(n, quick):
    if n == (4, 2) and not quick:
        return [
            ("make", 3, 1), ("make", 2, 1), ("make", 3, 0), ("make", 1, 1), ("first", 3), ("make", 2, 0),
            ("make", 0, 1), ("later", 3, 0), ("make", 1, 0), ("later", 3, 1), ("first", 2), ("make", 0, 0), ("made",),
            ("later", 2, 0), ("later", 2, 1), ("first", 1), ("later", 1, 0), ("later", 1, 1),
        ]
    far = n[0] - 1
    plan = [("make", k, l) for l in range(n[1] - 1, -1, -1) for k in range(far, -1, -1)] + [("made",)]
    for k in range(far, 0, -1):
        plan += [("first", k), ("later", k, 0), ("later", k, 1)]
    return plan


class Scatter:
    def __init__(self, grid, sender, part, bufs, sems, halves, cut, quick):
        self.grid, self.sender, self.part, self.quick = grid, sender, part, quick
        self.bufs, self.sems, self.halves, self.cut = bufs, sems, halves, cut

    def slot(self, axis, target, from_below):
        if self.grid.n[axis] == 2:
            return 0
        return target + jnp.where(from_below, 1, 0)

    def take(self, kind, stage, axis, other, target, from_below, half, when, slot_index):
        buf, sem = self.bufs[kind][stage], self.sems[kind][stage]
        slot = self.slot(axis, target, from_below)

        def add():
            ref = buf.at[other, slot, half]
            pltpu.make_async_copy(ref, ref, sem.at[other, slot, half]).wait()
            mine = self.part(slot_index, half, kind)
            mine[...] = (mine[...].astype(jnp.float32) + ref[...].astype(jnp.float32)).astype(mine.dtype)

        if when is None:
            add()
        else:
            pl.when(when)(add)

    def incoming(self, axis, target):
        m, n = self.grid.me[axis], self.grid.n[axis]
        if n == 2:
            return None
        up = target > m
        return (up & (m > 0)) | (jnp.logical_not(up) & (m < n - 1))

    def toward(self, kind, stage, axis, other, target, half, slow, fast, when=None):
        grid = self.grid
        m, n = grid.me[axis], grid.n[axis]
        up = target > m
        index = grid.index(slow, fast)
        if n > 2:
            incoming = self.incoming(axis, target)
            self.take(kind, stage, axis, other, target, up, half, incoming if when is None else incoming & when, index)
        buf, sem = self.bufs[kind][stage], self.sems[kind][stage]
        slot = self.slot(axis, target, up)
        spot = 1 - m if n == 2 else jnp.where(up, m + 1, m - 1)
        self.sender.send(
            self.part(index, half, kind), buf.at[other, slot, half], sem.at[other, slot, half],
            grid.device(axis, spot), when)

    def last(self, kind, stage, axis, other, half, slow, fast):
        grid = self.grid
        m, n = grid.me[axis], grid.n[axis]
        index = grid.index(slow, fast)
        if n == 2:
            self.take(kind, stage, axis, other, m, m > 0, half, None, index)
        elif n > 2:
            self.take(kind, stage, axis, other, m, jnp.bool_(True), half, m > 0, index)
            self.take(kind, stage, axis, other, m, jnp.bool_(False), half, m < n - 1, index)

    def run(self, produce, made=lambda: None, late=lambda: None):
        grid, n, me = self.grid, self.grid.n, self.grid.me
        lagging = []

        def chain(k, half, begins):
            slow = grid.nearest(0, k)
            incoming = self.incoming(0, slow)
            if incoming is None:
                if begins:
                    self.last(0, 0, 1, slow, half, slow, me[1])
                    self.toward(0, 1, 0, 0, slow, half, slow, me[1])
                return
            when = jnp.logical_not(incoming) if begins else incoming
            pl.when(when)(lambda: self.last(0, 0, 1, slow, half, slow, me[1]))
            self.toward(0, 1, 0, 0, slow, half, slow, me[1], when)

        def catch_up():
            for step in lagging:
                self.toward(*step)
            lagging.clear()

        def make(k, l):
            slow, fast = grid.nearest(0, k), grid.nearest(1, l)
            produce(slow, fast)
            if self.cut[0] and l > 0:
                for half in range(self.halves):
                    self.toward(0, 0, 1, slow, fast, half, slow, fast)
            catch_up()
            if self.cut[1] and k > 0:
                for half in range(self.halves):
                    lagging.append((1, 0, 0, fast, slow, half, slow, fast))

        for step in scatter_plan(n, self.quick):
            if step[0] == "make":
                make(*step[1:])
            elif step[0] == "made":
                catch_up()
                made()
            elif step[0] == "first" and self.cut[0]:
                for half in range(self.halves):
                    chain(step[1], half, True)
            elif self.cut[0]:
                chain(step[1], step[2], False)
        if self.cut[1]:
            for half in range(self.halves):
                for l in reversed(range(n[1])):
                    fast = grid.nearest(1, l)
                    self.last(1, 0, 0, fast, half, me[0], fast)
                    if l > 0:
                        self.toward(1, 1, 1, 0, fast, half, me[0], fast)
        late()
        if self.cut[0]:
            for half in range(self.halves):
                self.last(0, 0, 1, me[0], half, me[0], me[1])
        for half in range(self.halves):
            if self.cut[1]:
                self.last(1, 1, 1, 0, half, me[0], me[1])
            if self.cut[0]:
                self.last(0, 1, 0, 0, half, me[0], me[1])


def scatter_scratch(sizes, halves, rows, cols, cut):
    bufs, sems = [], []
    for kind, stages in ((0, (1, 0)), (1, (0, 1))):
        for stage, axis in enumerate(stages):
            lead = (sizes[1 - axis] if stage == 0 else 1, scatter_slots(sizes[axis]), halves)
            width = max(cut[kind], 128)
            bufs.append(pltpu.VMEM(lead + (rows // halves, width), jnp.bfloat16))
            sems.append(pltpu.SemaphoreType.DMA(lead))
    return bufs, sems


def scatter_sends(sizes, halves):
    return halves * 2 * (sizes[0] * sizes[1] + sizes[0] + sizes[1])


def lines_of(seq):
    fast = 2 if seq <= 8 else 4
    return (seq // fast, fast)


ATT_TILE = 256


def span(index, size):
    return pl.ds(pl.multiple_of(index * size, size), size)


SCALE = HEAD_DIM ** (-0.5)


def dot_nt(left, right):
    return lax.dot_general(left, right, (((1,), (1,)), ((), ())), preferred_element_type=jnp.float32)


def dot_tn(left, right):
    return lax.dot_general(left, right, (((0,), (0,)), ((), ())), preferred_element_type=jnp.float32)


def rotary_frequencies():
    half_rot = ROT // 2
    frequency = 10000.0 ** (-2.0 * jnp.arange(half_rot, dtype=jnp.float32) / ROT)
    return jnp.tile(frequency, HEAD_DIM // half_rot)[None, :]


def first_rows(lengths, row):
    start, end = jnp.zeros_like(row), jnp.int32(0)
    for example in range(EXB):
        end = end + lengths[example]
        start = jnp.where(row >= end, end, start)
    return start


def rotary_planes(position, frequencies):
    half_rot = ROT // 2
    angles = position.astype(jnp.float32) * frequencies
    cos, sin = jnp.cos(angles), jnp.sin(angles)
    lane = lax.broadcasted_iota(jnp.int32, angles.shape, 1)
    return (
        jnp.where(lane < ROT, cos, 1.0),
        jnp.where((lane >= half_rot) & (lane < ROT), sin, 0.0),
        jnp.where(lane < half_rot, -sin, 0.0),
    )


def turn(vector, cos, from_below, from_above):
    half_rot = ROT // 2
    return (
        vector * cos
        + pltpu.roll(vector, half_rot, 1) * from_below
        + pltpu.roll(vector, HEAD_DIM - half_rot, 1) * from_above
    )


def tile_mask(start_col, query_tile, key_tile):
    shape = (ATT_TILE, ATT_TILE)
    query_ids = query_tile * ATT_TILE + lax.broadcasted_iota(jnp.int32, shape, 0)
    key_ids = key_tile * ATT_TILE + lax.broadcasted_iota(jnp.int32, shape, 1)
    return (key_ids >= start_col) & (key_ids <= query_ids)


def tile_starts(lengths, tile):
    rows = tile * ATT_TILE + lax.broadcasted_iota(jnp.int32, (ATT_TILE, 1), 0)
    return first_rows(lengths, rows), first_rows(lengths, tile * ATT_TILE) // ATT_TILE


def attention_forward(qkv, lengths, heads):
    tiles = BLOCK // ATT_TILE

    def kernel(lengths_ref, qkv_ref, ctx_ref, lse_ref):
        tile = pl.program_id(0)
        start, first = tile_starts(lengths_ref, tile)
        here = span(tile, ATT_TILE)
        queries = [qkv_ref[here, 3 * head * HEAD_DIM : (3 * head + 1) * HEAD_DIM] for head in range(heads)]

        def step(key_tile, carry):
            rows = span(key_tile, ATT_TILE)
            allowed = tile_mask(start, tile, key_tile)
            found = []
            for head in range(heads):
                top, total, acc = carry[head]
                keys = qkv_ref[rows, (3 * head + 1) * HEAD_DIM : (3 * head + 2) * HEAD_DIM]
                values = qkv_ref[rows, (3 * head + 2) * HEAD_DIM : (3 * head + 3) * HEAD_DIM]
                scores = jnp.where(allowed, dot_nt(queries[head], keys) * SCALE, -1e30)
                new_top = jnp.maximum(top, jnp.max(scores, axis=1, keepdims=True))
                shrink = jnp.exp(top - new_top)
                weights = jnp.exp(scores - new_top)
                total = total * shrink + jnp.sum(weights, axis=1, keepdims=True)
                acc = acc * shrink + jnp.dot(
                    weights.astype(jnp.bfloat16), values, preferred_element_type=jnp.float32
                )
                found.append((new_top, total, acc))
            return tuple(found)

        begin = (
            jnp.full((ATT_TILE, 1), -1e30, jnp.float32),
            jnp.zeros((ATT_TILE, 1), jnp.float32),
            jnp.zeros((ATT_TILE, HEAD_DIM), jnp.float32),
        )
        result = lax.fori_loop(first, tile, step, step(tile, (begin,) * heads))
        for head in range(heads):
            top, total, acc = result[head]
            ctx_ref[:, head * HEAD_DIM : (head + 1) * HEAD_DIM] = (acc / total).astype(jnp.bfloat16)
            lse_ref[head] = top + jnp.log(total)

    return pl.pallas_call(
        kernel,
        grid_spec=pltpu.PrefetchScalarGridSpec(
            num_scalar_prefetch=1,
            grid=(tiles,),
            in_specs=[pl.BlockSpec(qkv.shape, lambda i, lengths: (0, 0))],
            out_specs=[
                pl.BlockSpec((ATT_TILE, heads * HEAD_DIM), lambda i, lengths: (i, 0)),
                pl.BlockSpec((heads, ATT_TILE, 1), lambda i, lengths: (0, i, 0)),
            ],
        ),
        out_shape=[
            jax.ShapeDtypeStruct((BLOCK, heads * HEAD_DIM), jnp.bfloat16),
            jax.ShapeDtypeStruct((heads, BLOCK, 1), jnp.float32),
        ],
        compiler_params=pltpu.CompilerParams(vmem_limit_bytes=VMEM_LIMIT),
    )(lengths, qkv)


def attention_backward(qkv, lengths, heads, ctx, lse, grad_ctx, planes):
    tiles = BLOCK // ATT_TILE

    def kernel(
        lengths_ref, qkv_ref, ctx_ref, lse_ref, do_ref, cos_ref, below_ref, above_ref, out_ref, sums_ref, dk_ref,
        dv_ref,
    ):
        tile = pl.program_id(0)

        @pl.when(tile == 0)
        def _():
            dk_ref[...] = jnp.zeros_like(dk_ref)
            dv_ref[...] = jnp.zeros_like(dv_ref)

        start, first = tile_starts(lengths_ref, tile)
        here = span(tile, ATT_TILE)
        fixed = []
        for head in range(heads):
            lanes = slice(head * HEAD_DIM, (head + 1) * HEAD_DIM)
            grads = do_ref[:, lanes]
            inner = jnp.sum(
                grads.astype(jnp.float32) * ctx_ref[:, lanes].astype(jnp.float32), axis=1, keepdims=True
            )
            queries = qkv_ref[here, 3 * head * HEAD_DIM : (3 * head + 1) * HEAD_DIM]
            fixed.append((queries, grads, inner, lse_ref[head]))

        def step(key_tile, carry):
            rows = span(key_tile, ATT_TILE)
            allowed = tile_mask(start, tile, key_tile)
            found = []
            for head in range(heads):
                queries, grads, inner, lse_rows = fixed[head]
                lanes = slice(head * HEAD_DIM, (head + 1) * HEAD_DIM)
                keys = qkv_ref[rows, (3 * head + 1) * HEAD_DIM : (3 * head + 2) * HEAD_DIM]
                values = qkv_ref[rows, (3 * head + 2) * HEAD_DIM : (3 * head + 3) * HEAD_DIM]
                scores = dot_nt(queries, keys) * SCALE
                probs = jnp.where(allowed, jnp.exp(scores - lse_rows), 0.0)
                grad_scores = (probs * (dot_nt(grads, values) - inner)).astype(jnp.bfloat16)
                dv_ref[rows, lanes] += dot_tn(probs.astype(jnp.bfloat16), grads)
                dk_ref[rows, lanes] += dot_tn(grad_scores, queries)
                found.append(carry[head] + jnp.dot(grad_scores, keys, preferred_element_type=jnp.float32))
            return tuple(found)

        none = jnp.zeros((ATT_TILE, HEAD_DIM), jnp.float32)
        result = lax.fori_loop(first, tile + 1, step, (none,) * heads)
        for head in range(heads):
            out_ref[here, 3 * head * HEAD_DIM : (3 * head + 1) * HEAD_DIM] = turn(
                result[head] * SCALE, cos_ref[here, :], -below_ref[here, :], -above_ref[here, :]
            ).astype(jnp.bfloat16)

        @pl.when(tile == tiles - 1)
        def _():
            def finish(index, sums):
                rows = span(index, ATT_TILE)
                for head in range(heads):
                    lanes = slice(head * HEAD_DIM, (head + 1) * HEAD_DIM)
                    out_ref[rows, (3 * head + 1) * HEAD_DIM : (3 * head + 2) * HEAD_DIM] = turn(
                        dk_ref[rows, lanes] * SCALE, cos_ref[rows, :], -below_ref[rows, :], -above_ref[rows, :]
                    ).astype(jnp.bfloat16)
                    out_ref[rows, (3 * head + 2) * HEAD_DIM : (3 * head + 3) * HEAD_DIM] = dv_ref[rows, lanes].astype(
                        jnp.bfloat16
                    )
                return sums + jnp.sum(out_ref[rows, :].astype(jnp.float32), axis=0, keepdims=True)

            sums_ref[...] = lax.fori_loop(
                0, tiles, finish, jnp.zeros((1, 3 * heads * HEAD_DIM), jnp.float32)
            )

    def whole(shape):
        return pl.BlockSpec(shape, lambda i, lengths: (0,) * len(shape))

    return pl.pallas_call(
        kernel,
        grid_spec=pltpu.PrefetchScalarGridSpec(
            num_scalar_prefetch=1,
            grid=(tiles,),
            in_specs=[
                whole(qkv.shape),
                pl.BlockSpec((ATT_TILE, heads * HEAD_DIM), lambda i, lengths: (i, 0)),
                pl.BlockSpec((heads, ATT_TILE, 1), lambda i, lengths: (0, i, 0)),
                pl.BlockSpec((ATT_TILE, heads * HEAD_DIM), lambda i, lengths: (i, 0)),
                whole((BLOCK, HEAD_DIM)),
                whole((BLOCK, HEAD_DIM)),
                whole((BLOCK, HEAD_DIM)),
            ],
            out_specs=[whole(qkv.shape), whole((1, qkv.shape[1]))],
            scratch_shapes=[
                pltpu.VMEM((BLOCK, heads * HEAD_DIM), jnp.float32),
                pltpu.VMEM((BLOCK, heads * HEAD_DIM), jnp.float32),
            ],
        ),
        out_shape=[
            jax.ShapeDtypeStruct(qkv.shape, jnp.bfloat16),
            jax.ShapeDtypeStruct((1, qkv.shape[1]), jnp.float32),
        ],
        compiler_params=pltpu.CompilerParams(vmem_limit_bytes=VMEM_LIMIT),
    )(lengths, qkv, ctx, lse, grad_ctx, *planes)


def gather_cut(sizes):
    return (1792, 256) if sizes == (4, 2) else (D // 2, D // 2)


def scatter_cut(sizes):
    return (1664, 384) if sizes == (4, 2) else (D // 2, D // 2)


def columns_of(cut, kind):
    return pl.ds(0, cut[0]) if kind == 0 else pl.ds(cut[0], cut[1])


def tile_of(width):
    return 512 if width % 512 == 0 else 256 if width % 256 == 0 else 128


ANY = pl.BlockSpec(memory_space=pl.ANY)
VMEM = pl.BlockSpec(memory_space=pltpu.VMEM)
SMEM = pl.BlockSpec(memory_space=pltpu.SMEM)


def row_kernel(kernel, collective, out_shape, in_specs, out_specs, scratch, cost, before=()):
    def body(*refs):
        kernel(*refs[len(before):])

    def call(*args):
        return pl.pallas_call(
            body,
            out_shape=out_shape,
            in_specs=[ANY] * len(before) + in_specs,
            out_specs=out_specs,
            scratch_shapes=scratch,
            cost_estimate=pl.CostEstimate(flops=cost, bytes_accessed=2**28 if cost > 1 else 1, transcendentals=0),
            compiler_params=pltpu.CompilerParams(
                collective_id=collective, has_side_effects=True, vmem_limit_bytes=VMEM_LIMIT
            ),
        )(*before, *args)

    return call


def gather_scratch(sizes, rows):
    shards = sizes[0] * sizes[1]
    return [
        pltpu.VMEM((shards, rows, D), jnp.bfloat16),
        pltpu.SemaphoreType.DMA((gather_sends(sizes, HALVES),)),
        pltpu.SemaphoreType.DMA((2, HALVES, shards)),
    ]


def run_gather(grid, sizes, rows, full, send_sems, recv_sems, ready):
    cut = gather_cut(sizes)
    step = rows // HALVES
    sender = Sender(send_sems)

    def piece(slot, half, kind):
        return full.at[slot, pl.ds(half * step, step), columns_of(cut, kind)]

    gather_rounds(grid, sender, piece, recv_sems, HALVES, cut, ready)
    sender.finish()


def sum_scratch(sizes, rows):
    shards = sizes[0] * sizes[1]
    bufs, sems = scatter_scratch(sizes, HALVES, rows, D, scatter_cut(sizes))
    return (
        [pltpu.VMEM((shards, rows, D), jnp.bfloat16)]
        + bufs
        + sems
        + [pltpu.SemaphoreType.DMA((scatter_sends(sizes, HALVES),))]
    )


def run_scatter(grid, sizes, rows, scratch, produce, *hooks, quick=False):
    cut = scatter_cut(sizes)
    step = rows // HALVES
    parts, b0, b1, b2, b3, s0, s1, s2, s3, send_sems = scratch
    sender = Sender(send_sems)

    def part(slot, half, kind):
        return parts.at[slot, pl.ds(half * step, step), columns_of(cut, kind)]

    scatter = Scatter(
        grid, sender, part, ((b0, b1), (b2, b3)), ((s0, s1), (s2, s3)), HALVES, cut, quick
    )
    scatter.run(produce, *hooks)
    sender.finish()


def production_order(grid, quick=False):
    return [
        grid.index(grid.nearest(0, k), grid.nearest(1, l))
        for action, k, l in [step for step in scatter_plan(grid.n, quick) if step[0] == "make"]
    ]


ROW_TILE = 64


def tile_stats(values):
    centered = values - jnp.mean(values, axis=1, keepdims=True)
    inverse = lax.rsqrt(jnp.mean(centered * centered, axis=1, keepdims=True) + EPSILON)
    return centered, inverse


def open_rows(own, sizes, collective, norms, qkv_flat, qkv_bias, up_weight, up_bias, lengths):
    rows = own.shape[0]
    shards = sizes[0] * sizes[1]
    width, hidden = qkv_flat.shape[1], up_weight.shape[1]
    heads = width // (3 * HEAD_DIM)

    def kernel(
        own_ref, norms_ref, qkvw_any, qkvb_ref, upw_any, upb_ref, lengths_ref, freq_ref,
        plain_any, one_any, two_any, qkv_any, act_any, slope_any, cos_ref, below_ref, above_ref,
        full, send_sems, recv_sems, qkvw, upw, load_sems, plain, one, two, qkv, act, slope, out_sems,
    ):
        grid = Grid2(sizes)
        loads = [
            pltpu.make_async_copy(qkvw_any, qkvw, load_sems.at[0]),
            pltpu.make_async_copy(upw_any, upw, load_sems.at[1]),
        ]
        for copy in loads:
            copy.start()
        full[grid.index(*grid.me)] = own_ref[...]
        grid.barrier()
        open_copies = []

        def outs(place, slot):
            pairs = ((plain, plain_any), (one, one_any), (two, two_any), (qkv, qkv_any), (act, act_any), (slope, slope_any))
            return [
                pltpu.make_async_copy(here.at[slot], there.at[place], out_sems.at[slot, i])
                for i, (here, there) in enumerate(pairs)
            ]

        def ready(slow, fast, order):
            place = grid.index(slow, fast)
            slot = order % 2
            if order == 0:
                for copy in loads:
                    copy.wait()
            if order >= 2:
                for copy in open_copies.pop(0):
                    copy.wait()

            def norm_tile(index, _):
                here = span(index, ROW_TILE)
                centered, inverse = tile_stats(full[place, here].astype(jnp.float32))
                normed = centered * inverse
                plain[slot, here] = normed.astype(jnp.bfloat16)
                one[slot, here] = (normed * norms_ref[0:1] + norms_ref[1:2]).astype(jnp.bfloat16)
                two[slot, here] = (normed * norms_ref[2:3] + norms_ref[3:4]).astype(jnp.bfloat16)
                return _

            lax.fori_loop(0, rows // ROW_TILE, norm_tile, 0)
            places = pl.ds(pl.multiple_of(place * rows, rows), rows)
            row = place * rows + lax.broadcasted_iota(jnp.int32, (rows, 1), 0)
            cos, below, above = rotary_planes(row - first_rows(lengths_ref, row), freq_ref[...])
            cos_ref[places, :], below_ref[places, :], above_ref[places, :] = cos, below, above
            whole = jnp.dot(one[slot], qkvw[...], preferred_element_type=jnp.float32) + qkvb_ref[...]
            for head in range(heads):
                first = head * 3 * HEAD_DIM
                found = whole[:, first : first + 3 * HEAD_DIM]
                qkv[slot, :, first : first + HEAD_DIM] = turn(
                    found[:, :HEAD_DIM], cos, below, above
                ).astype(jnp.bfloat16)
                qkv[slot, :, first + HEAD_DIM : first + 2 * HEAD_DIM] = turn(
                    found[:, HEAD_DIM : 2 * HEAD_DIM], cos, below, above
                ).astype(jnp.bfloat16)
                qkv[slot, :, first + 2 * HEAD_DIM : first + 3 * HEAD_DIM] = found[
                    :, 2 * HEAD_DIM :
                ].astype(jnp.bfloat16)
            tile = tile_of(hidden)

            def up_tile(index, _):
                here = span(index, tile)
                pre = jnp.dot(two[slot], upw[:, here], preferred_element_type=jnp.float32) + upb_ref[:, here]
                share = 0.5 * (1.0 + lax.erf(pre * 0.7071067811865476))
                act[slot, :, here] = (pre * share).astype(jnp.bfloat16)
                slope[slot, :, here] = (
                    share + pre * (jnp.exp(-0.5 * pre * pre) * 0.3989422804014327)
                ).astype(jnp.bfloat16)
                return _

            lax.fori_loop(0, hidden // tile, up_tile, 0)
            copies = outs(place, slot)
            for copy in copies:
                copy.start()
            open_copies.append(copies)

        run_gather(grid, sizes, rows, full, send_sems, recv_sems, ready)
        for copies in open_copies:
            for copy in copies:
                copy.wait()

    def out(columns):
        return jax.ShapeDtypeStruct((shards, rows, columns), jnp.bfloat16)

    def staged(columns):
        return pltpu.VMEM((2, rows, columns), jnp.bfloat16)

    return row_kernel(
        kernel, collective,
        [out(D), out(D), out(D), out(width), out(hidden), out(hidden)]
        + [jax.ShapeDtypeStruct((shards * rows, HEAD_DIM), jnp.float32)] * 3,
        [VMEM, VMEM, ANY, VMEM, ANY, VMEM, SMEM, VMEM],
        [ANY] * 6 + [VMEM] * 3,
        gather_scratch(sizes, rows)
        + [
            pltpu.VMEM(qkv_flat.shape, jnp.bfloat16),
            pltpu.VMEM(up_weight.shape, jnp.bfloat16),
            pltpu.SemaphoreType.DMA((2,)),
            staged(D), staged(D), staged(D), staged(width), staged(hidden), staged(hidden),
            pltpu.SemaphoreType.DMA((2, 6)),
        ],
        2 * BLOCK * D * (width + hidden),
    )(own, norms, qkv_flat, qkv_bias, up_weight, up_bias, lengths, rotary_frequencies())


def branch_rows(own, ctx, act, out_flat, down_weight, norms, sizes, collective):
    rows = own.shape[0]
    shards = sizes[0] * sizes[1]
    inner, hidden = out_flat.shape[0], down_weight.shape[0]

    def kernel(
        own_ref, ctx_any, act_any, outw_any, downw_any, norms_ref, out_ref, final_ref, normed_ref, inverse_ref,
        ctx, act, outw, downw, load_sems, *scratch,
    ):
        grid = Grid2(sizes)
        parts = scratch[0]
        weights = [
            pltpu.make_async_copy(outw_any, outw, load_sems.at[0, 0]),
            pltpu.make_async_copy(downw_any, downw, load_sems.at[0, 1]),
        ]
        order = production_order(grid)
        loads = [
            [
                pltpu.make_async_copy(ctx_any.at[place], ctx.at[place], load_sems.at[1 + i, 0]),
                pltpu.make_async_copy(act_any.at[place], act.at[place], load_sems.at[1 + i, 1]),
            ]
            for i, place in enumerate(order)
        ]
        for copy in loads[0] + weights:
            copy.start()
        for copies in loads[1:]:
            for copy in copies:
                copy.start()
        grid.barrier()
        for copy in weights:
            copy.wait()

        def produce(slow, fast):
            place = grid.index(slow, fast)
            for copy in loads.pop(0):
                copy.wait()

            def columns(index, _):
                here = span(index, 512)
                parts[place, :, here] = (
                    jnp.dot(ctx[place], outw[:, here], preferred_element_type=jnp.float32)
                    + jnp.dot(act[place], downw[:, here], preferred_element_type=jnp.float32)
                ).astype(jnp.bfloat16)
                return _

            lax.fori_loop(0, D // 512, columns, 0)

        run_scatter(grid, sizes, rows, scratch, produce)
        mine = grid.index(*grid.me)

        def norm_tile(index, _):
            here = span(index, ROW_TILE)
            stream = own_ref[here].astype(jnp.float32) + parts[mine, here].astype(jnp.float32) + norms_ref[2:3]
            out_ref[here] = stream.astype(jnp.bfloat16)
            centered, inverse = tile_stats(stream)
            normed = centered * inverse
            final_ref[here] = (normed * norms_ref[0:1] + norms_ref[1:2]).astype(jnp.bfloat16)
            normed_ref[here] = normed
            inverse_ref[here] = inverse
            return _

        lax.fori_loop(0, rows // ROW_TILE, norm_tile, 0)

    return row_kernel(
        kernel, collective,
        [
            jax.ShapeDtypeStruct((rows, D), jnp.bfloat16),
            jax.ShapeDtypeStruct((rows, D), jnp.bfloat16),
            jax.ShapeDtypeStruct((rows, D), jnp.float32),
            jax.ShapeDtypeStruct((rows, 1), jnp.float32),
        ],
        [VMEM, ANY, ANY, ANY, ANY, VMEM],
        [VMEM] * 4,
        [
            pltpu.VMEM(ctx.shape, jnp.bfloat16),
            pltpu.VMEM(act.shape, jnp.bfloat16),
            pltpu.VMEM(out_flat.shape, jnp.bfloat16),
            pltpu.VMEM(down_weight.shape, jnp.bfloat16),
            pltpu.SemaphoreType.DMA((1 + shards, 2)),
        ]
        + sum_scratch(sizes, rows),
        2 * BLOCK * D * (inner + hidden),
    )(own, ctx, act, out_flat, down_weight, norms)


def logit_rows(final, head_weight, targets_col, sizes, collective):
    rows = final.shape[0]
    shards = sizes[0] * sizes[1]
    vocab = head_weight.shape[1]

    def kernel(
        own_ref, headw_any, target_ref, final_any, weights_any, stats_ref,
        full, send_sems, recv_sems, headw, load_sem, logits, weights, out_sems, row_sems,
    ):
        grid = Grid2(sizes)
        load = pltpu.make_async_copy(headw_any, headw, load_sem)
        load.start()
        full[grid.index(*grid.me)] = own_ref[...]
        grid.barrier()
        base = lax.axis_index("seq") * vocab
        open_copies, raw_copies = [], []

        def ready(slow, fast, order):
            place = grid.index(slow, fast)
            slot = order % 2
            if order == 0:
                load.wait()
            if order >= 2:
                open_copies.pop(0).wait()
            places = pl.ds(pl.multiple_of(place * rows, rows), rows)
            target = target_ref[places, :] - base

            def fold(values, join):
                total = values[:, :128]
                for first in range(128, values.shape[1], 128):
                    total = join(total, values[:, first : first + 128])
                return total

            def logit_tile(start, size, carry):
                top, pick = carry
                here = pl.ds(start, size)
                found = jnp.dot(full[place], headw[:, here], preferred_element_type=jnp.float32)
                logits[:, here] = found
                ids = start + lax.broadcasted_iota(jnp.int32, (rows, size), 1)
                top = jnp.maximum(top, fold(found, jnp.maximum))
                pick = pick + fold(jnp.where(ids == target, found, 0.0), jnp.add)
                return (top, pick)

            def tiled(step, carry):
                count = vocab // 512
                carry = lax.fori_loop(
                    0, count, lambda i, c: step(pl.multiple_of(i * 512, 512), 512, c), carry
                )
                if vocab % 512:
                    carry = step(count * 512, vocab % 512, carry)
                return carry

            top, pick = tiled(
                logit_tile,
                (jnp.full((rows, 128), -jnp.inf, jnp.float32), jnp.zeros((rows, 128), jnp.float32)),
            )
            top = jnp.max(top, axis=1, keepdims=True)
            pick = jnp.sum(pick, axis=1, keepdims=True)

            def weight_tile(start, size, total):
                here = pl.ds(start, size)
                found = jnp.exp(logits[:, here] - top)
                weights[slot, :, here] = found.astype(jnp.bfloat16)
                return total + fold(found, jnp.add)

            total = tiled(weight_tile, jnp.zeros((rows, 128), jnp.float32))
            total = jnp.sum(total, axis=1, keepdims=True)
            lane = lax.broadcasted_iota(jnp.int32, (rows, 128), 1)
            found = jnp.where(lane == 0, top, jnp.where(lane == 1, total, pick))
            stats_ref[:, places] = found.T[0:8]
            copy = pltpu.make_async_copy(weights.at[slot], weights_any.at[place], out_sems.at[slot])
            copy.start()
            open_copies.append(copy)
            raw = pltpu.make_async_copy(full.at[place], final_any.at[place], row_sems.at[order])
            raw.start()
            raw_copies.append(raw)

        run_gather(grid, sizes, rows, full, send_sems, recv_sems, ready)
        for copy in open_copies + raw_copies:
            copy.wait()

    return row_kernel(
        kernel, collective,
        [
            jax.ShapeDtypeStruct((shards, rows, D), jnp.bfloat16),
            jax.ShapeDtypeStruct((shards, rows, vocab), jnp.bfloat16),
            jax.ShapeDtypeStruct((8, shards * rows), jnp.float32),
        ],
        [VMEM, ANY, VMEM],
        [ANY, ANY, VMEM],
        gather_scratch(sizes, rows)
        + [
            pltpu.VMEM(head_weight.shape, jnp.bfloat16),
            pltpu.SemaphoreType.DMA,
            pltpu.VMEM((rows, vocab), jnp.float32),
            pltpu.VMEM((2, rows, vocab), jnp.bfloat16),
            pltpu.SemaphoreType.DMA((2,)),
            pltpu.SemaphoreType.DMA((shards,)),
        ],
        2 * BLOCK * D * vocab,
    )(final, head_weight, targets_col)


def final_grad_rows(grad_logits, head_weight, normed, inverse, gain, sizes, collective, before):
    shards, rows, vocab = grad_logits.shape

    def kernel(
        grads_any, headw_any, normed_ref, inverse_ref, gain_ref, stream_ref, down_ref, sums_ref,
        headw, grads, load_sems, *scratch,
    ):
        grid = Grid2(sizes)
        parts = scratch[0]
        order = production_order(grid)
        loads = [
            pltpu.make_async_copy(grads_any.at[place], grads.at[i % 2], load_sems.at[i])
            for i, place in enumerate(order)
        ]
        tile = 512
        weights = [
            pltpu.make_async_copy(
                headw_any.at[pl.ds(i * tile, tile)], headw.at[pl.ds(i * tile, tile)], load_sems.at[1 + shards + i]
            )
            for i in range(D // tile)
        ]
        loads[0].start()
        for copy in weights:
            copy.start()
        grid.barrier()
        count = [0]

        def produce(slow, fast):
            place = grid.index(slow, fast)
            i = count[0]
            count[0] += 1
            if i + 1 < shards:
                loads[i + 1].start()
            loads[i].wait()

            def columns(index, _):
                here = span(index, tile)
                parts[place, :, here] = dot_nt(grads[i % 2], headw[here, :]).astype(jnp.bfloat16)
                return _

            if i == 0:
                for index, copy in enumerate(weights):
                    copy.wait()
                    columns(index, 0)
            else:
                lax.fori_loop(0, D // tile, columns, 0)

        run_scatter(grid, sizes, rows, scratch, produce)
        mine = grid.index(*grid.me)
        sums_ref[...] = jnp.zeros_like(sums_ref)

        def norm_tile(index, _):
            here = span(index, ROW_TILE)
            grad = parts[mine, here].astype(jnp.float32)
            norm = normed_ref[here]
            scaled = grad * gain_ref[...]
            stream = inverse_ref[here] * (
                scaled
                - jnp.mean(scaled, axis=1, keepdims=True)
                - norm * jnp.mean(scaled * norm, axis=1, keepdims=True)
            )
            stream_ref[here] = stream
            down_ref[here] = stream.astype(jnp.bfloat16)
            sums_ref[0:1] += jnp.sum(grad * norm, axis=0, keepdims=True)
            sums_ref[1:2] += jnp.sum(grad, axis=0, keepdims=True)
            sums_ref[2:3] += jnp.sum(stream, axis=0, keepdims=True)
            return _

        lax.fori_loop(0, rows // ROW_TILE, norm_tile, 0)

    return row_kernel(
        kernel, collective,
        [
            jax.ShapeDtypeStruct((rows, D), jnp.float32),
            jax.ShapeDtypeStruct((rows, D), jnp.bfloat16),
            jax.ShapeDtypeStruct((8, D), jnp.float32),
        ],
        [ANY, ANY, VMEM, VMEM, VMEM],
        [VMEM] * 3,
        [
            pltpu.VMEM(head_weight.shape, jnp.bfloat16),
            pltpu.VMEM((2, rows, vocab), jnp.bfloat16),
            pltpu.SemaphoreType.DMA((1 + shards + D // 512,)),
        ]
        + sum_scratch(sizes, rows),
        2 * BLOCK * D * vocab,
        before,
    )(grad_logits, head_weight, normed, inverse, gain)


def branch_grad_rows(own, out_flat, down_weight, slope, ctx, act, second, sizes, collective, before):
    rows = own.shape[0]
    shards = sizes[0] * sizes[1]
    inner, hidden = out_flat.shape[0], down_weight.shape[0]
    half_width = D // 2

    def kernel(
        own_ref, outw_any, downw_any, slope_any, ctx_any, act_any, second_any,
        grad_ctx_any, grad_up_any, sums_ref, stream_away, stream_mine, up_away, up_mine,
        full, send_sems, recv_sems, outw, downw, load_sems, slope, slope_sem, grad_ctx, grad_up, out_sems,
        ctx, act, second, row_sems, out_total, down_total, up_total, part_sems,
    ):
        grid = Grid2(sizes)
        core = lax.rem(lax.axis_index("dp"), 2)
        loads = [
            pltpu.make_async_copy(outw_any, outw, load_sems.at[0]),
            pltpu.make_async_copy(downw_any, downw, load_sems.at[1]),
        ]
        for copy in loads:
            copy.start()
        slopes = pltpu.make_async_copy(slope_any, slope, slope_sem)
        slopes.start()
        order_of = [
            grid.index(grid.nearest(0, k), grid.nearest(1, l)) for k in range(sizes[0]) for l in range(sizes[1])
        ]
        row_loads = [
            [
                pltpu.make_async_copy(there.at[place], here.at[i % 2], row_sems.at[i % 2, j])
                for j, (there, here) in enumerate(((ctx_any, ctx), (act_any, act), (second_any, second)))
            ]
            for i, place in enumerate(order_of)
        ]
        for copy in row_loads[0]:
            copy.start()
        full[grid.index(*grid.me)] = own_ref[...]
        sums_ref[...] = jnp.zeros_like(sums_ref)
        grid.barrier()
        open_copies = []

        def ready(slow, fast, order):
            place = grid.index(slow, fast)
            slot = order % 2
            if order == 0:
                for copy in loads + [slopes]:
                    copy.wait()
            if order >= 2:
                for copy in open_copies.pop(0):
                    copy.wait()
            if order + 1 < shards:
                for copy in row_loads[order + 1]:
                    copy.start()
            grad_ctx[slot] = dot_nt(full[place], outw[...]).astype(jnp.bfloat16)
            tile = tile_of(hidden)

            def up_tile(index, _):
                here = span(index, tile)
                found = dot_nt(full[place], downw[here, :]) * slope[place, :, here].astype(jnp.float32)
                rounded = found.astype(jnp.bfloat16)
                grad_up[slot, :, here] = rounded
                sums_ref[0:1, here] += jnp.sum(rounded.astype(jnp.float32), axis=0, keepdims=True)
                return _

            lax.fori_loop(0, hidden // tile, up_tile, 0)
            copies = [
                pltpu.make_async_copy(grad_ctx.at[slot], grad_ctx_any.at[place], out_sems.at[slot, 0]),
                pltpu.make_async_copy(grad_up.at[slot], grad_up_any.at[place], out_sems.at[slot, 1]),
            ]
            for copy in copies:
                copy.start()
            open_copies.append(copies)
            for copy in row_loads[order]:
                copy.wait()

            def add(total, here, found):
                if order == 0:
                    total[:, here] = found
                else:
                    total[:, here] += found

            def stream_tile(index, _):
                here = span(index, 512)
                grads = full[place, :, here]
                add(out_total, here, dot_tn(ctx[slot], grads))
                add(down_total, here, dot_tn(act[slot], grads))
                return _

            lax.fori_loop(0, D // 512, stream_tile, 0)

            def up_grad_tile(index, _):
                here = span(index, tile)
                add(up_total, here, dot_tn(second[slot], grad_up[slot, :, here]))
                return _

            lax.fori_loop(0, hidden // tile, up_grad_tile, 0)

        run_gather(grid, sizes, rows, full, send_sems, recv_sems, ready)
        for copies in open_copies:
            for copy in copies:
                copy.wait()
        stores = []

        def store(total, there, row, column, height, width):
            index = len(stores)
            if index < 2 * shards:
                here = full.at[index // 2, :, pl.ds((index % 2) * half_width, width)]
            else:
                here = slope.at[index - 2 * shards, :, pl.ds(0, width)]
            here[...] = total[
                pl.ds(pl.multiple_of(row, rows), rows), pl.ds(pl.multiple_of(column, 128), width)
            ].astype(jnp.bfloat16)
            copy = pltpu.make_async_copy(here, there.at[pl.ds(height, rows)], part_sems.at[index])
            copy.start()
            stores.append(copy)

        for which, wide in ((1 - core, (stream_away, up_away)), (core, (stream_mine, up_mine))):
            for total, begin, count in ((out_total, 0, inner), (down_total, inner, hidden)):
                for height in range(0, count, rows):
                    store(total, wide[0], height, which * half_width, begin + height, half_width)
            for height in range(0, half_width, rows):
                store(up_total, wide[1], which * half_width + height, 0, height, hidden)
        for copy in stores:
            copy.wait()

    def out(columns):
        return jax.ShapeDtypeStruct((shards, rows, columns), jnp.bfloat16)

    parts = [
        jax.ShapeDtypeStruct(shape, jnp.bfloat16)
        for shape in ((inner + hidden, half_width), (half_width, hidden))
        for _ in range(2)
    ]
    stores = 2 * (inner // rows + hidden // rows + half_width // rows)
    return row_kernel(
        kernel, collective,
        [out(inner), out(hidden), jax.ShapeDtypeStruct((8, hidden), jnp.float32)] + parts,
        [VMEM] + [ANY] * 6,
        [ANY, ANY, VMEM] + [ANY] * 4,
        gather_scratch(sizes, rows)
        + [
            pltpu.VMEM(out_flat.shape, jnp.bfloat16),
            pltpu.VMEM(down_weight.shape, jnp.bfloat16),
            pltpu.SemaphoreType.DMA((2,)),
            pltpu.VMEM((shards, rows, hidden), jnp.bfloat16),
            pltpu.SemaphoreType.DMA,
            pltpu.VMEM((2, rows, inner), jnp.bfloat16),
            pltpu.VMEM((2, rows, hidden), jnp.bfloat16),
            pltpu.SemaphoreType.DMA((2, 2)),
            pltpu.VMEM((2, rows, inner), jnp.bfloat16),
            pltpu.VMEM((2, rows, hidden), jnp.bfloat16),
            pltpu.VMEM((2, rows, D), jnp.bfloat16),
            pltpu.SemaphoreType.DMA((2, 3)),
            pltpu.VMEM((inner, D), jnp.float32),
            pltpu.VMEM((hidden, D), jnp.float32),
            pltpu.VMEM((D, hidden), jnp.float32),
            pltpu.SemaphoreType.DMA((stores,)),
        ],
        4 * BLOCK * D * (inner + hidden) + 2 * BLOCK * D * hidden,
        before,
    )(own, out_flat, down_weight, slope, ctx, act, second)


class SmallSum:
    def __init__(self, shards, sums, total, scratch):
        self.shards, self.sums, self.total = shards, sums, total
        self.came, self.spread_send, self.spread_recv, self.back_send, self.back_recv = scratch
        self.here = lax.axis_index("seq")
        self.width = D // shards
        self.others = [(step, lax.rem(self.here + step, shards)) for step in range(1, shards)]

    @staticmethod
    def scratch(shards):
        dma = pltpu.SemaphoreType.DMA
        return [pltpu.VMEM((shards, 8, D // shards), jnp.float32)] + [dma((shards,))] * 4

    def barrier(self):
        sem = pltpu.get_barrier_semaphore()
        for _, place in self.others:
            pl.semaphore_signal(sem, inc=1, device_id={"seq": place}, device_id_type=MESH)
        pl.semaphore_wait(sem, self.shards - 1)

    def copy(self, place, src, dst, send, recv):
        return pltpu.make_async_remote_copy(
            src_ref=src, dst_ref=dst, send_sem=send, recv_sem=recv, device_id={"seq": place}, device_id_type=MESH
        )

    def columns(self, place):
        return pl.ds(pl.multiple_of(place * self.width, self.width), self.width)

    def spread(self):
        self.first = [
            self.copy(
                place, self.sums.at[:, self.columns(place)], self.came.at[step], self.spread_send.at[step],
                self.spread_recv.at[step],
            )
            for step, place in self.others
        ]
        for copy in self.first:
            copy.start()

    def collect(self):
        here = self.columns(self.here)
        total = self.sums[:, here]
        for (step, _), copy in zip(self.others, self.first):
            copy.wait_recv()
            total = total + self.came[step]
        self.total[:, here] = total
        self.second = [
            self.copy(
                place, self.total.at[:, here], self.total.at[:, here], self.back_send.at[step], self.back_recv.at[step]
            )
            for step, place in self.others
        ]
        for copy in self.second:
            copy.start()

    def finish(self):
        for step, _ in self.others:
            source = lax.rem(self.here + self.shards - step, self.shards)
            there = self.total.at[:, self.columns(source)]
            self.copy(source, there, there, self.back_send.at[step], self.back_recv.at[step]).wait_recv()
        for copy in self.first + self.second:
            copy.wait_send()


def score_rows(stats, lengths, labels, reference, sizes, replicas, collective):
    shards = sizes[0] * sizes[1]
    width = BLOCK // shards

    def kernel(
        stats_ref, lengths_ref, labels_ref, reference_ref, coef_ref, losses_ref,
        came, full, ratio, ratios, spread_send, spread_recv, back_send, back_recv, cross_send, cross_recv,
    ):
        seq, dp = lax.axis_index("seq"), lax.axis_index("dp")
        peers = {
            "seq": [(step, lax.rem(seq + step, shards)) for step in range(1, shards)],
            "dp": [(step, lax.rem(dp + step, replicas)) for step in range(1, replicas)],
        }
        barrier = pltpu.get_barrier_semaphore()
        for axis in peers:
            for _, place in peers[axis]:
                pl.semaphore_signal(barrier, inc=1, device_id={axis: place}, device_id_type=MESH)
        pl.semaphore_wait(barrier, shards + replicas - 2)

        def columns(place):
            return pl.ds(pl.multiple_of(place * width, width), width)

        def copy(axis, place, src, dst, send, recv):
            return pltpu.make_async_remote_copy(
                src_ref=src, dst_ref=dst, send_sem=send, recv_sem=recv, device_id={axis: place}, device_id_type=MESH
            )

        sent = [
            copy("seq", place, stats_ref.at[:, columns(place)], came.at[step], spread_send.at[step], spread_recv.at[step])
            for step, place in peers["seq"]
        ]
        for one in sent:
            one.start()
        mine = stats_ref[:, columns(seq)]
        top, total, pick = mine[0:1], mine[1:2], mine[2:3]
        for (step, _), one in zip(peers["seq"], sent):
            one.wait_recv()
            other = came[step]
            joint = jnp.maximum(top, other[0:1])
            total = total * jnp.exp(top - joint) + other[1:2] * jnp.exp(other[0:1] - joint)
            pick = pick + other[2:3]
            top = joint
        log_total = top + jnp.log(total)
        here = columns(seq)
        full[0:1, here] = log_total
        full[1:2, here] = pick - log_total
        back = [
            copy("seq", place, full.at[:, here], full.at[:, here], back_send.at[step], back_recv.at[step])
            for step, place in peers["seq"]
        ]
        for one in back:
            one.start()
        for step, _ in peers["seq"]:
            source = lax.rem(seq + shards - step, shards)
            there = full.at[:, columns(source)]
            copy("seq", source, there, there, back_send.at[step], back_recv.at[step]).wait_recv()
        example = lax.broadcasted_iota(jnp.int32, (EXB, 1), 0)
        start, end = jnp.zeros_like(example), jnp.zeros_like(example)
        sign, reference = jnp.zeros((EXB, 1), jnp.float32), jnp.zeros((EXB, 1), jnp.float32)
        reached = jnp.int32(0)
        for index in range(EXB):
            start = jnp.where(example == index, reached, start)
            reached = reached + lengths_ref[index]
            end = jnp.where(example == index, reached, end)
            sign = jnp.where(example == index, (2 * labels_ref[index] - 1).astype(jnp.float32), sign)
            reference = jnp.where(example == index, reference_ref[index], reference)
        counts = (end - start).astype(jnp.float32)
        row = lax.broadcasted_iota(jnp.int32, (EXB, BLOCK), 1)
        member = (row >= start) & (row < end)
        mean = jnp.sum(jnp.where(member, full[1:2, :], 0.0), axis=1, keepdims=True) / counts
        log_ratio = mean - reference
        ratio[...] = jnp.broadcast_to(jnp.sum(log_ratio, axis=0, keepdims=True), ratio.shape)
        crossed = [
            copy("dp", place, ratio, ratios.at[dp], cross_send.at[step], cross_recv.at[step])
            for step, place in peers["dp"]
        ]
        for one in crossed:
            one.start()
        for one in crossed:
            one.wait_recv()
        ratios[dp] = ratio[...]
        whole = ratios[0]
        for place in range(1, replicas):
            whole = whole + ratios[place]
        center = whole[:, 0:1] / (replicas * EXB)
        squashed = jax.nn.sigmoid(BETA * sign * (log_ratio - center))
        losses_ref[...] = jnp.broadcast_to(1.0 - squashed, losses_ref.shape)
        grad = -LOSS_SCALE * BETA * sign * squashed * (1.0 - squashed) / counts
        token = jnp.sum(jnp.where(member, grad, 0.0), axis=0, keepdims=True)
        coef_ref[...] = jnp.zeros_like(coef_ref)
        coef_ref[0:1, :] = token
        coef_ref[1:2, :] = token * jnp.exp(stats_ref[0:1, :] - full[0:1, :])
        for one in sent + back + crossed:
            one.wait_send()

    dma = pltpu.SemaphoreType.DMA
    return pl.pallas_call(
        kernel,
        out_shape=[
            jax.ShapeDtypeStruct((8, BLOCK), jnp.float32),
            jax.ShapeDtypeStruct((EXB, 128), jnp.float32),
        ],
        in_specs=[VMEM] + [SMEM] * 3,
        out_specs=[VMEM] * 2,
        scratch_shapes=[
            pltpu.VMEM((shards, 8, width), jnp.float32),
            pltpu.VMEM((8, BLOCK), jnp.float32),
            pltpu.VMEM((EXB, 128), jnp.float32),
            pltpu.VMEM((replicas, EXB, 128), jnp.float32),
            dma((shards,)), dma((shards,)), dma((shards,)), dma((shards,)), dma((replicas,)), dma((replicas,)),
        ],
        compiler_params=pltpu.CompilerParams(collective_id=collective, has_side_effects=True),
    )(stats, lengths, labels, reference)


def input_grad_rows(
    own, grad_stream, plain, grad_qkv, grad_up, qkv_flat, up_weight, gains, end_sums, sizes, collective,
    before,
):
    shards, rows, width = grad_qkv.shape
    hidden = grad_up.shape[2]

    def kernel(
        own_ref, stream_ref, normed_any, qkv_any, up_any, qkvw_any, upw_any, gains_ref, end_ref,
        out_ref, total_ref,
        qkvw, upw, weight_sems, normed, qkv, up, load_sems, sums_ref, *scratch,
    ):
        grid = Grid2(sizes)
        small = SmallSum(shards, sums_ref, total_ref, scratch[:5])
        scratch = scratch[5:]
        parts = scratch[0]
        order = production_order(grid)

        def loads(i):
            place = order[i]
            return [
                pltpu.make_async_copy(normed_any.at[place], normed.at[i % 2], load_sems.at[i, 0]),
                pltpu.make_async_copy(qkv_any.at[place], qkv.at[i % 2], load_sems.at[i, 1]),
                pltpu.make_async_copy(up_any.at[place], up.at[i % 2], load_sems.at[i, 2]),
            ]

        copies = [loads(i) for i in range(shards)]
        weights = [
            pltpu.make_async_copy(qkvw_any, qkvw, weight_sems.at[0]),
            pltpu.make_async_copy(upw_any, upw, weight_sems.at[1]),
        ]
        for copy in copies[0] + weights:
            copy.start()
        sums_ref[...] = jnp.zeros_like(sums_ref)
        small.barrier()
        for copy in weights:
            copy.wait()
        count = [0]

        def produce(slow, fast):
            place = grid.index(slow, fast)
            i = count[0]
            count[0] += 1
            if i + 1 < shards:
                for copy in copies[i + 1]:
                    copy.start()
            for copy in copies[i]:
                copy.wait()
            slot = i % 2

            def columns(index, _):
                here = span(index, 512)
                one = dot_nt(qkv[slot], qkvw[here, :])
                two = dot_nt(up[slot], upw[here, :])
                norm = normed[slot, :, here].astype(jnp.float32)
                parts[place, :, here] = (one * gains_ref[0:1, here] + two * gains_ref[1:2, here]).astype(
                    jnp.bfloat16
                )
                sums_ref[0:1, here] += jnp.sum(one * norm, axis=0, keepdims=True)
                sums_ref[1:2, here] += jnp.sum(one, axis=0, keepdims=True)
                sums_ref[2:3, here] += jnp.sum(two * norm, axis=0, keepdims=True)
                sums_ref[3:4, here] += jnp.sum(two, axis=0, keepdims=True)
                return _

            lax.fori_loop(0, D // 512, columns, 0)

        def made():
            sums_ref[4:8] = end_ref[0:4]
            small.spread()

        run_scatter(grid, sizes, rows, scratch, produce, made, small.collect)
        mine = grid.index(*grid.me)

        def norm_tile(index, _):
            here = span(index, ROW_TILE)
            grad = parts[mine, here].astype(jnp.float32)
            centered, inverse = tile_stats(own_ref[here].astype(jnp.float32))
            normed = centered * inverse
            out_ref[here] = stream_ref[here] + inverse * (
                grad
                - jnp.mean(grad, axis=1, keepdims=True)
                - normed * jnp.mean(grad * normed, axis=1, keepdims=True)
            )
            return _

        lax.fori_loop(0, rows // ROW_TILE, norm_tile, 0)
        small.finish()

    return row_kernel(
        kernel, collective,
        [jax.ShapeDtypeStruct((rows, D), jnp.float32), jax.ShapeDtypeStruct((8, D), jnp.float32)],
        [VMEM, VMEM, ANY, ANY, ANY, ANY, ANY, VMEM, VMEM],
        [VMEM, VMEM],
        [
            pltpu.VMEM(qkv_flat.shape, jnp.bfloat16),
            pltpu.VMEM(up_weight.shape, jnp.bfloat16),
            pltpu.SemaphoreType.DMA((2,)),
            pltpu.VMEM((2, rows, D), jnp.bfloat16),
            pltpu.VMEM((2, rows, width), jnp.bfloat16),
            pltpu.VMEM((2, rows, hidden), jnp.bfloat16),
            pltpu.SemaphoreType.DMA((shards, 3)),
            pltpu.VMEM((8, D), jnp.float32),
        ]
        + SmallSum.scratch(shards)
        + sum_scratch(sizes, rows),
        1,
        before,
    )(own, grad_stream, plain, grad_qkv, grad_up, qkv_flat, up_weight, gains, end_sums)


def settle_halves(core, mine, backs, shapes, places, passed=(), before=()):
    depth, most = 4, 256
    count = len(mine[0])
    steps = []
    for index, (_, _, rows) in enumerate(places):
        size = min(most, rows)
        for which in (0, 1):
            for first in range(0, rows, size):
                steps.append((index, which, first, size))
    width = max(arrays[0].shape[1] for arrays in mine)
    deep = [shape for shape in shapes if len(shape) == 3]

    def kernel(core_ref, *refs):
        sources = [
            [refs[(index * 2 + which) * count : (index * 2 + which + 1) * count] for which in (0, 1)]
            for index, _, _ in places
        ]
        rest = refs[2 * count * len(mine) :]
        through, rest = rest[: len(passed)], rest[len(passed) + len(before) :]
        outs, rest = rest[: len(shapes)], rest[len(shapes) :]
        passed_out, rest = rest[: len(passed)], rest[len(passed) :]
        taken, given, split, in_sems, out_sems, pass_sems, *staged = rest
        ins = [pltpu.make_async_copy(through[i], here, pass_sems.at[0, i]) for i, here in enumerate(staged)]
        copies = [pltpu.make_async_copy(here, passed_out[i], pass_sems.at[1, i]) for i, here in enumerate(staged)]
        for copy in ins:
            copy.start()

        def loads(i):
            index, which, first, size = steps[i]
            number, begin, _ = places[index]
            columns = mine[number][0].shape[1]
            return [
                pltpu.make_async_copy(
                    source.at[pl.ds(begin + first, size)],
                    taken.at[i % depth, j, pl.ds(0, size), pl.ds(0, columns)],
                    in_sems.at[i % depth, j],
                )
                for j, source in enumerate(sources[index][which])
            ]

        def store(i):
            index, which, first, size = steps[i]
            number, _, rows = places[index]
            columns = mine[number][0].shape[1]
            place = core_ref[0] if which == 0 else 1 - core_ref[0]
            if len(shapes[index]) == 2 and shapes[index][0] == rows:
                there = outs[index].at[pl.ds(first, size), pl.ds(pl.multiple_of(place * columns, columns), columns)]
            else:
                there = outs[index].at[pl.ds(pl.multiple_of(place * rows + first, size), size)]
            here = given.at[i % depth, pl.ds(0, size), pl.ds(0, columns)]
            if len(shapes[index]) == 3:
                here = split.at[i % depth, pl.ds(0, size)]
            return pltpu.make_async_copy(here, there, out_sems.at[i % depth])

        for i in range(min(depth - 1, len(steps))):
            for copy in loads(i):
                copy.start()
        for i, (index, which, first, size) in enumerate(steps):
            if i + depth - 1 < len(steps):
                for copy in loads(i + depth - 1):
                    copy.start()
            for copy in loads(i):
                copy.wait()
            if i >= depth:
                store(i - depth).wait()
            columns = mine[places[index][0]][0].shape[1]

            def convert(row, _, i=i, index=index, columns=columns):
                here = span(row, 32)
                found = taken[i % depth, 0, here, :columns].astype(jnp.float32)
                for j in range(1, count):
                    found = found + taken[i % depth, j, here, :columns].astype(jnp.float32)
                if len(shapes[index]) == 3:
                    for head in range(shapes[index][1]):
                        split[i % depth, here, head, :] = found[
                            :, head * shapes[index][2] : (head + 1) * shapes[index][2]
                        ]
                else:
                    given[i % depth, here, :columns] = found
                return _

            lax.fori_loop(0, size // 32, convert, 0)
            store(i).start()
            if i == 0:
                for taking, copy in zip(ins, copies):
                    taking.wait()
                    copy.start()
        for i in range(max(len(steps) - depth, 0), len(steps)):
            store(i).wait()
        for copy in copies:
            copy.wait()

    dma = pltpu.SemaphoreType.DMA
    return pl.pallas_call(
        kernel,
        out_shape=[jax.ShapeDtypeStruct(shape, jnp.float32) for shape in shapes]
        + [jax.ShapeDtypeStruct(array.shape, array.dtype) for array in passed],
        in_specs=[SMEM] + [ANY] * (2 * count * len(mine) + len(passed) + len(before)),
        out_specs=[ANY] * (len(shapes) + len(passed)),
        scratch_shapes=[
            pltpu.VMEM((depth, count, most, width), jnp.bfloat16),
            pltpu.VMEM((depth, most, width), jnp.float32),
            pltpu.VMEM((depth, most) + deep[0][1:] if deep else (1, 8, 128), jnp.float32),
            dma((depth, count)),
            dma((depth,)),
            dma((2, max(len(passed), 1))),
        ]
        + [pltpu.VMEM(array.shape, array.dtype) for array in passed],
        cost_estimate=pl.CostEstimate(flops=1, bytes_accessed=1, transcendentals=0),
        compiler_params=pltpu.CompilerParams(vmem_limit_bytes=VMEM_LIMIT),
    )(core, *[array for pair in zip(mine, backs) for half in pair for array in half], *passed, *before)


def row_of(vector):
    return vector.astype(jnp.float32)[None, :]


def held(values):
    return lax.optimization_barrier(values)


def half_of(values, which):
    half = values.shape[1] // 2
    return lax.dynamic_slice_in_dim(values, which * half, half, 1)


def pairs(step):
    return [(place, place ^ step) for place in range(lax.axis_size("dp"))]


class PairSum:
    def __init__(self, away, mine):
        self.plain = lax.axis_size("dp") != 4
        self.core = lax.rem(lax.axis_index("dp"), 2)
        came = lax.ppermute(away, "dp", pairs(1))
        self.sum = (mine.astype(jnp.float32) + came.astype(jnp.float32)).astype(jnp.bfloat16)

    def cross(self):
        if self.plain:
            none = jnp.zeros_like(self.sum)
            both = jnp.stack([jnp.where(self.core == which, self.sum, none) for which in (0, 1)])
            self.other, self.first_back = lax.psum(both, "dp"), self.sum
        else:
            self.other = lax.ppermute(self.sum, "dp", pairs(2))
            self.first_back = lax.ppermute(self.sum, "dp", pairs(1))
        return self


def after(values, *earlier):
    def kernel(*refs):
        del refs

    return pl.pallas_call(
        kernel,
        out_shape=[jax.ShapeDtypeStruct(v.shape, v.dtype) for v in values],
        in_specs=[ANY] * (len(values) + len(earlier)),
        out_specs=[ANY] * len(values),
        input_output_aliases={i: i for i in range(len(values))},
    )(*values, *earlier)


def give_back(sums, earlier):
    if sums[0].plain:
        for one in sums:
            one.mine, one.back = [one.other[0]], [one.other[1]]
        return
    for one, other in zip(sums, after([one.other for one in sums], earlier)):
        one.mine = [one.sum, other]
        one.back = [one.first_back, lax.ppermute(other, "dp", pairs(1))]


def settle_all(sums, shapes, places, passed=(), before=()):
    core = jnp.zeros((1,), jnp.int32) if sums[0].plain else sums[0].core[None]
    return settle_halves(core, [one.mine for one in sums], [one.back for one in sums], shapes, places, passed, before)


def pair_product(product):
    core = lax.rem(lax.axis_index("dp"), 2)
    return PairSum(product(1 - core).astype(jnp.bfloat16), held(product(core)))


def sum_over_dp(values):
    if lax.axis_size("dp") != 4:
        return lax.psum(values, "dp")
    for step in (1, 2):
        values = values + lax.ppermute(values, "dp", pairs(step))
    return values


def per_device(
    hidden, targets, lengths, labels, ref_logps, ln1_gain, ln1_bias, ln2_gain, ln2_bias, qkv_weight, qv_bias,
    out_weight, up_weight, up_bias, down_weight, branch_bias, lnf_gain, lnf_bias, head_weight,
):
    sizes = lines_of(lax.axis_size("seq"))
    own = hidden[0]
    local_heads = qkv_weight.shape[1]
    local_vocab = head_weight.shape[1]
    local_hidden = up_weight.shape[1]
    width = local_heads * 3 * HEAD_DIM
    inner = local_heads * HEAD_DIM
    qv_float = qv_bias.astype(jnp.float32)
    full_bias = jnp.concatenate(
        [qv_float[:, :HEAD_DIM], jnp.zeros_like(qv_float[:, :HEAD_DIM]), qv_float[:, HEAD_DIM:]], axis=-1
    ).reshape(1, width)
    qkv_flat = qkv_weight.reshape(D, width)
    out_flat = out_weight.reshape(inner, D)
    block_lengths = lengths[0]
    norms = jnp.concatenate([row_of(v) for v in (ln1_gain, ln1_bias, ln2_gain, ln2_bias)], axis=0)
    plain, first_full, second_full, qkv, act, slope, *planes = open_rows(
        own, sizes, 0, norms, qkv_flat, full_bias, up_weight, row_of(up_bias), block_lengths
    )
    flat_qkv = qkv.reshape(BLOCK, width)
    ctx, lse = attention_forward(flat_qkv, block_lengths, local_heads)
    shards, rows = plain.shape[0], plain.shape[1]
    end_norms = jnp.concatenate([row_of(v) for v in (lnf_gain, lnf_bias, branch_bias)], axis=0)
    output, final, normed, inverse = branch_rows(
        own, ctx.reshape(shards, rows, inner), act, out_flat, down_weight, end_norms, sizes, 1
    )
    targets_col = targets[0][:, None]
    final_full, weights, stats = logit_rows(final, head_weight, targets_col, sizes, 2)

    coef, losses = score_rows(
        stats, block_lengths, labels[0], ref_logps[0], sizes, lax.axis_size("dp"), 6
    )
    vocab_ids = lax.axis_index("seq") * local_vocab + jnp.arange(local_vocab, dtype=jnp.int32)
    grad_logits = held((
        jnp.where(vocab_ids[None, :] == targets_col, coef[0][:, None], 0.0)
        - weights.reshape(BLOCK, local_vocab).astype(jnp.float32) * coef[1][:, None]
    ).astype(jnp.bfloat16))
    final_rows = final_full.reshape(BLOCK, D)
    head_sum = pair_product(lambda which: dot_tn(half_of(final_rows, which), grad_logits)).cross()

    grad_stream, grad_own, end_sums = final_grad_rows(
        grad_logits.reshape(shards, rows, local_vocab), head_weight, normed, inverse, row_of(lnf_gain), sizes, 3,
        (head_sum.sum,),
    )
    grad_ctx, grad_up, up_sums, *halves = branch_grad_rows(
        grad_own, out_flat, down_weight, slope, ctx.reshape(shards, rows, inner), act, second_full, sizes, 4,
        (head_sum.first_back,),
    )
    sums = [PairSum(*halves[2 * i : 2 * i + 2]).cross() for i in range(2)]
    grad_qkv, qkv_sums = attention_backward(
        flat_qkv, block_lengths, local_heads, ctx, lse, grad_ctx.reshape(BLOCK, inner), planes
    )
    (first_rows,) = after([first_full.reshape(BLOCK, D)], sums[0].sum, sums[1].sum)
    sums.append(pair_product(lambda which: dot_tn(half_of(first_rows, which), grad_qkv)).cross())
    qkv_sums = qkv_sums.reshape(local_heads, 3 * HEAD_DIM)
    qv_grad = jnp.concatenate([qkv_sums[:, :HEAD_DIM], qkv_sums[:, 2 * HEAD_DIM :]], axis=-1)
    split = local_heads * 2 * HEAD_DIM
    biases = jnp.concatenate([qv_grad.reshape(-1), up_sums[0]])
    biases = jnp.pad(biases[None, :], ((0, 0), (0, D - biases.shape[0])))
    give_back([head_sum], grad_qkv)
    gains = jnp.concatenate([row_of(ln1_gain), row_of(ln2_gain)], axis=0)
    grad_input, group_sums = input_grad_rows(
        own, grad_stream, plain, grad_qkv.reshape(shards, rows, width), grad_up, qkv_flat, up_weight, gains,
        end_sums, sizes, 5, [one.first_back for one in sums],
    )
    give_back(sums[:2], group_sums)
    head_grad, output, grad_input = settle_all(
        [head_sum], [(D, local_vocab)], [(0, 0, D // 2)], (output, grad_input)
    )
    out_grad, down_grad, up_grad = settle_all(
        sums[:2],
        [(inner, D), (local_hidden, D), (D, local_hidden)],
        [(0, 0, inner), (0, inner, local_hidden), (1, 0, D // 2)],
        before=(head_grad,),
    )
    small = sum_over_dp(jnp.concatenate([group_sums[:7], biases], axis=0))
    give_back(sums[2:], head_grad)
    (qkv_grad,) = settle_all(sums[2:], [qkv_weight.shape], [(0, 0, D // 2)])
    return (
        losses[:, 0][None],
        output[None],
        grad_input[None],
        small[0],
        small[1],
        small[2],
        small[3],
        qkv_grad,
        small[7, :split].reshape(local_heads, 2 * HEAD_DIM),
        out_grad.reshape(out_weight.shape),
        up_grad,
        small[7, split : split + local_hidden],
        down_grad,
        small[6],
        small[4],
        small[5],
        head_grad,
    )


def solution(mesh):
    return jax.shard_map(
        per_device,
        mesh=mesh,
        in_specs=(
            P("dp", "seq", None),
            P("dp", None),
            P("dp", None),
            P("dp", None),
            P("dp", None),
            P(),
            P(),
            P(),
            P(),
            P(None, "seq", None),
            P("seq", None),
            P("seq", None, None),
            P(None, "seq"),
            P("seq"),
            P("seq", None),
            P(),
            P(),
            P(),
            P(None, "seq"),
        ),
        out_specs=(
            P("dp", None),
            P("dp", "seq", None),
            P("dp", "seq", None),
            P(),
            P(),
            P(),
            P(),
            P(None, "seq", None),
            P("seq", None),
            P("seq", None, None),
            P(None, "seq"),
            P("seq"),
            P("seq", None),
            P(),
            P(),
            P(),
            P(None, "seq"),
        ),
        check_vma=False,
    )
```
